32 devices in a mesh: batch: 4 (over y, x), seq: 8 (over z, core).
Axes of the slice: x: 2, y: 2, z: 4, core: 2. Of those that a mesh axis runs over, the one named last changes fastest.
Arguments:
- states: bfloat16 [16384, 768], P(('batch', 'seq')), may hold values from -6 to 6
- lengths: int32 [16], replicated, may hold values from 64 to 1024, as said below
- first_gain: bfloat16 [768], replicated, may hold values from 0.5 to 1.5
- query_weight: bfloat16 [768, 768], replicated, may hold values from -0.21875 to 0.21875
- key_weight: bfloat16 [768, 768], replicated, may hold values from -0.21875 to 0.21875
- value_weight: bfloat16 [768, 768], replicated, may hold values from -0.21875 to 0.21875
- output_weight: bfloat16 [768, 768], replicated, may hold values from -0.875 to 0.875
- second_gain: bfloat16 [768], replicated, may hold values from 0.5 to 1.5
- gate_weight: bfloat16 [768, 2048], replicated, may hold values from -0.21875 to 0.21875
- up_weight: bfloat16 [768, 2048], replicated, may hold values from -0.21875 to 0.21875
- down_weight: bfloat16 [2048, 768], replicated, may hold values from -0.125 to 0.125
- cotangent: bfloat16 [16384, 768], P(('batch', 'seq')), may hold values from -6 to 6
Outputs:
- layer_out: bfloat16 [16384, 768], P(('batch', 'seq'))
- input_grad: bfloat16 [16384, 768], P(('batch', 'seq'))
- grad_first: float32 [768], replicated
- grad_query: float32 [768, 768], P('seq', 'batch')
- grad_key: float32 [768, 768], P('seq', 'batch')
- grad_value: float32 [768, 768], P('seq', 'batch')
- grad_output: float32 [768, 768], P('seq', 'batch')
- grad_second: float32 [768], replicated
- grad_gate: float32 [768, 2048], P('seq', 'batch')
- grad_up: float32 [768, 2048], P('seq', 'batch')
- grad_down: float32 [2048, 768], P('seq', 'batch')
The draws below stay inside these ranges and needn't reach their ends.
Inputs may be any that keep to these rules, and one draw needn't show every extreme that they name: `lengths`: in each aligned block of 2 sequences exactly one sequence, drawn from the seed, has length 1024; some sequence has length 64.
All inputs are finite; a program needn't handle non-finite values.
Results may differ from the reference program's by a relative error of at most 0.017.
Values may be sent and summed in bfloat16 or wider, within the bound.
No kernel may reach another device: no remote copies, remote signals or barrier semaphores. Data moves between devices by JAX's collectives and lax.ppermute only.
A program may use at most 128 MiB of HBM per device.

```python
import math
from functools import partial
import jax
import jax.numpy as jnp
from jax import lax

D = 768
HEADS = 12
HEAD_FEATURES = 64
FF = 2048
SEQ_GRP = 2
MAXLEN = 1024
MINLEN = 64
GROUP = 4
SEQS = 16
TOKENS = 16384
N_BATCH = 4
N_SEQ = 8


def draw_lengths(key, part):
    key = jax.random.fold_in(key, 7)
    key_exponent, key_shortfall, key_full, key_group = jax.random.split(key, 4)
    group_count = SEQS // SEQ_GRP
    length_span = MAXLEN - MINLEN
    exponent = jax.random.randint(key_exponent, (SEQS,), 0, 4)
    reach_bound = length_span // jnp.left_shift(1, 2 * exponent) + 1
    shortfall = jax.random.randint(key_shortfall, (SEQS,), 0, reach_bound)
    slot_index = jnp.arange(SEQS, dtype=jnp.int32) % SEQ_GRP
    group_index = jnp.arange(SEQS, dtype=jnp.int32) // SEQ_GRP
    full_slot = jnp.repeat(jax.random.randint(key_full, (group_count,), 0, SEQ_GRP), SEQ_GRP)
    least_group = jax.random.randint(key_group, (), 0, group_count)
    drawn = jnp.minimum(MAXLEN - shortfall, MAXLEN - 1)
    drawn = jnp.where(slot_index == full_slot, MAXLEN, drawn)
    least_slot = (full_slot + 1) % SEQ_GRP
    drawn = jnp.where((group_index == least_group) & (slot_index == least_slot), MINLEN, drawn)
    return drawn.astype(jnp.int32)


def block_levels(rng, extent, cuts, least, largest):
    gain = 1.0
    for axis_at, shards_of in cuts:
        heights = jax.random.uniform(jax.random.fold_in(jax.random.fold_in(rng, 6), axis_at), (shards_of,), jnp.float32, least / len(cuts), largest / len(cuts))
        gain = gain * jnp.repeat(jnp.exp(heights), extent[axis_at] // shards_of).reshape((-1,) + (1,) * (len(extent) - 1 - axis_at))
    return gain


def noise(key, dims, deviation, bound, pieces=(), held_as=jnp.bfloat16):
    entries = jax.random.normal(key, dims, jnp.float32) * deviation
    if len(pieces) > 0:
        entries = block_levels(key, dims, pieces, -0.22, 0.18) * entries
    return jnp.clip(entries, min=-bound, max=bound).astype(held_as)


def setup_inputs(seed: int = 0) -> dict:
    streams_of = jax.random.split(jax.random.key(seed), 13)
    return {
        "states": noise(streams_of[0], (TOKENS, D), 1.0, 6.0, ((0, 32),)),
        "lengths": draw_lengths(jax.random.fold_in(streams_of[12], 71), 0),
        "first_gain": jnp.clip(1.0 + 0.1 * jax.random.normal(streams_of[2], (D,), jnp.float32), 0.5, 1.5).astype(jnp.bfloat16),
        "query_weight": noise(streams_of[3], (D, D), D ** -0.5, 0.21875),
        "key_weight": noise(streams_of[4], (D, D), D ** -0.5, 0.21875),
        "value_weight": noise(streams_of[5], (D, D), D ** -0.5, 0.21875),
        "output_weight": noise(streams_of[6], (D, D), (D // 16) ** -0.5, 0.875),
        "second_gain": jnp.clip(1.0 + 0.1 * jax.random.normal(streams_of[7], (D,), jnp.float32), 0.5, 1.5).astype(jnp.bfloat16),
        "gate_weight": noise(streams_of[8], (D, FF), D ** -0.5, 0.21875),
        "up_weight": noise(streams_of[9], (D, FF), D ** -0.5, 0.21875),
        "down_weight": noise(streams_of[10], (FF, D), FF ** -0.5, 0.125),
        "cotangent": noise(streams_of[11], (TOKENS, D), 1.0, 6.0, ((0, 32),)),
    }


epsilon = 1e-06
masked_score = -1e+30
highest_setting = lax.Precision.HIGHEST

@jax.custom_vjp
def lowered_copy(v):
    return lax.optimization_barrier(v.astype(jnp.bfloat16)).astype(jnp.float32)

@jax.custom_vjp
def low_back(v):
    return v

def low_keep(v):
    return (lowered_copy(v), None)

def low_pass(kept, grad):
    return (grad,)

def back_keep(v):
    return (v, None)

def back_low(kept, grad):
    return (lowered_copy(grad),)
lowered_copy.defvjp(low_keep, low_pass)
low_back.defvjp(back_keep, back_low)

def normalize(values, gain_vector):
    factor = lax.rsqrt(lax.optimization_barrier(jnp.mean(values * values, axis=-1, keepdims=True)) + epsilon)
    return values * factor * gain_vector

def rope_tables(positions):
    middle = HEAD_FEATURES // 2
    frequency = 10000.0 ** (-jnp.arange(middle, dtype=jnp.float32) * 2.0 / HEAD_FEATURES)
    angles = positions.astype(jnp.float32)[:, None] * frequency[None, :]
    angles = jnp.concatenate([angles, angles], axis=1)
    return (jnp.cos(angles), jnp.sin(angles))

def rotate(values, cosine_table, sine_table):
    middle = values.shape[-1] // 2
    turned = jnp.concatenate([-values[..., middle:], values[..., :middle]], axis=-1)
    return values * cosine_table + turned * sine_table

def head_attention(live_rows, packed):
    head_queries, head_keys, head_values = packed
    positions = jnp.arange(MAXLEN, dtype=jnp.int32)
    score_matrix = jnp.einsum('nrw,niw->nri', head_queries, head_keys, precision=highest_setting) * (1.0 / math.sqrt(HEAD_FEATURES))
    score_matrix = low_back(score_matrix)
    causal = positions[:, None] >= positions[None, :]
    score_matrix = jnp.where(causal[None], score_matrix, masked_score)
    row_max = lax.optimization_barrier(jnp.max(score_matrix, axis=-1, keepdims=True))
    weights = jnp.exp(score_matrix - row_max)
    attention_probability = weights / lax.optimization_barrier(jnp.sum(weights, axis=-1, keepdims=True))
    rows_mixed = jnp.einsum('cgs,csz->cgz', lowered_copy(attention_probability), head_values, precision=highest_setting)
    return rows_mixed * live_rows

def head_major(values):
    return jnp.transpose(values, (2, 0, 1, 3))

def layer_forward(lengths_block, states, first_gain, query_weight, key_weight, value_weight, output_weight, second_gain, gate_weight, up_weight, down_weight):
    sequence_count = states.shape[0]
    positions = jnp.arange(MAXLEN, dtype=jnp.int32)
    live_rows = (positions[None, :] < lengths_block[:, None]).astype(jnp.float32)[:, :, None]
    normed = lowered_copy(normalize(states, first_gain))
    cosine_table, sine_table = rope_tables(positions)
    cosine_table = cosine_table[:, None, :]
    sine_table = sine_table[:, None, :]

    def project(weight_matrix):
        product = jnp.einsum('bld,de->ble', normed, weight_matrix, precision=highest_setting)
        return product.reshape(sequence_count, MAXLEN, HEADS, HEAD_FEATURES)
    queries = lowered_copy(rotate(low_back(project(query_weight)), cosine_table, sine_table))
    key_heads = lowered_copy(rotate(low_back(project(key_weight)), cosine_table, sine_table))
    value_heads = lowered_copy(low_back(project(value_weight)))
    attended = lax.map(jax.checkpoint(partial(head_attention, live_rows)), (head_major(queries), head_major(key_heads), head_major(value_heads)))
    attended = jnp.transpose(attended, (1, 2, 0, 3)).reshape(sequence_count, MAXLEN, D)
    attended = lowered_copy(low_back(attended))
    hidden = states + low_back(jnp.einsum('bld,de->ble', attended, output_weight, precision=highest_setting))
    second_normed = lowered_copy(normalize(hidden, second_gain))
    gate_values = low_back(jnp.einsum('bld,df->blf', second_normed, gate_weight, precision=highest_setting))
    up_values = low_back(jnp.einsum('bld,df->blf', second_normed, up_weight, precision=highest_setting))
    activated = lowered_copy(jax.nn.silu(gate_values) * up_values)
    down_branch = low_back(jnp.einsum('blf,fd->bld', activated, down_weight, precision=highest_setting))
    return (hidden + down_branch) * live_rows

def reference(states, lengths, first_gain, query_weight, key_weight, value_weight, output_weight, second_gain, gate_weight, up_weight, down_weight, cotangent):
    step_size = math.gcd(SEQS, max(1, 4096 // MAXLEN))
    step_count = SEQS // step_size
    params = tuple((weight.astype(jnp.float32) for weight in (first_gain, query_weight, key_weight, value_weight, output_weight, second_gain, gate_weight, up_weight, down_weight)))

    def to_sequences(row_array):
        shaped = row_array.astype(jnp.float32).reshape(N_BATCH, N_SEQ // GROUP, GROUP, SEQ_GRP, MAXLEN // GROUP, D)
        shaped = jnp.transpose(shaped, (0, 1, 3, 2, 4, 5))
        return shaped.reshape(step_count, step_size, MAXLEN, D)

    def from_sequences(blocks):
        shaped = blocks.reshape(N_BATCH, N_SEQ // GROUP, SEQ_GRP, GROUP, MAXLEN // GROUP, D)
        return jnp.transpose(shaped, (0, 1, 3, 2, 4, 5)).reshape(TOKENS, D)
    states_split = to_sequences(states)
    cotangent_split = to_sequences(cotangent)
    lengths_split = lengths.astype(jnp.int32).reshape(step_count, step_size)

    def one_step(totals, block_item):
        block_states, block_lengths, block_cotangent = block_item
        result, pullback = jax.vjp(partial(layer_forward, block_lengths), block_states, *params)
        gradients = pullback(block_cotangent)
        totals = jax.tree.map(jnp.add, totals, tuple(gradients[1:]))
        return (totals, (result.astype(jnp.bfloat16), gradients[0].astype(jnp.bfloat16)))
    starting = tuple((jnp.zeros(parameter.shape, jnp.float32) for parameter in params))
    totals, outputs = lax.scan(one_step, starting, (states_split, lengths_split, cotangent_split))
    return (from_sequences(outputs[0]), from_sequences(outputs[1]), totals[0], totals[1], totals[2], totals[3], totals[4], totals[5], totals[6], totals[7], totals[8])
```

```python
import functools
import math

import jax
import jax.numpy as jnp
import numpy as np
from jax import lax
from jax.experimental import pallas as pl
from jax.experimental.pallas import tpu as pltpu
from jax.sharding import PartitionSpec as P

HEADS = 12
HEAD_FEATURES = 64
MAXLEN = 1024
GROUP = 4
PIECE = MAXLEN // GROUP
PAIR = 2 * HEAD_FEATURES

epsilon = 1e-06
masked_score = -1e30
f32 = jnp.float32
bf16 = jnp.bfloat16
MIB = 1024 * 1024


def mm(a, b):
    return lax.dot_general(a, b, (((1,), (0,)), ((), ())), preferred_element_type=f32)


def mm_nt(a, b):
    return lax.dot_general(a, b, (((1,), (1,)), ((), ())), preferred_element_type=f32)


def mm_tn(a, b):
    return lax.dot_general(a, b, (((0,), (0,)), ((), ())), preferred_element_type=f32)


def call(body, grid, in_specs, out_specs, out_shape, scratch=(), aliases=None, vmem=56, flops=0, nbytes=0):
    return pl.pallas_call(
        body,
        grid_spec=pltpu.PrefetchScalarGridSpec(
            num_scalar_prefetch=1,
            grid=grid,
            in_specs=in_specs,
            out_specs=out_specs,
            scratch_shapes=list(scratch),
        ),
        out_shape=out_shape,
        input_output_aliases=aliases or {},
        compiler_params=pltpu.CompilerParams(
            dimension_semantics=("arbitrary",) * len(grid), vmem_limit_bytes=vmem * MIB
        ),
        cost_estimate=pl.CostEstimate(flops=flops, bytes_accessed=nbytes, transcendentals=0),
    )


def whole(shape):
    return pl.BlockSpec(shape, lambda *a: (0,) * len(shape))


def sds(shape, dtype):
    return jax.ShapeDtypeStruct(shape, dtype)


def rope_tables():
    middle = HEAD_FEATURES // 2
    frequency = 10000.0 ** (-np.arange(middle, dtype=np.float64) * 2.0 / HEAD_FEATURES)
    angles = np.arange(MAXLEN, dtype=np.float64)[:, None] * frequency[None, :]
    cosine, sine = np.cos(angles), np.sin(angles)
    none = np.zeros_like(sine)
    table = np.stack(
        [
            np.concatenate([cosine, cosine] * 2, axis=1),
            np.concatenate([-sine, none] * 2, axis=1),
            np.concatenate([none, sine] * 2, axis=1),
        ]
    )
    return table.astype(np.float32)


def rotate(u, table, sign):
    up = pltpu.roll(u, PAIR - HEAD_FEATURES // 2, 1)
    down = pltpu.roll(u, HEAD_FEATURES // 2, 1)
    if sign > 0:
        return u * table[0] + (up * table[1] + down * table[2])
    return u * table[0] - (up * table[1] + down * table[2])


def project_body(s, own, part, gain, wq, wk, wv, table, *rest):
    qkv, normed = rest[-2:]
    x = jnp.where(pl.program_id(0) == s[0], own[...], part[...]).astype(f32)
    r = lax.rsqrt(jnp.mean(x * x, axis=-1, keepdims=True) + epsilon)
    low = (x * r * gain[...].astype(f32)).astype(bf16)
    normed[...] = low
    width = wq.shape[1]
    for m, w in enumerate((wq, wk, wv)):
        u = mm(low, w[...])
        if m == 0:
            u = u * (1.0 / math.sqrt(HEAD_FEATURES))
        for p in range(width // PAIR):
            v = u[:, p * PAIR : (p + 1) * PAIR]
            if m < 2:
                v = rotate(v, table, 1)
            at = m * width + p * PAIR
            qkv[:, at : at + PAIR] = v.astype(bf16)


def project(scalars, own, part, half, gain, weights, table, filled):
    width = weights[0].shape[0]
    cols = width // 2
    place = lambda t, s: (s[half] * 2 + t, 0)
    weight_spec = pl.BlockSpec((width, cols), lambda t, s: (0, s[0]))
    in_specs = [
        whole((PIECE, width)),
        whole((PIECE, width)),
        whole((1, width)),
        weight_spec,
        weight_spec,
        weight_spec,
        pl.BlockSpec((3, PIECE, PAIR), lambda t, s: (0, s[half] * 2 + t, 0)),
    ]
    args = [scalars, own, part, gain, *weights, table]
    aliases = None
    if filled is not None:
        in_specs += [pl.BlockSpec(memory_space=pl.ANY)] * 2
        aliases = {len(args): 0, len(args) + 1: 1}
        args += list(filled)
    return call(
        project_body,
        (2,),
        in_specs,
        [pl.BlockSpec((PIECE, 3 * cols), place), pl.BlockSpec((PIECE, width), place)],
        [sds((MAXLEN, 3 * cols), bf16), sds((MAXLEN, width), bf16)],
        aliases=aliases,
        flops=2 * 512 * width * 3 * cols,
        nbytes=4 * MIB,
    )(*args)


def head_mask(h):
    lane = lax.broadcasted_iota(jnp.int32, (1, PAIR), 1)
    return lane < HEAD_FEATURES if h == 0 else lane >= HEAD_FEATURES


def attend_body(s, q, k, v, out, lse):
    row = lax.broadcasted_iota(jnp.int32, (PIECE, PIECE), 0)
    col = lax.broadcasted_iota(jnp.int32, (PIECE, PIECE), 1)
    lane = lax.broadcasted_iota(jnp.int32, (PIECE, PAIR), 1)
    for b in range(GROUP):
        at = b * PIECE
        joined, logs = None, None
        for h in range(2):
            qh = jnp.where(head_mask(h), q[at : at + PIECE, :], jnp.zeros((), bf16))
            near = mm_nt(qh, k[at : at + PIECE, :])
            near = jnp.where(row >= col, near, masked_score)
            top = jnp.max(near, axis=-1, keepdims=True)
            if b > 0:
                far = mm_nt(qh, k[:at, :])
                top = jnp.maximum(top, jnp.max(far, axis=-1, keepdims=True))
            near = jnp.exp(near - top)
            total = jnp.sum(near, axis=-1, keepdims=True)
            mixed = mm(near.astype(bf16), v[at : at + PIECE, :])
            if b > 0:
                far = jnp.exp(far - top)
                total = total + jnp.sum(far, axis=-1, keepdims=True)
                mixed = mixed + mm(far.astype(bf16), v[:at, :])
            mixed = mixed * (1.0 / total)
            logged = top + jnp.log(total)
            if h == 0:
                joined, logs = mixed, jnp.broadcast_to(logged, (PIECE, PAIR))
            else:
                joined = jnp.where(head_mask(0), joined, mixed)
                logs = jnp.where(lane == 0, logs, logged)
        slot = at + lax.broadcasted_iota(jnp.int32, (PIECE, 1), 0)
        out[at : at + PIECE, :] = jnp.where(slot < s[2], joined, 0.0).astype(bf16)
        lse[0, :, at : at + PIECE] = jnp.transpose(logs)[:8]


def attend(scalars, qkv):
    pairs = qkv.shape[1] // 3 // PAIR
    spec = lambda m: pl.BlockSpec((MAXLEN, PAIR), lambda p, s, m=m: (0, m * pairs + p))
    return call(
        attend_body,
        (pairs,),
        [spec(0), spec(1), spec(2)],
        [pl.BlockSpec((MAXLEN, PAIR), lambda p, s: (0, p)), pl.BlockSpec((1, 8, MAXLEN), lambda p, s: (p, 0, 0))],
        [sds((MAXLEN, pairs * PAIR), bf16), sds((pairs, 8, MAXLEN), f32)],
        flops=8 * 1000 * MIB,
        nbytes=4 * MIB,
    )(scalars, qkv, qkv, qkv)


def attend_back_body(s, q, k, v, o, lse, own, part, wo, table, out, da, dq, dk, dv):
    core = s[0]
    for half in range(2):
        for source, place in ((own, core), (part, 1 - core)):
            at = pl.multiple_of(half * 2 * PIECE + place * PIECE, PIECE)
            slot = at + lax.broadcasted_iota(jnp.int32, (PIECE, 1), 0)
            d = mm_nt(source[half], wo[...])
            da[pl.ds(at, PIECE), :] = jnp.where(slot < s[2], d, 0.0).astype(bf16)
    product = da[...].astype(f32) * o[...].astype(f32)
    ones = jnp.where(
        lax.broadcasted_iota(jnp.int32, (8, PAIR), 0)
        == lax.broadcasted_iota(jnp.int32, (8, PAIR), 1) // HEAD_FEATURES,
        1.0,
        0.0,
    ).astype(f32)
    inner = lax.dot_general(
        ones, product, (((1,), (1,)), ((), ())), preferred_element_type=f32, precision=lax.Precision.HIGHEST
    )
    dq[...] = jnp.zeros_like(dq)
    key = lax.broadcasted_iota(jnp.int32, (PIECE, PIECE), 0)
    query = lax.broadcasted_iota(jnp.int32, (PIECE, PIECE), 1)
    zero = jnp.zeros((), bf16)
    for b in range(GROUP):
        at = b * PIECE
        kb, vb = k[at : at + PIECE, :], v[at : at + PIECE, :]
        key_grad, value_grad = None, None
        for h in range(2):
            mask = head_mask(h)
            kh = jnp.where(mask, kb, zero)
            vh = jnp.where(mask, vb, zero)
            for a in range(b, GROUP):
                to = a * PIECE
                qa = jnp.where(mask, q[to : to + PIECE, :], zero)
                ga = jnp.where(mask, da[to : to + PIECE, :], zero)
                score = mm_nt(kb, qa) - lse[0, h : h + 1, to : to + PIECE]
                if a == b:
                    score = jnp.where(query >= key, score, masked_score)
                prob = jnp.exp(score)
                delta = mm_nt(vb, ga) - inner[h : h + 1, to : to + PIECE]
                ds = (prob * delta).astype(bf16)
                vg = mm(prob.astype(bf16), ga)
                kg = mm(ds, qa)
                value_grad = vg if value_grad is None else value_grad + vg
                key_grad = kg if key_grad is None else key_grad + kg
                dq[to : to + PIECE, :] += mm_tn(ds, kh)
        dk[at : at + PIECE, :] = key_grad
        dv[at : at + PIECE, :] = value_grad
    out[0] = rotate(dq[...] * (1.0 / math.sqrt(HEAD_FEATURES)), table, -1).astype(bf16)
    out[1] = rotate(dk[...], table, -1).astype(bf16)
    out[2] = dv[...].astype(bf16)


def attend_back(scalars, qkv, attn, lse, own, part, wo, table):
    pairs = attn.shape[1] // PAIR
    width = wo.shape[1]
    spec = lambda m: pl.BlockSpec((MAXLEN, PAIR), lambda p, s, m=m: (0, m * pairs + p))
    return call(
        attend_back_body,
        (pairs,),
        [
            spec(0),
            spec(1),
            spec(2),
            spec(0),
            pl.BlockSpec((1, 8, MAXLEN), lambda p, s: (p, 0, 0)),
            whole((2, PIECE, width)),
            whole((2, PIECE, width)),
            pl.BlockSpec((PAIR, width), lambda p, s: (s[0] * pairs + p, 0)),
            whole((3, MAXLEN, PAIR)),
        ],
        pl.BlockSpec((3, MAXLEN, PAIR), lambda p, s: (0, 0, p)),
        sds((3, MAXLEN, pairs * PAIR), bf16),
        scratch=[pltpu.VMEM((MAXLEN, PAIR), bf16)] + [pltpu.VMEM((MAXLEN, PAIR), f32)] * 3,
        flops=16 * 1000 * MIB,
        nbytes=8 * MIB,
    )(scalars, qkv, qkv, qkv, attn, lse, own, part, wo, table)


def split_rows(total, core, count, rows):
    keep = [total[pl.ds(pl.multiple_of((2 * z + core) * rows, 8), rows), :] for z in range(count)]
    send = [total[pl.ds(pl.multiple_of((2 * z + 1 - core) * rows, 8), rows), :] for z in range(count)]
    return keep, send


def feed_body(n_seq, s, x, dy, mine, theirs, wo_mine, wo_theirs, gain, wg, wu, wd, *rest):
    (out, dh, dhb, second, gate_keep, gate_send, up_keep, up_send, down_keep, down_send) = rest[:10]
    hidden, low, low_t, dyb, dyb_t, down, back, acts, dgs, dus, total = rest[10:]
    f = pl.program_id(0)
    core = s[0]
    tokens, width = x.shape
    scale = gain[...].astype(f32)

    def live(t):
        slot = t * 2 * PIECE + core * PIECE + lax.broadcasted_iota(jnp.int32, (PIECE, 1), 0)
        return slot < s[2]

    @pl.when(f == 0)
    def _():
        for t in range(2):
            rows = slice(t * PIECE, (t + 1) * PIECE)
            h = x[rows, :].astype(f32) + mm(mine[t, 0], wo_mine[0]) + mm(theirs[t], wo_theirs[0])
            hidden[rows, :] = h
            r = lax.rsqrt(jnp.mean(h * h, axis=-1, keepdims=True) + epsilon)
            low[rows, :] = (h * r * scale).astype(bf16)
            dyb[rows, :] = jnp.where(live(t), dy[rows, :], jnp.zeros((), bf16))
        low_t[...] = jnp.transpose(low[...])
        dyb_t[...] = jnp.transpose(dyb[...])
        down[...] = jnp.zeros_like(down)
        back[...] = jnp.zeros_like(back)

    for t in range(2):
        rows = slice(t * PIECE, (t + 1) * PIECE)
        gate = mm(low[rows, :], wg[...])
        up = mm(low[rows, :], wu[...])
        dact = mm_nt(dyb[rows, :], wd[...])
        sig = jax.nn.sigmoid(gate)
        silu = gate * sig
        act = (silu * up).astype(bf16)
        dg = (dact * up * (sig * (1.0 + gate * (1.0 - sig)))).astype(bf16)
        du = (dact * silu).astype(bf16)
        acts[rows, :] = act
        dgs[rows, :] = dg
        dus[rows, :] = du
        down[rows, :] += mm(act, wd[...])
        back[rows, :] += mm_nt(dg, wg[...]) + mm_nt(du, wu[...])

    rows = width // n_seq
    count = n_seq // 2
    for grads, keep, send in ((dgs, gate_keep, gate_send), (dus, up_keep, up_send)):
        g = mm(low_t[...], grads[...])
        if rows % 16 == 0:
            total[...] = g
            kept, sent = split_rows(total, core, count, rows)
            for z in range(count):
                keep[z, 0] = kept[z].astype(bf16)
                send[z, 0] = sent[z].astype(bf16)
        else:
            keep[0] = g.astype(bf16)
            send[0] = jnp.zeros_like(send[0])
    g = mm(dyb_t[...], acts[...])
    lanes = down_keep.shape[-1]
    if rows % 16 == 0:
        total[...] = g
        batches = down_keep.shape[1]
        step = width // batches
        for b in range(batches):
            part = slice(b * step, (b + 1) * step)
            down_keep[0, b] = total[part, pl.ds(pl.multiple_of(core * lanes, 128), lanes)].astype(bf16)
            down_send[0, b] = total[part, pl.ds(pl.multiple_of((1 - core) * lanes, 128), lanes)].astype(bf16)
    else:
        down_keep[0] = g.astype(bf16)
        down_send[0] = jnp.zeros_like(down_send[0])

    @pl.when(f == pl.num_programs(0) - 1)
    def _():
        sums = jnp.zeros((1, width), f32)
        for t in range(2):
            rows = slice(t * PIECE, (t + 1) * PIECE)
            h = hidden[rows, :]
            r = lax.rsqrt(jnp.mean(h * h, axis=-1, keepdims=True) + epsilon)
            out[t] = jnp.where(live(t), h + down[rows, :], 0.0).astype(bf16)
            upstream = jnp.where(live(t), dy[rows, :].astype(f32), 0.0)
            dn = back[rows, :]
            sums = sums + jnp.sum(dn * h * r, axis=0, keepdims=True)
            scaled = dn * scale
            inner = jnp.mean(scaled * h, axis=-1, keepdims=True)
            d = upstream + r * scaled - h * (r * r * r) * inner
            dh[t] = d
            dhb[t] = d.astype(bf16)
        second[...] = sums


def feed(scalars, x, dy, attn, theirs, wo, gain, wg, wu, wd, n_seq):
    tokens, width = x.shape
    hidden_units = wg.shape[1]
    heads = attn.shape[1]
    blocks = 4
    cols = hidden_units // blocks
    count, rows = n_seq // 2, width // n_seq
    fast = rows % 16 == 0
    if fast:
        side = pl.BlockSpec((count, 1, rows, cols), lambda f, s: (0, f, 0, 0))
        side_shape = sds((count, blocks, rows, cols), bf16)
        lanes = hidden_units // n_seq
        foot = pl.BlockSpec((1, 4, width // 4, lanes), lambda f, s: (f, 0, 0, 0))
        foot_shape = sds((count, 4, width // 4, lanes), bf16)
        assert cols == 2 * lanes
    else:
        side = pl.BlockSpec((1, width, cols), lambda f, s: (f, 0, 0))
        side_shape = sds((blocks, width, cols), bf16)
        foot = side
        foot_shape = side_shape
    pieces = attn.reshape(2, 2, PIECE, heads)
    wo_parts = wo.reshape(2, heads, width)
    return call(
        functools.partial(feed_body, n_seq),
        (blocks,),
        [
            whole((tokens, width)),
            whole((tokens, width)),
            pl.BlockSpec((2, 1, PIECE, heads), lambda f, s: (0, s[0], 0, 0)),
            whole((2, PIECE, heads)),
            pl.BlockSpec((1, heads, width), lambda f, s: (s[0], 0, 0)),
            pl.BlockSpec((1, heads, width), lambda f, s: (1 - s[0], 0, 0)),
            whole((1, width)),
            pl.BlockSpec((width, cols), lambda f, s: (0, f)),
            pl.BlockSpec((width, cols), lambda f, s: (0, f)),
            pl.BlockSpec((cols, width), lambda f, s: (f, 0)),
        ],
        [whole((2, PIECE, width))] * 3 + [whole((1, width))] + [side] * 4 + [foot] * 2,
        [
            sds((2, PIECE, width), bf16),
            sds((2, PIECE, width), f32),
            sds((2, PIECE, width), bf16),
            sds((1, width), f32),
        ]
        + [side_shape] * 4
        + [foot_shape] * 2,
        scratch=[
            pltpu.VMEM((tokens, width), f32),
            pltpu.VMEM((tokens, width), bf16),
            pltpu.VMEM((width, tokens), bf16),
            pltpu.VMEM((tokens, width), bf16),
            pltpu.VMEM((width, tokens), bf16),
            pltpu.VMEM((tokens, width), f32),
            pltpu.VMEM((tokens, width), f32),
            pltpu.VMEM((tokens, cols), bf16),
            pltpu.VMEM((tokens, cols), bf16),
            pltpu.VMEM((tokens, cols), bf16),
            pltpu.VMEM((width, cols), f32),
        ],
        flops=16 * 1000 * MIB,
        nbytes=24 * MIB,
    )(scalars, x, dy, pieces, theirs, wo_parts, wo_parts, gain, wg, wu, wd)


def emit_rows(total, keep, send, core, n_seq, width):
    rows = width // n_seq
    count = total.shape[0] // rows // 2
    if rows % 16 == 0:
        kept, sent = split_rows(total, core, count, rows)
        for z in range(count):
            keep(z, kept[z].astype(bf16))
            send(z, sent[z].astype(bf16))


def output_grad_body(n_seq, s, attn, own, part, keep, send, total):
    core = s[0]
    width = own.shape[2]
    acc = None
    for half in range(2):
        for source, place in ((own, core), (part, 1 - core)):
            at = pl.multiple_of(half * 2 * PIECE + place * PIECE, PIECE)
            g = mm_tn(attn[pl.ds(at, PIECE), :], source[half])
            acc = g if acc is None else acc + g
    rows = width // n_seq
    if rows % 16 == 0:
        total[...] = acc
        count = total.shape[0] // rows // 2
        kept, sent = split_rows(total, core, count, rows)
        for z in range(count):
            for y in range(2):
                part_of = slice(y * width // 2, (y + 1) * width // 2)
                keep[z, y] = kept[z][:, part_of].astype(bf16)
                send[z, y] = sent[z][:, part_of].astype(bf16)
    else:
        keep[...] = acc.astype(bf16)
        send[...] = jnp.zeros_like(send)


def output_grad(scalars, attn, own, part, n_seq):
    heads = attn.shape[1]
    width = own.shape[2]
    rows = width // n_seq
    shape = (heads // rows // 2, 2, rows, width // 2) if rows % 16 == 0 else (heads, width)
    return call(
        functools.partial(output_grad_body, n_seq),
        (1,),
        [whole(attn.shape), whole(own.shape), whole(part.shape)],
        [whole(shape)] * 2,
        [sds(shape, bf16)] * 2,
        scratch=[pltpu.VMEM((heads, width), f32)],
        flops=2 * 1024 * heads * width,
        nbytes=4 * MIB,
    )(scalars, attn, own, part)


def input_grads_body(n_seq, s, normed, d, keep, send, total):
    core = s[0]
    width = normed.shape[1]
    total[...] = mm_tn(normed[...], d[0])
    rows = width // n_seq
    if rows % 16 == 0:
        count = n_seq // 2
        kept, sent = split_rows(total, core, count, rows)
        for z in range(count):
            keep[0, z] = kept[z].astype(bf16)
            send[0, z] = sent[z].astype(bf16)
    else:
        keep[0] = total[...].astype(bf16)
        send[0] = jnp.zeros_like(send[0])


def input_grads(scalars, normed, d, n_seq):
    width = normed.shape[1]
    heads = d.shape[2]
    rows = width // n_seq
    shape = (3, n_seq // 2, rows, heads) if rows % 16 == 0 else (3, width, heads)
    spec = pl.BlockSpec((1,) + shape[1:], lambda m, s: (m,) + (0,) * (len(shape) - 1))
    return call(
        functools.partial(input_grads_body, n_seq),
        (3,),
        [whole(normed.shape), pl.BlockSpec((1,) + d.shape[1:], lambda m, s: (m, 0, 0))],
        [spec] * 2,
        [sds(shape, bf16)] * 2,
        scratch=[pltpu.VMEM((width, heads), f32)],
        flops=2 * 1024 * 3 * heads * width,
        nbytes=6 * MIB,
    )(scalars, normed, d)


def norm_grad_body(s, d, wq, wk, wv, keep, send):
    core = s[0]
    for half in range(2):
        for place, target in ((core, keep), (1 - core, send)):
            at = pl.multiple_of(half * 2 * PIECE + place * PIECE, PIECE)
            acc = None
            for m, w in enumerate((wq, wk, wv)):
                g = mm_nt(d[m, pl.ds(at, PIECE), :], w[...])
                acc = g if acc is None else acc + g
            target[half] = acc.astype(target.dtype)


def norm_grad(scalars, d, weights):
    width = weights[0].shape[0]
    heads = d.shape[2]
    weight_spec = pl.BlockSpec((width, heads), lambda m, s: (0, s[0]))
    shape = (2, PIECE, width)
    return call(
        norm_grad_body,
        (1,),
        [whole(d.shape), weight_spec, weight_spec, weight_spec],
        [whole(shape)] * 2,
        [sds(shape, f32), sds(shape, bf16)],
        flops=2 * 1024 * 3 * heads * width,
        nbytes=8 * MIB,
    )(scalars, d, *weights)


def finish_body(s, x, keep, recv, dh, gain, out, first):
    scale = gain[...].astype(f32)
    sums = jnp.zeros((1, x.shape[1]), f32)
    for t in range(2):
        rows = slice(t * PIECE, (t + 1) * PIECE)
        h = x[rows, :].astype(f32)
        dn = keep[t] + recv[t].astype(f32)
        r = lax.rsqrt(jnp.mean(h * h, axis=-1, keepdims=True) + epsilon)
        sums = sums + jnp.sum(dn * h * r, axis=0, keepdims=True)
        scaled = dn * scale
        inner = jnp.mean(scaled * h, axis=-1, keepdims=True)
        out[t] = (dh[t] + r * scaled - h * (r * r * r) * inner).astype(bf16)
    first[...] = sums


def finish(scalars, x, keep, recv, dh, gain):
    width = x.shape[1]
    shape = (2, PIECE, width)
    return call(
        finish_body,
        (1,),
        [whole(x.shape), whole(shape), whole(shape), whole(shape), whole((1, width))],
        [whole(shape), whole((1, width))],
        [sds(shape, bf16), sds((1, width), f32)],
        flops=20 * 512 * width,
        nbytes=6 * MIB,
    )(scalars, x, keep, recv, dh, gain)


def exchange(block, axis, bit):
    count = lax.axis_size(axis)
    return lax.ppermute(block, axis, [(a, a ^ (1 << bit)) for a in range(count)])


def pick(block, index, dim):
    return lax.dynamic_index_in_dim(block, index, dim, keepdims=False)


class Bits:
    def __init__(self):
        self.seq_bits = int(math.log2(lax.axis_size("seq")))
        self.batch_bits = int(math.log2(lax.axis_size("batch")))
        self.chip_seq = [("seq", b) for b in reversed(range(1, self.seq_bits))]
        self.chip_batch = [("batch", b) for b in reversed(range(self.batch_bits))]

    def own(self, name):
        axis, bit = name
        return lax.axis_index(axis) >> bit & 1


def reduce_stage(array, names, name, bits, last=False):
    dim = names.index(name)
    own = bits.own(name)
    sent = pick(array, 1 - own, dim)
    kept = pick(array, own, dim)
    arrived = exchange(sent, *name)
    out = kept.astype(f32) + arrived.astype(f32)
    if not last:
        out = out.astype(bf16)
    return out, names[:dim] + names[dim + 1 :]


def reduce_all(array, names, order, bits):
    for at, name in enumerate(order):
        array, names = reduce_stage(array, names, name, bits, last=at == len(order) - 1)
    return array


def body(
    states,
    lengths,
    first_gain,
    query_weight,
    key_weight,
    value_weight,
    output_weight,
    second_gain,
    gate_weight,
    up_weight,
    down_weight,
    cotangent,
):
    tokens, width = states.shape
    n_seq, n_batch = lax.axis_size("seq"), lax.axis_size("batch")
    bits = Bits()
    place = lax.axis_index("seq")
    core = place & 1
    chip = place >> 1 & 1
    sequence = (lax.axis_index("batch") * (n_seq // GROUP) + place // GROUP) * 2 + chip
    length = pick(lengths, sequence, 0)
    scalars = jnp.stack([core, chip, length, 1 - chip]).astype(jnp.int32)
    table = jnp.asarray(rope_tables())
    gain_first = first_gain.reshape(1, width)
    gain_second = second_gain.reshape(1, width)
    weights = (query_weight, key_weight, value_weight)

    held = states.reshape(2, PIECE, width)
    mine = pick(held, chip, 0)
    arrived = exchange(pick(held, 1 - chip, 0), "seq", 1)
    mine_pair = exchange(mine, "seq", 0)
    arrived_pair = exchange(arrived, "seq", 0)
    held_back = cotangent.reshape(2, PIECE, width)
    back_mine = pick(held_back, chip, 0)
    back_arrived = exchange(pick(held_back, 1 - chip, 0), "seq", 1)

    def in_order(a, b):
        return jnp.concatenate([jnp.where(chip == 0, a, b), jnp.where(chip == 0, b, a)], axis=0)

    filled = project(scalars, mine, mine_pair, 1, gain_first, weights, table, None)
    qkv, normed = project(scalars, arrived, arrived_pair, 3, gain_first, weights, table, filled)
    attn, lse = attend(scalars, qkv)
    heads = attn.shape[1]
    x_own = in_order(mine, arrived)
    dy_own = in_order(back_mine, back_arrived)
    theirs = exchange(pick(attn.reshape(2, 2, PIECE, heads), 1 - core, 1), "seq", 0)
    (layer, dh, dhb, second, gate_keep, gate_send, up_keep, up_send, down_keep, down_send) = feed(
        scalars, x_own, dy_own, attn, theirs, output_weight, gain_second, gate_weight, up_weight, down_weight, n_seq
    )
    dhb_pair = exchange(dhb, "seq", 0)

    rows = width // n_seq
    fast = rows % 16 == 0
    count = n_seq // 2
    if not fast:

        def by_rows(array):
            array = array.reshape(n_batch, count, 2, rows, -1)
            return tuple(jnp.swapaxes(pick(array, a, 2), 0, 1) for a in (core, 1 - core))

        def by_lanes(array):
            array = jnp.swapaxes(array, 0, 1).reshape(n_batch, width // n_batch, count, 2, -1)
            return tuple(jnp.moveaxis(pick(array, a, 3), 2, 0) for a in (core, 1 - core))

        gate_keep, gate_send = by_rows(gate_keep)
        up_keep, up_send = by_rows(up_keep)
        down_keep, down_send = by_lanes(down_keep)

    chip_shape = (2,) * (bits.seq_bits - 1)
    batch_shape = (2,) * bits.batch_bits
    names = bits.chip_seq + bits.chip_batch
    *_, high, low = [None] + bits.chip_batch
    along = list(reversed(bits.chip_seq))

    def summed(keep, send):
        arrived = exchange(send, "seq", 0)
        out = (keep.astype(f32) + arrived.astype(f32)).astype(bf16)
        return out.reshape(chip_shape + batch_shape + out.shape[-2:])

    gate_grad = reduce_all(summed(gate_keep, gate_send), names, [low, high] + along, bits)
    up_grad = reduce_all(summed(up_keep, up_send), names, [high, low] + along, bits)
    down_grad = reduce_all(summed(down_keep, down_send), names, along[:1] + [low, high] + along[1:], bits)

    out_keep, out_send = output_grad(scalars, attn, dhb, dhb_pair, n_seq)
    if not fast:

        def out_rows(array):
            array = array.reshape(count // 2, 2, rows, 2, width // 2)
            return tuple(jnp.swapaxes(pick(array, a, 1), 1, 2) for a in (core, 1 - core))

        out_keep, out_send = out_rows(out_keep)
    out_arrived = exchange(out_send, "seq", 0)
    first_half = jnp.where(core == 0, out_keep, out_arrived)
    second_half = jnp.where(core == 0, out_arrived, out_keep)
    out_whole = jnp.concatenate([first_half, second_half], axis=0)
    narrow = bits.chip_seq + [high]

    def finish_columns(array, names, order):
        for name in order:
            array, names = reduce_stage(array, names, name, bits)
        halves = array.reshape(array.shape[0], 2, -1)
        sent = jnp.where(bits.own(low) == 0, halves[:, 1], halves[:, 0])
        kept = jnp.where(bits.own(low) == 0, halves[:, 0], halves[:, 1])
        return kept.astype(f32) + exchange(sent, *low).astype(f32)

    out_whole = out_whole.reshape(chip_shape + (2,) + out_whole.shape[-2:])
    output_grad_shard = finish_columns(out_whole, narrow, along + [high])

    d = attend_back(scalars, qkv, attn, lse, dhb, dhb_pair, output_weight, table)
    keep3, send3 = input_grads(scalars, normed, d, n_seq)
    if not fast:
        parted = keep3.reshape(3, count, 2, rows, heads)
        keep3, send3 = pick(parted, core, 2), pick(parted, 1 - core, 2)
    arrived3 = exchange(send3, "seq", 0)
    left = jnp.where(core == 0, keep3, arrived3)
    right = jnp.where(core == 0, arrived3, keep3)
    joined = jnp.stack([left, right], axis=2)
    joined = joined.reshape((3,) + chip_shape + (2,) + joined.shape[-2:])
    shards = [
        finish_columns(joined[0], narrow, [high] + along),
        finish_columns(joined[1], narrow, along[:1] + [high] + along[1:]),
        finish_columns(joined[2], narrow, along[:1] + [high] + along[1:]),
    ]

    norm_keep, norm_send = norm_grad(scalars, d, weights)
    norm_arrived = exchange(norm_send, "seq", 0)
    grad, first = finish(scalars, x_own, norm_keep, norm_arrived, dh, gain_first)

    def give_back(array):
        kept = pick(array, chip, 0)
        arrived = exchange(pick(array, 1 - chip, 0), "seq", 1)
        return in_order(kept, arrived)

    layer_out = give_back(layer)
    input_grad = give_back(grad)

    gains = jnp.concatenate([first, second], axis=0)
    for name in [("seq", 0)] + bits.chip_batch + bits.chip_seq:
        gains = gains + exchange(gains, *name)

    return (
        layer_out,
        input_grad,
        gains[0],
        shards[0],
        shards[1],
        shards[2],
        output_grad_shard,
        gains[1],
        gate_grad,
        up_grad,
        jnp.transpose(down_grad),
    )


def solution(mesh):
    split = P(("batch", "seq"), None)
    in_specs = (split,) + (P(),) * 10 + (split,)
    shard = P("seq", "batch")
    out_specs = (split, split, P(), shard, shard, shard, shard, P(), shard, shard, shard)
    return jax.shard_map(body, mesh=mesh, in_specs=in_specs, out_specs=out_specs, check_vma=False)
```

```python
import functools
import math

import jax
import jax.numpy as jnp
import numpy as np
from jax import lax
from jax.experimental import pallas as pl
from jax.experimental.pallas import tpu as pltpu
from jax.sharding import PartitionSpec as P

HEADS = 12
HEAD_FEATURES = 64
MAXLEN = 1024
GROUP = 4
PIECE = MAXLEN // GROUP
PAIR = 2 * HEAD_FEATURES
LOG2E = math.log2(math.e)

epsilon = 1e-06
masked_score = -1e30
f32 = jnp.float32
bf16 = jnp.bfloat16
MIB = 1024 * 1024

CORE, CHIP, LENGTH, OTHER_CHIP, OWN_B, OWN_Z = range(6)


def mm(a, b):
    return lax.dot_general(a, b, (((1,), (0,)), ((), ())), preferred_element_type=f32)


def mm_nt(a, b):
    return lax.dot_general(a, b, (((1,), (1,)), ((), ())), preferred_element_type=f32)


def mm_tn(a, b):
    return lax.dot_general(a, b, (((0,), (0,)), ((), ())), preferred_element_type=f32)


def call(body, grid, in_specs, out_specs, out_shape, scratch=(), aliases=None, vmem=56):
    return pl.pallas_call(
        body,
        grid_spec=pltpu.PrefetchScalarGridSpec(
            num_scalar_prefetch=1,
            grid=grid,
            in_specs=in_specs,
            out_specs=out_specs,
            scratch_shapes=list(scratch),
        ),
        out_shape=out_shape,
        input_output_aliases=aliases or {},
        compiler_params=pltpu.CompilerParams(
            dimension_semantics=("arbitrary",) * len(grid), vmem_limit_bytes=vmem * MIB
        ),
        cost_estimate=pl.CostEstimate(flops=1000, bytes_accessed=1000, transcendentals=0),
    )


def whole(shape):
    return pl.BlockSpec(shape, lambda *a: (0,) * len(shape))


def sds(shape, dtype):
    return jax.ShapeDtypeStruct(shape, dtype)


def rope_tables():
    middle = HEAD_FEATURES // 2
    frequency = 10000.0 ** (-np.arange(middle, dtype=np.float64) * 2.0 / HEAD_FEATURES)
    angles = np.arange(MAXLEN, dtype=np.float64)[:, None] * frequency[None, :]
    cosine, sine = np.cos(angles), np.sin(angles)
    none = np.zeros_like(sine)
    table = np.stack(
        [
            np.concatenate([cosine, cosine] * 2, axis=1),
            np.concatenate([-sine, none] * 2, axis=1),
            np.concatenate([none, sine] * 2, axis=1),
        ]
    )
    return table.astype(np.float32)


def rotate(u, table, sign):
    up = pltpu.roll(u, PAIR - HEAD_FEATURES // 2, 1)
    down = pltpu.roll(u, HEAD_FEATURES // 2, 1)
    if sign > 0:
        return u * table[0] + (up * table[1] + down * table[2])
    return u * table[0] - (up * table[1] + down * table[2])


def slots(start):
    return start + lax.broadcasted_iota(jnp.int32, (PIECE, 1), 0)


def piece_rows(half, place):
    return pl.ds(pl.multiple_of(half * 2 * PIECE + place * PIECE, PIECE), PIECE)


def project_body(s, own, part, gain, wq, wk, wv, table, *rest):
    qkv, normed, copy = rest[-3:]
    low_x = jnp.where(pl.program_id(0) == s[CORE], own[0], part[0])
    copy[...] = low_x
    x = low_x.astype(f32)
    r = lax.rsqrt(jnp.mean(x * x, axis=-1, keepdims=True) + epsilon)
    low = (x * r * gain[...].astype(f32)).astype(bf16)
    normed[...] = low
    width = wq.shape[1]
    for m, w in enumerate((wq, wk, wv)):
        u = mm(low, w[...])
        if m == 0:
            u = u * (1.0 / math.sqrt(HEAD_FEATURES))
        for p in range(width // PAIR):
            v = u[:, p * PAIR : (p + 1) * PAIR]
            if m < 2:
                v = rotate(v, table, 1)
            at = m * width + p * PAIR
            qkv[:, at : at + PAIR] = v.astype(bf16)


def project(scalars, own, part, half, gain, weights, table, filled):
    width = weights[0].shape[0]
    cols = width // 2
    place = lambda t, s: (s[half] * 2 + t, 0)
    source = lambda a: pl.BlockSpec((1, PIECE, width), lambda t, s: (s[CHIP] if a.shape[0] > 1 else 0, 0, 0))
    weight_spec = pl.BlockSpec((width, cols), lambda t, s: (0, s[CORE]))
    in_specs = [
        source(own),
        source(part),
        whole((1, width)),
        weight_spec,
        weight_spec,
        weight_spec,
        pl.BlockSpec((3, PIECE, PAIR), lambda t, s: (0, s[half] * 2 + t, 0)),
    ]
    args = [scalars, own, part, gain, *weights, table]
    aliases = None
    if filled is not None:
        in_specs += [pl.BlockSpec(memory_space=pl.ANY)] * 3
        aliases = {len(args) + a: a for a in range(3)}
        args += list(filled)
    return call(
        project_body,
        (2,),
        in_specs,
        [pl.BlockSpec((PIECE, 3 * cols), place), pl.BlockSpec((PIECE, width), place), pl.BlockSpec((PIECE, width), place)],
        [sds((MAXLEN, 3 * cols), bf16), sds((MAXLEN, width), bf16), sds((MAXLEN, width), bf16)],
        aliases=aliases,
    )(*args)


def head_mask(h):
    lane = lax.broadcasted_iota(jnp.int32, (1, PAIR), 1)
    return lane < HEAD_FEATURES if h == 0 else lane >= HEAD_FEATURES


def attend_body(s, q, k, v, out, lse):
    row = lax.broadcasted_iota(jnp.int32, (PIECE, PIECE), 0)
    col = lax.broadcasted_iota(jnp.int32, (PIECE, PIECE), 1)
    lane = lax.broadcasted_iota(jnp.int32, (PIECE, PAIR), 1)
    ones = jnp.ones((MAXLEN, PAIR), bf16)

    def score(b, h):
        at = b * PIECE
        qh = jnp.where(head_mask(h), q[at : at + PIECE, :], jnp.zeros((), bf16))
        near = mm_nt(qh, k[at : at + PIECE, :])
        return near, mm_nt(qh, k[:at, :]) if b else None

    def mix(b, near, far):
        at = b * PIECE
        near = jnp.where(row >= col, near, masked_score)
        top = jnp.max(near, axis=-1, keepdims=True)
        if b:
            top = jnp.maximum(top, jnp.max(far, axis=-1, keepdims=True))
        shift = top * LOG2E
        near = jnp.exp2(near * LOG2E - shift).astype(bf16)
        mixed = mm(near, jnp.concatenate([v[at : at + PIECE, :], ones[:PIECE]], axis=1))
        if b:
            far = jnp.exp2(far * LOG2E - shift).astype(bf16)
            mixed = mixed + mm(far, jnp.concatenate([v[:at, :], ones[:at]], axis=1))
        total = mixed[:, PAIR:]
        return mixed[:, :PAIR] * (1.0 / total), top + jnp.log(total)

    units = [(b, h) for b in range(GROUP) for h in range(2)]
    ahead = score(*units[0])
    done = []
    for at, (b, h) in enumerate(units):
        now = ahead
        if at + 1 < len(units):
            ahead = score(*units[at + 1])
        done.append(mix(b, *now))
        if h == 1:
            rows = slice(b * PIECE, (b + 1) * PIECE)
            (left, left_log), (right, right_log) = done
            done = []
            joined = jnp.where(head_mask(0), left, right)
            out[rows, :] = jnp.where(slots(b * PIECE) < s[LENGTH], joined, 0.0).astype(bf16)
            lse[0, rows, :] = jnp.where(lane == 0, left_log, right_log)


def attend(scalars, qkv):
    pairs = qkv.shape[1] // 3 // PAIR
    spec = lambda m: pl.BlockSpec((MAXLEN, PAIR), lambda p, s, m=m: (0, m * pairs + p))
    return call(
        attend_body,
        (pairs,),
        [spec(0), spec(1), spec(2)],
        [pl.BlockSpec((MAXLEN, PAIR), lambda p, s: (0, p)), pl.BlockSpec((1, MAXLEN, PAIR), lambda p, s: (p, 0, 0))],
        [sds((MAXLEN, pairs * PAIR), bf16), sds((pairs, MAXLEN, PAIR), f32)],
    )(scalars, qkv, qkv, qkv)


def attend_back_body(
    n_seq, s, q, k, v, o, lse, hidden, dyb, dn_mine, dn_theirs, gain, wo, wq, wk, wv, normed, table, *rest
):
    (qkv_keep, qkv_send, out_keep, out_send, norm_keep, norm_send, dh_own, second) = rest[:8]
    dhb, dh, da, da_t, q_t, dk_t, dv_t, dq, grads, out_grad, dn = rest[8:]
    core = s[CORE]
    p = pl.program_id(0)
    width = normed.shape[1]
    zero = jnp.zeros((), bf16)

    @pl.when(p == 0)
    def _():
        scale = gain[...].astype(f32)
        sums = jnp.zeros((1, width), f32)
        for t in range(GROUP):
            rows = slice(t * PIECE, (t + 1) * PIECE)
            h = hidden[rows, :]
            r = lax.rsqrt(jnp.mean(h * h, axis=-1, keepdims=True) + epsilon)
            g = dn_mine[rows, :].astype(f32) + dn_theirs[rows, :].astype(f32)
            sums = sums + jnp.sum(g * h * r, axis=0, keepdims=True)
            scaled = g * scale
            inner = jnp.mean(scaled * h, axis=-1, keepdims=True)
            d = dyb[rows, :].astype(f32) + r * scaled - h * (r * r * r) * inner
            dh[rows, :] = d
            dhb[rows, :] = d.astype(bf16)
        second[...] = sums * 0.5
        for half in range(2):
            dh_own[half] = dh[piece_rows(half, core), :]

    for t in range(GROUP):
        rows = slice(t * PIECE, (t + 1) * PIECE)
        d = mm_nt(dhb[rows, :], wo[...])
        da[rows, :] = jnp.where(slots(t * PIECE) < s[LENGTH], d, 0.0).astype(bf16)
    out_grad[pl.ds(pl.multiple_of(p * PAIR, PAIR), PAIR), :] = mm_tn(o[...], dhb[...])
    da_t[...] = jnp.transpose(da[...])
    q_t[...] = jnp.transpose(q[...])

    row = lax.broadcasted_iota(jnp.int32, (PIECE, PIECE), 0)
    col = lax.broadcasted_iota(jnp.int32, (PIECE, PIECE), 1)

    def score(a, h):
        at = a * PIECE
        mask = head_mask(h)
        qh = jnp.where(mask, q[at : at + PIECE, :], zero)
        gh = jnp.where(mask, da[at : at + PIECE, :], zero)
        near = mm_nt(qh, k[at : at + PIECE, :]), mm_nt(gh, v[at : at + PIECE, :])
        far = (mm_nt(qh, k[:at, :]), mm_nt(gh, v[:at, :])) if a else None
        return near, far

    def back(a, h, near, far):
        at = a * PIECE
        rows = slice(at, at + PIECE)
        feats = slice(h * HEAD_FEATURES, (h + 1) * HEAD_FEATURES)
        mask = head_mask(h)
        shift = lse[0, rows, h : h + 1] * LOG2E
        product = da[rows, :].astype(f32) * o[rows, :].astype(f32)
        inner = jnp.sum(jnp.where(mask, product, 0.0), axis=-1, keepdims=True)
        near_prob = jnp.exp2(jnp.where(row >= col, near[0] * LOG2E - shift, masked_score))
        near_ds = (near_prob * (near[1] - inner)).astype(bf16)
        query_grad = mm(near_ds, jnp.where(mask, k[rows, :], zero))
        parts = [(rows, near_prob.astype(bf16), near_ds)]
        if a:
            far_prob = jnp.exp2(far[0] * LOG2E - shift)
            far_ds = (far_prob * (far[1] - inner)).astype(bf16)
            query_grad = query_grad + mm(far_ds, jnp.where(mask, k[:at, :], zero))
            parts.append((slice(0, at), far_prob.astype(bf16), far_ds))
        for cols, prob, ds in parts:
            value_grad = mm(da_t[feats, rows], prob)
            key_grad = mm(q_t[feats, rows], ds)
            if a == GROUP - 1:
                dv_t[feats, cols] = value_grad
                dk_t[feats, cols] = key_grad
            else:
                dv_t[feats, cols] += value_grad
                dk_t[feats, cols] += key_grad
        return query_grad

    units = [(a, h) for a in reversed(range(GROUP)) for h in range(2)]
    ahead = score(*units[0])
    held = None
    for at, (a, h) in enumerate(units):
        now = ahead
        if at + 1 < len(units):
            ahead = score(*units[at + 1])
        g = back(a, h, *now)
        if h == 0:
            held = g
        else:
            dq[a * PIECE : (a + 1) * PIECE, :] = held + g

    d = jnp.concatenate(
        [
            rotate(dq[...] * (1.0 / math.sqrt(HEAD_FEATURES)), table, -1).astype(bf16),
            rotate(jnp.transpose(dk_t[...]), table, -1).astype(bf16),
            jnp.transpose(dv_t[...].astype(bf16)),
        ],
        axis=1,
    )
    grads[p] = mm_tn(normed[...], d)
    w = jnp.concatenate([wq[...], wk[...], wv[...]], axis=1)
    step = mm_nt(d, w)

    @pl.when(p == 0)
    def _():
        dn[...] = step

    @pl.when(p > 0)
    def _():
        dn[...] += step

    rows = width // n_seq
    pairs = grads.shape[0]

    @pl.when(p == pairs - 1)
    def _():
        for half in range(2):
            norm_keep[half] = dn[piece_rows(half, core), :]
            norm_send[half] = dn[piece_rows(half, 1 - core), :].astype(bf16)
        if rows % 16:
            for m in range(3):
                qkv_keep[m] = jnp.concatenate(
                    [grads[b, :, m * PAIR : (m + 1) * PAIR] for b in range(pairs)], axis=1
                ).astype(bf16)
            out_keep[...] = out_grad[...].astype(bf16)
            return
        half_row, column = rows // 2, pairs * PAIR // 2

        def packed(block, at):
            lanes = slice(at, at + column)
            return jnp.concatenate([block[:half_row, lanes], block[half_row:, lanes]], axis=1).astype(bf16)

        for target_qkv, target_out, place in ((qkv_keep, out_keep, core), (qkv_send, out_send, 1 - core)):
            for z in range(n_seq // 2):
                at = pl.ds(pl.multiple_of((2 * z + place) * rows, 8), rows)
                for m in range(3):
                    block = jnp.concatenate(
                        [grads[b, at, m * PAIR : (m + 1) * PAIR] for b in range(pairs)], axis=1
                    )
                    for x in range(2):
                        target_qkv[z, x, m] = packed(block, x * column)
            for z in range(n_seq // 4):
                at = pl.ds(pl.multiple_of((2 * z + place) * rows, 8), rows)
                block = out_grad[at, :]
                for b in range(4):
                    target_out[z, b // 2, b % 2] = packed(block, b * column)


def attend_back(scalars, qkv, attn, lse, hidden, dyb, dn_mine, dn_theirs, gain, wo, weights, normed, table, n_seq):
    heads = attn.shape[1]
    pairs = heads // PAIR
    width = wo.shape[1]
    rows = width // n_seq
    spec = lambda m: pl.BlockSpec((MAXLEN, PAIR), lambda p, s, m=m: (0, m * pairs + p))
    weight_spec = pl.BlockSpec((width, PAIR), lambda p, s: (0, s[CORE] * pairs + p))
    if rows % 16 == 0:
        shapes = [(n_seq // 2, 2, 3, rows // 2, heads)] * 2 + [(n_seq // 4, 2, 2, rows // 2, heads)] * 2
    else:
        shapes = [(3, width, heads), (8, 128), (heads, width), (8, 128)]
    token_shape = (2, PIECE, width)
    return call(
        functools.partial(attend_back_body, n_seq),
        (pairs,),
        [
            spec(0),
            spec(1),
            spec(2),
            spec(0),
            pl.BlockSpec((1, MAXLEN, PAIR), lambda p, s: (p, 0, 0)),
            whole((MAXLEN, width)),
            whole((MAXLEN, width)),
            whole((MAXLEN, width)),
            whole((MAXLEN, width)),
            whole((1, width)),
            pl.BlockSpec((PAIR, width), lambda p, s: (s[CORE] * pairs + p, 0)),
            weight_spec,
            weight_spec,
            weight_spec,
            whole((MAXLEN, width)),
            whole((3, MAXLEN, PAIR)),
        ],
        [whole(a) for a in shapes] + [whole(token_shape)] * 3 + [whole((1, width))],
        [sds(a, bf16) for a in shapes]
        + [sds(token_shape, f32), sds(token_shape, bf16), sds(token_shape, f32), sds((1, width), f32)],
        scratch=[
            pltpu.VMEM((MAXLEN, width), bf16),
            pltpu.VMEM((MAXLEN, width), f32),
            pltpu.VMEM((MAXLEN, PAIR), bf16),
            pltpu.VMEM((PAIR, MAXLEN), bf16),
            pltpu.VMEM((PAIR, MAXLEN), bf16),
            pltpu.VMEM((PAIR, MAXLEN), f32),
            pltpu.VMEM((PAIR, MAXLEN), f32),
            pltpu.VMEM((MAXLEN, PAIR), f32),
            pltpu.VMEM((pairs, width, 3 * PAIR), f32),
            pltpu.VMEM((heads, width), f32),
            pltpu.VMEM((MAXLEN, width), f32),
        ],
    )(scalars, qkv, qkv, qkv, attn, lse, hidden, dyb, dn_mine, dn_theirs, gain, wo, *weights, normed, table)


def unit_block(step, s):
    return 2 * ((3 - step) ^ s[OWN_B]) + s[CORE]


def feed_body(
    packed, s, x, dy_mine, dy_mine_pair, dy_far, dy_far_pair, attn, attn_pair, wo_own, wo_pair, gain, wg, wu, wd, *rest
):
    (hidden, dyb, acts, dgs, dus, gate_send, gate_keep, up_send, up_keep, down_send, down_keep) = rest[:11]
    low, low_t, dyb_t, total = rest[11:]
    core = s[CORE]
    step = pl.program_id(0)
    width = x.shape[1]

    @pl.when(step == 0)
    def _():
        scale = gain[...].astype(f32)
        for source, half, place in (
            (dy_mine, s[CHIP], core),
            (dy_mine_pair, s[CHIP], 1 - core),
            (dy_far, s[OTHER_CHIP], core),
            (dy_far_pair, s[OTHER_CHIP], 1 - core),
        ):
            live = slots(half * 2 * PIECE + place * PIECE) < s[LENGTH]
            dyb[piece_rows(half, place), :] = jnp.where(live, source[0], jnp.zeros((), bf16))
        for t in range(GROUP):
            rows = slice(t * PIECE, (t + 1) * PIECE)
            h = x[rows, :].astype(f32) + mm(attn[rows, :], wo_own[0]) + mm(attn_pair[rows, :], wo_pair[0])
            hidden[rows, :] = h
            r = lax.rsqrt(jnp.mean(h * h, axis=-1, keepdims=True) + epsilon)
            low[rows, :] = (h * r * scale).astype(bf16)
        low_t[...] = jnp.transpose(low[...])
        dyb_t[...] = jnp.transpose(dyb[...])

    def products(t):
        rows = slice(t * PIECE, (t + 1) * PIECE)
        return mm(low[rows, :], wg[...]), mm(low[rows, :], wu[...]), mm_nt(dyb[rows, :], wd[...])

    def pointwise(t, gate, up, dact):
        rows = slice(t * PIECE, (t + 1) * PIECE)
        sig = 1.0 / (1.0 + jnp.exp2(gate * -LOG2E))
        silu = gate * sig
        acts[rows, :] = (silu * up).astype(bf16)
        dgs[rows, :] = (dact * up * (sig + silu * (1.0 - sig))).astype(bf16)
        dus[rows, :] = (dact * silu).astype(bf16)

    ahead = products(0)
    for t in range(GROUP):
        now = ahead
        if t + 1 < GROUP:
            ahead = products(t + 1)
        pointwise(t, *now)

    gate_grad = mm(low_t[...], dgs[...])
    up_grad = mm(low_t[...], dus[...])
    down_grad = mm(dyb_t[...], acts[...])
    if not packed:
        gate_keep[...] = gate_grad.astype(bf16)
        up_keep[...] = up_grad.astype(bf16)
        down_keep[...] = down_grad.astype(bf16)
        return

    def emit(grad, targets, own):
        total[...] = grad
        blocks = targets[0][1].shape[1]
        rows = width // blocks
        values = [
            total[pl.ds(pl.multiple_of((b ^ own) * rows, 16), rows), :].astype(bf16) for b in range(blocks)
        ]
        for when, target, index in targets:

            @pl.when(when)
            def _():
                for b in range(blocks):
                    target[index, b] = values[b]

    emit(gate_grad, [(step % 2 == 0, gate_send, 0), (step % 2 == 1, gate_keep, 0)], s[OWN_Z])
    emit(up_grad, [(step < 2, up_send, 0), (step >= 2, up_keep, 0)], s[OWN_Z])
    z = (unit_block(step, s) // 2) ^ s[OWN_Z]
    emit(down_grad, [(z % 2 == 1, down_send, z // 2), (z % 2 == 0, down_keep, z // 2)], s[OWN_B])


def feed(scalars, x, dy, dy_pair, dy_far, dy_far_pair, attn, attn_pair, wo, gain, wg, wu, wd, packed):
    tokens, width = x.shape
    heads = attn.shape[1]
    steps = 4
    cols = wg.shape[1] // 2 // steps
    piece = lambda which: pl.BlockSpec((1, PIECE, width), lambda f, s: (which(s), 0, 0))
    if packed:
        rows = width // 4
        shape = (2, 4, rows, cols)
        side = lambda index: pl.BlockSpec((1, 4, rows, cols), lambda f, s: (index(f), 0, 0, 0))
        late = lambda f: 1 - f // 2
        specs = [
            side(late),
            side(late),
            side(lambda f: 1 - jnp.minimum(f, 1)),
            side(lambda f: 1 - jnp.maximum(f - 2, 0)),
            whole(shape),
            whole(shape),
        ]
        shapes = [shape] * 6
    else:
        unused = pl.BlockSpec((8, 128), lambda f, s: (0, 0))
        plain = pl.BlockSpec((width, cols), lambda f, s: (0, unit_block(f, s) // 2))
        specs = [unused, plain] * 3
        shapes = [(8, 128), (width, steps * cols)] * 3
    wo_parts = wo.reshape(2, heads, width)
    return call(
        functools.partial(feed_body, packed),
        (steps,),
        [
            whole((tokens, width)),
            piece(lambda s: s[CHIP]),
            piece(lambda s: s[CHIP]),
            piece(lambda s: 0),
            piece(lambda s: 0),
            whole((tokens, heads)),
            whole((tokens, heads)),
            pl.BlockSpec((1, heads, width), lambda f, s: (s[CORE], 0, 0)),
            pl.BlockSpec((1, heads, width), lambda f, s: (1 - s[CORE], 0, 0)),
            whole((1, width)),
            pl.BlockSpec((width, cols), lambda f, s: (0, unit_block(f, s))),
            pl.BlockSpec((width, cols), lambda f, s: (0, unit_block(f, s))),
            pl.BlockSpec((cols, width), lambda f, s: (unit_block(f, s), 0)),
        ],
        [whole((tokens, width))] * 2 + [pl.BlockSpec((tokens, cols), lambda f, s: (0, f))] * 3 + specs,
        [sds((tokens, width), f32), sds((tokens, width), bf16)]
        + [sds((tokens, steps * cols), bf16)] * 3
        + [sds(a, bf16) for a in shapes],
        scratch=[
            pltpu.VMEM((tokens, width), bf16),
            pltpu.VMEM((width, tokens), bf16),
            pltpu.VMEM((width, tokens), bf16),
            pltpu.VMEM((width, cols), f32),
        ],
    )(scalars, x, dy, dy_pair, dy_far, dy_far_pair, attn, attn_pair, wo_parts, wo_parts, gain, wg, wu, wd)


def settle_body(s, acts, dgs, dus, wg, wu, wd, dn, down_keep, down_send, down, back):
    f = pl.program_id(0)
    for t in range(GROUP):
        rows = slice(t * PIECE, (t + 1) * PIECE)
        a = mm(acts[rows, :], wd[...])
        b = mm_nt(dgs[rows, :], wg[...]) + mm_nt(dus[rows, :], wu[...])

        @pl.when(f == 0)
        def _():
            down[rows, :] = a
            back[rows, :] = b

        @pl.when(f > 0)
        def _():
            down[rows, :] += a
            back[rows, :] += b

    @pl.when(f == pl.num_programs(0) - 1)
    def _():
        dn[...] = back[...].astype(bf16)
        for half in range(2):
            down_keep[half] = down[piece_rows(half, s[CORE]), :]
            down_send[half] = down[piece_rows(half, 1 - s[CORE]), :].astype(bf16)


def settle(scalars, acts, dgs, dus, wg, wu, wd):
    tokens, units = acts.shape
    width = wg.shape[0]
    steps = 4
    cols = units // steps
    unit_spec = pl.BlockSpec((tokens, cols), lambda f, s: (0, f))
    token_shape = (2, PIECE, width)
    return call(
        settle_body,
        (steps,),
        [
            unit_spec,
            unit_spec,
            unit_spec,
            pl.BlockSpec((width, cols), lambda f, s: (0, unit_block(f, s))),
            pl.BlockSpec((width, cols), lambda f, s: (0, unit_block(f, s))),
            pl.BlockSpec((cols, width), lambda f, s: (unit_block(f, s), 0)),
        ],
        [whole((tokens, width)), whole(token_shape), whole(token_shape)],
        [sds((tokens, width), bf16), sds(token_shape, f32), sds(token_shape, bf16)],
        scratch=[pltpu.VMEM((tokens, width), f32)] * 2,
    )(scalars, acts, dgs, dus, wg, wu, wd)


def finish_body(s, x, keep, recv, dh, gain, stay, leave, first):
    scale = gain[...].astype(f32)
    sums = jnp.zeros((1, x.shape[-1]), f32)
    for out, half in ((leave, s[OTHER_CHIP]), (stay, s[CHIP])):
        h = x[half, 0].astype(f32)
        dn = keep[half] + recv[half].astype(f32)
        r = lax.rsqrt(jnp.mean(h * h, axis=-1, keepdims=True) + epsilon)
        sums = sums + jnp.sum(dn * h * r, axis=0, keepdims=True)
        scaled = dn * scale
        inner = jnp.mean(scaled * h, axis=-1, keepdims=True)
        out[...] = (dh[half] + r * scaled - h * (r * r * r) * inner).astype(bf16)
    first[...] = sums


def finish(scalars, x, keep, recv, dh, gain):
    width = x.shape[1]
    shape = (2, PIECE, width)
    return call(
        finish_body,
        (1,),
        [
            pl.BlockSpec((2, 1, PIECE, width), lambda f, s: (0, s[CORE], 0, 0)),
            whole(shape),
            whole(shape),
            whole(shape),
            whole((1, width)),
        ],
        [whole((PIECE, width)), whole((PIECE, width)), whole((1, width))],
        [sds((PIECE, width), bf16), sds((PIECE, width), bf16), sds((1, width), f32)],
    )(scalars, x.reshape(2, 2, PIECE, width), keep, recv, dh, gain)


def exchange(block, axis, bit):
    count = lax.axis_size(axis)
    return lax.ppermute(block, axis, [(a, a ^ (1 << bit)) for a in range(count)])


def pick(block, index, dim):
    return lax.dynamic_index_in_dim(block, index, dim, keepdims=False)


def together(*values):
    return lax.optimization_barrier(values)


X, Y, Z0, Z1 = ("batch", 0), ("batch", 1), ("seq", 1), ("seq", 2)


class Reduction:
    def __init__(self, names, keep, send, first):
        self.names, self.keep, self.send, self.bit = list(names), keep, send, first

    @staticmethod
    def of(names, array, first):
        r = Reduction(names, None, None, first)
        r.keep, r.send = r.split(array, first)
        return r

    def split(self, array, bit):
        dim = self.names.index(bit)
        self.names = self.names[:dim] + self.names[dim + 1 :]
        return lax.index_in_dim(array, 0, dim, False), lax.index_in_dim(array, 1, dim, False)

    def go(self):
        self.arrived = exchange(self.send, *self.bit)
        return self

    def take(self, bit):
        self.bit = bit
        kept, sent = self.split(self.keep, bit) if False else (None, None)
        dim = self.names.index(bit)
        parts = []
        for index in range(2):
            a = lax.index_in_dim(self.keep, index, dim, False).astype(f32)
            b = lax.index_in_dim(self.arrived, index, dim, False).astype(f32)
            parts.append((a + b).astype(bf16))
        self.names = self.names[:dim] + self.names[dim + 1 :]
        self.keep, self.send = parts
        return self

    def total(self):
        return self.keep.astype(f32) + self.arrived.astype(f32)


def body(
    states,
    lengths,
    first_gain,
    query_weight,
    key_weight,
    value_weight,
    output_weight,
    second_gain,
    gate_weight,
    up_weight,
    down_weight,
    cotangent,
):
    tokens, width = states.shape
    n_seq, n_batch = lax.axis_size("seq"), lax.axis_size("batch")
    packed = n_seq == 8 and n_batch == 4
    place = lax.axis_index("seq")
    batch = lax.axis_index("batch")
    core = place & 1
    chip = place >> 1 & 1
    sequence = (batch * (n_seq // GROUP) + place // GROUP) * 2 + chip
    length = pick(lengths, sequence, 0)
    own_b, own_z = batch & 3, place >> 1 & 3
    scalars = jnp.stack([core, chip, length, 1 - chip, own_b, own_z]).astype(jnp.int32)
    table = jnp.asarray(rope_tables())
    gain_first = first_gain.reshape(1, width)
    gain_second = second_gain.reshape(1, width)
    weights = (query_weight, key_weight, value_weight)

    held = states.reshape(2, PIECE, width)
    held_back = cotangent.reshape(2, PIECE, width)
    far = exchange(pick(held, 1 - chip, 0), *Z0)[None]
    held_pair = exchange(held, "seq", 0)
    filled = project(scalars, held, held_pair, CHIP, gain_first, weights, table, None)
    far, *filled = together(far, *filled)
    far_pair = exchange(far, "seq", 0)
    leaving, far_pair = together(pick(held_back, 1 - chip, 0), far_pair)
    back_far = exchange(leaving, *Z0)[None]
    back_pair = exchange(held_back, "seq", 0)
    qkv, normed, x = project(scalars, far, far_pair, OTHER_CHIP, gain_first, weights, table, filled)
    attn, lse = attend(scalars, qkv)
    attn_pair = exchange(attn, "seq", 0)
    back_far, attn = together(back_far, attn)
    back_far_pair = exchange(back_far, "seq", 0)
    hidden, dyb, acts, dgs, dus, gate_send, gate_keep, up_send, up_keep, down_send, down_keep = feed(
        scalars,
        x,
        held_back,
        back_pair,
        back_far,
        back_far_pair,
        attn,
        attn_pair,
        output_weight,
        gain_second,
        gate_weight,
        up_weight,
        down_weight,
        packed,
    )
    if packed:
        two = lambda a: a.reshape((a.shape[0], 2, 2) + a.shape[2:])
        gate = Reduction([Y, Z1, Z0], two(gate_keep), two(gate_send), X).go()
        up = Reduction([X, Z1, Z0], two(up_keep), two(up_send), Y).go()
        down = Reduction([Z1, Y, X], two(down_keep), two(down_send), Z0).go()

    dn, layer_keep, layer_send = settle(scalars, acts, dgs, dus, gate_weight, up_weight, down_weight)
    dn_pair = exchange(dn, "seq", 0)
    layer_arrived = exchange(layer_send, "seq", 0)

    (
        qkv_keep,
        qkv_send,
        out_keep,
        out_send,
        norm_keep,
        norm_send,
        dh,
        second,
    ) = attend_back(
        scalars,
        qkv,
        attn,
        lse,
        hidden,
        dyb,
        dn,
        dn_pair,
        gain_second,
        output_weight,
        weights,
        normed,
        table,
        n_seq,
    )
    norm_arrived = exchange(norm_send, "seq", 0)

    at = lambda half: (
        pick(pick(hidden.reshape(2, 2, PIECE, width), core, 1), half, 0)
        + pick(layer_keep, half, 0)
        + pick(layer_arrived, half, 0).astype(f32)
    )
    own_slots = lambda half: half * 2 * PIECE + core * PIECE + jnp.arange(PIECE, dtype=jnp.int32)[:, None]
    layer_half = lambda half: jnp.where(own_slots(half) < length, at(half), 0.0).astype(bf16)

    def in_order(kept, arrived):
        return jnp.concatenate(
            [jnp.where(chip == 0, kept, arrived), jnp.where(chip == 0, arrived, kept)], axis=0
        )

    if packed:
        qkv_arrived = exchange(qkv_send, "seq", 0)
        out_arrived = exchange(out_send, "seq", 0)
        gate.take(Y).go()
        up.take(Z0).go()
        down.take(X).go()
        rows = width // n_seq // 2
        first_half = lambda a, b: (jnp.where(core == 0, a, b), jnp.where(core == 0, b, a))
        joined = jnp.concatenate(
            [
                jnp.stack(first_half(qkv_keep, qkv_arrived), axis=1),
                jnp.concatenate(first_half(out_keep, out_arrived), axis=0)[:, :, :, None],
            ],
            axis=3,
        )
        joined = joined.reshape(2, 2, 2, 2, 4 * rows, joined.shape[-1])
        names = [Z1, Z0, Y, X]
        flags = [own_z >> 1 & 1, own_z & 1, own_b >> 1 & 1, own_b & 1]
        flows = []
        for index, bit in enumerate((X, Y, Z0)):
            step = 4 * rows // 3
            part = joined[..., index * step : (index + 1) * step, :]
            flows.append(start_flow(names, flags, part, bit))
        orders = [(Y, Z0, Z1), (Z0, X, Z1), (X, Y, Z1)]
        gate.take(Z0).go()
        up.take(X).go()
        down.take(Y).go()
        for level in range(3):
            for flow, order in zip(flows, orders):
                flow.take_absolute(order[level], flags_of(names, flags)).go()
            if level == 0:
                for r in (gate, up, down):
                    r.take(Z1).go()
        sums = jnp.concatenate([flow.total() for flow in flows], axis=0).reshape(4, rows, -1)
        half = sums.shape[-1] // 2
        sums = jnp.concatenate([sums[..., :half], sums[..., half:]], axis=1)
        shards = [sums[m] for m in range(4)]
        sides = jnp.stack([gate.total(), up.total()])
        sides = sides.reshape(2, 2, sides.shape[1] // 2, sides.shape[2])
        side_keep, side_send = pick(sides, core, 1), pick(sides, 1 - core, 1).astype(bf16)
        side_arrived = exchange(side_send, "seq", 0).astype(f32)
        sides = jnp.concatenate(first_half(side_keep, side_arrived), axis=2)
        gate_grad, up_grad, down_grad = sides[0], sides[1], jnp.transpose(down.total())
    else:
        units = gate_keep.shape[1]
        zeros = lambda shape: jnp.zeros(shape, bf16)
        blocks = 4

        def spread(array):
            parts = array.reshape(width, blocks, 1, units // blocks)
            full = zeros((width, blocks, 2, units // blocks))
            return lax.dynamic_update_slice_in_dim(full, parts, core, 2).reshape(width, 2 * units)

        heads = attn.shape[1]
        columns = lambda a: lax.dynamic_update_slice_in_dim(zeros((width, width)), a, core * heads, 1)
        full = [columns(qkv_keep[m]) for m in range(3)]
        full.append(lax.dynamic_update_slice_in_dim(zeros((width, width)), out_keep, core * heads, 0))
        full += [spread(gate_keep), spread(up_keep), jnp.transpose(spread(down_keep))]
        full = [lax.psum_scatter(a.astype(f32), "seq", scatter_dimension=0, tiled=True) for a in full]
        full = [lax.psum_scatter(a, "batch", scatter_dimension=1, tiled=True) for a in full]
        shards, (gate_grad, up_grad, down_grad) = full[:4], full[4:]

    stay, leave, first = finish(scalars, x, norm_keep, norm_arrived, dh, gain_first)
    input_grad = in_order(stay, exchange(leave, *Z0))
    layer_out = in_order(layer_half(chip), exchange(layer_half(1 - chip), *Z0))

    gains = jnp.concatenate([first, second], axis=0)
    for axis in ("seq", "batch"):
        for bit in range(int(math.log2(lax.axis_size(axis)))):
            gains = gains + exchange(gains, axis, bit)

    return (
        layer_out,
        input_grad,
        gains[0],
        shards[0],
        shards[1],
        shards[2],
        shards[3],
        gains[1],
        gate_grad,
        up_grad,
        down_grad,
    )


def flags_of(names, flags):
    return dict(zip(names, flags))


class Flow:
    def __init__(self, names, flags, array, bit):
        self.names, self.flags, self.bit = list(names), dict(zip(names, flags)), bit
        dim = self.names.index(bit)
        own = self.flags[bit]
        self.keep, self.send = pick(array, own, dim), pick(array, 1 - own, dim)
        self.names.remove(bit)

    def go(self):
        self.arrived = exchange(self.send, *self.bit)
        return self

    def take_absolute(self, bit, _):
        dim = self.names.index(bit)
        own = self.flags[bit]
        pair = []
        for index in (own, 1 - own):
            a, b = pick(self.keep, index, dim), pick(self.arrived, index, dim)
            pair.append((a.astype(f32) + b.astype(f32)).astype(bf16))
        self.keep, self.send = pair
        self.names.remove(bit)
        self.bit = bit
        return self

    def total(self):
        return self.keep.astype(f32) + self.arrived.astype(f32)


def start_flow(names, flags, array, bit):
    return Flow(names, flags, array, bit).go()


def solution(mesh):
    split = P(("batch", "seq"), None)
    in_specs = (split,) + (P(),) * 10 + (split,)
    shard = P("seq", "batch")
    out_specs = (split, split, P(), shard, shard, shard, shard, P(), shard, shard, shard)
    return jax.shard_map(body, mesh=mesh, in_specs=in_specs, out_specs=out_specs, check_vma=False)
```

```python
import functools
import math

import jax
import jax.numpy as jnp
import numpy as np
from jax import lax
from jax.experimental import pallas as pl
from jax.experimental.pallas import tpu as pltpu
from jax.sharding import PartitionSpec as P

HEADS = 12
HEAD_FEATURES = 64
MAXLEN = 1024
GROUP = 4
PIECE = MAXLEN // GROUP
PAIR = 2 * HEAD_FEATURES
LOG2E = math.log2(math.e)

epsilon = 1e-06
masked_score = -1e30
f32 = jnp.float32
bf16 = jnp.bfloat16
MIB = 1024 * 1024

SIDES = ((0, 1), (2, 0), (1, 2))
HEAD_ORDER = tuple(h for left, right in SIDES for h in (2 * left, 2 * right + 1))

CORE, CHIP, LENGTH, OTHER_CHIP, OWN_B, OWN_Z = range(6)


def mm(a, b):
    return lax.dot_general(a, b, (((1,), (0,)), ((), ())), preferred_element_type=f32)


def mm_nt(a, b):
    return lax.dot_general(a, b, (((1,), (1,)), ((), ())), preferred_element_type=f32)


def mm_tn(a, b):
    return lax.dot_general(a, b, (((0,), (0,)), ((), ())), preferred_element_type=f32)


def call(body, grid, in_specs, out_specs, out_shape, scratch=(), aliases=None, vmem=64):
    return pl.pallas_call(
        body,
        grid_spec=pltpu.PrefetchScalarGridSpec(
            num_scalar_prefetch=1,
            grid=grid,
            in_specs=in_specs,
            out_specs=out_specs,
            scratch_shapes=list(scratch),
        ),
        out_shape=out_shape,
        input_output_aliases=aliases or {},
        compiler_params=pltpu.CompilerParams(
            dimension_semantics=("arbitrary",) * len(grid), vmem_limit_bytes=vmem * MIB
        ),
        cost_estimate=pl.CostEstimate(flops=1000, bytes_accessed=1000, transcendentals=0),
    )


def whole(shape):
    return pl.BlockSpec(shape, lambda *a: (0,) * len(shape))


def sds(shape, dtype):
    return jax.ShapeDtypeStruct(shape, dtype)


def rope_tables():
    middle = HEAD_FEATURES // 2
    frequency = 10000.0 ** (-np.arange(middle, dtype=np.float64) * 2.0 / HEAD_FEATURES)
    angles = np.arange(MAXLEN, dtype=np.float64)[:, None] * frequency[None, :]
    cosine, sine = np.cos(angles), np.sin(angles)
    none = np.zeros_like(sine)
    table = np.stack(
        [
            np.concatenate([cosine, cosine] * 2, axis=1),
            np.concatenate([-sine, none] * 2, axis=1),
            np.concatenate([none, sine] * 2, axis=1),
        ]
    )
    return table.astype(np.float32)


def rotate(u, table, sign):
    up = pltpu.roll(u, PAIR - HEAD_FEATURES // 2, 1)
    down = pltpu.roll(u, HEAD_FEATURES // 2, 1)
    if sign > 0:
        return u * table[0] + (up * table[1] + down * table[2])
    return u * table[0] - (up * table[1] + down * table[2])


def pair_of(value, side):
    left, right = (value[:, a * PAIR : (a + 1) * PAIR] for a in side)
    lane = lax.broadcasted_iota(jnp.int32, (1, PAIR), 1)
    return jnp.where(lane < HEAD_FEATURES, left, right)


def slots(start):
    return start + lax.broadcasted_iota(jnp.int32, (PIECE, 1), 0)


def piece_rows(half, place):
    return pl.ds(pl.multiple_of(half * 2 * PIECE + place * PIECE, PIECE), PIECE)


def project_body(s, own, part, gain, wq, wk, wv, table, *rest):
    qkv, normed, copy = rest[-3:]
    low_x = jnp.where(pl.program_id(0) == s[CORE], own[0], part[0])
    copy[...] = low_x
    x = low_x.astype(f32)
    r = lax.rsqrt(jnp.mean(x * x, axis=-1, keepdims=True) + epsilon)
    low = (x * r * gain[0:1, :].astype(f32)).astype(bf16)
    normed[...] = low
    width = wq.shape[1]
    for m, w in enumerate((wq, wk, wv)):
        u = mm(low, w[...])
        if m == 0:
            u = u * (1.0 / math.sqrt(HEAD_FEATURES))
        for p in range(width // PAIR):
            v = pair_of(u, SIDES[p])
            if m < 2:
                v = rotate(v, table, 1)
            at = m * width + p * PAIR
            qkv[:, at : at + PAIR] = v.astype(bf16)


def project(scalars, own, part, half, gain, weights, table, filled):
    width = weights[0].shape[0]
    cols = width // 2
    place = lambda t, s: (s[half] * 2 + t, 0)
    source = lambda a: pl.BlockSpec((1, PIECE, width), lambda t, s: (s[CHIP] if a.shape[0] > 1 else 0, 0, 0))
    weight_spec = pl.BlockSpec((width, cols), lambda t, s: (0, s[CORE]))
    in_specs = [
        source(own),
        source(part),
        whole((2, width)),
        weight_spec,
        weight_spec,
        weight_spec,
        pl.BlockSpec((3, PIECE, PAIR), lambda t, s: (0, s[half] * 2 + t, 0)),
    ]
    args = [scalars, own, part, gain, *weights, table]
    aliases = None
    if filled is not None:
        in_specs += [pl.BlockSpec(memory_space=pl.ANY)] * 3
        aliases = {len(args) + a: a for a in range(3)}
        args += list(filled)
    return call(
        project_body,
        (2,),
        in_specs,
        [pl.BlockSpec((PIECE, 3 * cols), place), pl.BlockSpec((PIECE, width), place), pl.BlockSpec((PIECE, width), place)],
        [sds((MAXLEN, 3 * cols), bf16), sds((MAXLEN, width), bf16), sds((MAXLEN, width), bf16)],
        aliases=aliases,
    )(*args)


def head_mask(h):
    lane = lax.broadcasted_iota(jnp.int32, (1, PAIR), 1)
    return lane < HEAD_FEATURES if h == 0 else lane >= HEAD_FEATURES


def attend_body(s, q, k, v, out, lse):
    row = lax.broadcasted_iota(jnp.int32, (PIECE, PIECE), 0)
    col = lax.broadcasted_iota(jnp.int32, (PIECE, PIECE), 1)
    lane = lax.broadcasted_iota(jnp.int32, (PIECE, PAIR), 1)
    ones = jnp.ones((MAXLEN, PAIR), bf16)

    def score(b, h):
        at = b * PIECE
        qh = jnp.where(head_mask(h), q[at : at + PIECE, :], jnp.zeros((), bf16))
        near = mm_nt(qh, k[at : at + PIECE, :])
        return near, mm_nt(qh, k[:at, :]) if b else None

    def mix(b, near, far):
        at = b * PIECE
        near = jnp.where(row >= col, near, masked_score)
        top = jnp.max(near, axis=-1, keepdims=True)
        if b:
            top = jnp.maximum(top, jnp.max(far, axis=-1, keepdims=True))
        shift = top * LOG2E
        near = jnp.exp2(near * LOG2E - shift).astype(bf16)
        mixed = mm(near, jnp.concatenate([v[at : at + PIECE, :], ones[:PIECE]], axis=1))
        if b:
            far = jnp.exp2(far * LOG2E - shift).astype(bf16)
            mixed = mixed + mm(far, jnp.concatenate([v[:at, :], ones[:at]], axis=1))
        total = mixed[:, PAIR:]
        return mixed[:, :PAIR] * (1.0 / total), top + jnp.log(total)

    units = [(b, h) for b in range(GROUP) for h in range(2)]
    ahead = score(*units[0])
    done = []
    for at, (b, h) in enumerate(units):
        now = ahead
        if at + 1 < len(units):
            ahead = score(*units[at + 1])
        done.append(mix(b, *now))
        if h == 1:
            rows = slice(b * PIECE, (b + 1) * PIECE)
            (left, left_log), (right, right_log) = done
            done = []
            joined = jnp.where(head_mask(0), left, right)
            out[rows, :] = jnp.where(slots(b * PIECE) < s[LENGTH], joined, 0.0).astype(bf16)
            lse[0, rows, :] = jnp.where(lane == 0, left_log, right_log)


def attend(scalars, qkv):
    pairs = qkv.shape[1] // 3 // PAIR
    spec = lambda m: pl.BlockSpec((MAXLEN, PAIR), lambda p, s, m=m: (0, m * pairs + p))
    return call(
        attend_body,
        (pairs,),
        [spec(0), spec(1), spec(2)],
        [pl.BlockSpec((MAXLEN, PAIR), lambda p, s: (0, p)), pl.BlockSpec((1, MAXLEN, PAIR), lambda p, s: (p, 0, 0))],
        [sds((MAXLEN, pairs * PAIR), bf16), sds((pairs, MAXLEN, PAIR), f32)],
    )(scalars, qkv, qkv, qkv)


def pack_rows(block):
    half = block.shape[0] // 2
    lane = lax.broadcasted_iota(jnp.int32, (1, PAIR), 1)
    top, bottom = block[:half], block[half:]
    left = jnp.where(lane < HEAD_FEATURES, top, pltpu.roll(bottom, HEAD_FEATURES, 1))
    right = jnp.where(lane < HEAD_FEATURES, pltpu.roll(top, HEAD_FEATURES, 1), bottom)
    return left, right


def plane_blocks(s, keep, arrived, targets, rows, with_out):
    size = 2 * rows if with_out else rows
    core = s[CORE]
    for r, target in enumerate(targets):
        place = s[OWN_B] ^ r
        for z in range(4):
            at = pl.ds(pl.multiple_of((2 * z + place % 2) * rows, 16), rows)
            target[z * size : z * size + rows, :] = jnp.where(place // 2 == core, keep[at, :], arrived[at, :])
            if with_out:
                at = pl.ds(pl.multiple_of((8 + z % 2 * 4 + place) * rows, 16), rows)
                target[z * size + rows : (z + 1) * size, :] = jnp.where(z // 2 == core, keep[at, :], arrived[at, :])


def attend_back_body(pair, n_seq, s, *refs):
    first, last = pair == 0, pair == len(SIDES) - 1
    refs = list(refs)
    take = lambda count: [refs.pop(0) for _ in range(count)]
    qkv_hbm, attn_hbm, lse_hbm = take(3)
    if first:
        hidden_hbm, dyb_hbm, mine_hbm, theirs_hbm, gain, layer_hbm, layer_far_hbm = take(7)
    else:
        (dhb_hbm,) = take(1)
    wo_hbm, wq_hbm, wk_hbm, wv_hbm, normed_hbm, table_hbm = take(6)
    earlier = take(len(SIDES) - 1) if last else []
    sent = [] if first else take(2) if n_seq == 8 else []
    if last:
        stay_hbm, leave_hbm, x_hbm, second_in = take(4)
    (keep_out,) = take(1)
    packed = n_seq == 8
    if not (last and packed):
        (send_out,) = take(1)
    if first:
        dhb_out, second, layer_stay, layer_leave = take(4)
    if last:
        norm_keep, norm_send, gains, layer_out = take(4)
        if packed:
            send_out = norm_send.at[pl.ds(MAXLEN, norm_send.shape[0] - MAXLEN), :]
    else:
        (d_out,) = take(1)
    plane = take(4) if sent else []
    q, k, v, o, lse, wo, weights, normed, table, sems = take(10)
    da, da_t, q_t, dk_t, dv_t, dq, grads = take(7)
    if first:
        hidden, dyb, mine, theirs, attn, out_grad, layer, layer_far = take(8)
        dhb = dhb_out
    else:
        (dhb,) = take(1)
    if last:
        before, joined, x, gain_rows = take(4)
    before_sent = take(2) if sent else []
    core = s[CORE]
    width = normed.shape[1]
    zero = jnp.zeros((), bf16)
    pairs = len(SIDES)
    heads = pairs * PAIR
    copies = []

    def fetch(source, target):
        copy = pltpu.make_async_copy(source, target, sems.at[len(copies)])
        copy.start()
        copies.append(copy)
        return copy

    lanes_of = lambda m: slice((m * pairs + pair) * PAIR, (m * pairs + pair + 1) * PAIR)
    chunks = [slice(t * PIECE, (t + 1) * PIECE) for t in range(GROUP)]
    chunk_copies = []
    if first:
        for rows in chunks:
            chunk_copies.append(
                [
                    fetch(source.at[rows, :], target.at[rows, :])
                    for source, target in (
                        (mine_hbm, mine),
                        (theirs_hbm, theirs),
                        (hidden_hbm, hidden),
                        (dyb_hbm, dyb),
                    )
                ]
            )
    wo_copies = [
        fetch(
            wo_hbm.at[pl.ds(pl.multiple_of(core * heads + head * HEAD_FEATURES, HEAD_FEATURES), HEAD_FEATURES), :],
            wo.at[index * HEAD_FEATURES : (index + 1) * HEAD_FEATURES, :],
        )
        for index, head in enumerate(HEAD_ORDER[2 * pair : 2 * pair + 2])
    ]
    if first:
        attn_copy = fetch(attn_hbm, attn)
        lane_o = slice(0, PAIR)
    else:
        dhb_copy = fetch(dhb_hbm, dhb)
    q_copies = [fetch(qkv_hbm.at[:, lanes_of(0)], q), fetch(qkv_hbm.at[:, lanes_of(1)], k)]
    v_copies = [
        fetch(qkv_hbm.at[:, lanes_of(2)], v),
        fetch(attn_hbm.at[:, pair * PAIR : (pair + 1) * PAIR], o),
        fetch(lse_hbm.at[pair], lse),
    ]
    late_copies = [fetch(normed_hbm, normed), fetch(table_hbm, table)]
    late_copies += [fetch(source, target) for source, target in zip(sent, before_sent)]
    for m, w in enumerate((wq_hbm, wk_hbm, wv_hbm)):
        if last:
            late_copies.append(fetch(w.at[:, pl.ds(pl.multiple_of(core * heads, PAIR), heads)], weights.at[m]))
    if first:
        layer_copies = [fetch(layer_hbm, layer), fetch(layer_far_hbm, layer_far)]
    if last:
        late_copies.append(fetch(x_hbm, x))
        late_copies.append(fetch(stay_hbm, layer_out.at[s[CHIP]]))
        late_copies.append(fetch(leave_hbm, layer_out.at[s[OTHER_CHIP]]))
        for at, source in enumerate(earlier):
            late_copies.append(fetch(source, before.at[:, at * heads : (at + 1) * heads]))

    if first:
        scale = gain[1:2, :].astype(f32)
        sums = jnp.zeros((1, width), f32)
        for rows, waiting in zip(chunks, chunk_copies):
            for copy in waiting:
                copy.wait()
            h = hidden[rows, :].astype(f32)
            r = lax.rsqrt(jnp.mean(h * h, axis=-1, keepdims=True) + epsilon)
            g = mine[rows, :].astype(f32) + theirs[rows, :].astype(f32)
            sums = sums + jnp.sum(g * h * r, axis=0, keepdims=True)
            scaled = g * scale
            inner = jnp.mean(scaled * h, axis=-1, keepdims=True)
            d = dyb[rows, :].astype(f32) + r * scaled - h * (r * r * r) * inner
            dhb[rows, :] = d.astype(bf16)
        second[...] = sums * 0.5
    else:
        dhb_copy.wait()
    for copy in wo_copies + q_copies:
        copy.wait()
    for t, rows in enumerate(chunks):
        d = mm_nt(dhb[rows, :], wo[...])
        da[rows, :] = jnp.where(slots(t * PIECE) < s[LENGTH], d, 0.0).astype(bf16)
    da_t[...] = jnp.transpose(da[...])
    q_t[...] = jnp.transpose(q[...])
    for copy in v_copies:
        copy.wait()

    row = lax.broadcasted_iota(jnp.int32, (PIECE, PIECE), 0)
    col = lax.broadcasted_iota(jnp.int32, (PIECE, PIECE), 1)

    def score(a, h):
        at = a * PIECE
        mask = head_mask(h)
        qh = jnp.where(mask, q[at : at + PIECE, :], zero)
        gh = jnp.where(mask, da[at : at + PIECE, :], zero)
        near = mm_nt(qh, k[at : at + PIECE, :]), mm_nt(gh, v[at : at + PIECE, :])
        far = (mm_nt(qh, k[:at, :]), mm_nt(gh, v[:at, :])) if a else None
        return near, far

    def back(a, h, near, far):
        at = a * PIECE
        rows = slice(at, at + PIECE)
        feats = slice(h * HEAD_FEATURES, (h + 1) * HEAD_FEATURES)
        mask = head_mask(h)
        shift = lse[rows, h : h + 1] * LOG2E
        product = da[rows, :].astype(f32) * o[rows, :].astype(f32)
        inner = jnp.sum(jnp.where(mask, product, 0.0), axis=-1, keepdims=True)
        near_prob = jnp.exp2(jnp.where(row >= col, near[0] * LOG2E - shift, masked_score))
        near_ds = (near_prob * (near[1] - inner)).astype(bf16)
        query_grad = mm(near_ds, jnp.where(mask, k[rows, :], zero))
        parts = [(rows, near_prob.astype(bf16), near_ds)]
        if a:
            far_prob = jnp.exp2(far[0] * LOG2E - shift)
            far_ds = (far_prob * (far[1] - inner)).astype(bf16)
            query_grad = query_grad + mm(far_ds, jnp.where(mask, k[:at, :], zero))
            parts.append((slice(0, at), far_prob.astype(bf16), far_ds))
        for cols, prob, ds in parts:
            value_grad = mm(da_t[feats, rows], prob)
            key_grad = mm(q_t[feats, rows], ds)
            if a == GROUP - 1:
                dv_t[feats, cols] = value_grad
                dk_t[feats, cols] = key_grad
            else:
                dv_t[feats, cols] += value_grad
                dk_t[feats, cols] += key_grad
        return query_grad

    units = [(a, h) for a in reversed(range(GROUP)) for h in range(2)]
    ahead = score(*units[0])
    held = None
    for at, (a, h) in enumerate(units):
        now = ahead
        if at + 1 < len(units):
            ahead = score(*units[at + 1])
        g = back(a, h, *now)
        if h == 0:
            held = g
        else:
            dq[a * PIECE : (a + 1) * PIECE, :] = held + g

    for copy in late_copies:
        copy.wait()
    d = jnp.concatenate(
        [
            rotate(dq[...] * (1.0 / math.sqrt(HEAD_FEATURES)), table, -1).astype(bf16),
            rotate(jnp.transpose(dk_t[...]), table, -1).astype(bf16),
            jnp.transpose(dv_t[...].astype(bf16)),
        ],
        axis=1,
    )
    if last:
        before[:, (pairs - 1) * heads :] = d
    else:
        d_out[...] = d
    grads[...] = mm_tn(normed[...], d)
    if sent:
        plane_blocks(s, *before_sent, plane, width // n_seq // 2, pair == 1)

    rows = width // n_seq
    half_row = rows // 2
    if rows % 16:
        keep_out[:width, :] = grads[...].astype(bf16)
    else:
        left_x = SIDES[pair][0] * 2 // pairs
        for target, place in ((keep_out, core), (send_out, 1 - core)):
            for z in range(n_seq // 2):
                at = pl.ds(pl.multiple_of((2 * z + place) * rows, 8), rows)
                for m in range(3):
                    lanes = slice(m * PAIR, (m + 1) * PAIR)
                    left, right = pack_rows(grads[at, lanes])
                    for x_of, value in ((left_x, left), (1 - left_x, right)):
                        to = (2 * z + x_of) * half_row
                        target[to : to + half_row, lanes] = value.astype(bf16)

    if first:
        for copy in layer_copies:
            copy.wait()
        for target, half in ((layer_leave, s[OTHER_CHIP]), (layer_stay, s[CHIP])):
            value = layer[half] + layer_far[half].astype(f32)
            live = slots(half * 2 * PIECE + core * PIECE) < s[LENGTH]
            target[...] = jnp.where(live, value, 0.0).astype(bf16)
        attn_copy.wait()
        g = mm_tn(attn[...], dhb[...])
        for index, head in enumerate(HEAD_ORDER):
            out_grad[head * HEAD_FEATURES : (head + 1) * HEAD_FEATURES, :] = g[
                index * HEAD_FEATURES : (index + 1) * HEAD_FEATURES, :
            ]
        if rows % 16:
            keep_out[width:, :] = jnp.concatenate([out_grad[:, :heads], out_grad[:, heads:]], axis=0).astype(bf16)
        else:
            column = width // 4
            for target, place in ((keep_out, core), (send_out, 1 - core)):
                for z in range(n_seq // 4):
                    block = out_grad[pl.ds(pl.multiple_of((2 * z + place) * rows, 8), rows), :]
                    for b in range(4):
                        lanes = slice(b * column, (b + 1) * column)
                        to = (n_seq + 4 * z + b) * half_row
                        target[to : to + half_row, :] = jnp.concatenate(
                            [block[:half_row, lanes], block[half_row:, lanes]], axis=1
                        ).astype(bf16)
    if last:
        for p, side in enumerate(SIDES):
            for m in range(3):
                at = p * heads + m * PAIR
                joined[:, at : at + PAIR] = pair_of(weights[m], side)
        sums = jnp.zeros((1, width), f32)
        for half in range(2):
            for target, place in ((norm_send, 1 - core), (norm_keep, core)):
                where = piece_rows(half, place)
                part = mm_nt(before[where, :], joined[...])
                if target is norm_keep:
                    target[half] = part.astype(bf16)
                else:
                    for side in range(2):
                        at = (2 * half + side) * PIECE
                        target[at : at + PIECE, :] = part[:, side * heads : (side + 1) * heads].astype(bf16)
                h = x[where, :].astype(f32)
                sums = sums + jnp.sum(part * (h * lax.rsqrt(jnp.mean(h * h, axis=-1, keepdims=True) + epsilon)), axis=0, keepdims=True)
        gain_rows[...] = jnp.zeros_like(gain_rows)
        for index, value in enumerate((sums, second_in[...])):
            for part in range(2):
                gain_rows[2 * index + part : 2 * index + part + 1, :] = value[:, part * heads : (part + 1) * heads]
        high = gain_rows[...].astype(bf16)
        low = (gain_rows[...] - high.astype(f32)).astype(bf16)
        gains[...] = jnp.concatenate([high, low], axis=0)
        if rows % 16 == 0:
            send_out[n_seq * half_row :, :] = gains[...]


def attend_back(pair, scalars, qkv, attn, lse, given, wo, weights, normed, table, earlier, n_seq, sent=()):
    first, last = pair == 0, pair == len(SIDES) - 1
    heads = attn.shape[1]
    width = wo.shape[1]
    rows = width // n_seq
    token_shape = (2, PIECE, width)
    if rows % 16 == 0:
        count = n_seq * rows // 2 * (2 if first else 1)
        shapes = [(count, heads)] * 2
    else:
        shapes = [(2 * width if first else width, heads), (8, 128)]
    extra = shapes[1][0] + 16 if n_seq == 8 else 0
    outs = [sds(a, bf16) for a in shapes[: 1 if last and n_seq == 8 else 2]]
    if first:
        outs += [sds((MAXLEN, width), bf16), sds((1, width), f32)]
        outs += [sds((PIECE, width), bf16)] * 2
    if last:
        outs += [sds(token_shape, bf16), sds((MAXLEN + extra, heads), bf16), sds((16, heads), bf16)]
        outs += [sds(token_shape, bf16)]
    else:
        outs += [sds((MAXLEN, heads), bf16)]
    outs += [sds((2 * rows * (2 if pair == 1 else 1), heads), bf16)] * (4 if sent else 0)
    later = list(earlier[: len(SIDES) - 1]) + list(sent) + list(earlier[len(SIDES) - 1 :])
    args = [qkv, attn, lse, *given, wo, *weights, normed, table, *later]
    in_specs = [pl.BlockSpec(memory_space=pl.ANY)] * len(args)
    if first:
        in_specs[7] = whole((2, width))
    if last:
        in_specs[-1] = whole((1, width))
    scratch = [
        pltpu.VMEM((MAXLEN, PAIR), bf16),
        pltpu.VMEM((MAXLEN, PAIR), bf16),
        pltpu.VMEM((MAXLEN, PAIR), bf16),
        pltpu.VMEM((MAXLEN, PAIR), bf16),
        pltpu.VMEM((MAXLEN, PAIR), f32),
        pltpu.VMEM((PAIR, width), bf16),
        pltpu.VMEM((3, width, heads) if last else (3, 16, 128), bf16),
        pltpu.VMEM((MAXLEN, width), bf16),
        pltpu.VMEM((3, MAXLEN, PAIR), f32),
        pltpu.SemaphoreType.DMA((32,)),
        pltpu.VMEM((MAXLEN, PAIR), bf16),
        pltpu.VMEM((PAIR, MAXLEN), bf16),
        pltpu.VMEM((PAIR, MAXLEN), bf16),
        pltpu.VMEM((PAIR, MAXLEN), f32),
        pltpu.VMEM((PAIR, MAXLEN), f32),
        pltpu.VMEM((MAXLEN, PAIR), f32),
        pltpu.VMEM((width, heads), f32),
    ]
    if first:
        scratch += [
            pltpu.VMEM((MAXLEN, width), bf16),
            pltpu.VMEM((MAXLEN, width), bf16),
            pltpu.VMEM((MAXLEN, width), bf16),
            pltpu.VMEM((MAXLEN, width), bf16),
            pltpu.VMEM((MAXLEN, heads), bf16),
            pltpu.VMEM((heads, width), f32),
            pltpu.VMEM(token_shape, f32),
            pltpu.VMEM(token_shape, bf16),
        ]
    else:
        scratch += [pltpu.VMEM((MAXLEN, width), bf16)]
    if last:
        scratch += [
            pltpu.VMEM((MAXLEN, len(SIDES) * heads), bf16),
            pltpu.VMEM((width, len(SIDES) * heads), bf16),
            pltpu.VMEM((MAXLEN, width), bf16),
            pltpu.VMEM((8, heads), f32),
        ]
    if sent:
        scratch += [pltpu.VMEM(a.shape, bf16) for a in sent]
    return call(
        functools.partial(attend_back_body, pair, n_seq),
        (1,),
        in_specs,
        [whole(a.shape) for a in outs],
        outs,
        scratch=scratch,
    )(scalars, *args)


def feed_body(
    packed, s, x_hbm, dy_hbm, dy_pair_hbm, dy_far_hbm, dy_far_pair_hbm, attn_hbm, attn_pair_hbm, wo_hbm, gain, *refs
):
    refs = list(refs)
    take = lambda count: [refs.pop(0) for _ in range(count)]
    wg_hbm, wu_hbm, wd_hbm = take(3)
    hidden_out, dyb_out, dn_out, layer_out, send_out = take(5)
    grads_out = take(6 if packed else 3)
    x, attn, wo, wg, wu, wd, dyb = take(7)
    hidden, hidden_low, low, low_t, dyb_t, acts, dgs, dus, total, dn, layer, send = take(12)
    blocks = take(6 if packed else 3)
    (sems,) = take(1)
    core = s[CORE]
    tokens, width = x.shape
    heads = width // 2
    steps = 4
    cols = wg.shape[1] // steps
    used = [0]

    def copy(source, target):
        made = pltpu.make_async_copy(source, target, sems.at[used[0]])
        used[0] += 1
        made.start()
        return made

    chunks = [slice(t * PIECE, (t + 1) * PIECE) for t in range(GROUP)]
    unit = [2 * ((3 - step) ^ s[OWN_B]) + core for step in range(steps)]

    wo_copies = [
        copy(
            wo_hbm.at[pl.ds(pl.multiple_of(place * heads + head * HEAD_FEATURES, HEAD_FEATURES), HEAD_FEATURES), :],
            wo.at[at * heads + index * HEAD_FEATURES : at * heads + (index + 1) * HEAD_FEATURES, :],
        )
        for at, place in enumerate((core, 1 - core))
        for index, head in enumerate(HEAD_ORDER)
    ]
    token_copies = [
        [
            copy(x_hbm.at[rows, :], x.at[rows, :]),
            copy(attn_hbm.at[rows, :], attn.at[rows, :heads]),
            copy(attn_pair_hbm.at[rows, :], attn.at[rows, heads:]),
        ]
        for rows in chunks
    ]
    def weights_of(step):
        at = pl.ds(pl.multiple_of(unit[step] * cols, cols), cols)
        here = slice(step * cols, (step + 1) * cols)
        return [
            copy(wg_hbm.at[:, at], wg.at[:, here]),
            copy(wu_hbm.at[:, at], wu.at[:, here]),
            copy(wd_hbm.at[at, :], wd.at[here, :]),
        ]

    dy_copies = [
        copy(source, dyb.at[piece_rows(half, place), :])
        for source, half, place in (
            (dy_hbm.at[s[CHIP]], s[CHIP], core),
            (dy_pair_hbm.at[s[CHIP]], s[CHIP], 1 - core),
            (dy_far_hbm.at[0], s[OTHER_CHIP], core),
            (dy_far_pair_hbm.at[0], s[OTHER_CHIP], 1 - core),
        )
    ]
    out_copies = []

    for made in wo_copies:
        made.wait()
    scale = gain[1:2, :].astype(f32)
    weight_copies = [weights_of(0)]
    for t, rows in enumerate(chunks):
        for made in token_copies[t]:
            made.wait()
        h = x[rows, :].astype(f32) + mm(attn[rows, :], wo[...])
        hidden[rows, :] = h
        hidden_low[rows, :] = h.astype(bf16)
        out_copies.append(copy(hidden_low.at[rows, :], hidden_out.at[rows, :]))
        r = lax.rsqrt(jnp.mean(h * h, axis=-1, keepdims=True) + epsilon)
        low[rows, :] = (h * r * scale).astype(bf16)
    low_t[...] = jnp.transpose(low[...])
    for made in dy_copies:
        made.wait()
    for t, rows in enumerate(chunks):
        dyb[rows, :] = jnp.where(slots(t * PIECE) < s[LENGTH], dyb[rows, :], jnp.zeros((), bf16))
    dyb_t[...] = jnp.transpose(dyb[...])
    out_copies.append(copy(dyb, dyb_out))

    def products(step, t):
        if t == 0:
            for made in weight_copies.pop():
                made.wait()
            if step + 1 < steps:
                weight_copies.append(weights_of(step + 1))
        rows, here = chunks[t], slice(step * cols, (step + 1) * cols)
        return mm(low[rows, :], wg[:, here]), mm(low[rows, :], wu[:, here]), mm_nt(dyb[rows, :], wd[here, :])

    def pointwise(step, t, gate, up, dact):
        rows, here = chunks[t], slice(step * cols, (step + 1) * cols)
        sig = 1.0 / (1.0 + jnp.exp2(gate * -LOG2E))
        silu = gate * sig
        acts[rows, here] = (silu * up).astype(bf16)
        dgs[rows, here] = (dact * up * (sig + silu * (1.0 - sig))).astype(bf16)
        dus[rows, here] = (dact * silu).astype(bf16)

    def emit(grad, own, write):
        total[...] = grad
        rows = width // 4
        for b in range(4):
            write(b // 2, b % 2, total[pl.ds(pl.multiple_of((b ^ own) * rows, 16), rows), :].astype(bf16))

    def weight_grads(step, which):
        here = slice(step * cols, (step + 1) * cols)
        if which == 0:
            grad = mm(low_t[...], dgs[:, here])
        elif which == 1:
            grad = mm(low_t[...], dus[:, here])
        else:
            grad = mm(dyb_t[...], acts[:, here])
        if not packed:
            at = pl.ds(pl.multiple_of(unit[step] // 2 * cols, cols), cols)
            blocks[which][:, here] = grad.astype(bf16)
            out_copies.append(copy(blocks[which].at[:, here], grads_out[which].at[:, at]))
            return
        y, x_side = (3 - step) // 2, (3 - step) % 2
        if which == 0:
            target, target_out = (blocks[0], grads_out[0]) if x_side else (blocks[1], grads_out[1])

            def write(z1, z0, value):
                target[y, z0, z1] = value

            emit(grad, s[OWN_Z], write)
            out_copies.append(copy(target.at[y], target_out.at[y]))
        elif which == 1:
            target, target_out = (blocks[2], grads_out[2]) if y else (blocks[3], grads_out[3])

            def write(z1, z0, value):
                target[z0, z1, x_side] = value

            emit(grad, s[OWN_Z], write)
            out_copies.append(copy(target.at[:, :, x_side], target_out.at[:, :, x_side]))
        else:
            z = (unit[step] // 2) ^ s[OWN_Z]

            def write(y, x, value):
                @pl.when(z % 2 == 1)
                def _():
                    blocks[4][x, z // 2, y] = value

                @pl.when(z % 2 == 0)
                def _():
                    blocks[5][x, z // 2, y] = value

            emit(grad, s[OWN_B], write)
            if step == steps - 1:
                for at in (4, 5):
                    out_copies.append(copy(blocks[at], grads_out[at]))

    units = [(step, t) for step in range(steps) for t in range(GROUP)]
    ahead = products(*units[0])
    for index, (step, t) in enumerate(units):
        now = ahead
        if index + 1 < len(units):
            ahead = products(*units[index + 1])
        pointwise(step, t, *now)
        if step and t < 3:
            weight_grads(step - 1, t)
    for which in range(3):
        weight_grads(steps - 1, which)
    for rows in chunks:
        dn[rows, :] = (mm_nt(dgs[rows, :], wg[...]) + mm_nt(dus[rows, :], wu[...])).astype(bf16)
        out_copies.append(copy(dn.at[rows, :], dn_out.at[rows, :]))
    for half in range(2):
        send[half] = mm(acts[piece_rows(half, 1 - core), :], wd[...]).astype(bf16)
        out_copies.append(copy(send.at[half], send_out.at[half]))
    for half in range(2):
        rows = piece_rows(half, core)
        layer[half] = hidden[rows, :] + mm(acts[rows, :], wd[...])
        out_copies.append(copy(layer.at[half], layer_out.at[half]))
    for made in out_copies:
        made.wait()


def feed(scalars, x, dy, dy_pair, dy_far, dy_far_pair, attn, attn_pair, wo, gain, wg, wu, wd, packed):
    tokens, width = x.shape
    units = wg.shape[1] // 2
    cols = units // 4
    token_shape = (2, PIECE, width)
    if packed:
        shapes = [(2, 2, 2, width // 4, cols)] * 6
    else:
        shapes = [(width, units)] * 3
    outs = [
        sds((tokens, width), bf16),
        sds((tokens, width), bf16),
        sds((tokens, width), bf16),
        sds(token_shape, f32),
        sds(token_shape, bf16),
    ] + [sds(a, bf16) for a in shapes]
    args = [x, dy, dy_pair, dy_far, dy_far_pair, attn, attn_pair, wo, gain, wg, wu, wd]
    in_specs = [pl.BlockSpec(memory_space=pl.ANY)] * len(args)
    in_specs[8] = whole((2, width))
    low = pltpu.VMEM((tokens, width), bf16)
    high = pltpu.VMEM((tokens, width), f32)
    turned = pltpu.VMEM((width, tokens), bf16)
    hidden_units = pltpu.VMEM((tokens, units), bf16)
    return call(
        functools.partial(feed_body, packed),
        (1,),
        in_specs,
        [pl.BlockSpec(memory_space=pl.ANY)] * len(outs),
        outs,
        scratch=[
            low,
            low,
            pltpu.VMEM((width, width), bf16),
            pltpu.VMEM((width, units), bf16),
            pltpu.VMEM((width, units), bf16),
            pltpu.VMEM((units, width), bf16),
            low,
            high,
            low,
            low,
            turned,
            turned,
            hidden_units,
            hidden_units,
            hidden_units,
            pltpu.VMEM((width, cols), f32),
            low,
            pltpu.VMEM(token_shape, f32),
            pltpu.VMEM(token_shape, bf16),
        ]
        + [pltpu.VMEM(a, bf16) for a in shapes]
        + [pltpu.SemaphoreType.DMA((80,))],
    )(scalars, *args)


def piece_of(half, side):
    return pl.ds(pl.multiple_of((2 * half + side) * PIECE, PIECE), PIECE)


def finish_body(s, x, keep, recv, dh, gain, stay, leave):
    scale = gain[0:1, :].astype(f32)
    for out, half in ((leave, s[OTHER_CHIP]), (stay, s[CHIP])):
        h = x[half, 0].astype(f32)
        there = jnp.concatenate([recv[piece_of(half, side), :] for side in range(2)], axis=1)
        dn = keep[half].astype(f32) + there.astype(f32)
        r = lax.rsqrt(jnp.mean(h * h, axis=-1, keepdims=True) + epsilon)
        scaled = dn * scale
        inner = jnp.mean(scaled * h, axis=-1, keepdims=True)
        out[...] = (dh[half, 0].astype(f32) + r * scaled - h * (r * r * r) * inner).astype(bf16)


def finish(scalars, x, keep, recv, dh, gain):
    width = x.shape[1]
    shape = (2, PIECE, width)
    own = pl.BlockSpec((2, 1, PIECE, width), lambda f, s: (0, s[CORE], 0, 0))
    return call(
        finish_body,
        (1,),
        [own, whole(shape), whole((MAXLEN, recv.shape[1])), own, whole((2, width))],
        [whole((PIECE, width))] * 2,
        [sds((PIECE, width), bf16)] * 2,
    )(scalars, x.reshape(2, 2, PIECE, width), keep, recv, dh.reshape(2, 2, PIECE, width), gain)


def decode(coded):
    return coded[:8].astype(f32) + coded[8:].astype(f32)


def encode(value):
    high = value.astype(bf16)
    return jnp.concatenate([high, (value - high.astype(f32)).astype(bf16)], axis=0)


def sum_parts(fetch, groups, scratch):
    loads = []
    for group in groups:
        loads.append([])
        for source in group:
            target = scratch.pop(0)
            loads[-1].append((fetch(source, target), target))

    def total(group):
        value = None
        for made, target in group:
            made.wait()
            part = target[...].astype(f32)
            value = part if value is None else value + part
        return value

    return [functools.partial(total, group) for group in loads]


def fetcher(sems):
    used = [0]

    def fetch(source, target):
        made = pltpu.make_async_copy(source, target, sems.at[used[0]])
        used[0] += 1
        made.start()
        return made

    return fetch


def feed_step_body(paths, s, *refs):
    refs = list(refs)
    groups = [[refs.pop(0).at[path] for path in group] for group in paths]
    outs = [refs.pop(0) for _ in groups]
    sems = refs.pop()
    for out, total in zip(outs, sum_parts(fetcher(sems), groups, refs)):
        out[...] = total().astype(bf16)


def feed_step(scalars, reductions):
    groups = [r.paths(1) for r in reductions]
    args = [array for group in groups for array, _ in group]
    paths = [[path for _, path in group] for group in groups]
    slices = [array.shape[len(path) :] for group in groups for array, path in group]
    outs = [sds(group[0][0].shape[len(group[0][1]) :], bf16) for group in groups]
    return call(
        functools.partial(feed_step_body, paths),
        (1,),
        [pl.BlockSpec(memory_space=pl.ANY)] * len(args),
        [whole(a.shape) for a in outs],
        outs,
        scratch=[pltpu.VMEM(a, bf16) for a in slices] + [pltpu.SemaphoreType.DMA((len(args),))],
    )(scalars, *args)


def third_step_body(paths, s, keep_hbm, arrived_hbm, gains, *refs):
    refs = list(refs)
    groups = [[refs.pop(0).at[path] for path in group] for group in paths]
    parts_hbm = [refs.pop(0) for _ in range(4)]
    plane = [refs.pop(0) for _ in range(4)]
    line_send, line_keep = refs.pop(0), refs.pop(0)
    sends, kept = [refs.pop(0) for _ in range(3)], refs.pop(0)
    keep, arrived = refs.pop(0), refs.pop(0)
    parts = [refs.pop(0) for _ in range(4)]
    sems = refs.pop()
    fetch = fetcher(sems)
    rows = keep.shape[0] // 8
    first = [
        fetch(keep_hbm, keep),
        fetch(arrived_hbm.at[pl.ds(MAXLEN, arrived.shape[0]), :], arrived),
    ]
    second = [fetch(source, target) for source, target in zip(parts_hbm, parts)]
    totals = sum_parts(fetch, groups, refs)
    for made in first:
        made.wait()
    plane_blocks(s, keep, arrived, plane, rows, False)
    coded = encode(decode(gains[...]) + decode(arrived[8 * rows :, :]))
    for target in plane:
        target[4 * rows :, :] = coded
    for made in second:
        made.wait()
    size = line_keep.shape[0] // 2
    own = s[OWN_Z] % 2
    for target, z0 in ((line_send, 1 - own), (line_keep, own)):
        for z1 in range(2):
            at = pl.ds(pl.multiple_of((2 * z1 + z0) * size, 16), size)
            total = None
            for part in parts:
                value = part[at, :].astype(f32)
                total = value if total is None else total + value
            target[z1 * size : (z1 + 1) * size, :] = total.astype(bf16)
    for index in range(3):
        sends[index][...] = totals[index]().astype(bf16)
        kept[index] = totals[3 + index]()


def third_step(scalars, keep, arrived, gains, parts, reductions):
    groups = [r.paths(1) for r in reductions] + [r.paths(0) for r in reductions]
    sums = [array for group in groups for array, _ in group]
    paths = [[path for _, path in group] for group in groups]
    slices = [array.shape[len(path) :] for group in groups for array, path in group]
    rows, columns = keep.shape
    outs = [sds((rows // 2 + 16, columns), bf16)] * 4
    outs += [sds((parts[0].shape[0] // 2, columns), bf16)] * 2
    outs += [sds(slices[0], bf16)] * 3 + [sds((3,) + slices[0], f32)]
    hbm = pl.BlockSpec(memory_space=pl.ANY)
    return call(
        functools.partial(third_step_body, paths),
        (1,),
        [hbm, hbm, whole(gains.shape)] + [hbm] * (len(sums) + 4),
        [whole(a.shape) for a in outs],
        outs,
        scratch=[pltpu.VMEM(keep.shape, bf16), pltpu.VMEM((rows + 16, columns), bf16)]
        + [pltpu.VMEM(a.shape, bf16) for a in parts]
        + [pltpu.VMEM(a, bf16) for a in slices]
        + [pltpu.SemaphoreType.DMA((len(sums) + 6,))],
    )(scalars, keep, arrived, gains, *sums, *parts)


def second_line_body(s, *refs):
    middle, last, (keep0, arrived0), outs = refs[:4], refs[4:8], refs[8:10], refs[10:]
    rows = middle[0].shape[0] // 4
    coded = [ref[4 * rows :, :] for ref in last]
    gains = encode((decode(coded[0]) + decode(coded[1])) + (decode(coded[2]) + decode(coded[3])))
    for r, target in enumerate(outs[:4]):
        at = pl.ds(pl.multiple_of((s[OWN_Z] ^ r) * rows, 16), rows)
        for index, parts in enumerate((middle, last)):
            total = None
            for part in parts:
                value = part[at, :].astype(f32)
                total = value if total is None else total + value
            target[index * rows : (index + 1) * rows, :] = total.astype(bf16)
        target[2 * rows :, :] = gains
    size = keep0.shape[0] // 2
    own = s[OWN_Z] // 2
    for target, z1 in ((outs[4], own), (outs[5], 1 - own)):
        at = pl.ds(pl.multiple_of(z1 * size, 16), size)
        target[...] = (keep0[at, :].astype(f32) + arrived0[at, :].astype(f32)).astype(bf16)


def second_line(scalars, middle, last, keep0, arrived0):
    rows, columns = middle[0].shape[0] // 4, middle[0].shape[1]
    outs = [sds((2 * rows + 16, columns), bf16)] * 4 + [sds((keep0.shape[0] // 2, columns), bf16)] * 2
    args = [*middle, *last, keep0, arrived0]
    return call(
        second_line_body,
        (1,),
        [whole(a.shape) for a in args],
        [whole(a.shape) for a in outs],
        outs,
    )(scalars, *args)


def feed_total_body(s, keep, gate, up, down, side_keep, side_send, down_out):
    rows = side_keep.shape[1]
    for index in range(2):
        value = keep[index] + (gate, up)[index][...].astype(f32)
        for part in range(2):
            block = value[part * rows : (part + 1) * rows]

            @pl.when(s[CORE] == part)
            def _():
                side_keep[index] = block

            @pl.when(s[CORE] != part)
            def _():
                side_send[index] = block.astype(bf16)

    down_out[...] = keep[2] + down[...].astype(f32)


def feed_total(scalars, keep, arrived):
    rows, cols = keep.shape[1:]
    outs = [sds((2, rows // 2, cols), f32), sds((2, rows // 2, cols), bf16), sds((rows, cols), f32)]
    args = [keep, *arrived]
    return call(
        feed_total_body,
        (1,),
        [whole(a.shape) for a in args],
        [whole(a.shape) for a in outs],
        outs,
    )(scalars, *args)


def shards_body(s, keep0, arrived0, line0, line1, line2, line3, side_keep, side_arrived, stay, back, *outs):
    half, width = outs[0].shape[0] // 2, outs[0].shape[1]
    first = keep0[...].astype(f32) + arrived0[...].astype(f32)
    rest = (line0[...].astype(f32) + line1[...].astype(f32)) + (line2[...].astype(f32) + line3[...].astype(f32))
    out = first[half:]
    outs[3][:half, :] = out[:, :width]
    outs[3][half:, :] = out[:, width:]
    for pair, part in enumerate((first[:half], rest[:half], rest[half : 2 * half])):
        lanes = slice(pair * HEAD_FEATURES, (pair + 1) * HEAD_FEATURES)
        for m in range(3):
            at = m * PAIR
            outs[m][:half, lanes] = part[:, at : at + HEAD_FEATURES]
            outs[m][half:, lanes] = part[:, at + HEAD_FEATURES : at + PAIR]
    gains = rest[2 * half : 2 * half + 8] + rest[2 * half + 8 :]
    for index in range(2):
        row = jnp.concatenate([gains[2 * index : 2 * index + 1], gains[2 * index + 1 : 2 * index + 2]], axis=1)
        for at in range(outs[6].shape[0]):
            outs[6 + index][at : at + 1, :] = row[:, at * PAIR : (at + 1) * PAIR]
    cols = side_keep.shape[2]
    for index in range(2):
        for core in range(2):

            @pl.when(s[CORE] == core)
            def _():
                outs[4 + index][:, core * cols : (core + 1) * cols] = side_keep[index]
                outs[4 + index][:, (1 - core) * cols : (2 - core) * cols] = side_arrived[index].astype(f32)

    outs[8][s[CHIP]] = stay[...]
    outs[8][s[OTHER_CHIP]] = back[...]


def make_shards(scalars, args, rows, columns, width):
    side = sds((rows, 2 * args[6].shape[-1]), f32)
    outs = [sds((rows, columns), f32)] * 4 + [side] * 2 + [sds((width // PAIR, PAIR), f32)] * 2
    outs.append(sds((2,) + args[-1].shape, bf16))
    return call(
        shards_body,
        (1,),
        [whole(a.shape) for a in args],
        [whole(a.shape) for a in outs],
        outs,
    )(scalars, *args)


def exchange_by(block, axis, difference, name):
    count = lax.axis_size(axis)
    with jax.named_scope(name):
        return lax.ppermute(block, axis, [(a, a ^ difference) for a in range(count)])


def exchange(block, axis, bit, name="swap"):
    return exchange_by(block, axis, 1 << bit, name)


def pick(block, index, dim):
    return lax.dynamic_index_in_dim(block, index, dim, keepdims=False)


def together(*values):
    return lax.optimization_barrier(values)


X, Y, Z0, Z1 = ("batch", 0), ("batch", 1), ("seq", 1), ("seq", 2)


class Reduction:
    def __init__(self, order, keep, send):
        self.order, self.level, self.send, self.parts = order, 0, send, [keep]

    def go(self):
        bit = self.order[self.level]
        self.arrived = exchange(self.send, *bit, "feed_" + "_".join(map(str, bit)))
        return self

    def paths(self, side):
        found = []
        for index, array in enumerate([*self.parts, self.arrived]):
            found.append((array, (0,) * (self.level - max(index - 1, 0)) + (side,)))
        return found

    def next(self, send):
        self.parts.append(self.arrived)
        self.send = send
        self.level += 1
        return self


def start_all(reductions, *others):
    sends = together(*[r.send for r in reductions], *others)
    for r, send in zip(reductions, sends):
        r.send = send
        r.go()
    return sends[len(reductions) :]


def wait_all(reductions, *others):
    values = together(*[r.arrived for r in reductions], *others)
    for r, arrived in zip(reductions, values):
        r.arrived = arrived
    return values[len(reductions) :]


def body(
    states,
    lengths,
    first_gain,
    query_weight,
    key_weight,
    value_weight,
    output_weight,
    second_gain,
    gate_weight,
    up_weight,
    down_weight,
    cotangent,
):
    tokens, width = states.shape
    n_seq, n_batch = lax.axis_size("seq"), lax.axis_size("batch")
    packed = n_seq == 8 and n_batch == 4
    place = lax.axis_index("seq")
    batch = lax.axis_index("batch")
    core = place & 1
    chip = place >> 1 & 1
    sequence = (batch * (n_seq // GROUP) + place // GROUP) * 2 + chip
    length = pick(lengths, sequence, 0)
    own_b, own_z = batch & 3, place >> 1 & 3
    scalars = jnp.stack([core, chip, length, 1 - chip, own_b, own_z]).astype(jnp.int32)
    table = jnp.asarray(rope_tables())
    both_gains = jnp.stack([first_gain, second_gain])
    weights = (query_weight, key_weight, value_weight)

    held = states.reshape(2, PIECE, width)
    held_back = cotangent.reshape(2, PIECE, width)
    far = exchange(pick(held, 1 - chip, 0), *Z0, "states_far")[None]
    held_pair = exchange(held, "seq", 0, "states_pair")
    filled = project(scalars, held, held_pair, CHIP, both_gains, weights, table, None)
    far, leaving, *filled = together(far, pick(held_back, 1 - chip, 0), *filled)
    far_pair = exchange(far, "seq", 0, "states_far_pair")
    back_far = exchange(leaving, *Z0, "cotangent_far")[None]
    back_pair = exchange(held_back, "seq", 0, "cotangent_pair")
    qkv, normed, x = project(scalars, far, far_pair, OTHER_CHIP, both_gains, weights, table, filled)
    attn, lse = attend(scalars, qkv)
    attn_pair = exchange(attn, "seq", 0, "attn_pair")
    back_far, attn = together(back_far, attn)
    back_far_pair = exchange(back_far, "seq", 0, "cotangent_far_pair")
    hidden, dyb, dn, layer_keep, layer_send, *feed_grads = feed(
        scalars,
        x,
        held_back,
        back_pair,
        back_far,
        back_far_pair,
        attn,
        attn_pair,
        output_weight,
        both_gains,
        gate_weight,
        up_weight,
        down_weight,
        packed,
    )
    if packed:
        gate_send, gate_keep, up_send, up_keep, down_send, down_keep = feed_grads
        gate = Reduction([X, Y, Z0, Z1], gate_keep, gate_send).go()
        up = Reduction([Y, Z0, Z1, X], up_keep, up_send).go()
        down = Reduction([Z0, X, Z1, Y], down_keep, down_send).go()
    dn_pair = exchange(dn, "seq", 0, "dn_pair")
    layer_arrived = exchange(layer_send, "seq", 0, "layer_pair")

    def back(pair, given, later, sent=()):
        return attend_back(
            pair, scalars, qkv, attn, lse, given, output_weight, weights, normed, table, later, n_seq, sent
        )

    keep0, send0, dhb, second, layer_stay, layer_leave, d0 = back(
        0, [hidden, dyb, dn, dn_pair, both_gains, layer_keep, layer_arrived], []
    )

    def in_order(kept, arrived):
        return jnp.concatenate(
            [jnp.where(chip == 0, kept, arrived), jnp.where(chip == 0, arrived, kept)], axis=0
        )

    if packed:
        rows = width // n_seq // 2

        def to_plane(parts, name):
            return [parts[0]] + [exchange_by(parts[r], "batch", r, name + str(r)) for r in (1, 2, 3)]

        feeds = [gate, up, down]
        keep0, send0, dhb, second, layer_stay, layer_leave, d0 = wait_all(
            feeds, keep0, send0, dhb, second, layer_stay, layer_leave, d0
        )
        arrived0 = exchange(send0, "seq", 0, "grad0_pair")
        layer_back = exchange(layer_leave, *Z0, "layer_back")
        for r, send in zip(feeds, feed_step(scalars, feeds)):
            r.next(send)
        (dhb,) = start_all(feeds, dhb)
        keep1, send1, d1, *plane0 = back(1, [dhb], [], (keep0, arrived0))

        layer_back, keep1, send1, d1, *plane0 = wait_all(feeds, layer_back, keep1, send1, d1, *plane0)
        arrived1 = exchange(send1, "seq", 0, "grad1_pair")
        flow0 = to_plane(plane0, "plane0_")
        for r, send in zip(feeds, feed_step(scalars, feeds)):
            r.next(send)
        (arrived1, d1) = start_all(feeds, arrived1, d1)
        keep2, norm_keep, norm_send, gains, layer_out, *plane1 = back(
            2, [dhb], [d0, d1, layer_stay, layer_back, x, second], (keep1, arrived1)
        )

        flow0[1], flow0[2], flow0[3], keep2, norm_keep, norm_send, gains, layer_out, *plane1 = wait_all(
            feeds, *flow0[1:], keep2, norm_keep, norm_send, gains, layer_out, *plane1
        )
        layer_out = layer_out.reshape(tokens, width)
        norm_arrived = exchange(norm_send, "seq", 0, "dn1_pair")
        flow1 = to_plane(plane1, "plane1_")
        *plane2, line0_send, line0_keep, gate_send, up_send, down_send, feed_keep = third_step(
            scalars, keep2, norm_arrived, gains, flow0, feeds
        )
        flow2 = to_plane(plane2, "plane2_")
        arrived0 = exchange(line0_send, *Z0, "line0")
        for r, send in zip(feeds, (gate_send, up_send, down_send)):
            r.next(send).go()
        stay, leave = finish(scalars, x, norm_keep, norm_arrived, dhb, both_gains)
        grad_back = exchange(leave, *Z0, "grad_back")
        stay, line0_keep, arrived0, *flow12 = together(stay, line0_keep, arrived0, *flow1, *flow2)
        flow1, flow2 = flow12[:4], flow12[4:]
        *lines, last_keep, last_send = second_line(scalars, flow1, flow2, line0_keep, arrived0)
        lines = [lines[0]] + [exchange_by(lines[r], "seq", 2 * r, "line12_" + str(r)) for r in (1, 2, 3)]
        last_arrived = exchange(last_send, *Z1, "line0_last")
        (last_keep,) = wait_all(feeds, last_keep)
        side_keep, side_send, down_grad = feed_total(scalars, feed_keep, [r.arrived for r in feeds])
        down_grad = jnp.transpose(down_grad)
        side_arrived = exchange(side_send, "seq", 0, "feed_pair")
        *shards, gate_grad, up_grad, first, second, input_grad = make_shards(
            scalars,
            [last_keep, last_arrived, *lines, side_keep, side_arrived, stay, grad_back],
            2 * rows,
            width // n_batch,
            width,
        )
        first, second, input_grad = first.reshape(width), second.reshape(width), input_grad.reshape(tokens, width)
    else:
        keep1, _, d1 = back(1, [dhb], [])
        layer_back = exchange(layer_leave, *Z0)
        keep2, _, norm_keep, norm_send, gains, layer_out = back(2, [dhb], [d0, d1, layer_stay, layer_back, x, second])
        norm_arrived = exchange(norm_send, "seq", 0)
        stay, leave = finish(scalars, x, norm_keep, norm_arrived, dhb, both_gains)
        layer_out = layer_out.reshape(tokens, width)
        input_grad = in_order(stay, exchange(leave, *Z0))
        gains = gains[:8].astype(f32) + gains[8:].astype(f32)
        for axis in ("seq", "batch"):
            for bit in range(int(math.log2(lax.axis_size(axis)))):
                gains = gains + exchange(gains, axis, bit)
        first, second = gains[:2].reshape(width), gains[2:4].reshape(width)
        gate_keep, up_keep, down_keep = feed_grads
        units = gate_keep.shape[1]
        zeros = lambda shape: jnp.zeros(shape, bf16)
        blocks = 4

        def spread(array):
            parts = array.reshape(width, blocks, 1, units // blocks)
            full = zeros((width, blocks, 2, units // blocks))
            return lax.dynamic_update_slice_in_dim(full, parts, core, 2).reshape(width, 2 * units)

        heads = attn.shape[1]
        out_keep = jnp.concatenate([keep0[width : width + heads], keep0[width + heads :]], axis=1)
        columns = lambda a: lax.dynamic_update_slice_in_dim(zeros((width, width)), a, core * heads, 1)

        def by_head(m):
            found = {}
            for index, head in enumerate(HEAD_ORDER):
                at = m * PAIR + index % 2 * HEAD_FEATURES
                found[head] = (keep0, keep1, keep2)[index // 2][:width, at : at + HEAD_FEATURES]
            return jnp.concatenate([found[head] for head in sorted(found)], axis=1)

        full = [columns(by_head(m)) for m in range(3)]
        full.append(lax.dynamic_update_slice_in_dim(zeros((width, width)), out_keep, core * heads, 0))
        full += [spread(gate_keep), spread(up_keep), jnp.transpose(spread(down_keep))]
        full = [lax.psum_scatter(a.astype(f32), "seq", scatter_dimension=0, tiled=True) for a in full]
        full = [lax.psum_scatter(a, "batch", scatter_dimension=1, tiled=True) for a in full]
        shards, (gate_grad, up_grad, down_grad) = full[:4], full[4:]

    return (
        layer_out,
        input_grad,
        first,
        shards[0],
        shards[1],
        shards[2],
        shards[3],
        second,
        gate_grad,
        up_grad,
        down_grad,
    )


def solution(mesh):
    split = P(("batch", "seq"), None)
    in_specs = (split,) + (P(),) * 10 + (split,)
    shard = P("seq", "batch")
    out_specs = (split, split, P(), shard, shard, shard, shard, P(), shard, shard, shard)
    return jax.shard_map(body, mesh=mesh, in_specs=in_specs, out_specs=out_specs, check_vma=False)
```

```python
import functools
import math

import jax
import jax.numpy as jnp
import numpy as np
from jax import lax
from jax.experimental import pallas as pl
from jax.experimental.pallas import tpu as pltpu
from jax.sharding import PartitionSpec as P

HEADS = 12
HEAD_FEATURES = 64
MAXLEN = 1024
GROUP = 4
PIECE = MAXLEN // GROUP
PAIR = 2 * HEAD_FEATURES
LOG2E = math.log2(math.e)

epsilon = 1e-06
masked_score = -1e30
f32 = jnp.float32
bf16 = jnp.bfloat16
MIB = 1024 * 1024

SIDES = ((0, 1), (2, 0), (1, 2))
HEAD_ORDER = tuple(h for left, right in SIDES for h in (2 * left, 2 * right + 1))

CORE, CHIP, LENGTH, OTHER_CHIP, OWN_B, OWN_Z = range(6)


def mm(a, b):
    return lax.dot_general(a, b, (((1,), (0,)), ((), ())), preferred_element_type=f32)


def mm_nt(a, b):
    return lax.dot_general(a, b, (((1,), (1,)), ((), ())), preferred_element_type=f32)


def mm_tn(a, b):
    return lax.dot_general(a, b, (((0,), (0,)), ((), ())), preferred_element_type=f32)


def call(body, grid, in_specs, out_specs, out_shape, scratch=(), aliases=None, vmem=64):
    return pl.pallas_call(
        body,
        grid_spec=pltpu.PrefetchScalarGridSpec(
            num_scalar_prefetch=1,
            grid=grid,
            in_specs=in_specs,
            out_specs=out_specs,
            scratch_shapes=list(scratch),
        ),
        out_shape=out_shape,
        input_output_aliases=aliases or {},
        compiler_params=pltpu.CompilerParams(
            dimension_semantics=("arbitrary",) * len(grid), vmem_limit_bytes=vmem * MIB
        ),
        cost_estimate=pl.CostEstimate(flops=1000, bytes_accessed=1000, transcendentals=0),
    )


def whole(shape):
    return pl.BlockSpec(shape, lambda *a: (0,) * len(shape))


def sds(shape, dtype):
    return jax.ShapeDtypeStruct(shape, dtype)


def rope_tables():
    middle = HEAD_FEATURES // 2
    frequency = 10000.0 ** (-np.arange(middle, dtype=np.float64) * 2.0 / HEAD_FEATURES)
    angles = np.arange(MAXLEN, dtype=np.float64)[:, None] * frequency[None, :]
    cosine, sine = np.cos(angles), np.sin(angles)
    table = np.stack([np.concatenate([cosine, cosine] * 2, axis=1), np.concatenate([-sine, sine] * 2, axis=1)])
    return table.astype(np.float32)


def rotate(u, table, sign):
    up = pltpu.roll(u, PAIR - HEAD_FEATURES // 2, 1)
    down = pltpu.roll(u, HEAD_FEATURES // 2, 1)
    lane = lax.broadcasted_iota(jnp.int32, (1, PAIR), 1)
    turned = jnp.where(lane % HEAD_FEATURES < HEAD_FEATURES // 2, up, down) * table[1]
    return u * table[0] + turned if sign > 0 else u * table[0] - turned


def pair_of(value, side):
    left, right = (value[:, a * PAIR : (a + 1) * PAIR] for a in side)
    lane = lax.broadcasted_iota(jnp.int32, (1, PAIR), 1)
    return jnp.where(lane < HEAD_FEATURES, left, right)


def slots(start):
    return start + lax.broadcasted_iota(jnp.int32, (PIECE, 1), 0)


def piece_rows(half, place):
    return pl.ds(pl.multiple_of(half * 2 * PIECE + place * PIECE, PIECE), PIECE)


def project_body(s, own, part, gain, wq, wk, wv, table, *rest):
    qkv, normed, copy = rest[-3:]
    low_x = jnp.where(pl.program_id(0) == s[CORE], own[0], part[0])
    copy[...] = low_x
    x = low_x.astype(f32)
    r = lax.rsqrt(jnp.mean(x * x, axis=-1, keepdims=True) + epsilon)
    low = (x * r * gain[0:1, :].astype(f32)).astype(bf16)
    normed[...] = low
    width = wq.shape[1]
    for m, w in enumerate((wq, wk, wv)):
        u = mm(low, w[...])
        if m == 0:
            u = u * (1.0 / math.sqrt(HEAD_FEATURES))
        for p in range(width // PAIR):
            v = pair_of(u, SIDES[p])
            if m < 2:
                v = rotate(v, table, 1)
            at = m * width + p * PAIR
            qkv[:, at : at + PAIR] = v.astype(bf16)


def project(scalars, own, part, half, gain, weights, table, filled):
    width = weights[0].shape[0]
    cols = width // 2
    place = lambda t, s: (s[half] * 2 + t, 0)
    source = lambda a: pl.BlockSpec((1, PIECE, width), lambda t, s: (s[CHIP] if a.shape[0] > 1 else 0, 0, 0))
    weight_spec = pl.BlockSpec((width, cols), lambda t, s: (0, s[CORE]))
    in_specs = [
        source(own),
        source(part),
        whole((2, width)),
        weight_spec,
        weight_spec,
        weight_spec,
        pl.BlockSpec((2, PIECE, PAIR), lambda t, s: (0, s[half] * 2 + t, 0)),
    ]
    args = [scalars, own, part, gain, *weights, table]
    aliases = None
    if filled is not None:
        in_specs += [pl.BlockSpec(memory_space=pl.ANY)] * 3
        aliases = {len(args) + a: a for a in range(3)}
        args += list(filled)
    return call(
        project_body,
        (2,),
        in_specs,
        [pl.BlockSpec((PIECE, 3 * cols), place), pl.BlockSpec((PIECE, width), place), pl.BlockSpec((PIECE, width), place)],
        [sds((MAXLEN, 3 * cols), bf16), sds((MAXLEN, width), bf16), sds((MAXLEN, width), bf16)],
        aliases=aliases,
    )(*args)


def head_mask(h):
    lane = lax.broadcasted_iota(jnp.int32, (1, PAIR), 1)
    return lane < HEAD_FEATURES if h == 0 else lane >= HEAD_FEATURES


def attend_body(s, q, k, v, out, lse):
    row = lax.broadcasted_iota(jnp.int32, (PIECE, PIECE), 0)
    col = lax.broadcasted_iota(jnp.int32, (PIECE, PIECE), 1)
    lane = lax.broadcasted_iota(jnp.int32, (PIECE, PAIR), 1)
    ones = jnp.ones((MAXLEN, PAIR), bf16)

    def score(b, h):
        at = b * PIECE
        qh = jnp.where(head_mask(h), q[at : at + PIECE, :], jnp.zeros((), bf16))
        near = mm_nt(qh, k[at : at + PIECE, :])
        return near, mm_nt(qh, k[:at, :]) if b else None

    def mix(b, near, far):
        at = b * PIECE
        near = jnp.where(row >= col, near, masked_score)
        top = jnp.max(near, axis=-1, keepdims=True)
        if b:
            top = jnp.maximum(top, jnp.max(far, axis=-1, keepdims=True))
        shift = top * LOG2E
        near = jnp.exp2(near * LOG2E - shift).astype(bf16)
        mixed = mm(near, jnp.concatenate([v[at : at + PIECE, :], ones[:PIECE]], axis=1))
        if b:
            far = jnp.exp2(far * LOG2E - shift).astype(bf16)
            mixed = mixed + mm(far, jnp.concatenate([v[:at, :], ones[:at]], axis=1))
        total = mixed[:, PAIR:]
        return mixed[:, :PAIR] * (1.0 / total), top + jnp.log(total)

    units = [(b, h) for b in range(GROUP) for h in range(2)]
    ahead = score(*units[0])
    done = []
    for at, (b, h) in enumerate(units):
        now = ahead
        if at + 1 < len(units):
            ahead = score(*units[at + 1])
        done.append(mix(b, *now))
        if h == 1:
            rows = slice(b * PIECE, (b + 1) * PIECE)
            (left, left_log), (right, right_log) = done
            done = []
            joined = jnp.where(head_mask(0), left, right)
            out[rows, :] = jnp.where(slots(b * PIECE) < s[LENGTH], joined, 0.0).astype(bf16)
            lse[0, :, rows] = jnp.transpose(jnp.where(lane == 0, left_log, right_log))[:8]


def attend(scalars, qkv):
    pairs = qkv.shape[1] // 3 // PAIR
    spec = lambda m: pl.BlockSpec((MAXLEN, PAIR), lambda p, s, m=m: (0, m * pairs + p))
    return call(
        attend_body,
        (pairs,),
        [spec(0), spec(1), spec(2)],
        [pl.BlockSpec((MAXLEN, PAIR), lambda p, s: (0, p)), pl.BlockSpec((1, 8, MAXLEN), lambda p, s: (p, 0, 0))],
        [sds((MAXLEN, pairs * PAIR), bf16), sds((pairs, 8, MAXLEN), f32)],
    )(scalars, qkv, qkv, qkv)


def pack_rows(block):
    half = block.shape[0] // 2
    lane = lax.broadcasted_iota(jnp.int32, (1, PAIR), 1)
    top, bottom = block[:half], block[half:]
    left = jnp.where(lane < HEAD_FEATURES, top, pltpu.roll(bottom, HEAD_FEATURES, 1))
    right = jnp.where(lane < HEAD_FEATURES, pltpu.roll(top, HEAD_FEATURES, 1), bottom)
    return left, right


def plane_blocks(s, keep, arrived, targets, rows, with_out):
    size = 2 * rows if with_out else rows
    core = s[CORE]
    for r, target in enumerate(targets):
        place = s[OWN_B] ^ r
        for z in range(4):
            at = pl.ds(pl.multiple_of((2 * z + place % 2) * rows, 16), rows)
            target[z * size : z * size + rows, :] = jnp.where(place // 2 == core, keep[at, :], arrived[at, :])
            if with_out:
                at = pl.ds(pl.multiple_of((8 + z % 2 * 4 + place) * rows, 16), rows)
                target[z * size + rows : (z + 1) * size, :] = jnp.where(z // 2 == core, keep[at, :], arrived[at, :])


def attend_back_body(pair, n_seq, s, *refs):
    first, last = pair == 0, pair == len(SIDES) - 1
    refs = list(refs)
    take = lambda count: [refs.pop(0) for _ in range(count)]
    qkv_hbm, attn_hbm, lse_hbm = take(3)
    if first:
        hidden_hbm, dyb_hbm, mine_hbm, theirs_hbm, gain = take(5)
    else:
        (da_hbm,) = take(1)
    middle = pair == 1
    if middle:
        layer_hbm, layer_far_hbm = take(2)
    if last:
        wq_hbm, wk_hbm, wv_hbm, gain = take(4)
    if first:
        (wo_hbm,) = take(1)
    normed_hbm, table_hbm = take(2)
    earlier = take(len(SIDES) - 1) if last else []
    sent = [] if first else take(2) if n_seq == 8 else []
    if last:
        (second_in,) = take(1)
    (keep_out,) = take(1)
    packed = n_seq == 8
    if not (last and packed):
        (send_out,) = take(1)
    if first:
        dhb_out, second, da_out = take(3)
    if middle:
        layer_stay, layer_leave = take(2)
    if last:
        norm_keep, norm_send, gains = take(3)
        if packed:
            send_out = norm_send.at[pl.ds(MAXLEN, norm_send.shape[0] - MAXLEN), :]
    else:
        (d_out,) = take(1)
    plane = take(4) if sent else []
    q, k, v, o, lse, normed, table, sems = take(8)
    da, da_t, q_t, dk_t, dv_t, dq, grads = take(7)
    (shifts,) = take(1)
    if first:
        hidden, dyb, mine, theirs, attn, out_grad, wo = take(7)
        dhb = dhb_out
    if middle:
        layer, layer_far = take(2)
    if last:
        before, joined, gain_rows, weights = take(4)
    before_sent = take(2) if sent else []
    core = s[CORE]
    width = normed.shape[1]
    zero = jnp.zeros((), bf16)
    pairs = len(SIDES)
    heads = pairs * PAIR
    copies = []

    def fetch(source, target):
        copy = pltpu.make_async_copy(source, target, sems.at[len(copies)])
        copy.start()
        copies.append(copy)
        return copy

    lanes_of = lambda m: slice((m * pairs + pair) * PAIR, (m * pairs + pair + 1) * PAIR)
    chunks = [slice(t * PIECE, (t + 1) * PIECE) for t in range(GROUP)]
    chunk_copies = []
    if first:
        for rows in chunks:
            chunk_copies.append(
                [
                    fetch(source.at[rows, :], target.at[rows, :])
                    for source, target in (
                        (mine_hbm, mine),
                        (theirs_hbm, theirs),
                        (hidden_hbm, hidden),
                        (dyb_hbm, dyb),
                    )
                ]
            )
    if first:
        wo_copies = [
            fetch(
                wo_hbm.at[pl.ds(pl.multiple_of(core * heads + head * HEAD_FEATURES, HEAD_FEATURES), HEAD_FEATURES), :],
                wo.at[index * HEAD_FEATURES : (index + 1) * HEAD_FEATURES, :],
            )
            for index, head in enumerate(HEAD_ORDER)
        ]
    else:
        wo_copies = [fetch(da_hbm.at[:, pair * PAIR : (pair + 1) * PAIR], da)]
    q_copies = [
        fetch(qkv_hbm.at[:, lanes_of(0)], q),
        fetch(qkv_hbm.at[:, lanes_of(1)], k),
        fetch(qkv_hbm.at[:, lanes_of(2)], v),
        fetch(attn_hbm.at[:, pair * PAIR : (pair + 1) * PAIR], o),
        fetch(lse_hbm.at[pair], lse),
    ]

    def fetch_late():
        late = [fetch(normed_hbm, normed), fetch(table_hbm, table)]
        late += [fetch(source, target) for source, target in zip(sent, before_sent)]
        if last:
            for m, w in enumerate((wq_hbm, wk_hbm, wv_hbm)):
                late.append(fetch(w.at[:, pl.ds(pl.multiple_of(core * heads, PAIR), heads)], weights.at[m]))
            for at, source in enumerate(earlier):
                late.append(fetch(source, before.at[:, at * heads : (at + 1) * heads]))
        if first:
            late.append(fetch(attn_hbm, attn))
        if middle:
            late += [fetch(layer_hbm, layer), fetch(layer_far_hbm, layer_far)]
        return late

    late_copies = fetch_late()
    if first:
        scale = gain[1:2, :].astype(f32)
        sums = jnp.zeros((1, width), f32)
        for rows, waiting in zip(chunks, chunk_copies):
            for copy in waiting:
                copy.wait()
            h = hidden[rows, :].astype(f32)
            r = lax.rsqrt(jnp.mean(h * h, axis=-1, keepdims=True) + epsilon)
            g = mine[rows, :].astype(f32) + theirs[rows, :].astype(f32)
            sums = sums + jnp.sum(g * h * r, axis=0, keepdims=True)
            scaled = g * scale
            inner = jnp.mean(scaled * h, axis=-1, keepdims=True)
            d = dyb[rows, :].astype(f32) + r * scaled - h * (r * r * r) * inner
            dhb[rows, :] = d.astype(bf16)
        second[...] = sums * 0.5
    for copy in wo_copies:
        copy.wait()
    if first:
        for t, rows in enumerate(chunks):
            d = mm_nt(dhb[rows, :], wo[...])
            da_out[rows, :] = jnp.where(slots(t * PIECE) < s[LENGTH], d, 0.0).astype(bf16)
        da[...] = da_out[:, :PAIR]
    da_t[...] = jnp.transpose(da[...])
    for copy in q_copies:
        copy.wait()
    q_t[...] = jnp.transpose(q[...])
    shifts[...] = jnp.transpose(lse[...]) * LOG2E

    row = lax.broadcasted_iota(jnp.int32, (PIECE, PIECE), 0)
    col = lax.broadcasted_iota(jnp.int32, (PIECE, PIECE), 1)

    def score(a, h):
        at = a * PIECE
        mask = head_mask(h)
        qh = jnp.where(mask, q[at : at + PIECE, :], zero)
        gh = jnp.where(mask, da[at : at + PIECE, :], zero)
        near = mm_nt(qh, k[at : at + PIECE, :]), mm_nt(gh, v[at : at + PIECE, :])
        far = (mm_nt(qh, k[:at, :]), mm_nt(gh, v[:at, :])) if a else None
        return near, far

    def back(a, h, near, far):
        at = a * PIECE
        rows = slice(at, at + PIECE)
        feats = slice(h * HEAD_FEATURES, (h + 1) * HEAD_FEATURES)
        mask = head_mask(h)
        shift = shifts[rows, h : h + 1]
        product = da[rows, :].astype(f32) * o[rows, :].astype(f32)
        inner = jnp.sum(jnp.where(mask, product, 0.0), axis=-1, keepdims=True)
        near_prob = jnp.exp2(jnp.where(row >= col, near[0] * LOG2E - shift, masked_score))
        near_ds = (near_prob * (near[1] - inner)).astype(bf16)
        query_grad = mm(near_ds, jnp.where(mask, k[rows, :], zero))
        parts = [(rows, near_prob.astype(bf16), near_ds)]
        if a:
            far_prob = jnp.exp2(far[0] * LOG2E - shift)
            far_ds = (far_prob * (far[1] - inner)).astype(bf16)
            query_grad = query_grad + mm(far_ds, jnp.where(mask, k[:at, :], zero))
            parts.append((slice(0, at), far_prob.astype(bf16), far_ds))
        for cols, prob, ds in parts:
            value_grad = mm(da_t[feats, rows], prob)
            key_grad = mm(q_t[feats, rows], ds)
            if a == GROUP - 1:
                dv_t[feats, cols] = value_grad
                dk_t[feats, cols] = key_grad
            else:
                dv_t[feats, cols] += value_grad
                dk_t[feats, cols] += key_grad
        return query_grad

    units = [(a, h) for a in reversed(range(GROUP)) for h in range(2)]
    ahead = score(*units[0])
    held = None
    for at, (a, h) in enumerate(units):
        now = ahead
        if at + 1 < len(units):
            ahead = score(*units[at + 1])
        g = back(a, h, *now)
        if h == 0:
            held = g
        else:
            dq[a * PIECE : (a + 1) * PIECE, :] = held + g

    for copy in late_copies:
        copy.wait()
    if sent:
        plane_blocks(s, *before_sent, plane, width // n_seq // 2, pair == 1)
    d = jnp.concatenate(
        [
            rotate(dq[...] * (1.0 / math.sqrt(HEAD_FEATURES)), table, -1).astype(bf16),
            rotate(jnp.transpose(dk_t[...]), table, -1).astype(bf16),
            jnp.transpose(dv_t[...].astype(bf16)),
        ],
        axis=1,
    )
    if last:
        before[:, (pairs - 1) * heads :] = d
    else:
        d_out[...] = d
    grads[...] = mm_tn(normed[...], d)

    rows = width // n_seq
    half_row = rows // 2
    if rows % 16:
        keep_out[:width, :] = grads[...].astype(bf16)
    else:
        left_x = SIDES[pair][0] * 2 // pairs
        for target, place in ((keep_out, core), (send_out, 1 - core)):
            for z in range(n_seq // 2):
                at = pl.ds(pl.multiple_of((2 * z + place) * rows, 8), rows)
                for m in range(3):
                    lanes = slice(m * PAIR, (m + 1) * PAIR)
                    left, right = pack_rows(grads[at, lanes])
                    for x_of, value in ((left_x, left), (1 - left_x, right)):
                        to = (2 * z + x_of) * half_row
                        target[to : to + half_row, lanes] = value.astype(bf16)

    if middle:
        for target, half in ((layer_leave, s[OTHER_CHIP]), (layer_stay, s[CHIP])):
            value = layer[half] + layer_far[half].astype(f32)
            live = slots(half * 2 * PIECE + core * PIECE) < s[LENGTH]
            target[...] = jnp.where(live, value, 0.0).astype(bf16)
    if first:
        g = mm_tn(attn[...], dhb[...])
        for index, head in enumerate(HEAD_ORDER):
            out_grad[head * HEAD_FEATURES : (head + 1) * HEAD_FEATURES, :] = g[
                index * HEAD_FEATURES : (index + 1) * HEAD_FEATURES, :
            ]
        if rows % 16:
            keep_out[width:, :] = jnp.concatenate([out_grad[:, :heads], out_grad[:, heads:]], axis=0).astype(bf16)
        else:
            column = width // 4
            for target, place in ((keep_out, core), (send_out, 1 - core)):
                for z in range(n_seq // 4):
                    block = out_grad[pl.ds(pl.multiple_of((2 * z + place) * rows, 8), rows), :]
                    for b in range(4):
                        lanes = slice(b * column, (b + 1) * column)
                        to = (n_seq + 4 * z + b) * half_row
                        target[to : to + half_row, :] = jnp.concatenate(
                            [block[:half_row, lanes], block[half_row:, lanes]], axis=1
                        ).astype(bf16)
    if last:
        for p, side in enumerate(SIDES):
            for m in range(3):
                at = p * heads + m * PAIR
                joined[:, at : at + PAIR] = pair_of(weights[m], side)
        sums = jnp.zeros((1, width), f32)
        for half in range(2):
            for target, place in ((norm_send, 1 - core), (norm_keep, core)):
                where = piece_rows(half, place)
                part = mm_nt(before[where, :], joined[...])
                if target is norm_keep:
                    target[half] = part.astype(bf16)
                else:
                    for side in range(2):
                        at = (2 * half + side) * PIECE
                        target[at : at + PIECE, :] = part[:, side * heads : (side + 1) * heads].astype(bf16)
                sums = sums + jnp.sum(part * normed[where, :].astype(f32), axis=0, keepdims=True)
        sums = sums / gain[0:1, :].astype(f32)
        gain_rows[...] = jnp.zeros_like(gain_rows)
        for index, value in enumerate((sums, second_in[...])):
            for part in range(2):
                gain_rows[2 * index + part : 2 * index + part + 1, :] = value[:, part * heads : (part + 1) * heads]
        high = gain_rows[...].astype(bf16)
        low = (gain_rows[...] - high.astype(f32)).astype(bf16)
        gains[...] = jnp.concatenate([high, low], axis=0)
        if rows % 16 == 0:
            send_out[n_seq * half_row :, :] = gains[...]


def attend_back(pair, scalars, qkv, attn, lse, given, wo, weights, gains, normed, table, earlier, n_seq, sent=()):
    first, last = pair == 0, pair == len(SIDES) - 1
    heads = attn.shape[1]
    width = wo.shape[1]
    rows = width // n_seq
    token_shape = (2, PIECE, width)
    if rows % 16 == 0:
        count = n_seq * rows // 2 * (2 if first else 1)
        shapes = [(count, heads)] * 2
    else:
        shapes = [(2 * width if first else width, heads), (8, 128)]
    extra = shapes[1][0] + 16 if n_seq == 8 else 0
    outs = [sds(a, bf16) for a in shapes[: 1 if last and n_seq == 8 else 2]]
    hbm = pl.BlockSpec(memory_space=pl.ANY)
    given, later = list(given), []
    given_specs = [hbm] * len(given)
    if first:
        outs += [sds((MAXLEN, width), bf16), sds((1, width), f32), sds((MAXLEN, heads), bf16)]
        given_specs[4] = whole((2, width))
        given.append(wo)
        given_specs.append(hbm)
    if pair == 1:
        outs += [sds((PIECE, width), bf16)] * 2
    if last:
        outs += [sds(token_shape, bf16), sds((MAXLEN + extra, heads), bf16), sds((16, heads), bf16)]
        given += [*weights, gains]
        given_specs += [hbm] * 3 + [whole((2, width))]
    else:
        outs += [sds((MAXLEN, heads), bf16)]
    outs += [sds((2 * rows * (2 if pair == 1 else 1), heads), bf16)] * (4 if sent else 0)
    later = list(earlier[: len(SIDES) - 1]) + list(sent) + list(earlier[len(SIDES) - 1 :])
    args = [qkv, attn, lse, *given, normed, table, *later]
    in_specs = [hbm] * 3 + given_specs + [hbm] * (2 + len(later))
    if last:
        in_specs[-1] = whole((1, width))
    scratch = [
        pltpu.VMEM((MAXLEN, PAIR), bf16),
        pltpu.VMEM((MAXLEN, PAIR), bf16),
        pltpu.VMEM((MAXLEN, PAIR), bf16),
        pltpu.VMEM((MAXLEN, PAIR), bf16),
        pltpu.VMEM((8, MAXLEN), f32),
        pltpu.VMEM((MAXLEN, width), bf16),
        pltpu.VMEM((2, MAXLEN, PAIR), f32),
        pltpu.SemaphoreType.DMA((48,)),
        pltpu.VMEM((MAXLEN, PAIR), bf16),
        pltpu.VMEM((PAIR, MAXLEN), bf16),
        pltpu.VMEM((PAIR, MAXLEN), bf16),
        pltpu.VMEM((PAIR, MAXLEN), f32),
        pltpu.VMEM((PAIR, MAXLEN), f32),
        pltpu.VMEM((MAXLEN, PAIR), f32),
        pltpu.VMEM((width, heads), f32),
        pltpu.VMEM((MAXLEN, 8), f32),
    ]
    if first:
        scratch += [pltpu.VMEM((MAXLEN, width), bf16)] * 4
        scratch += [
            pltpu.VMEM((MAXLEN, heads), bf16),
            pltpu.VMEM((heads, width), f32),
            pltpu.VMEM((heads, width), bf16),
        ]
    if pair == 1:
        scratch += [pltpu.VMEM(token_shape, f32), pltpu.VMEM(token_shape, bf16)]
    if last:
        scratch += [
            pltpu.VMEM((MAXLEN, len(SIDES) * heads), bf16),
            pltpu.VMEM((width, len(SIDES) * heads), bf16),
            pltpu.VMEM((8, heads), f32),
            pltpu.VMEM((3, width, heads), bf16),
        ]
    if sent:
        scratch += [pltpu.VMEM(a.shape, bf16) for a in sent]
    return call(
        functools.partial(attend_back_body, pair, n_seq),
        (1,),
        in_specs,
        [whole(a.shape) for a in outs],
        outs,
        scratch=scratch,
    )(scalars, *args)


def feed_body(
    packed, s, x_hbm, dy_hbm, dy_pair_hbm, dy_far_hbm, dy_far_pair_hbm, attn_hbm, attn_pair_hbm, wo_hbm, gain, *refs
):
    refs = list(refs)
    take = lambda count: [refs.pop(0) for _ in range(count)]
    wg_hbm, wu_hbm, wd_hbm = take(3)
    hidden_out, dyb_out, dn_out, layer_out, send_out = take(5)
    grads_out = take(6 if packed else 3)
    x, attn, wo, wg, wu, wd, dyb = take(7)
    hidden, hidden_low, low, low_t, dyb_t, acts, dgs, dus, dn, layer, send = take(11)
    blocks = take(12)
    (sems,) = take(1)
    core = s[CORE]
    tokens, width = x.shape
    heads = width // 2
    steps = 4
    cols = wg.shape[1] // steps
    used = [0]

    def copy(source, target):
        made = pltpu.make_async_copy(source, target, sems.at[used[0]])
        used[0] += 1
        made.start()
        return made

    chunks = [slice(t * PIECE, (t + 1) * PIECE) for t in range(GROUP)]
    unit = [2 * ((3 - step) ^ s[OWN_B]) + core for step in range(steps)]

    wo_copies = [
        copy(
            wo_hbm.at[pl.ds(pl.multiple_of(place * heads + head * HEAD_FEATURES, HEAD_FEATURES), HEAD_FEATURES), :],
            wo.at[at * heads + index * HEAD_FEATURES : at * heads + (index + 1) * HEAD_FEATURES, :],
        )
        for at, place in enumerate((core, 1 - core))
        for index, head in enumerate(HEAD_ORDER)
    ]
    token_copies = [
        [
            copy(x_hbm.at[rows, :], x.at[rows, :]),
            copy(attn_hbm.at[rows, :], attn.at[rows, :heads]),
            copy(attn_pair_hbm.at[rows, :], attn.at[rows, heads:]),
        ]
        for rows in chunks
    ]
    def weights_of(step):
        at = pl.ds(pl.multiple_of(unit[step] * cols, cols), cols)
        here = slice(step * cols, (step + 1) * cols)
        return [
            copy(wg_hbm.at[:, at], wg.at[:, here]),
            copy(wu_hbm.at[:, at], wu.at[:, here]),
            copy(wd_hbm.at[at, :], wd.at[here, :]),
        ]

    dy_copies = [
        copy(source, dyb.at[piece_rows(half, place), :])
        for source, half, place in (
            (dy_hbm.at[s[CHIP]], s[CHIP], core),
            (dy_pair_hbm.at[s[CHIP]], s[CHIP], 1 - core),
            (dy_far_hbm.at[0], s[OTHER_CHIP], core),
            (dy_far_pair_hbm.at[0], s[OTHER_CHIP], 1 - core),
        )
    ]
    out_copies, side_copies = [], []

    for made in wo_copies:
        made.wait()
    scale = gain[1:2, :].astype(f32)
    weight_copies = [weights_of(0)]
    for t, rows in enumerate(chunks):
        for made in token_copies[t]:
            made.wait()
        h = x[rows, :].astype(f32) + mm(attn[rows, :], wo[...])
        hidden[rows, :] = h
        hidden_low[rows, :] = h.astype(bf16)
        out_copies.append(copy(hidden_low.at[rows, :], hidden_out.at[rows, :]))
        r = lax.rsqrt(jnp.mean(h * h, axis=-1, keepdims=True) + epsilon)
        low[rows, :] = (h * r * scale).astype(bf16)
    low_t[...] = jnp.transpose(low[...])
    for made in dy_copies:
        made.wait()
    for t, rows in enumerate(chunks):
        dyb[rows, :] = jnp.where(slots(t * PIECE) < s[LENGTH], dyb[rows, :], jnp.zeros((), bf16))
    dyb_t[...] = jnp.transpose(dyb[...])
    out_copies.append(copy(dyb, dyb_out))

    def products(step, t):
        if t == 0:
            for made in weight_copies.pop():
                made.wait()
            if step + 1 < steps:
                weight_copies.append(weights_of(step + 1))
        rows, here = chunks[t], slice(step * cols, (step + 1) * cols)
        return mm(low[rows, :], wg[:, here]), mm(low[rows, :], wu[:, here]), mm_nt(dyb[rows, :], wd[here, :])

    def pointwise(step, t, gate, up, dact):
        rows, here = chunks[t], slice(step * cols, (step + 1) * cols)
        sig = 1.0 / (1.0 + jnp.exp2(gate * -LOG2E))
        silu = gate * sig
        acts[rows, here] = (silu * up).astype(bf16)
        dgs[rows, here] = (dact * up * (sig + silu * (1.0 - sig))).astype(bf16)
        dus[rows, here] = (dact * silu).astype(bf16)

    def weight_grads(step, which):
        here = slice(step * cols, (step + 1) * cols)
        left, right = ((low_t, dgs), (low_t, dus), (dyb_t, acts))[which]
        grad = blocks[3 * step + which]
        grad[...] = mm(left[...], right[:, here]).astype(bf16)
        if not packed:
            at = pl.ds(pl.multiple_of(unit[step] // 2 * cols, cols), cols)
            out_copies.append(copy(grad, grads_out[which].at[:, at]))
            return
        rows = width // 4
        y, x = (3 - step) // 2, (3 - step) % 2
        own = s[OWN_B] if which == 2 else s[OWN_Z]
        z = (unit[step] // 2) ^ s[OWN_Z]
        for high in range(2):
            for low_bit in range(2):
                source = grad.at[pl.ds(pl.multiple_of(((2 * high + low_bit) ^ own) * rows, 16), rows), :]
                if which == 0:
                    out_copies.append(copy(source, grads_out[0 if x else 1].at[y, low_bit, high]))
                elif which == 1:
                    out_copies.append(copy(source, grads_out[2 if y else 3].at[low_bit, x, high]))
                else:
                    sem = sems.at[used[0]]
                    used[0] += 1
                    for side, target in ((1, grads_out[4]), (0, grads_out[5])):
                        made = pltpu.make_async_copy(source, target.at[low_bit, high, z // 2], sem)
                        pl.when(z % 2 == side)(made.start)
                        side_copies.append((z % 2 == side, made))

    units = [(step, t) for step in range(steps) for t in range(GROUP)]
    ahead = products(*units[0])
    for index, (step, t) in enumerate(units):
        now = ahead
        if index + 1 < len(units):
            ahead = products(*units[index + 1])
        pointwise(step, t, *now)
        if step and t < 3:
            weight_grads(step - 1, t)
    for which in range(3):
        weight_grads(steps - 1, which)
    for half in range(2):
        send[half] = mm(acts[piece_rows(half, 1 - core), :], wd[...]).astype(bf16)
        out_copies.append(copy(send.at[half], send_out.at[half]))
    for half in range(2):
        rows = piece_rows(half, core)
        layer[half] = hidden[rows, :] + mm(acts[rows, :], wd[...])
        out_copies.append(copy(layer.at[half], layer_out.at[half]))
    for rows in chunks:
        dn[rows, :] = (mm_nt(dgs[rows, :], wg[...]) + mm_nt(dus[rows, :], wu[...])).astype(bf16)
        out_copies.append(copy(dn.at[rows, :], dn_out.at[rows, :]))
    for made in out_copies:
        made.wait()
    for when, made in side_copies:
        pl.when(when)(made.wait)


def feed(scalars, x, dy, dy_pair, dy_far, dy_far_pair, attn, attn_pair, wo, gain, wg, wu, wd, packed):
    tokens, width = x.shape
    units = wg.shape[1] // 2
    cols = units // 4
    token_shape = (2, PIECE, width)
    if packed:
        shapes = [(2, 2, 2, width // 4, cols)] * 6
    else:
        shapes = [(width, units)] * 3
    outs = [
        sds((tokens, width), bf16),
        sds((tokens, width), bf16),
        sds((tokens, width), bf16),
        sds(token_shape, f32),
        sds(token_shape, bf16),
    ] + [sds(a, bf16) for a in shapes]
    args = [x, dy, dy_pair, dy_far, dy_far_pair, attn, attn_pair, wo, gain, wg, wu, wd]
    in_specs = [pl.BlockSpec(memory_space=pl.ANY)] * len(args)
    in_specs[8] = whole((2, width))
    low = pltpu.VMEM((tokens, width), bf16)
    high = pltpu.VMEM((tokens, width), f32)
    turned = pltpu.VMEM((width, tokens), bf16)
    hidden_units = pltpu.VMEM((tokens, units), bf16)
    return call(
        functools.partial(feed_body, packed),
        (1,),
        in_specs,
        [pl.BlockSpec(memory_space=pl.ANY)] * len(outs),
        outs,
        scratch=[
            low,
            low,
            pltpu.VMEM((width, width), bf16),
            pltpu.VMEM((width, units), bf16),
            pltpu.VMEM((width, units), bf16),
            pltpu.VMEM((units, width), bf16),
            low,
            high,
            low,
            low,
            turned,
            turned,
            hidden_units,
            hidden_units,
            hidden_units,
            low,
            pltpu.VMEM(token_shape, f32),
            pltpu.VMEM(token_shape, bf16),
        ]
        + [pltpu.VMEM((width, cols), bf16)] * 12
        + [pltpu.SemaphoreType.DMA((112,))],
    )(scalars, *args)


def piece_of(half, side):
    return pl.ds(pl.multiple_of((2 * half + side) * PIECE, PIECE), PIECE)


def finish_body(s, x, keep, recv, dh, gain, stay, leave):
    scale = gain[0:1, :].astype(f32)
    for out, half in ((leave, s[OTHER_CHIP]), (stay, s[CHIP])):
        h = x[half, 0].astype(f32)
        there = jnp.concatenate([recv[piece_of(half, side), :] for side in range(2)], axis=1)
        dn = keep[half].astype(f32) + there.astype(f32)
        r = lax.rsqrt(jnp.mean(h * h, axis=-1, keepdims=True) + epsilon)
        scaled = dn * scale
        inner = jnp.mean(scaled * h, axis=-1, keepdims=True)
        out[...] = (dh[half, 0].astype(f32) + r * scaled - h * (r * r * r) * inner).astype(bf16)


def finish(scalars, x, keep, recv, dh, gain):
    width = x.shape[1]
    shape = (2, PIECE, width)
    own = pl.BlockSpec((2, 1, PIECE, width), lambda f, s: (0, s[CORE], 0, 0))
    return call(
        finish_body,
        (1,),
        [own, whole(shape), whole((MAXLEN, recv.shape[1])), own, whole((2, width))],
        [whole((PIECE, width))] * 2,
        [sds((PIECE, width), bf16)] * 2,
    )(scalars, x.reshape(2, 2, PIECE, width), keep, recv, dh.reshape(2, 2, PIECE, width), gain)


def decode(coded):
    return coded[:8].astype(f32) + coded[8:].astype(f32)


def encode(value):
    high = value.astype(bf16)
    return jnp.concatenate([high, (value - high.astype(f32)).astype(bf16)], axis=0)


def sum_parts(fetch, groups, scratch):
    loads = []
    for group in groups:
        loads.append([])
        for source in group:
            target = scratch.pop(0)
            loads[-1].append((fetch(source, target), target))

    def total(group):
        value = None
        for made, target in group:
            made.wait()
            part = target[...].astype(f32)
            value = part if value is None else value + part
        return value

    return [functools.partial(total, group) for group in loads]


def fetcher(sems):
    used = [0]

    def fetch(source, target):
        made = pltpu.make_async_copy(source, target, sems.at[used[0]])
        used[0] += 1
        made.start()
        return made

    return fetch


def feed_step_body(paths, s, *refs):
    refs = list(refs)
    groups = [[refs.pop(0).at[path] for path in group] for group in paths]
    outs = [refs.pop(0) for _ in groups]
    sems = refs.pop()
    for out, total in zip(outs, sum_parts(fetcher(sems), groups, refs)):
        out[...] = total().astype(bf16)


def feed_step(scalars, reductions):
    groups = [r.paths(1) for r in reductions]
    args = [array for group in groups for array, _ in group]
    paths = [[path for _, path in group] for group in groups]
    slices = [array.shape[len(path) :] for group in groups for array, path in group]
    outs = [sds(group[0][0].shape[len(group[0][1]) :], bf16) for group in groups]
    return call(
        functools.partial(feed_step_body, paths),
        (1,),
        [pl.BlockSpec(memory_space=pl.ANY)] * len(args),
        [whole(a.shape) for a in outs],
        outs,
        scratch=[pltpu.VMEM(a, bf16) for a in slices] + [pltpu.SemaphoreType.DMA((len(args),))],
    )(scalars, *args)


def third_step_body(paths, s, keep_hbm, arrived_hbm, gains, *refs):
    refs = list(refs)
    groups = [[refs.pop(0).at[path] for path in group] for group in paths]
    parts_hbm = [refs.pop(0) for _ in range(4)]
    plane = [refs.pop(0) for _ in range(4)]
    line_send, line_keep = refs.pop(0), refs.pop(0)
    sends, kept = refs.pop(0), refs.pop(0)
    keep, arrived = refs.pop(0), refs.pop(0)
    parts = [refs.pop(0) for _ in range(4)]
    sems = refs.pop()
    fetch = fetcher(sems)
    rows = keep.shape[0] // 8
    first = [
        fetch(keep_hbm, keep),
        fetch(arrived_hbm.at[pl.ds(MAXLEN, arrived.shape[0]), :], arrived),
    ]
    second = [fetch(source, target) for source, target in zip(parts_hbm, parts)]
    totals = sum_parts(fetch, groups, refs)
    for made in first:
        made.wait()
    plane_blocks(s, keep, arrived, plane, rows, False)
    coded = encode(decode(gains[...]) + decode(arrived[8 * rows :, :]))
    for target in plane:
        target[4 * rows :, :] = coded
    for made in second:
        made.wait()
    size = line_keep.shape[0] // 2
    own = s[OWN_Z] % 2
    for target, z0 in ((line_send, 1 - own), (line_keep, own)):
        for z1 in range(2):
            at = pl.ds(pl.multiple_of((2 * z1 + z0) * size, 16), size)
            total = None
            for part in parts:
                value = part[at, :].astype(f32)
                total = value if total is None else total + value
            target[z1 * size : (z1 + 1) * size, :] = total.astype(bf16)
    for index in range(3):
        sends[index] = totals[index]().astype(bf16)
        kept[index] = totals[3 + index]()


def third_step(scalars, keep, arrived, gains, parts, reductions):
    groups = [r.paths(1) for r in reductions] + [r.paths(0) for r in reductions]
    sums = [array for group in groups for array, _ in group]
    paths = [[path for _, path in group] for group in groups]
    slices = [array.shape[len(path) :] for group in groups for array, path in group]
    rows, columns = keep.shape
    outs = [sds((rows // 2 + 16, columns), bf16)] * 4
    outs += [sds((parts[0].shape[0] // 2, columns), bf16)] * 2
    outs += [sds((3,) + slices[0], bf16), sds((3,) + slices[0], f32)]
    hbm = pl.BlockSpec(memory_space=pl.ANY)
    return call(
        functools.partial(third_step_body, paths),
        (1,),
        [hbm, hbm, whole(gains.shape)] + [hbm] * (len(sums) + 4),
        [whole(a.shape) for a in outs],
        outs,
        scratch=[pltpu.VMEM(keep.shape, bf16), pltpu.VMEM((rows + 16, columns), bf16)]
        + [pltpu.VMEM(a.shape, bf16) for a in parts]
        + [pltpu.VMEM(a, bf16) for a in slices]
        + [pltpu.SemaphoreType.DMA((len(sums) + 6,))],
    )(scalars, keep, arrived, gains, *sums, *parts)


def second_line_body(s, *refs):
    refs = list(refs)
    take = lambda count: [refs.pop(0) for _ in range(count)]
    middle_hbm, last_hbm, line_hbm = take(4), take(4), take(2)
    layer_stay_hbm, layer_back_hbm = take(2)
    lines, (last_keep,) = take(4), take(1)
    (layer_out,) = take(1)
    middle, last, (keep0, arrived0) = take(4), take(4), take(2)
    (sems,) = take(1)
    fetch = fetcher(sems)
    first = [fetch(a, b) for a, b in zip(middle_hbm + last_hbm + line_hbm, middle + last + [keep0, arrived0])]
    third = [
        fetch(layer_stay_hbm, layer_out.at[s[CHIP]]),
        fetch(layer_back_hbm, layer_out.at[s[OTHER_CHIP]]),
    ]
    for made in first:
        made.wait()
    rows = middle[0].shape[0] // 4
    coded = [ref[4 * rows :, :] for ref in last]
    gains = encode((decode(coded[0]) + decode(coded[1])) + (decode(coded[2]) + decode(coded[3])))
    for r, target in enumerate(lines):
        at = pl.ds(pl.multiple_of((s[OWN_Z] ^ r) * rows, 16), rows)
        for index, parts in enumerate((middle, last)):
            total = None
            for part in parts:
                value = part[at, :].astype(f32)
                total = value if total is None else total + value
            target[index * rows : (index + 1) * rows, :] = total.astype(bf16)
        target[2 * rows : 2 * rows + 16, :] = gains
    size = keep0.shape[0] // 2
    own = s[OWN_Z] // 2
    for target, z1 in ((last_keep, own), (lines[2].at[2 * rows + 16 :, :], 1 - own)):
        at = pl.ds(pl.multiple_of(z1 * size, 16), size)
        target[...] = (keep0[at, :].astype(f32) + arrived0[at, :].astype(f32)).astype(bf16)
    for made in third:
        made.wait()


def second_line(scalars, middle, last, keep0, arrived0, layer_stay, layer_back):
    rows, columns = middle[0].shape[0] // 4, middle[0].shape[1]
    size = keep0.shape[0] // 2
    outs = [sds((2 * rows + 16 + (size if r == 2 else 0), columns), bf16) for r in range(4)]
    outs += [sds((size, columns), bf16)]
    outs += [sds((2,) + layer_stay.shape, bf16)]
    args = [*middle, *last, keep0, arrived0, layer_stay, layer_back]
    return call(
        second_line_body,
        (1,),
        [pl.BlockSpec(memory_space=pl.ANY)] * len(args),
        [whole(a.shape) for a in outs],
        outs,
        scratch=[pltpu.VMEM(a.shape, a.dtype) for a in args[:-2]] + [pltpu.SemaphoreType.DMA((len(args),))],
    )(scalars, *args)


def feed_total_body(s, feed_keep, feed_arrived, side_keep, side_send, down_out):
    rows = side_keep.shape[1]
    for index in range(2):
        value = feed_keep[index] + feed_arrived[index].astype(f32)
        for part in range(2):
            block = value[part * rows : (part + 1) * rows]

            @pl.when(s[CORE] == part)
            def _():
                side_keep[index] = block

            @pl.when(s[CORE] != part)
            def _():
                side_send[index] = block.astype(bf16)

    down_out[...] = feed_keep[2] + feed_arrived[2].astype(f32)

def feed_total(scalars, keep, arrived):
    rows, cols = keep.shape[1:]
    outs = [sds((2, rows // 2, cols), f32), sds((2, rows // 2, cols), bf16), sds((rows, cols), f32)]
    args = [keep, arrived]
    return call(
        feed_total_body,
        (1,),
        [whole(a.shape) for a in args],
        [whole(a.shape) for a in outs],
        outs,
    )(scalars, *args)


def shards_body(s, keep0, line0, line1, line2, line3, side_keep, side_arrived, stay, back, *outs):
    half, width = outs[0].shape[0] // 2, outs[0].shape[1]
    count = line0.shape[0]
    first = keep0[...].astype(f32) + line2[count:, :].astype(f32)
    rest = (line0[...].astype(f32) + line1[...].astype(f32)) + (
        line2[:count, :].astype(f32) + line3[...].astype(f32)
    )
    out = first[half:]
    outs[3][:half, :] = out[:, :width]
    outs[3][half:, :] = out[:, width:]
    for pair, part in enumerate((first[:half], rest[:half], rest[half : 2 * half])):
        lanes = slice(pair * HEAD_FEATURES, (pair + 1) * HEAD_FEATURES)
        for m in range(3):
            at = m * PAIR
            outs[m][:half, lanes] = part[:, at : at + HEAD_FEATURES]
            outs[m][half:, lanes] = part[:, at + HEAD_FEATURES : at + PAIR]
    gains = rest[2 * half : 2 * half + 8] + rest[2 * half + 8 :]
    for index in range(2):
        row = jnp.concatenate([gains[2 * index : 2 * index + 1], gains[2 * index + 1 : 2 * index + 2]], axis=1)
        for at in range(outs[6].shape[0]):
            outs[6 + index][at : at + 1, :] = row[:, at * PAIR : (at + 1) * PAIR]
    cols = side_keep.shape[2]
    for index in range(2):
        for core in range(2):

            @pl.when(s[CORE] == core)
            def _():
                outs[4 + index][:, core * cols : (core + 1) * cols] = side_keep[index]
                outs[4 + index][:, (1 - core) * cols : (2 - core) * cols] = side_arrived[index].astype(f32)

    outs[8][s[CHIP]] = stay[...]
    outs[8][s[OTHER_CHIP]] = back[...]


def make_shards(scalars, args, rows, columns, width):
    side = sds((rows, 2 * args[5].shape[-1]), f32)
    outs = [sds((rows, columns), f32)] * 4 + [side] * 2 + [sds((width // PAIR, PAIR), f32)] * 2
    outs.append(sds((2,) + args[-1].shape, bf16))
    return call(
        shards_body,
        (1,),
        [whole(a.shape) for a in args],
        [whole(a.shape) for a in outs],
        outs,
    )(scalars, *args)


def exchange_by(block, axis, difference, name):
    count = lax.axis_size(axis)
    with jax.named_scope(name):
        return lax.ppermute(block, axis, [(a, a ^ difference) for a in range(count)])


def exchange(block, axis, bit, name="swap"):
    return exchange_by(block, axis, 1 << bit, name)


def pick(block, index, dim):
    return lax.dynamic_index_in_dim(block, index, dim, keepdims=False)


def together(*values):
    return lax.optimization_barrier(values)


X, Y, Z0, Z1 = ("batch", 0), ("batch", 1), ("seq", 1), ("seq", 2)


class Reduction:
    def __init__(self, order, keep, send):
        self.order, self.level, self.send, self.parts = order, 0, send, [keep]

    def go(self):
        bit = self.order[self.level]
        self.arrived = exchange(self.send, *bit, "feed_" + "_".join(map(str, bit)))
        return self

    def paths(self, side):
        found = []
        for index, array in enumerate([*self.parts, self.arrived]):
            found.append((array, (0,) * (self.level - max(index - 1, 0)) + (side,)))
        return found

    def next(self, send):
        self.parts.append(self.arrived)
        self.send = send
        self.level += 1
        return self


def start_all(reductions, *others):
    sends = together(*[r.send for r in reductions], *others)
    for r, send in zip(reductions, sends):
        r.send = send
        r.go()
    return sends[len(reductions) :]


def wait_all(reductions, *others):
    values = together(*[r.arrived for r in reductions], *others)
    for r, arrived in zip(reductions, values):
        r.arrived = arrived
    return values[len(reductions) :]


def body(
    states,
    lengths,
    first_gain,
    query_weight,
    key_weight,
    value_weight,
    output_weight,
    second_gain,
    gate_weight,
    up_weight,
    down_weight,
    cotangent,
):
    tokens, width = states.shape
    n_seq, n_batch = lax.axis_size("seq"), lax.axis_size("batch")
    packed = n_seq == 8 and n_batch == 4
    place = lax.axis_index("seq")
    batch = lax.axis_index("batch")
    core = place & 1
    chip = place >> 1 & 1
    sequence = (batch * (n_seq // GROUP) + place // GROUP) * 2 + chip
    length = pick(lengths, sequence, 0)
    own_b, own_z = batch & 3, place >> 1 & 3
    scalars = jnp.stack([core, chip, length, 1 - chip, own_b, own_z]).astype(jnp.int32)
    table = jnp.asarray(rope_tables())
    both_gains = jnp.stack([first_gain, second_gain])
    weights = (query_weight, key_weight, value_weight)

    held = states.reshape(2, PIECE, width)
    held_back = cotangent.reshape(2, PIECE, width)
    far = exchange(pick(held, 1 - chip, 0), *Z0, "states_far")[None]
    held_pair = exchange(held, "seq", 0, "states_pair")
    filled = project(scalars, held, held_pair, CHIP, both_gains, weights, table, None)
    far, leaving, *filled = together(far, pick(held_back, 1 - chip, 0), *filled)
    far_pair = exchange(far, "seq", 0, "states_far_pair")
    back_far = exchange(leaving, *Z0, "cotangent_far")[None]
    back_pair = exchange(held_back, "seq", 0, "cotangent_pair")
    qkv, normed, x = project(scalars, far, far_pair, OTHER_CHIP, both_gains, weights, table, filled)
    attn, lse = attend(scalars, qkv)
    attn_pair = exchange(attn, "seq", 0, "attn_pair")
    back_far, attn = together(back_far, attn)
    back_far_pair = exchange(back_far, "seq", 0, "cotangent_far_pair")
    hidden, dyb, dn, layer_keep, layer_send, *feed_grads = feed(
        scalars,
        x,
        held_back,
        back_pair,
        back_far,
        back_far_pair,
        attn,
        attn_pair,
        output_weight,
        both_gains,
        gate_weight,
        up_weight,
        down_weight,
        packed,
    )
    if packed:
        gate_send, gate_keep, up_send, up_keep, down_send, down_keep = feed_grads
        gate = Reduction([X, Y, Z0, Z1], gate_keep, gate_send).go()
        up = Reduction([Y, Z0, X, Z1], up_keep, up_send).go()
        down = Reduction([Z0, X, Y, Z1], down_keep, down_send).go()
    dn_pair = exchange(dn, "seq", 0, "dn_pair")

    def back(pair, given, later, sent=()):
        return attend_back(
            pair, scalars, qkv, attn, lse, given, output_weight, weights, both_gains, normed, table, later, n_seq, sent
        )

    keep0, send0, dhb, second, da, d0 = back(0, [hidden, dyb, dn, dn_pair, both_gains], [])

    def in_order(kept, arrived):
        return jnp.concatenate(
            [jnp.where(chip == 0, kept, arrived), jnp.where(chip == 0, arrived, kept)], axis=0
        )

    if packed:
        rows = width // n_seq // 2

        def to_plane(parts, name):
            return [parts[0]] + [exchange_by(parts[r], "batch", r, name + str(r)) for r in (1, 2, 3)]

        feeds = [gate, up, down]
        keep0, send0, dhb, second, da, d0, layer_send = wait_all(feeds, keep0, send0, dhb, second, da, d0, layer_send)
        layer_arrived = exchange(layer_send, "seq", 0, "layer_pair")
        arrived0 = exchange(send0, "seq", 0, "grad0_pair")
        for r, send in zip(feeds, feed_step(scalars, feeds)):
            r.next(send)
        (da,) = start_all(feeds, da)
        keep1, send1, layer_stay, layer_leave, d1, *plane0 = back(
            1, [da, layer_keep, layer_arrived], [], (keep0, arrived0)
        )

        keep1, send1, layer_stay, layer_leave, d1, *plane0 = wait_all(
            feeds, keep1, send1, layer_stay, layer_leave, d1, *plane0
        )
        arrived1 = exchange(send1, "seq", 0, "grad1_pair")
        flow0 = to_plane(plane0, "plane0_")
        for r, send in zip(feeds, feed_step(scalars, feeds)):
            r.next(send)
        (arrived1, d1) = start_all(feeds, arrived1, d1)
        keep2, norm_keep, norm_send, gains, *plane1 = back(2, [da], [d0, d1, second], (keep1, arrived1))

        flow0[1], flow0[2], flow0[3], keep2, norm_keep, norm_send, gains, layer_leave, *plane1 = wait_all(
            feeds, *flow0[1:], keep2, norm_keep, norm_send, gains, layer_leave, *plane1
        )
        norm_arrived = exchange(norm_send, "seq", 0, "dn1_pair")
        layer_back = exchange(layer_leave, *Z0, "layer_back")
        flow1 = to_plane(plane1, "plane1_")
        *plane2, line0_send, line0_keep, feed_send, feed_keep = third_step(
            scalars, keep2, norm_arrived, gains, flow0, feeds
        )
        line0_send, line0_keep, feed_send, feed_keep, layer_back, *planes = together(
            line0_send, line0_keep, feed_send, feed_keep, layer_back, *plane2, *flow1
        )
        plane2, flow1 = planes[:4], planes[4:]
        flow2 = to_plane(plane2, "plane2_")
        feed_arrived = exchange(feed_send, *Z1, "feed_last")
        arrived0 = exchange(line0_send, *Z0, "line0")
        norm_keep, line0_keep = together(norm_keep, line0_keep)
        stay, leave = finish(scalars, x, norm_keep, norm_arrived, dhb, both_gains)
        leave, stay, arrived0, *flow2 = together(leave, stay, arrived0, *flow2)
        grad_back = exchange(leave, *Z0, "grad_back")
        stay, layer_back, line0_keep, arrived0, *flow12 = together(stay, layer_back, line0_keep, arrived0, *flow1, *flow2)
        *lines, last_keep, layer_out = second_line(
            scalars, flow12[:4], flow12[4:], line0_keep, arrived0, layer_stay, layer_back
        )
        last_keep, feed_arrived, feed_keep = together(last_keep, feed_arrived, feed_keep)
        side_keep, side_send, down_grad = feed_total(scalars, feed_keep, feed_arrived)
        lines = [lines[0]] + [exchange_by(lines[r], "seq", 2 * r, "line12_" + str(r)) for r in (1, 2, 3)]
        side_arrived = exchange(side_send, "seq", 0, "feed_pair")
        down_grad, layer_out = jnp.transpose(down_grad), layer_out.reshape(tokens, width)
        *shards, gate_grad, up_grad, first, second, input_grad = make_shards(
            scalars,
            [last_keep, *lines, side_keep, side_arrived, stay, grad_back],
            2 * rows,
            width // n_batch,
            width,
        )
        first, second, input_grad = first.reshape(width), second.reshape(width), input_grad.reshape(tokens, width)
    else:
        layer_arrived = exchange(layer_send, "seq", 0)
        keep1, _, layer_stay, layer_leave, d1 = back(1, [da, layer_keep, layer_arrived], [])
        layer_back = exchange(layer_leave, *Z0)
        keep2, _, norm_keep, norm_send, gains = back(2, [da], [d0, d1, second])
        norm_arrived = exchange(norm_send, "seq", 0)
        stay, leave = finish(scalars, x, norm_keep, norm_arrived, dhb, both_gains)
        layer_out = in_order(layer_stay, layer_back)
        input_grad = in_order(stay, exchange(leave, *Z0))
        gains = gains[:8].astype(f32) + gains[8:].astype(f32)
        for axis in ("seq", "batch"):
            for bit in range(int(math.log2(lax.axis_size(axis)))):
                gains = gains + exchange(gains, axis, bit)
        first, second = gains[:2].reshape(width), gains[2:4].reshape(width)
        gate_keep, up_keep, down_keep = feed_grads
        units = gate_keep.shape[1]
        zeros = lambda shape: jnp.zeros(shape, bf16)
        blocks = 4

        def spread(array):
            parts = array.reshape(width, blocks, 1, units // blocks)
            full = zeros((width, blocks, 2, units // blocks))
            return lax.dynamic_update_slice_in_dim(full, parts, core, 2).reshape(width, 2 * units)

        heads = attn.shape[1]
        out_keep = jnp.concatenate([keep0[width : width + heads], keep0[width + heads :]], axis=1)
        columns = lambda a: lax.dynamic_update_slice_in_dim(zeros((width, width)), a, core * heads, 1)

        def by_head(m):
            found = {}
            for index, head in enumerate(HEAD_ORDER):
                at = m * PAIR + index % 2 * HEAD_FEATURES
                found[head] = (keep0, keep1, keep2)[index // 2][:width, at : at + HEAD_FEATURES]
            return jnp.concatenate([found[head] for head in sorted(found)], axis=1)

        full = [columns(by_head(m)) for m in range(3)]
        full.append(lax.dynamic_update_slice_in_dim(zeros((width, width)), out_keep, core * heads, 0))
        full += [spread(gate_keep), spread(up_keep), jnp.transpose(spread(down_keep))]
        full = [lax.psum_scatter(a.astype(f32), "seq", scatter_dimension=0, tiled=True) for a in full]
        full = [lax.psum_scatter(a, "batch", scatter_dimension=1, tiled=True) for a in full]
        shards, (gate_grad, up_grad, down_grad) = full[:4], full[4:]

    return (
        layer_out,
        input_grad,
        first,
        shards[0],
        shards[1],
        shards[2],
        shards[3],
        second,
        gate_grad,
        up_grad,
        down_grad,
    )


def solution(mesh):
    split = P(("batch", "seq"), None)
    in_specs = (split,) + (P(),) * 10 + (split,)
    shard = P("seq", "batch")
    out_specs = (split, split, P(), shard, shard, shard, shard, P(), shard, shard, shard)
    return jax.shard_map(body, mesh=mesh, in_specs=in_specs, out_specs=out_specs, check_vma=False)
```

```python
import functools
import math

import jax
import jax.numpy as jnp
import numpy as np
from jax import lax
from jax.experimental import pallas as pl
from jax.experimental.pallas import tpu as pltpu
from jax.sharding import PartitionSpec as P

HEADS = 12
HEAD_FEATURES = 64
MAXLEN = 1024
GROUP = 4
PIECE = MAXLEN // GROUP
PAIR = 2 * HEAD_FEATURES
LOG2E = math.log2(math.e)

epsilon = 1e-06
masked_score = -1e30
f32 = jnp.float32
bf16 = jnp.bfloat16
MIB = 1024 * 1024

SIDES = ((0, 1), (2, 0), (1, 2))
HEAD_ORDER = tuple(h for left, right in SIDES for h in (2 * left, 2 * right + 1))

CORE, CHIP, LENGTH, OTHER_CHIP, OWN_B, OWN_Z = range(6)


def mm(a, b):
    return lax.dot_general(a, b, (((1,), (0,)), ((), ())), preferred_element_type=f32)


def mm_nt(a, b):
    return lax.dot_general(a, b, (((1,), (1,)), ((), ())), preferred_element_type=f32)


def mm_tn(a, b):
    return lax.dot_general(a, b, (((0,), (0,)), ((), ())), preferred_element_type=f32)


def call(body, grid, in_specs, out_specs, out_shape, scratch=(), aliases=None, vmem=64):
    return pl.pallas_call(
        body,
        grid_spec=pltpu.PrefetchScalarGridSpec(
            num_scalar_prefetch=1,
            grid=grid,
            in_specs=in_specs,
            out_specs=out_specs,
            scratch_shapes=list(scratch),
        ),
        out_shape=out_shape,
        input_output_aliases=aliases or {},
        compiler_params=pltpu.CompilerParams(
            dimension_semantics=("arbitrary",) * len(grid), vmem_limit_bytes=vmem * MIB
        ),
        cost_estimate=pl.CostEstimate(flops=1000, bytes_accessed=1000, transcendentals=0),
    )


def whole(shape):
    return pl.BlockSpec(shape, lambda *a: (0,) * len(shape))


def sds(shape, dtype):
    return jax.ShapeDtypeStruct(shape, dtype)


def rope_tables():
    middle = HEAD_FEATURES // 2
    frequency = 10000.0 ** (-np.arange(middle, dtype=np.float64) * 2.0 / HEAD_FEATURES)
    angles = np.arange(MAXLEN, dtype=np.float64)[:, None] * frequency[None, :]
    cosine, sine = np.cos(angles), np.sin(angles)
    table = np.stack([np.concatenate([cosine, cosine] * 2, axis=1), np.concatenate([-sine, sine] * 2, axis=1)])
    return table.astype(np.float32)


def rotate(u, table, sign):
    up = pltpu.roll(u, PAIR - HEAD_FEATURES // 2, 1)
    down = pltpu.roll(u, HEAD_FEATURES // 2, 1)
    lane = lax.broadcasted_iota(jnp.int32, (1, PAIR), 1)
    turned = jnp.where(lane % HEAD_FEATURES < HEAD_FEATURES // 2, up, down) * table[1]
    return u * table[0] + turned if sign > 0 else u * table[0] - turned


def pair_of(value, side):
    left, right = (value[:, a * PAIR : (a + 1) * PAIR] for a in side)
    lane = lax.broadcasted_iota(jnp.int32, (1, PAIR), 1)
    return jnp.where(lane < HEAD_FEATURES, left, right)


def slots(start):
    return start + lax.broadcasted_iota(jnp.int32, (PIECE, 1), 0)


def piece_rows(half, place):
    return pl.ds(pl.multiple_of(half * 2 * PIECE + place * PIECE, PIECE), PIECE)


def project_body(s, own, part, gain, wq, wk, wv, table, *rest):
    qkv, normed, copy = rest[-3:]
    low_x = jnp.where(pl.program_id(0) == s[CORE], own[0], part[0])
    copy[...] = low_x
    x = low_x.astype(f32)
    r = lax.rsqrt(jnp.mean(x * x, axis=-1, keepdims=True) + epsilon)
    low = (x * r * gain[0:1, :].astype(f32)).astype(bf16)
    normed[...] = low
    width = wq.shape[1]
    for m, w in enumerate((wq, wk, wv)):
        u = mm(low, w[...])
        if m == 0:
            u = u * (1.0 / math.sqrt(HEAD_FEATURES))
        for p in range(width // PAIR):
            v = pair_of(u, SIDES[p])
            if m < 2:
                v = rotate(v, table, 1)
            at = m * width + p * PAIR
            qkv[:, at : at + PAIR] = v.astype(bf16)


def project(scalars, own, part, half, gain, weights, table, filled):
    width = weights[0].shape[0]
    cols = width // 2
    place = lambda t, s: (s[half] * 2 + t, 0)
    source = lambda a: pl.BlockSpec((1, PIECE, width), lambda t, s: (s[CHIP] if a.shape[0] > 1 else 0, 0, 0))
    weight_spec = pl.BlockSpec((width, cols), lambda t, s: (0, s[CORE]))
    in_specs = [
        source(own),
        source(part),
        whole((2, width)),
        weight_spec,
        weight_spec,
        weight_spec,
        pl.BlockSpec((2, PIECE, PAIR), lambda t, s: (0, s[half] * 2 + t, 0)),
    ]
    args = [scalars, own, part, gain, *weights, table]
    aliases = None
    if filled is not None:
        in_specs += [pl.BlockSpec(memory_space=pl.ANY)] * 3
        aliases = {len(args) + a: a for a in range(3)}
        args += list(filled)
    return call(
        project_body,
        (2,),
        in_specs,
        [pl.BlockSpec((PIECE, 3 * cols), place), pl.BlockSpec((PIECE, width), place), pl.BlockSpec((PIECE, width), place)],
        [sds((MAXLEN, 3 * cols), bf16), sds((MAXLEN, width), bf16), sds((MAXLEN, width), bf16)],
        aliases=aliases,
    )(*args)


def head_mask(h):
    lane = lax.broadcasted_iota(jnp.int32, (1, PAIR), 1)
    return lane < HEAD_FEATURES if h == 0 else lane >= HEAD_FEATURES


def attend_pair(s, q, k, v, out, lse):
    row = lax.broadcasted_iota(jnp.int32, (PIECE, PIECE), 0)
    col = lax.broadcasted_iota(jnp.int32, (PIECE, PIECE), 1)
    lane = lax.broadcasted_iota(jnp.int32, (PIECE, PAIR), 1)
    ones = jnp.ones((MAXLEN, PAIR), bf16)

    def score(b, h):
        at = b * PIECE
        qh = jnp.where(head_mask(h), q[at : at + PIECE, :], jnp.zeros((), bf16))
        near = mm_nt(qh, k[at : at + PIECE, :])
        return near, mm_nt(qh, k[:at, :]) if b else None

    def mix(b, near, far):
        at = b * PIECE
        near = jnp.where(row >= col, near, masked_score)
        top = jnp.max(near, axis=-1, keepdims=True)
        if b:
            top = jnp.maximum(top, jnp.max(far, axis=-1, keepdims=True))
        shift = top * LOG2E
        near = jnp.exp2(near * LOG2E - shift).astype(bf16)
        mixed = mm(near, jnp.concatenate([v[at : at + PIECE, :], ones[:PIECE]], axis=1))
        if b:
            far = jnp.exp2(far * LOG2E - shift).astype(bf16)
            mixed = mixed + mm(far, jnp.concatenate([v[:at, :], ones[:at]], axis=1))
        total = mixed[:, PAIR:]
        return mixed[:, :PAIR] * (1.0 / total), top + jnp.log(total)

    units = [(b, h) for b in range(GROUP) for h in range(2)]
    ahead = score(*units[0])
    done = []
    for at, (b, h) in enumerate(units):
        now = ahead
        if at + 1 < len(units):
            ahead = score(*units[at + 1])
        done.append(mix(b, *now))
        if h == 1:
            rows = slice(b * PIECE, (b + 1) * PIECE)
            (left, left_log), (right, right_log) = done
            done = []
            joined = jnp.where(head_mask(0), left, right)
            out[rows, :] = jnp.where(slots(b * PIECE) < s[LENGTH], joined, 0.0).astype(bf16)
            lse[:, rows] = jnp.transpose(jnp.where(lane == 0, left_log, right_log))[:8]


def attend_body(s, far_hbm, far_pair_hbm, gain, *refs):
    weights_hbm, table_hbm, qkv_in = refs[:3], refs[3], refs[4]
    qkv_out, normed_out, x_out, out, lse = refs[7:12]
    qkv, pieces, lows, weights, table, sems = refs[12:]
    core, half = s[CORE], s[OTHER_CHIP]
    width = weights.shape[1]
    cols = weights.shape[2]
    fetch = fetcher(sems)
    rows_of = lambda side: pl.ds(pl.multiple_of(side * 2 * PIECE, 2 * PIECE), 2 * PIECE)
    first = [fetch(far_hbm.at[0], pieces.at[core]), fetch(far_pair_hbm.at[0], pieces.at[1 - core])]
    for m, w in enumerate(weights_hbm):
        first.append(fetch(w.at[:, pl.ds(pl.multiple_of(core * cols, PAIR), cols)], weights.at[m]))
    first.append(fetch(table_hbm.at[:, rows_of(half), :], table))
    second = fetch(qkv_in.at[rows_of(s[CHIP]), :], qkv.at[rows_of(s[CHIP]), :])
    for made in first:
        made.wait()
    for t in range(2):
        x = pieces[t].astype(f32)
        r = lax.rsqrt(jnp.mean(x * x, axis=-1, keepdims=True) + epsilon)
        low = (x * r * gain[0:1, :].astype(f32)).astype(bf16)
        lows[t] = low
        rows = piece_rows(half, t)
        turn = [table[a, t * PIECE : (t + 1) * PIECE, :] for a in range(2)]
        for m in range(3):
            u = mm(low, weights[m])
            if m == 0:
                u = u * (1.0 / math.sqrt(HEAD_FEATURES))
            for p, side in enumerate(SIDES):
                v = pair_of(u, side)
                if m < 2:
                    v = rotate(v, turn, 1)
                at = m * cols + p * PAIR
                qkv[rows, at : at + PAIR] = v.astype(bf16)
    made = [fetch(qkv.at[rows_of(half), :], qkv_out.at[rows_of(half), :])]
    for t in range(2):
        made.append(fetch(lows.at[t], normed_out.at[piece_rows(half, t), :]))
        made.append(fetch(pieces.at[t], x_out.at[piece_rows(half, t), :]))
    second.wait()
    for p in range(len(SIDES)):
        q, k, v = (qkv.at[:, m * cols + p * PAIR : m * cols + (p + 1) * PAIR] for m in range(3))
        attend_pair(s, q, k, v, out.at[:, p * PAIR : (p + 1) * PAIR], lse.at[p])
    for copy in made:
        copy.wait()


def attend(scalars, far, far_pair, gain, weights, table, filled):
    width = weights[0].shape[0]
    cols = width // 2
    hbm = pl.BlockSpec(memory_space=pl.ANY)
    args = [far, far_pair, gain, *weights, table, *filled]
    outs = [sds(a.shape, a.dtype) for a in filled]
    outs += [sds((MAXLEN, cols), bf16), sds((len(SIDES), 8, MAXLEN), f32)]
    return call(
        attend_body,
        (1,),
        [hbm, hbm, whole(gain.shape)] + [hbm] * 7,
        [hbm] * 3 + [whole(a.shape) for a in outs[3:]],
        outs,
        scratch=[
            pltpu.VMEM((MAXLEN, 3 * cols), bf16),
            pltpu.VMEM((2, PIECE, width), bf16),
            pltpu.VMEM((2, PIECE, width), bf16),
            pltpu.VMEM((3, width, cols), bf16),
            pltpu.VMEM((2, 2 * PIECE, PAIR), f32),
            pltpu.SemaphoreType.DMA((16,)),
        ],
        aliases={8: 0, 9: 1, 10: 2},
    )(scalars, *args)


def pack_rows(block):
    half = block.shape[0] // 2
    lane = lax.broadcasted_iota(jnp.int32, (1, PAIR), 1)
    top, bottom = block[:half], block[half:]
    left = jnp.where(lane < HEAD_FEATURES, top, pltpu.roll(bottom, HEAD_FEATURES, 1))
    right = jnp.where(lane < HEAD_FEATURES, pltpu.roll(top, HEAD_FEATURES, 1), bottom)
    return left, right


def plane_blocks(s, keep, arrived, targets, rows, with_out):
    size = 2 * rows if with_out else rows
    core = s[CORE]
    for r, target in enumerate(targets):
        place = s[OWN_B] ^ r
        for z in range(4):
            at = pl.ds(pl.multiple_of((2 * z + place % 2) * rows, 16), rows)
            target[z * size : z * size + rows, :] = jnp.where(place // 2 == core, keep[at, :], arrived[at, :])
            if with_out:
                at = pl.ds(pl.multiple_of((8 + z % 2 * 4 + place) * rows, 16), rows)
                target[z * size + rows : (z + 1) * size, :] = jnp.where(z // 2 == core, keep[at, :], arrived[at, :])


def attend_back_body(pair, n_seq, s, *refs):
    first, last = pair == 0, pair == len(SIDES) - 1
    refs = list(refs)
    take = lambda count: [refs.pop(0) for _ in range(count)]
    qkv_hbm, attn_hbm, lse_hbm = take(3)
    if first:
        hidden_hbm, dyb_hbm, mine_hbm, theirs_hbm, gain = take(5)
    else:
        (da_hbm,) = take(1)
    middle = pair == 1
    if middle:
        layer_hbm, layer_far_hbm = take(2)
    if last:
        wq_hbm, wk_hbm, wv_hbm, gain = take(4)
    if first:
        (wo_hbm,) = take(1)
    normed_hbm, table_hbm = take(2)
    earlier = take(len(SIDES) - 1) if last else []
    sent = [] if first else take(2) if n_seq == 8 else []
    if last:
        (second_in,) = take(1)
    (keep_out,) = take(1)
    packed = n_seq == 8
    if not (last and packed):
        (send_out,) = take(1)
    if first:
        dhb_out, second, da_out = take(3)
    if middle:
        layer_stay, layer_leave = take(2)
    if last:
        norm_keep, norm_send, gains = take(3)
        if packed:
            send_out = norm_send.at[pl.ds(MAXLEN, norm_send.shape[0] - MAXLEN), :]
    else:
        (d_out,) = take(1)
    plane = take(4) if sent else []
    q, k, v, o, lse, normed, table, sems = take(8)
    da, da_t, q_t, dk_t, dv_t, dq, grads = take(7)
    (shifts,) = take(1)
    if first:
        hidden, dyb, mine, theirs, attn, out_grad, wo = take(7)
        dhb = dhb_out
    if middle:
        layer, layer_far = take(2)
    if last:
        before, joined, gain_rows, weights = take(4)
    before_sent = take(2) if sent else []
    core = s[CORE]
    width = normed.shape[1]
    zero = jnp.zeros((), bf16)
    pairs = len(SIDES)
    heads = pairs * PAIR
    copies = []

    def fetch(source, target):
        copy = pltpu.make_async_copy(source, target, sems.at[len(copies)])
        copy.start()
        copies.append(copy)
        return copy

    lanes_of = lambda m: slice((m * pairs + pair) * PAIR, (m * pairs + pair + 1) * PAIR)
    chunks = [slice(t * PIECE, (t + 1) * PIECE) for t in range(GROUP)]
    chunk_copies = []
    if first:
        for rows in chunks:
            chunk_copies.append(
                [
                    fetch(source.at[rows, :], target.at[rows, :])
                    for source, target in (
                        (mine_hbm, mine),
                        (theirs_hbm, theirs),
                        (hidden_hbm, hidden),
                        (dyb_hbm, dyb),
                    )
                ]
            )
    if first:
        wo_copies = [
            fetch(
                wo_hbm.at[pl.ds(pl.multiple_of(core * heads + head * HEAD_FEATURES, HEAD_FEATURES), HEAD_FEATURES), :],
                wo.at[index * HEAD_FEATURES : (index + 1) * HEAD_FEATURES, :],
            )
            for index, head in enumerate(HEAD_ORDER)
        ]
    else:
        wo_copies = [fetch(da_hbm.at[:, pair * PAIR : (pair + 1) * PAIR], da)]
    q_copies = [
        fetch(qkv_hbm.at[:, lanes_of(0)], q),
        fetch(qkv_hbm.at[:, lanes_of(1)], k),
        fetch(qkv_hbm.at[:, lanes_of(2)], v),
        fetch(attn_hbm.at[:, pair * PAIR : (pair + 1) * PAIR], o),
        fetch(lse_hbm.at[pair], lse),
    ]

    def fetch_late():
        late = [fetch(normed_hbm, normed), fetch(table_hbm, table)]
        late += [fetch(source, target) for source, target in zip(sent, before_sent)]
        if last:
            for m, w in enumerate((wq_hbm, wk_hbm, wv_hbm)):
                late.append(fetch(w.at[:, pl.ds(pl.multiple_of(core * heads, PAIR), heads)], weights.at[m]))
            for at, source in enumerate(earlier):
                late.append(fetch(source, before.at[:, at * heads : (at + 1) * heads]))
        if first:
            late.append(fetch(attn_hbm, attn))
        if middle:
            late += [fetch(layer_hbm, layer), fetch(layer_far_hbm, layer_far)]
        return late

    late_copies = fetch_late()
    if first:
        scale = gain[1:2, :].astype(f32)
        sums = jnp.zeros((1, width), f32)
        for rows, waiting in zip(chunks, chunk_copies):
            for copy in waiting:
                copy.wait()
            h = hidden[rows, :].astype(f32)
            r = lax.rsqrt(jnp.mean(h * h, axis=-1, keepdims=True) + epsilon)
            g = mine[rows, :].astype(f32) + theirs[rows, :].astype(f32)
            sums = sums + jnp.sum(g * h * r, axis=0, keepdims=True)
            scaled = g * scale
            inner = jnp.mean(scaled * h, axis=-1, keepdims=True)
            d = dyb[rows, :].astype(f32) + r * scaled - h * (r * r * r) * inner
            dhb[rows, :] = d.astype(bf16)
        second[...] = sums * 0.5
    for copy in wo_copies:
        copy.wait()
    if first:
        for t, rows in enumerate(chunks):
            d = mm_nt(dhb[rows, :], wo[...])
            da_out[rows, :] = jnp.where(slots(t * PIECE) < s[LENGTH], d, 0.0).astype(bf16)
        da[...] = da_out[:, :PAIR]
    da_t[...] = jnp.transpose(da[...])
    for copy in q_copies:
        copy.wait()
    q_t[...] = jnp.transpose(q[...])
    shifts[...] = jnp.transpose(lse[...]) * LOG2E

    row = lax.broadcasted_iota(jnp.int32, (PIECE, PIECE), 0)
    col = lax.broadcasted_iota(jnp.int32, (PIECE, PIECE), 1)

    def score(a, h):
        at = a * PIECE
        mask = head_mask(h)
        qh = jnp.where(mask, q[at : at + PIECE, :], zero)
        gh = jnp.where(mask, da[at : at + PIECE, :], zero)
        near = mm_nt(qh, k[at : at + PIECE, :]), mm_nt(gh, v[at : at + PIECE, :])
        far = (mm_nt(qh, k[:at, :]), mm_nt(gh, v[:at, :])) if a else None
        return near, far

    def back(a, h, near, far):
        at = a * PIECE
        rows = slice(at, at + PIECE)
        feats = slice(h * HEAD_FEATURES, (h + 1) * HEAD_FEATURES)
        mask = head_mask(h)
        shift = shifts[rows, h : h + 1]
        product = da[rows, :].astype(f32) * o[rows, :].astype(f32)
        inner = jnp.sum(jnp.where(mask, product, 0.0), axis=-1, keepdims=True)
        near_prob = jnp.exp2(jnp.where(row >= col, near[0] * LOG2E - shift, masked_score))
        near_ds = (near_prob * (near[1] - inner)).astype(bf16)
        query_grad = mm(near_ds, jnp.where(mask, k[rows, :], zero))
        parts = [(rows, near_prob.astype(bf16), near_ds)]
        if a:
            far_prob = jnp.exp2(far[0] * LOG2E - shift)
            far_ds = (far_prob * (far[1] - inner)).astype(bf16)
            query_grad = query_grad + mm(far_ds, jnp.where(mask, k[:at, :], zero))
            parts.append((slice(0, at), far_prob.astype(bf16), far_ds))
        for cols, prob, ds in parts:
            value_grad = mm(da_t[feats, rows], prob)
            key_grad = mm(q_t[feats, rows], ds)
            if a == GROUP - 1:
                dv_t[feats, cols] = value_grad
                dk_t[feats, cols] = key_grad
            else:
                dv_t[feats, cols] += value_grad
                dk_t[feats, cols] += key_grad
        return query_grad

    units = [(a, h) for a in reversed(range(GROUP)) for h in range(2)]
    ahead = score(*units[0])
    held = None
    for at, (a, h) in enumerate(units):
        now = ahead
        if at + 1 < len(units):
            ahead = score(*units[at + 1])
        g = back(a, h, *now)
        if h == 0:
            held = g
        else:
            dq[a * PIECE : (a + 1) * PIECE, :] = held + g

    for copy in late_copies:
        copy.wait()
    if sent:
        plane_blocks(s, *before_sent, plane, width // n_seq // 2, pair == 1)
    d = jnp.concatenate(
        [
            rotate(dq[...] * (1.0 / math.sqrt(HEAD_FEATURES)), table, -1).astype(bf16),
            rotate(jnp.transpose(dk_t[...]), table, -1).astype(bf16),
            jnp.transpose(dv_t[...].astype(bf16)),
        ],
        axis=1,
    )
    if last:
        before[:, (pairs - 1) * heads :] = d
    else:
        d_out[...] = d
    grads[...] = mm_tn(normed[...], d)

    rows = width // n_seq
    half_row = rows // 2
    if rows % 16:
        keep_out[:width, :] = grads[...].astype(bf16)
    else:
        left_x = SIDES[pair][0] * 2 // pairs
        for target, place in ((keep_out, core), (send_out, 1 - core)):
            for z in range(n_seq // 2):
                at = pl.ds(pl.multiple_of((2 * z + place) * rows, 8), rows)
                for m in range(3):
                    lanes = slice(m * PAIR, (m + 1) * PAIR)
                    left, right = pack_rows(grads[at, lanes])
                    for x_of, value in ((left_x, left), (1 - left_x, right)):
                        to = (2 * z + x_of) * half_row
                        target[to : to + half_row, lanes] = value.astype(bf16)

    if middle:
        for target, half in ((layer_leave, s[OTHER_CHIP]), (layer_stay, s[CHIP])):
            value = layer[half] + layer_far[half].astype(f32)
            live = slots(half * 2 * PIECE + core * PIECE) < s[LENGTH]
            target[...] = jnp.where(live, value, 0.0).astype(bf16)
    if first:
        g = mm_tn(attn[...], dhb[...])
        for index, head in enumerate(HEAD_ORDER):
            out_grad[head * HEAD_FEATURES : (head + 1) * HEAD_FEATURES, :] = g[
                index * HEAD_FEATURES : (index + 1) * HEAD_FEATURES, :
            ]
        if rows % 16:
            keep_out[width:, :] = jnp.concatenate([out_grad[:, :heads], out_grad[:, heads:]], axis=0).astype(bf16)
        else:
            column = width // 4
            for target, place in ((keep_out, core), (send_out, 1 - core)):
                for z in range(n_seq // 4):
                    block = out_grad[pl.ds(pl.multiple_of((2 * z + place) * rows, 8), rows), :]
                    for b in range(4):
                        lanes = slice(b * column, (b + 1) * column)
                        to = (n_seq + 4 * z + b) * half_row
                        target[to : to + half_row, :] = jnp.concatenate(
                            [block[:half_row, lanes], block[half_row:, lanes]], axis=1
                        ).astype(bf16)
    if last:
        for p, side in enumerate(SIDES):
            for m in range(3):
                at = p * heads + m * PAIR
                joined[:, at : at + PAIR] = pair_of(weights[m], side)
        sums = jnp.zeros((1, width), f32)
        for half in range(2):
            for target, place in ((norm_send, 1 - core), (norm_keep, core)):
                where = piece_rows(half, place)
                part = mm_nt(before[where, :], joined[...])
                if target is norm_keep:
                    target[half] = part.astype(bf16)
                else:
                    for side in range(2):
                        at = (2 * half + side) * PIECE
                        target[at : at + PIECE, :] = part[:, side * heads : (side + 1) * heads].astype(bf16)
                sums = sums + jnp.sum(part * normed[where, :].astype(f32), axis=0, keepdims=True)
        sums = sums / gain[0:1, :].astype(f32)
        gain_rows[...] = jnp.zeros_like(gain_rows)
        for index, value in enumerate((sums, second_in[...])):
            for part in range(2):
                gain_rows[2 * index + part : 2 * index + part + 1, :] = value[:, part * heads : (part + 1) * heads]
        high = gain_rows[...].astype(bf16)
        low = (gain_rows[...] - high.astype(f32)).astype(bf16)
        gains[...] = jnp.concatenate([high, low], axis=0)
        if rows % 16 == 0:
            send_out[n_seq * half_row :, :] = gains[...]


def attend_back(pair, scalars, qkv, attn, lse, given, wo, weights, gains, normed, table, earlier, n_seq, sent=()):
    first, last = pair == 0, pair == len(SIDES) - 1
    heads = attn.shape[1]
    width = wo.shape[1]
    rows = width // n_seq
    token_shape = (2, PIECE, width)
    if rows % 16 == 0:
        count = n_seq * rows // 2 * (2 if first else 1)
        shapes = [(count, heads)] * 2
    else:
        shapes = [(2 * width if first else width, heads), (8, 128)]
    extra = shapes[1][0] + 16 if n_seq == 8 else 0
    outs = [sds(a, bf16) for a in shapes[: 1 if last and n_seq == 8 else 2]]
    hbm = pl.BlockSpec(memory_space=pl.ANY)
    given, later = list(given), []
    given_specs = [hbm] * len(given)
    if first:
        outs += [sds((MAXLEN, width), bf16), sds((1, width), f32), sds((MAXLEN, heads), bf16)]
        given_specs[4] = whole((2, width))
        given.append(wo)
        given_specs.append(hbm)
    if pair == 1:
        outs += [sds((PIECE, width), bf16)] * 2
    if last:
        outs += [sds(token_shape, bf16), sds((MAXLEN + extra, heads), bf16), sds((16, heads), bf16)]
        given += [*weights, gains]
        given_specs += [hbm] * 3 + [whole((2, width))]
    else:
        outs += [sds((MAXLEN, heads), bf16)]
    outs += [sds((2 * rows * (2 if pair == 1 else 1), heads), bf16)] * (4 if sent else 0)
    later = list(earlier[: len(SIDES) - 1]) + list(sent) + list(earlier[len(SIDES) - 1 :])
    args = [qkv, attn, lse, *given, normed, table, *later]
    in_specs = [hbm] * 3 + given_specs + [hbm] * (2 + len(later))
    if last:
        in_specs[-1] = whole((1, width))
    scratch = [
        pltpu.VMEM((MAXLEN, PAIR), bf16),
        pltpu.VMEM((MAXLEN, PAIR), bf16),
        pltpu.VMEM((MAXLEN, PAIR), bf16),
        pltpu.VMEM((MAXLEN, PAIR), bf16),
        pltpu.VMEM((8, MAXLEN), f32),
        pltpu.VMEM((MAXLEN, width), bf16),
        pltpu.VMEM((2, MAXLEN, PAIR), f32),
        pltpu.SemaphoreType.DMA((48,)),
        pltpu.VMEM((MAXLEN, PAIR), bf16),
        pltpu.VMEM((PAIR, MAXLEN), bf16),
        pltpu.VMEM((PAIR, MAXLEN), bf16),
        pltpu.VMEM((PAIR, MAXLEN), f32),
        pltpu.VMEM((PAIR, MAXLEN), f32),
        pltpu.VMEM((MAXLEN, PAIR), f32),
        pltpu.VMEM((width, heads), f32),
        pltpu.VMEM((MAXLEN, 8), f32),
    ]
    if first:
        scratch += [pltpu.VMEM((MAXLEN, width), bf16)] * 4
        scratch += [
            pltpu.VMEM((MAXLEN, heads), bf16),
            pltpu.VMEM((heads, width), f32),
            pltpu.VMEM((heads, width), bf16),
        ]
    if pair == 1:
        scratch += [pltpu.VMEM(token_shape, f32), pltpu.VMEM(token_shape, bf16)]
    if last:
        scratch += [
            pltpu.VMEM((MAXLEN, len(SIDES) * heads), bf16),
            pltpu.VMEM((width, len(SIDES) * heads), bf16),
            pltpu.VMEM((8, heads), f32),
            pltpu.VMEM((3, width, heads), bf16),
        ]
    if sent:
        scratch += [pltpu.VMEM(a.shape, bf16) for a in sent]
    return call(
        functools.partial(attend_back_body, pair, n_seq),
        (1,),
        in_specs,
        [whole(a.shape) for a in outs],
        outs,
        scratch=scratch,
    )(scalars, *args)


def feed_body(
    packed, s, x_hbm, dy_hbm, dy_pair_hbm, dy_far_hbm, dy_far_pair_hbm, attn_hbm, attn_pair_hbm, wo_hbm, gain, *refs
):
    refs = list(refs)
    take = lambda count: [refs.pop(0) for _ in range(count)]
    wg_hbm, wu_hbm, wd_hbm = take(3)
    hidden_out, dyb_out, dn_out, layer_out, send_out = take(5)
    grads_out = take(6 if packed else 3)
    x, attn, wo, wg, wu, wd, dyb = take(7)
    hidden, hidden_low, low, low_t, dyb_t, acts, dgs, dus, dn, layer, send = take(11)
    blocks = take(12)
    (sems,) = take(1)
    core = s[CORE]
    tokens, width = x.shape
    heads = width // 2
    steps = 4
    cols = wg.shape[1] // steps
    used = [0]

    def copy(source, target):
        made = pltpu.make_async_copy(source, target, sems.at[used[0]])
        used[0] += 1
        made.start()
        return made

    chunks = [slice(t * PIECE, (t + 1) * PIECE) for t in range(GROUP)]
    unit = [2 * ((3 - step) ^ s[OWN_B]) + core for step in range(steps)]

    wo_copies = [
        copy(
            wo_hbm.at[pl.ds(pl.multiple_of(place * heads + head * HEAD_FEATURES, HEAD_FEATURES), HEAD_FEATURES), :],
            wo.at[at * heads + index * HEAD_FEATURES : at * heads + (index + 1) * HEAD_FEATURES, :],
        )
        for at, place in enumerate((core, 1 - core))
        for index, head in enumerate(HEAD_ORDER)
    ]
    token_copies = [
        [
            copy(x_hbm.at[rows, :], x.at[rows, :]),
            copy(attn_hbm.at[rows, :], attn.at[rows, :heads]),
            copy(attn_pair_hbm.at[rows, :], attn.at[rows, heads:]),
        ]
        for rows in chunks
    ]
    def weights_of(step):
        at = pl.ds(pl.multiple_of(unit[step] * cols, cols), cols)
        here = slice(step * cols, (step + 1) * cols)
        return [
            copy(wg_hbm.at[:, at], wg.at[:, here]),
            copy(wu_hbm.at[:, at], wu.at[:, here]),
            copy(wd_hbm.at[at, :], wd.at[here, :]),
        ]

    dy_copies = [
        copy(source, dyb.at[piece_rows(half, place), :])
        for source, half, place in (
            (dy_hbm.at[s[CHIP]], s[CHIP], core),
            (dy_pair_hbm.at[s[CHIP]], s[CHIP], 1 - core),
            (dy_far_hbm.at[0], s[OTHER_CHIP], core),
            (dy_far_pair_hbm.at[0], s[OTHER_CHIP], 1 - core),
        )
    ]
    out_copies, side_copies = [], []

    for made in wo_copies:
        made.wait()
    scale = gain[1:2, :].astype(f32)
    weight_copies = [weights_of(0)]
    for t, rows in enumerate(chunks):
        for made in token_copies[t]:
            made.wait()
        h = x[rows, :].astype(f32) + mm(attn[rows, :], wo[...])
        hidden[rows, :] = h
        hidden_low[rows, :] = h.astype(bf16)
        out_copies.append(copy(hidden_low.at[rows, :], hidden_out.at[rows, :]))
        r = lax.rsqrt(jnp.mean(h * h, axis=-1, keepdims=True) + epsilon)
        low[rows, :] = (h * r * scale).astype(bf16)
    low_t[...] = jnp.transpose(low[...])
    for made in dy_copies:
        made.wait()
    for t, rows in enumerate(chunks):
        dyb[rows, :] = jnp.where(slots(t * PIECE) < s[LENGTH], dyb[rows, :], jnp.zeros((), bf16))
    dyb_t[...] = jnp.transpose(dyb[...])
    out_copies.append(copy(dyb, dyb_out))

    def products(step, t):
        if t == 0:
            for made in weight_copies.pop():
                made.wait()
            if step + 1 < steps:
                weight_copies.append(weights_of(step + 1))
        rows, here = chunks[t], slice(step * cols, (step + 1) * cols)
        return mm(low[rows, :], wg[:, here]), mm(low[rows, :], wu[:, here]), mm_nt(dyb[rows, :], wd[here, :])

    def pointwise(step, t, gate, up, dact):
        rows, here = chunks[t], slice(step * cols, (step + 1) * cols)
        sig = 1.0 / (1.0 + jnp.exp2(gate * -LOG2E))
        silu = gate * sig
        acts[rows, here] = (silu * up).astype(bf16)
        dgs[rows, here] = (dact * up * (sig + silu * (1.0 - sig))).astype(bf16)
        dus[rows, here] = (dact * silu).astype(bf16)

    def weight_grads(step, which):
        here = slice(step * cols, (step + 1) * cols)
        left, right = ((low_t, dgs), (low_t, dus), (dyb_t, acts))[which]
        grad = blocks[3 * step + which]
        grad[...] = mm(left[...], right[:, here]).astype(bf16)
        if not packed:
            at = pl.ds(pl.multiple_of(unit[step] // 2 * cols, cols), cols)
            out_copies.append(copy(grad, grads_out[which].at[:, at]))
            return
        rows = width // 4
        y, x = (3 - step) // 2, (3 - step) % 2
        own = s[OWN_B] if which == 2 else s[OWN_Z]
        z = (unit[step] // 2) ^ s[OWN_Z]
        for high in range(2):
            for low_bit in range(2):
                source = grad.at[pl.ds(pl.multiple_of(((2 * high + low_bit) ^ own) * rows, 16), rows), :]
                if which == 0:
                    out_copies.append(copy(source, grads_out[0 if x else 1].at[y, low_bit, high]))
                elif which == 1:
                    out_copies.append(copy(source, grads_out[2 if y else 3].at[low_bit, x, high]))
                else:
                    sem = sems.at[used[0]]
                    used[0] += 1
                    for side, target in ((1, grads_out[4]), (0, grads_out[5])):
                        made = pltpu.make_async_copy(source, target.at[low_bit, high, z // 2], sem)
                        pl.when(z % 2 == side)(made.start)
                        side_copies.append((z % 2 == side, made))

    units = [(step, t) for step in range(steps) for t in range(GROUP)]
    ahead = products(*units[0])
    for index, (step, t) in enumerate(units):
        now = ahead
        if index + 1 < len(units):
            ahead = products(*units[index + 1])
        pointwise(step, t, *now)
        if step and t < 3:
            weight_grads(step - 1, t)
    for which in range(3):
        weight_grads(steps - 1, which)
    for half in range(2):
        send[half] = mm(acts[piece_rows(half, 1 - core), :], wd[...]).astype(bf16)
        out_copies.append(copy(send.at[half], send_out.at[half]))
    for half in range(2):
        rows = piece_rows(half, core)
        layer[half] = hidden[rows, :] + mm(acts[rows, :], wd[...])
        out_copies.append(copy(layer.at[half], layer_out.at[half]))
    for rows in chunks:
        dn[rows, :] = (mm_nt(dgs[rows, :], wg[...]) + mm_nt(dus[rows, :], wu[...])).astype(bf16)
        out_copies.append(copy(dn.at[rows, :], dn_out.at[rows, :]))
    for made in out_copies:
        made.wait()
    for when, made in side_copies:
        pl.when(when)(made.wait)


def feed(scalars, x, dy, dy_pair, dy_far, dy_far_pair, attn, attn_pair, wo, gain, wg, wu, wd, packed):
    tokens, width = x.shape
    units = wg.shape[1] // 2
    cols = units // 4
    token_shape = (2, PIECE, width)
    if packed:
        shapes = [(2, 2, 2, width // 4, cols)] * 6
    else:
        shapes = [(width, units)] * 3
    outs = [
        sds((tokens, width), bf16),
        sds((tokens, width), bf16),
        sds((tokens, width), bf16),
        sds(token_shape, f32),
        sds(token_shape, bf16),
    ] + [sds(a, bf16) for a in shapes]
    args = [x, dy, dy_pair, dy_far, dy_far_pair, attn, attn_pair, wo, gain, wg, wu, wd]
    in_specs = [pl.BlockSpec(memory_space=pl.ANY)] * len(args)
    in_specs[8] = whole((2, width))
    low = pltpu.VMEM((tokens, width), bf16)
    high = pltpu.VMEM((tokens, width), f32)
    turned = pltpu.VMEM((width, tokens), bf16)
    hidden_units = pltpu.VMEM((tokens, units), bf16)
    return call(
        functools.partial(feed_body, packed),
        (1,),
        in_specs,
        [pl.BlockSpec(memory_space=pl.ANY)] * len(outs),
        outs,
        scratch=[
            low,
            low,
            pltpu.VMEM((width, width), bf16),
            pltpu.VMEM((width, units), bf16),
            pltpu.VMEM((width, units), bf16),
            pltpu.VMEM((units, width), bf16),
            low,
            high,
            low,
            low,
            turned,
            turned,
            hidden_units,
            hidden_units,
            hidden_units,
            low,
            pltpu.VMEM(token_shape, f32),
            pltpu.VMEM(token_shape, bf16),
        ]
        + [pltpu.VMEM((width, cols), bf16)] * 12
        + [pltpu.SemaphoreType.DMA((112,))],
    )(scalars, *args)


def piece_of(half, side):
    return pl.ds(pl.multiple_of((2 * half + side) * PIECE, PIECE), PIECE)


def finish_body(s, x, keep, recv, dh, gain, stay, leave):
    scale = gain[0:1, :].astype(f32)
    for out, half in ((leave, s[OTHER_CHIP]), (stay, s[CHIP])):
        h = x[half, 0].astype(f32)
        there = jnp.concatenate([recv[piece_of(half, side), :] for side in range(2)], axis=1)
        dn = keep[half].astype(f32) + there.astype(f32)
        r = lax.rsqrt(jnp.mean(h * h, axis=-1, keepdims=True) + epsilon)
        scaled = dn * scale
        inner = jnp.mean(scaled * h, axis=-1, keepdims=True)
        out[...] = (dh[half, 0].astype(f32) + r * scaled - h * (r * r * r) * inner).astype(bf16)


def finish(scalars, x, keep, recv, dh, gain):
    width = x.shape[1]
    shape = (2, PIECE, width)
    own = pl.BlockSpec((2, 1, PIECE, width), lambda f, s: (0, s[CORE], 0, 0))
    return call(
        finish_body,
        (1,),
        [own, whole(shape), whole((MAXLEN, recv.shape[1])), own, whole((2, width))],
        [whole((PIECE, width))] * 2,
        [sds((PIECE, width), bf16)] * 2,
    )(scalars, x.reshape(2, 2, PIECE, width), keep, recv, dh.reshape(2, 2, PIECE, width), gain)


def decode(coded):
    return coded[:8].astype(f32) + coded[8:].astype(f32)


def encode(value):
    high = value.astype(bf16)
    return jnp.concatenate([high, (value - high.astype(f32)).astype(bf16)], axis=0)


def sum_parts(fetch, groups, scratch):
    loads = []
    for group in groups:
        loads.append([])
        for source in group:
            target = scratch.pop(0)
            loads[-1].append((fetch(source, target), target))

    def total(group):
        value = None
        for made, target in group:
            made.wait()
            part = target[...].astype(f32)
            value = part if value is None else value + part
        return value

    return [functools.partial(total, group) for group in loads]


def fetcher(sems):
    used = [0]

    def fetch(source, target):
        made = pltpu.make_async_copy(source, target, sems.at[used[0]])
        used[0] += 1
        made.start()
        return made

    return fetch


def feed_step_body(paths, s, *refs):
    refs = list(refs)
    groups = [[refs.pop(0).at[path] for path in group] for group in paths]
    outs = [refs.pop(0) for _ in groups]
    sems = refs.pop()
    for out, total in zip(outs, sum_parts(fetcher(sems), groups, refs)):
        out[...] = total().astype(bf16)


def feed_step(scalars, reductions):
    groups = [r.paths(1) for r in reductions]
    args = [array for group in groups for array, _ in group]
    paths = [[path for _, path in group] for group in groups]
    slices = [array.shape[len(path) :] for group in groups for array, path in group]
    outs = [sds(group[0][0].shape[len(group[0][1]) :], bf16) for group in groups]
    return call(
        functools.partial(feed_step_body, paths),
        (1,),
        [pl.BlockSpec(memory_space=pl.ANY)] * len(args),
        [whole(a.shape) for a in outs],
        outs,
        scratch=[pltpu.VMEM(a, bf16) for a in slices] + [pltpu.SemaphoreType.DMA((len(args),))],
    )(scalars, *args)


def third_step_body(paths, s, keep_hbm, arrived_hbm, gains, *refs):
    refs = list(refs)
    groups = [[refs.pop(0).at[path] for path in group] for group in paths]
    parts_hbm = [refs.pop(0) for _ in range(4)]
    plane = [refs.pop(0) for _ in range(4)]
    line_send, line_keep = refs.pop(0), refs.pop(0)
    sends, kept = refs.pop(0), refs.pop(0)
    keep, arrived = refs.pop(0), refs.pop(0)
    parts = [refs.pop(0) for _ in range(4)]
    sems = refs.pop()
    fetch = fetcher(sems)
    rows = keep.shape[0] // 8
    first = [
        fetch(keep_hbm, keep),
        fetch(arrived_hbm.at[pl.ds(MAXLEN, arrived.shape[0]), :], arrived),
    ]
    second = [fetch(source, target) for source, target in zip(parts_hbm, parts)]
    totals = sum_parts(fetch, groups, refs)
    for made in first:
        made.wait()
    plane_blocks(s, keep, arrived, plane, rows, False)
    coded = encode(decode(gains[...]) + decode(arrived[8 * rows :, :]))
    for target in plane:
        target[4 * rows :, :] = coded
    for made in second:
        made.wait()
    size = line_keep.shape[0] // 2
    own = s[OWN_Z] % 2
    for target, z0 in ((line_send, 1 - own), (line_keep, own)):
        for z1 in range(2):
            at = pl.ds(pl.multiple_of((2 * z1 + z0) * size, 16), size)
            total = None
            for part in parts:
                value = part[at, :].astype(f32)
                total = value if total is None else total + value
            target[z1 * size : (z1 + 1) * size, :] = total.astype(bf16)
    for index in range(3):
        sends[index] = totals[index]().astype(bf16)
        kept[index] = totals[3 + index]()


def third_step(scalars, keep, arrived, gains, parts, reductions):
    groups = [r.paths(1) for r in reductions] + [r.paths(0) for r in reductions]
    sums = [array for group in groups for array, _ in group]
    paths = [[path for _, path in group] for group in groups]
    slices = [array.shape[len(path) :] for group in groups for array, path in group]
    rows, columns = keep.shape
    outs = [sds((rows // 2 + 16, columns), bf16)] * 4
    outs += [sds((parts[0].shape[0] // 2, columns), bf16)] * 2
    outs += [sds((3,) + slices[0], bf16), sds((3,) + slices[0], f32)]
    hbm = pl.BlockSpec(memory_space=pl.ANY)
    return call(
        functools.partial(third_step_body, paths),
        (1,),
        [hbm, hbm, whole(gains.shape)] + [hbm] * (len(sums) + 4),
        [whole(a.shape) for a in outs],
        outs,
        scratch=[pltpu.VMEM(keep.shape, bf16), pltpu.VMEM((rows + 16, columns), bf16)]
        + [pltpu.VMEM(a.shape, bf16) for a in parts]
        + [pltpu.VMEM(a, bf16) for a in slices]
        + [pltpu.SemaphoreType.DMA((len(sums) + 6,))],
    )(scalars, keep, arrived, gains, *sums, *parts)


def second_line_body(s, *refs):
    refs = list(refs)
    take = lambda count: [refs.pop(0) for _ in range(count)]
    middle_hbm, last_hbm, line_hbm = take(4), take(4), take(2)
    layer_stay_hbm, layer_back_hbm = take(2)
    lines, (last_keep,) = take(4), take(1)
    (layer_out,) = take(1)
    middle, last, (keep0, arrived0) = take(4), take(4), take(2)
    (sems,) = take(1)
    fetch = fetcher(sems)
    first = [fetch(a, b) for a, b in zip(middle_hbm + last_hbm + line_hbm, middle + last + [keep0, arrived0])]
    third = [
        fetch(layer_stay_hbm, layer_out.at[s[CHIP]]),
        fetch(layer_back_hbm, layer_out.at[s[OTHER_CHIP]]),
    ]
    for made in first:
        made.wait()
    rows = middle[0].shape[0] // 4
    coded = [ref[4 * rows :, :] for ref in last]
    gains = encode((decode(coded[0]) + decode(coded[1])) + (decode(coded[2]) + decode(coded[3])))
    for r, target in enumerate(lines):
        at = pl.ds(pl.multiple_of((s[OWN_Z] ^ r) * rows, 16), rows)
        for index, parts in enumerate((middle, last)):
            total = None
            for part in parts:
                value = part[at, :].astype(f32)
                total = value if total is None else total + value
            target[index * rows : (index + 1) * rows, :] = total.astype(bf16)
        target[2 * rows : 2 * rows + 16, :] = gains
    size = keep0.shape[0] // 2
    own = s[OWN_Z] // 2
    for target, z1 in ((last_keep, own), (lines[2].at[2 * rows + 16 :, :], 1 - own)):
        at = pl.ds(pl.multiple_of(z1 * size, 16), size)
        target[...] = (keep0[at, :].astype(f32) + arrived0[at, :].astype(f32)).astype(bf16)
    for made in third:
        made.wait()


def second_line(scalars, middle, last, keep0, arrived0, layer_stay, layer_back):
    rows, columns = middle[0].shape[0] // 4, middle[0].shape[1]
    size = keep0.shape[0] // 2
    outs = [sds((2 * rows + 16 + (size if r == 2 else 0), columns), bf16) for r in range(4)]
    outs += [sds((size, columns), bf16)]
    outs += [sds((2,) + layer_stay.shape, bf16)]
    args = [*middle, *last, keep0, arrived0, layer_stay, layer_back]
    return call(
        second_line_body,
        (1,),
        [pl.BlockSpec(memory_space=pl.ANY)] * len(args),
        [whole(a.shape) for a in outs],
        outs,
        scratch=[pltpu.VMEM(a.shape, a.dtype) for a in args[:-2]] + [pltpu.SemaphoreType.DMA((len(args),))],
    )(scalars, *args)


def feed_total_body(s, feed_keep, feed_arrived, side_keep, side_send, down_out):
    rows = side_keep.shape[1]
    for index in range(2):
        value = feed_keep[index] + feed_arrived[index].astype(f32)
        for part in range(2):
            block = value[part * rows : (part + 1) * rows]

            @pl.when(s[CORE] == part)
            def _():
                side_keep[index] = block

            @pl.when(s[CORE] != part)
            def _():
                side_send[index] = block.astype(bf16)

    down_out[...] = feed_keep[2] + feed_arrived[2].astype(f32)

def feed_total(scalars, keep, arrived):
    rows, cols = keep.shape[1:]
    outs = [sds((2, rows // 2, cols), f32), sds((2, rows // 2, cols), bf16), sds((rows, cols), f32)]
    args = [keep, arrived]
    return call(
        feed_total_body,
        (1,),
        [whole(a.shape) for a in args],
        [whole(a.shape) for a in outs],
        outs,
    )(scalars, *args)


def shards_body(s, keep0, line0, line1, line2, line3, side_keep, side_arrived, stay, back, *outs):
    half, width = outs[0].shape[0] // 2, outs[0].shape[1]
    count = line0.shape[0]
    first = keep0[...].astype(f32) + line2[count:, :].astype(f32)
    rest = (line0[...].astype(f32) + line1[...].astype(f32)) + (
        line2[:count, :].astype(f32) + line3[...].astype(f32)
    )
    out = first[half:]
    outs[3][:half, :] = out[:, :width]
    outs[3][half:, :] = out[:, width:]
    for pair, part in enumerate((first[:half], rest[:half], rest[half : 2 * half])):
        lanes = slice(pair * HEAD_FEATURES, (pair + 1) * HEAD_FEATURES)
        for m in range(3):
            at = m * PAIR
            outs[m][:half, lanes] = part[:, at : at + HEAD_FEATURES]
            outs[m][half:, lanes] = part[:, at + HEAD_FEATURES : at + PAIR]
    gains = rest[2 * half : 2 * half + 8] + rest[2 * half + 8 :]
    for index in range(2):
        row = jnp.concatenate([gains[2 * index : 2 * index + 1], gains[2 * index + 1 : 2 * index + 2]], axis=1)
        for at in range(outs[6].shape[0]):
            outs[6 + index][at : at + 1, :] = row[:, at * PAIR : (at + 1) * PAIR]
    cols = side_keep.shape[2]
    for index in range(2):
        for core in range(2):

            @pl.when(s[CORE] == core)
            def _():
                outs[4 + index][:, core * cols : (core + 1) * cols] = side_keep[index]
                outs[4 + index][:, (1 - core) * cols : (2 - core) * cols] = side_arrived[index].astype(f32)

    outs[8][s[CHIP]] = stay[...]
    outs[8][s[OTHER_CHIP]] = back[...]


def make_shards(scalars, args, rows, columns, width):
    side = sds((rows, 2 * args[5].shape[-1]), f32)
    outs = [sds((rows, columns), f32)] * 4 + [side] * 2 + [sds((width // PAIR, PAIR), f32)] * 2
    outs.append(sds((2,) + args[-1].shape, bf16))
    return call(
        shards_body,
        (1,),
        [whole(a.shape) for a in args],
        [whole(a.shape) for a in outs],
        outs,
    )(scalars, *args)


def exchange_by(block, axis, difference, name):
    count = lax.axis_size(axis)
    with jax.named_scope(name):
        return lax.ppermute(block, axis, [(a, a ^ difference) for a in range(count)])


def exchange(block, axis, bit, name="swap"):
    return exchange_by(block, axis, 1 << bit, name)


def pick(block, index, dim):
    return lax.dynamic_index_in_dim(block, index, dim, keepdims=False)


def together(*values):
    return lax.optimization_barrier(values)


X, Y, Z0, Z1 = ("batch", 0), ("batch", 1), ("seq", 1), ("seq", 2)


class Reduction:
    def __init__(self, order, keep, send):
        self.order, self.level, self.send, self.parts = order, 0, send, [keep]

    def go(self):
        bit = self.order[self.level]
        self.arrived = exchange(self.send, *bit, "feed_" + "_".join(map(str, bit)))
        return self

    def paths(self, side):
        found = []
        for index, array in enumerate([*self.parts, self.arrived]):
            found.append((array, (0,) * (self.level - max(index - 1, 0)) + (side,)))
        return found

    def next(self, send):
        self.parts.append(self.arrived)
        self.send = send
        self.level += 1
        return self


def start_all(reductions, *others):
    sends = together(*[r.send for r in reductions], *others)
    for r, send in zip(reductions, sends):
        r.send = send
        r.go()
    return sends[len(reductions) :]


def wait_all(reductions, *others):
    values = together(*[r.arrived for r in reductions], *others)
    for r, arrived in zip(reductions, values):
        r.arrived = arrived
    return values[len(reductions) :]


def body(
    states,
    lengths,
    first_gain,
    query_weight,
    key_weight,
    value_weight,
    output_weight,
    second_gain,
    gate_weight,
    up_weight,
    down_weight,
    cotangent,
):
    tokens, width = states.shape
    n_seq, n_batch = lax.axis_size("seq"), lax.axis_size("batch")
    packed = n_seq == 8 and n_batch == 4
    place = lax.axis_index("seq")
    batch = lax.axis_index("batch")
    core = place & 1
    chip = place >> 1 & 1
    sequence = (batch * (n_seq // GROUP) + place // GROUP) * 2 + chip
    length = pick(lengths, sequence, 0)
    own_b, own_z = batch & 3, place >> 1 & 3
    scalars = jnp.stack([core, chip, length, 1 - chip, own_b, own_z]).astype(jnp.int32)
    table = jnp.asarray(rope_tables())
    both_gains = jnp.stack([first_gain, second_gain])
    weights = (query_weight, key_weight, value_weight)

    held = states.reshape(2, PIECE, width)
    held_back = cotangent.reshape(2, PIECE, width)
    far = exchange(pick(held, 1 - chip, 0), *Z0, "states_far")[None]
    held_pair = exchange(held, "seq", 0, "states_pair")
    filled = project(scalars, held, held_pair, CHIP, both_gains, weights, table, None)
    far, leaving, *filled = together(far, pick(held_back, 1 - chip, 0), *filled)
    far_pair = exchange(far, "seq", 0, "states_far_pair")
    back_far = exchange(leaving, *Z0, "cotangent_far")[None]
    back_pair = exchange(held_back, "seq", 0, "cotangent_pair")
    qkv, normed, x, attn, lse = attend(scalars, far, far_pair, both_gains, weights, table, filled)
    attn_pair = exchange(attn, "seq", 0, "attn_pair")
    back_far, attn = together(back_far, attn)
    back_far_pair = exchange(back_far, "seq", 0, "cotangent_far_pair")
    hidden, dyb, dn, layer_keep, layer_send, *feed_grads = feed(
        scalars,
        x,
        held_back,
        back_pair,
        back_far,
        back_far_pair,
        attn,
        attn_pair,
        output_weight,
        both_gains,
        gate_weight,
        up_weight,
        down_weight,
        packed,
    )
    if packed:
        gate_send, gate_keep, up_send, up_keep, down_send, down_keep = feed_grads
        gate = Reduction([X, Y, Z0, Z1], gate_keep, gate_send).go()
        up = Reduction([Y, Z0, X, Z1], up_keep, up_send).go()
        down = Reduction([Z0, X, Y, Z1], down_keep, down_send).go()
    dn_pair = exchange(dn, "seq", 0, "dn_pair")

    def back(pair, given, later, sent=()):
        return attend_back(
            pair, scalars, qkv, attn, lse, given, output_weight, weights, both_gains, normed, table, later, n_seq, sent
        )

    keep0, send0, dhb, second, da, d0 = back(0, [hidden, dyb, dn, dn_pair, both_gains], [])

    def in_order(kept, arrived):
        return jnp.concatenate(
            [jnp.where(chip == 0, kept, arrived), jnp.where(chip == 0, arrived, kept)], axis=0
        )

    if packed:
        rows = width // n_seq // 2

        def to_plane(parts, name):
            return [parts[0]] + [exchange_by(parts[r], "batch", r, name + str(r)) for r in (1, 2, 3)]

        feeds = [gate, up, down]
        keep0, send0, dhb, second, da, d0, layer_send = wait_all(feeds, keep0, send0, dhb, second, da, d0, layer_send)
        layer_arrived = exchange(layer_send, "seq", 0, "layer_pair")
        arrived0 = exchange(send0, "seq", 0, "grad0_pair")
        for r, send in zip(feeds, feed_step(scalars, feeds)):
            r.next(send)
        (da,) = start_all(feeds, da)
        keep1, send1, layer_stay, layer_leave, d1, *plane0 = back(
            1, [da, layer_keep, layer_arrived], [], (keep0, arrived0)
        )

        keep1, send1, layer_stay, layer_leave, d1, *plane0 = wait_all(
            feeds, keep1, send1, layer_stay, layer_leave, d1, *plane0
        )
        arrived1 = exchange(send1, "seq", 0, "grad1_pair")
        flow0 = to_plane(plane0, "plane0_")
        for r, send in zip(feeds, feed_step(scalars, feeds)):
            r.next(send)
        (arrived1, d1) = start_all(feeds, arrived1, d1)
        keep2, norm_keep, norm_send, gains, *plane1 = back(2, [da], [d0, d1, second], (keep1, arrived1))

        flow0[1], flow0[2], flow0[3], keep2, norm_keep, norm_send, gains, layer_leave, *plane1 = wait_all(
            feeds, *flow0[1:], keep2, norm_keep, norm_send, gains, layer_leave, *plane1
        )
        norm_arrived = exchange(norm_send, "seq", 0, "dn1_pair")
        layer_back = exchange(layer_leave, *Z0, "layer_back")
        flow1 = to_plane(plane1, "plane1_")
        *plane2, line0_send, line0_keep, feed_send, feed_keep = third_step(
            scalars, keep2, norm_arrived, gains, flow0, feeds
        )
        line0_send, line0_keep, feed_send, feed_keep, layer_back, *planes = together(
            line0_send, line0_keep, feed_send, feed_keep, layer_back, *plane2, *flow1
        )
        plane2, flow1 = planes[:4], planes[4:]
        flow2 = to_plane(plane2, "plane2_")
        feed_arrived = exchange(feed_send, *Z1, "feed_last")
        arrived0 = exchange(line0_send, *Z0, "line0")
        norm_keep, line0_keep = together(norm_keep, line0_keep)
        stay, leave = finish(scalars, x, norm_keep, norm_arrived, dhb, both_gains)
        leave, stay, arrived0, *flow2 = together(leave, stay, arrived0, *flow2)
        grad_back = exchange(leave, *Z0, "grad_back")
        stay, layer_back, line0_keep, arrived0, *flow12 = together(stay, layer_back, line0_keep, arrived0, *flow1, *flow2)
        *lines, last_keep, layer_out = second_line(
            scalars, flow12[:4], flow12[4:], line0_keep, arrived0, layer_stay, layer_back
        )
        last_keep, feed_arrived, feed_keep = together(last_keep, feed_arrived, feed_keep)
        side_keep, side_send, down_grad = feed_total(scalars, feed_keep, feed_arrived)
        lines = [lines[0]] + [exchange_by(lines[r], "seq", 2 * r, "line12_" + str(r)) for r in (1, 2, 3)]
        side_arrived = exchange(side_send, "seq", 0, "feed_pair")
        down_grad, layer_out = jnp.transpose(down_grad), layer_out.reshape(tokens, width)
        *shards, gate_grad, up_grad, first, second, input_grad = make_shards(
            scalars,
            [last_keep, *lines, side_keep, side_arrived, stay, grad_back],
            2 * rows,
            width // n_batch,
            width,
        )
        first, second, input_grad = first.reshape(width), second.reshape(width), input_grad.reshape(tokens, width)
    else:
        layer_arrived = exchange(layer_send, "seq", 0)
        keep1, _, layer_stay, layer_leave, d1 = back(1, [da, layer_keep, layer_arrived], [])
        layer_back = exchange(layer_leave, *Z0)
        keep2, _, norm_keep, norm_send, gains = back(2, [da], [d0, d1, second])
        norm_arrived = exchange(norm_send, "seq", 0)
        stay, leave = finish(scalars, x, norm_keep, norm_arrived, dhb, both_gains)
        layer_out = in_order(layer_stay, layer_back)
        input_grad = in_order(stay, exchange(leave, *Z0))
        gains = gains[:8].astype(f32) + gains[8:].astype(f32)
        for axis in ("seq", "batch"):
            for bit in range(int(math.log2(lax.axis_size(axis)))):
                gains = gains + exchange(gains, axis, bit)
        first, second = gains[:2].reshape(width), gains[2:4].reshape(width)
        gate_keep, up_keep, down_keep = feed_grads
        units = gate_keep.shape[1]
        zeros = lambda shape: jnp.zeros(shape, bf16)
        blocks = 4

        def spread(array):
            parts = array.reshape(width, blocks, 1, units // blocks)
            full = zeros((width, blocks, 2, units // blocks))
            return lax.dynamic_update_slice_in_dim(full, parts, core, 2).reshape(width, 2 * units)

        heads = attn.shape[1]
        out_keep = jnp.concatenate([keep0[width : width + heads], keep0[width + heads :]], axis=1)
        columns = lambda a: lax.dynamic_update_slice_in_dim(zeros((width, width)), a, core * heads, 1)

        def by_head(m):
            found = {}
            for index, head in enumerate(HEAD_ORDER):
                at = m * PAIR + index % 2 * HEAD_FEATURES
                found[head] = (keep0, keep1, keep2)[index // 2][:width, at : at + HEAD_FEATURES]
            return jnp.concatenate([found[head] for head in sorted(found)], axis=1)

        full = [columns(by_head(m)) for m in range(3)]
        full.append(lax.dynamic_update_slice_in_dim(zeros((width, width)), out_keep, core * heads, 0))
        full += [spread(gate_keep), spread(up_keep), jnp.transpose(spread(down_keep))]
        full = [lax.psum_scatter(a.astype(f32), "seq", scatter_dimension=0, tiled=True) for a in full]
        full = [lax.psum_scatter(a, "batch", scatter_dimension=1, tiled=True) for a in full]
        shards, (gate_grad, up_grad, down_grad) = full[:4], full[4:]

    return (
        layer_out,
        input_grad,
        first,
        shards[0],
        shards[1],
        shards[2],
        shards[3],
        second,
        gate_grad,
        up_grad,
        down_grad,
    )


def solution(mesh):
    split = P(("batch", "seq"), None)
    in_specs = (split,) + (P(),) * 10 + (split,)
    shard = P("seq", "batch")
    out_specs = (split, split, P(), shard, shard, shard, shard, P(), shard, shard, shard)
    return jax.shard_map(body, mesh=mesh, in_specs=in_specs, out_specs=out_specs, check_vma=False)
```

```python
import functools
import math

import jax
import jax.numpy as jnp
import numpy as np
from jax import lax
from jax.experimental import pallas as pl
from jax.experimental.pallas import tpu as pltpu
from jax.sharding import PartitionSpec as P

HEADS = 12
HEAD_FEATURES = 64
MAXLEN = 1024
GROUP = 4
PIECE = MAXLEN // GROUP
PAIR = 2 * HEAD_FEATURES
LOG2E = math.log2(math.e)

epsilon = 1e-06
masked_score = -1e30
f32 = jnp.float32
bf16 = jnp.bfloat16
MIB = 1024 * 1024

SIDES = ((0, 1), (2, 0), (1, 2))
HEAD_ORDER = tuple(h for left, right in SIDES for h in (2 * left, 2 * right + 1))

CORE, CHIP, LENGTH, OTHER_CHIP, OWN_B, OWN_Z = range(6)


def mm(a, b):
    return lax.dot_general(a, b, (((1,), (0,)), ((), ())), preferred_element_type=f32)


def mm_nt(a, b):
    return lax.dot_general(a, b, (((1,), (1,)), ((), ())), preferred_element_type=f32)


def mm_tn(a, b):
    return lax.dot_general(a, b, (((0,), (0,)), ((), ())), preferred_element_type=f32)


def call(body, grid, in_specs, out_specs, out_shape, scratch=(), aliases=None, vmem=64):
    return pl.pallas_call(
        body,
        grid_spec=pltpu.PrefetchScalarGridSpec(
            num_scalar_prefetch=1,
            grid=grid,
            in_specs=in_specs,
            out_specs=out_specs,
            scratch_shapes=list(scratch),
        ),
        out_shape=out_shape,
        input_output_aliases=aliases or {},
        compiler_params=pltpu.CompilerParams(
            dimension_semantics=("arbitrary",) * len(grid), vmem_limit_bytes=vmem * MIB
        ),
        cost_estimate=pl.CostEstimate(flops=1000, bytes_accessed=1000, transcendentals=0),
    )


def whole(shape):
    return pl.BlockSpec(shape, lambda *a: (0,) * len(shape))


def sds(shape, dtype):
    return jax.ShapeDtypeStruct(shape, dtype)


def rope_tables():
    middle = HEAD_FEATURES // 2
    frequency = 10000.0 ** (-np.arange(middle, dtype=np.float64) * 2.0 / HEAD_FEATURES)
    angles = np.arange(MAXLEN, dtype=np.float64)[:, None] * frequency[None, :]
    cosine, sine = np.cos(angles), np.sin(angles)
    half = lax.optimization_barrier(jnp.asarray(np.stack([cosine, sine]).astype(np.float32)))
    return jnp.stack([jnp.tile(half[0], (1, 4)), jnp.concatenate([-half[1], half[1]] * 2, axis=1)])


def rotate(u, table, sign):
    up = pltpu.roll(u, PAIR - HEAD_FEATURES // 2, 1)
    down = pltpu.roll(u, HEAD_FEATURES // 2, 1)
    lane = lax.broadcasted_iota(jnp.int32, (1, PAIR), 1)
    turned = jnp.where(lane % HEAD_FEATURES < HEAD_FEATURES // 2, up, down) * table[1]
    return u * table[0] + turned if sign > 0 else u * table[0] - turned


def pair_of(value, side):
    left, right = (value[:, a * PAIR : (a + 1) * PAIR] for a in side)
    lane = lax.broadcasted_iota(jnp.int32, (1, PAIR), 1)
    return jnp.where(lane < HEAD_FEATURES, left, right)


def slots(start):
    return start + lax.broadcasted_iota(jnp.int32, (PIECE, 1), 0)


def piece_rows(half, place):
    return pl.ds(pl.multiple_of(half * 2 * PIECE + place * PIECE, PIECE), PIECE)


def project_body(s, own, part, gain, wq, wk, wv, table, *rest):
    qkv, normed, copy = rest[-3:]
    low_x = jnp.where(pl.program_id(0) == s[CORE], own[0], part[0])
    copy[...] = low_x
    x = low_x.astype(f32)
    r = lax.rsqrt(jnp.mean(x * x, axis=-1, keepdims=True) + epsilon)
    low = (x * r * gain[0:1, :].astype(f32)).astype(bf16)
    normed[...] = low
    width = wq.shape[1]
    for m, w in enumerate((wq, wk, wv)):
        u = mm(low, w[...])
        if m == 0:
            u = u * (1.0 / math.sqrt(HEAD_FEATURES))
        for p in range(width // PAIR):
            v = pair_of(u, SIDES[p])
            if m < 2:
                v = rotate(v, table, 1)
            at = m * width + p * PAIR
            qkv[:, at : at + PAIR] = v.astype(bf16)


def project(scalars, own, part, half, gain, weights, table, filled):
    width = weights[0].shape[0]
    cols = width // 2
    place = lambda t, s: (s[half] * 2 + t, 0)
    source = lambda a: pl.BlockSpec((1, PIECE, width), lambda t, s: (s[CHIP] if a.shape[0] > 1 else 0, 0, 0))
    weight_spec = pl.BlockSpec((width, cols), lambda t, s: (0, s[CORE]))
    in_specs = [
        source(own),
        source(part),
        whole((2, width)),
        weight_spec,
        weight_spec,
        weight_spec,
        pl.BlockSpec((2, PIECE, PAIR), lambda t, s: (0, s[half] * 2 + t, 0)),
    ]
    args = [scalars, own, part, gain, *weights, table]
    aliases = None
    if filled is not None:
        in_specs += [pl.BlockSpec(memory_space=pl.ANY)] * 3
        aliases = {len(args) + a: a for a in range(3)}
        args += list(filled)
    return call(
        project_body,
        (2,),
        in_specs,
        [pl.BlockSpec((PIECE, 3 * cols), place), pl.BlockSpec((PIECE, width), place), pl.BlockSpec((PIECE, width), place)],
        [sds((MAXLEN, 3 * cols), bf16), sds((MAXLEN, width), bf16), sds((MAXLEN, width), bf16)],
        aliases=aliases,
    )(*args)


def head_mask(h):
    lane = lax.broadcasted_iota(jnp.int32, (1, PAIR), 1)
    return lane < HEAD_FEATURES if h == 0 else lane >= HEAD_FEATURES


def attend_pair(s, q, k, v, out, lse):
    row = lax.broadcasted_iota(jnp.int32, (PIECE, PIECE), 0)
    col = lax.broadcasted_iota(jnp.int32, (PIECE, PIECE), 1)
    lane = lax.broadcasted_iota(jnp.int32, (PIECE, PAIR), 1)
    ones = jnp.ones((MAXLEN, PAIR), bf16)

    def score(b, h):
        at = b * PIECE
        qh = jnp.where(head_mask(h), q[at : at + PIECE, :], jnp.zeros((), bf16))
        near = mm_nt(qh, k[at : at + PIECE, :])
        return near, mm_nt(qh, k[:at, :]) if b else None

    def mix(b, near, far):
        at = b * PIECE
        near = jnp.where(row >= col, near, masked_score)
        top = jnp.max(near, axis=-1, keepdims=True)
        if b:
            top = jnp.maximum(top, jnp.max(far, axis=-1, keepdims=True))
        shift = top * LOG2E
        near = jnp.exp2(near * LOG2E - shift).astype(bf16)
        mixed = mm(near, jnp.concatenate([v[at : at + PIECE, :], ones[:PIECE]], axis=1))
        if b:
            far = jnp.exp2(far * LOG2E - shift).astype(bf16)
            mixed = mixed + mm(far, jnp.concatenate([v[:at, :], ones[:at]], axis=1))
        total = mixed[:, PAIR:]
        return mixed[:, :PAIR] * (1.0 / total), top + jnp.log(total)

    units = [(b, h) for b in range(GROUP) for h in range(2)]
    ahead = score(*units[0])
    done = []
    for at, (b, h) in enumerate(units):
        now = ahead
        if at + 1 < len(units):
            ahead = score(*units[at + 1])
        done.append(mix(b, *now))
        if h == 1:
            rows = slice(b * PIECE, (b + 1) * PIECE)
            (left, left_log), (right, right_log) = done
            done = []
            joined = jnp.where(head_mask(0), left, right)
            out[rows, :] = jnp.where(slots(b * PIECE) < s[LENGTH], joined, 0.0).astype(bf16)
            lse[:, rows] = jnp.transpose(jnp.where(lane == 0, left_log, right_log))[:8]


def attend_body(s, far_hbm, far_pair_hbm, gain, *refs):
    weights_hbm, table_hbm, qkv_in = refs[:3], refs[3], refs[4]
    qkv_out, normed_out, x_out, out, lse = refs[7:12]
    qkv, pieces, lows, weights, table, sems = refs[12:]
    core, half = s[CORE], s[OTHER_CHIP]
    width = weights.shape[1]
    cols = weights.shape[2]
    fetch = fetcher(sems)
    rows_of = lambda side: pl.ds(pl.multiple_of(side * 2 * PIECE, 2 * PIECE), 2 * PIECE)
    first = [fetch(far_hbm.at[0], pieces.at[core]), fetch(far_pair_hbm.at[0], pieces.at[1 - core])]
    for m, w in enumerate(weights_hbm):
        first.append(fetch(w.at[:, pl.ds(pl.multiple_of(core * cols, PAIR), cols)], weights.at[m]))
    first.append(fetch(table_hbm.at[:, rows_of(half), :], table))
    second = fetch(qkv_in.at[rows_of(s[CHIP]), :], qkv.at[rows_of(s[CHIP]), :])
    for made in first:
        made.wait()
    for t in range(2):
        x = pieces[t].astype(f32)
        r = lax.rsqrt(jnp.mean(x * x, axis=-1, keepdims=True) + epsilon)
        low = (x * r * gain[0:1, :].astype(f32)).astype(bf16)
        lows[t] = low
        rows = piece_rows(half, t)
        turn = [table[a, t * PIECE : (t + 1) * PIECE, :] for a in range(2)]
        for m in range(3):
            u = mm(low, weights[m])
            if m == 0:
                u = u * (1.0 / math.sqrt(HEAD_FEATURES))
            for p, side in enumerate(SIDES):
                v = pair_of(u, side)
                if m < 2:
                    v = rotate(v, turn, 1)
                at = m * cols + p * PAIR
                qkv[rows, at : at + PAIR] = v.astype(bf16)
    made = [fetch(qkv.at[rows_of(half), :], qkv_out.at[rows_of(half), :])]
    for t in range(2):
        made.append(fetch(lows.at[t], normed_out.at[piece_rows(half, t), :]))
        made.append(fetch(pieces.at[t], x_out.at[piece_rows(half, t), :]))
    second.wait()

    @pl.loop(0, len(SIDES))
    def _(p):
        q, k, v = (qkv.at[:, pl.ds(pl.multiple_of(m * cols + p * PAIR, PAIR), PAIR)] for m in range(3))
        attend_pair(s, q, k, v, out.at[:, pl.ds(pl.multiple_of(p * PAIR, PAIR), PAIR)], lse.at[p])

    for copy in made:
        copy.wait()


def attend(scalars, far, far_pair, gain, weights, table, filled):
    width = weights[0].shape[0]
    cols = width // 2
    hbm = pl.BlockSpec(memory_space=pl.ANY)
    args = [far, far_pair, gain, *weights, table, *filled]
    outs = [sds(a.shape, a.dtype) for a in filled]
    outs += [sds((MAXLEN, cols), bf16), sds((len(SIDES), 8, MAXLEN), f32)]
    return call(
        attend_body,
        (1,),
        [hbm, hbm, whole(gain.shape)] + [hbm] * 7,
        [hbm] * 3 + [whole(a.shape) for a in outs[3:]],
        outs,
        scratch=[
            pltpu.VMEM((MAXLEN, 3 * cols), bf16),
            pltpu.VMEM((2, PIECE, width), bf16),
            pltpu.VMEM((2, PIECE, width), bf16),
            pltpu.VMEM((3, width, cols), bf16),
            pltpu.VMEM((2, 2 * PIECE, PAIR), f32),
            pltpu.SemaphoreType.DMA((16,)),
        ],
        aliases={8: 0, 9: 1, 10: 2},
    )(scalars, *args)


def pack_rows(block):
    half = block.shape[0] // 2
    lane = lax.broadcasted_iota(jnp.int32, (1, PAIR), 1)
    top, bottom = block[:half], block[half:]
    left = jnp.where(lane < HEAD_FEATURES, top, pltpu.roll(bottom, HEAD_FEATURES, 1))
    right = jnp.where(lane < HEAD_FEATURES, pltpu.roll(top, HEAD_FEATURES, 1), bottom)
    return left, right


def plane_blocks(s, keep, arrived, targets, rows, with_out):
    size = 2 * rows if with_out else rows
    core = s[CORE]
    for r, target in enumerate(targets):
        place = s[OWN_B] ^ r
        for z in range(4):
            at = pl.ds(pl.multiple_of((2 * z + place % 2) * rows, 16), rows)
            target[z * size : z * size + rows, :] = jnp.where(place // 2 == core, keep[at, :], arrived[at, :])
            if with_out:
                at = pl.ds(pl.multiple_of((8 + z % 2 * 4 + place) * rows, 16), rows)
                target[z * size + rows : (z + 1) * size, :] = jnp.where(z // 2 == core, keep[at, :], arrived[at, :])


def attend_back_body(pair, n_seq, s, *refs):
    first, last = pair == 0, pair == len(SIDES) - 1
    refs = list(refs)
    take = lambda count: [refs.pop(0) for _ in range(count)]
    qkv_hbm, attn_hbm, lse_hbm = take(3)
    if first:
        hidden_hbm, dyb_hbm, mine_hbm, theirs_hbm, gain = take(5)
    else:
        (da_hbm,) = take(1)
    middle = pair == 1
    if middle:
        layer_hbm, layer_far_hbm = take(2)
    if last:
        wq_hbm, wk_hbm, wv_hbm, gain = take(4)
    if first:
        (wo_hbm,) = take(1)
    normed_hbm, table_hbm = take(2)
    earlier = take(len(SIDES) - 1) if last else []
    sent = [] if first else take(2) if n_seq == 8 else []
    if last:
        (second_in,) = take(1)
    (keep_out,) = take(1)
    packed = n_seq == 8
    if not (last and packed):
        (send_out,) = take(1)
    if first:
        dhb_out, second, da_out = take(3)
    if middle:
        layer_stay, layer_leave = take(2)
    if last:
        norm_keep, norm_send, gains = take(3)
        if packed:
            send_out = norm_send.at[pl.ds(MAXLEN, norm_send.shape[0] - MAXLEN), :]
    else:
        (d_out,) = take(1)
    plane = take(4) if sent else []
    q, k, v, o, lse, normed, table, sems = take(8)
    da, da_t, q_t, dk_t, dv_t, dq, grads = take(7)
    (shifts,) = take(1)
    if first:
        hidden, dyb, mine, theirs, attn, out_grad, wo = take(7)
        dhb = dhb_out
    if middle:
        layer, layer_far = take(2)
    if last:
        before, joined, gain_rows, weights = take(4)
    before_sent = take(2) if sent else []
    core = s[CORE]
    width = normed.shape[1]
    zero = jnp.zeros((), bf16)
    pairs = len(SIDES)
    heads = pairs * PAIR
    copies = []

    def fetch(source, target):
        copy = pltpu.make_async_copy(source, target, sems.at[len(copies)])
        copy.start()
        copies.append(copy)
        return copy

    lanes_of = lambda m: slice((m * pairs + pair) * PAIR, (m * pairs + pair + 1) * PAIR)
    chunks = [slice(t * PIECE, (t + 1) * PIECE) for t in range(GROUP)]
    chunk_copies = []
    if first:
        for rows in chunks:
            chunk_copies.append(
                [
                    fetch(source.at[rows, :], target.at[rows, :])
                    for source, target in (
                        (mine_hbm, mine),
                        (theirs_hbm, theirs),
                        (hidden_hbm, hidden),
                        (dyb_hbm, dyb),
                    )
                ]
            )
    if first:
        wo_copies = [
            fetch(
                wo_hbm.at[pl.ds(pl.multiple_of(core * heads + head * HEAD_FEATURES, HEAD_FEATURES), HEAD_FEATURES), :],
                wo.at[index * HEAD_FEATURES : (index + 1) * HEAD_FEATURES, :],
            )
            for index, head in enumerate(HEAD_ORDER)
        ]
    else:
        wo_copies = [fetch(da_hbm.at[:, pair * PAIR : (pair + 1) * PAIR], da)]
    q_copies = [
        fetch(qkv_hbm.at[:, lanes_of(0)], q),
        fetch(qkv_hbm.at[:, lanes_of(1)], k),
        fetch(qkv_hbm.at[:, lanes_of(2)], v),
        fetch(attn_hbm.at[:, pair * PAIR : (pair + 1) * PAIR], o),
        fetch(lse_hbm.at[pair], lse),
    ]

    def fetch_late():
        late = [fetch(normed_hbm, normed), fetch(table_hbm, table)]
        late += [fetch(source, target) for source, target in zip(sent, before_sent)]
        if last:
            for m, w in enumerate((wq_hbm, wk_hbm, wv_hbm)):
                late.append(fetch(w.at[:, pl.ds(pl.multiple_of(core * heads, PAIR), heads)], weights.at[m]))
            for at, source in enumerate(earlier):
                late.append(fetch(source, before.at[:, at * heads : (at + 1) * heads]))
        if first:
            late.append(fetch(attn_hbm, attn))
        if middle:
            late += [fetch(layer_hbm, layer), fetch(layer_far_hbm, layer_far)]
        return late

    late_copies = fetch_late()
    if first:
        scale = gain[1:2, :].astype(f32)
        sums = jnp.zeros((1, width), f32)
        for rows, waiting in zip(chunks, chunk_copies):
            for copy in waiting:
                copy.wait()
            h = hidden[rows, :].astype(f32)
            r = lax.rsqrt(jnp.mean(h * h, axis=-1, keepdims=True) + epsilon)
            g = mine[rows, :].astype(f32) + theirs[rows, :].astype(f32)
            sums = sums + jnp.sum(g * h * r, axis=0, keepdims=True)
            scaled = g * scale
            inner = jnp.mean(scaled * h, axis=-1, keepdims=True)
            d = dyb[rows, :].astype(f32) + r * scaled - h * (r * r * r) * inner
            dhb[rows, :] = d.astype(bf16)
        second[...] = sums * 0.5
    for copy in wo_copies:
        copy.wait()
    if first:
        for t, rows in enumerate(chunks):
            d = mm_nt(dhb[rows, :], wo[...])
            da_out[rows, :] = jnp.where(slots(t * PIECE) < s[LENGTH], d, 0.0).astype(bf16)
        da[...] = da_out[:, :PAIR]
    da_t[...] = jnp.transpose(da[...])
    for copy in q_copies:
        copy.wait()
    q_t[...] = jnp.transpose(q[...])
    shifts[...] = jnp.transpose(lse[...]) * LOG2E

    row = lax.broadcasted_iota(jnp.int32, (PIECE, PIECE), 0)
    col = lax.broadcasted_iota(jnp.int32, (PIECE, PIECE), 1)

    def score(a, h):
        at = a * PIECE
        mask = head_mask(h)
        qh = jnp.where(mask, q[at : at + PIECE, :], zero)
        gh = jnp.where(mask, da[at : at + PIECE, :], zero)
        near = mm_nt(qh, k[at : at + PIECE, :]), mm_nt(gh, v[at : at + PIECE, :])
        far = (mm_nt(qh, k[:at, :]), mm_nt(gh, v[:at, :])) if a else None
        return near, far

    def back(a, h, near, far):
        at = a * PIECE
        rows = slice(at, at + PIECE)
        feats = slice(h * HEAD_FEATURES, (h + 1) * HEAD_FEATURES)
        mask = head_mask(h)
        shift = shifts[rows, h : h + 1]
        product = da[rows, :].astype(f32) * o[rows, :].astype(f32)
        inner = jnp.sum(jnp.where(mask, product, 0.0), axis=-1, keepdims=True)
        near_prob = jnp.exp2(jnp.where(row >= col, near[0] * LOG2E - shift, masked_score))
        near_ds = (near_prob * (near[1] - inner)).astype(bf16)
        query_grad = mm(near_ds, jnp.where(mask, k[rows, :], zero))
        parts = [(rows, near_prob.astype(bf16), near_ds)]
        if a:
            far_prob = jnp.exp2(far[0] * LOG2E - shift)
            far_ds = (far_prob * (far[1] - inner)).astype(bf16)
            query_grad = query_grad + mm(far_ds, jnp.where(mask, k[:at, :], zero))
            parts.append((slice(0, at), far_prob.astype(bf16), far_ds))
        for cols, prob, ds in parts:
            value_grad = mm(da_t[feats, rows], prob)
            key_grad = mm(q_t[feats, rows], ds)
            if a == GROUP - 1:
                dv_t[feats, cols] = value_grad
                dk_t[feats, cols] = key_grad
            else:
                dv_t[feats, cols] += value_grad
                dk_t[feats, cols] += key_grad
        return query_grad

    units = [(a, h) for a in reversed(range(GROUP)) for h in range(2)]
    ahead = score(*units[0])
    held = None
    for at, (a, h) in enumerate(units):
        now = ahead
        if at + 1 < len(units):
            ahead = score(*units[at + 1])
        g = back(a, h, *now)
        if h == 0:
            held = g
        else:
            dq[a * PIECE : (a + 1) * PIECE, :] = held + g

    for copy in late_copies:
        copy.wait()
    if sent:
        plane_blocks(s, *before_sent, plane, width // n_seq // 2, pair == 1)
    d = jnp.concatenate(
        [
            rotate(dq[...] * (1.0 / math.sqrt(HEAD_FEATURES)), table, -1).astype(bf16),
            rotate(jnp.transpose(dk_t[...]), table, -1).astype(bf16),
            jnp.transpose(dv_t[...].astype(bf16)),
        ],
        axis=1,
    )
    if last:
        before[:, (pairs - 1) * heads :] = d
    else:
        d_out[...] = d
    grads[...] = mm_tn(normed[...], d)

    rows = width // n_seq
    half_row = rows // 2
    if rows % 16:
        keep_out[:width, :] = grads[...].astype(bf16)
    else:
        left_x = SIDES[pair][0] * 2 // pairs
        for target, place in ((keep_out, core), (send_out, 1 - core)):
            for z in range(n_seq // 2):
                at = pl.ds(pl.multiple_of((2 * z + place) * rows, 8), rows)
                for m in range(3):
                    lanes = slice(m * PAIR, (m + 1) * PAIR)
                    left, right = pack_rows(grads[at, lanes])
                    for x_of, value in ((left_x, left), (1 - left_x, right)):
                        to = (2 * z + x_of) * half_row
                        target[to : to + half_row, lanes] = value.astype(bf16)

    if middle:
        for target, half in ((layer_leave, s[OTHER_CHIP]), (layer_stay, s[CHIP])):
            value = layer[half] + layer_far[half].astype(f32)
            live = slots(half * 2 * PIECE + core * PIECE) < s[LENGTH]
            target[...] = jnp.where(live, value, 0.0).astype(bf16)
    if first:
        g = mm_tn(attn[...], dhb[...])
        for index, head in enumerate(HEAD_ORDER):
            out_grad[head * HEAD_FEATURES : (head + 1) * HEAD_FEATURES, :] = g[
                index * HEAD_FEATURES : (index + 1) * HEAD_FEATURES, :
            ]
        if rows % 16:
            keep_out[width:, :] = jnp.concatenate([out_grad[:, :heads], out_grad[:, heads:]], axis=0).astype(bf16)
        else:
            column = width // 4
            for target, place in ((keep_out, core), (send_out, 1 - core)):
                for z in range(n_seq // 4):
                    block = out_grad[pl.ds(pl.multiple_of((2 * z + place) * rows, 8), rows), :]
                    for b in range(4):
                        lanes = slice(b * column, (b + 1) * column)
                        to = (n_seq + 4 * z + b) * half_row
                        target[to : to + half_row, :] = jnp.concatenate(
                            [block[:half_row, lanes], block[half_row:, lanes]], axis=1
                        ).astype(bf16)
    if last:
        for p, side in enumerate(SIDES):
            for m in range(3):
                at = p * heads + m * PAIR
                joined[:, at : at + PAIR] = pair_of(weights[m], side)
        sums = jnp.zeros((1, width), f32)
        for half in range(2):
            for target, place in ((norm_send, 1 - core), (norm_keep, core)):
                where = piece_rows(half, place)
                part = mm_nt(before[where, :], joined[...])
                if target is norm_keep:
                    target[half] = part.astype(bf16)
                else:
                    for side in range(2):
                        at = (2 * half + side) * PIECE
                        target[at : at + PIECE, :] = part[:, side * heads : (side + 1) * heads].astype(bf16)
                sums = sums + jnp.sum(part * normed[where, :].astype(f32), axis=0, keepdims=True)
        sums = sums / gain[0:1, :].astype(f32)
        gain_rows[...] = jnp.zeros_like(gain_rows)
        for index, value in enumerate((sums, second_in[...])):
            for part in range(2):
                gain_rows[2 * index + part : 2 * index + part + 1, :] = value[:, part * heads : (part + 1) * heads]
        high = gain_rows[...].astype(bf16)
        low = (gain_rows[...] - high.astype(f32)).astype(bf16)
        gains[...] = jnp.concatenate([high, low], axis=0)
        if rows % 16 == 0:
            send_out[n_seq * half_row :, :] = gains[...]


def attend_back(pair, scalars, qkv, attn, lse, given, wo, weights, gains, normed, table, earlier, n_seq, sent=()):
    first, last = pair == 0, pair == len(SIDES) - 1
    heads = attn.shape[1]
    width = wo.shape[1]
    rows = width // n_seq
    token_shape = (2, PIECE, width)
    if rows % 16 == 0:
        count = n_seq * rows // 2 * (2 if first else 1)
        shapes = [(count, heads)] * 2
    else:
        shapes = [(2 * width if first else width, heads), (8, 128)]
    extra = shapes[1][0] + 16 if n_seq == 8 else 0
    outs = [sds(a, bf16) for a in shapes[: 1 if last and n_seq == 8 else 2]]
    hbm = pl.BlockSpec(memory_space=pl.ANY)
    given, later = list(given), []
    given_specs = [hbm] * len(given)
    if first:
        outs += [sds((MAXLEN, width), bf16), sds((1, width), f32), sds((MAXLEN, heads), bf16)]
        given_specs[4] = whole((2, width))
        given.append(wo)
        given_specs.append(hbm)
    if pair == 1:
        outs += [sds((PIECE, width), bf16)] * 2
    if last:
        outs += [sds(token_shape, bf16), sds((MAXLEN + extra, heads), bf16), sds((16, heads), bf16)]
        given += [*weights, gains]
        given_specs += [hbm] * 3 + [whole((2, width))]
    else:
        outs += [sds((MAXLEN, heads), bf16)]
    outs += [sds((2 * rows * (2 if pair == 1 else 1), heads), bf16)] * (4 if sent else 0)
    later = list(earlier[: len(SIDES) - 1]) + list(sent) + list(earlier[len(SIDES) - 1 :])
    args = [qkv, attn, lse, *given, normed, table, *later]
    in_specs = [hbm] * 3 + given_specs + [hbm] * (2 + len(later))
    if last:
        in_specs[-1] = whole((1, width))
    scratch = [
        pltpu.VMEM((MAXLEN, PAIR), bf16),
        pltpu.VMEM((MAXLEN, PAIR), bf16),
        pltpu.VMEM((MAXLEN, PAIR), bf16),
        pltpu.VMEM((MAXLEN, PAIR), bf16),
        pltpu.VMEM((8, MAXLEN), f32),
        pltpu.VMEM((MAXLEN, width), bf16),
        pltpu.VMEM((2, MAXLEN, PAIR), f32),
        pltpu.SemaphoreType.DMA((48,)),
        pltpu.VMEM((MAXLEN, PAIR), bf16),
        pltpu.VMEM((PAIR, MAXLEN), bf16),
        pltpu.VMEM((PAIR, MAXLEN), bf16),
        pltpu.VMEM((PAIR, MAXLEN), f32),
        pltpu.VMEM((PAIR, MAXLEN), f32),
        pltpu.VMEM((MAXLEN, PAIR), f32),
        pltpu.VMEM((width, heads), f32),
        pltpu.VMEM((MAXLEN, 8), f32),
    ]
    if first:
        scratch += [pltpu.VMEM((MAXLEN, width), bf16)] * 4
        scratch += [
            pltpu.VMEM((MAXLEN, heads), bf16),
            pltpu.VMEM((heads, width), f32),
            pltpu.VMEM((heads, width), bf16),
        ]
    if pair == 1:
        scratch += [pltpu.VMEM(token_shape, f32), pltpu.VMEM(token_shape, bf16)]
    if last:
        scratch += [
            pltpu.VMEM((MAXLEN, len(SIDES) * heads), bf16),
            pltpu.VMEM((width, len(SIDES) * heads), bf16),
            pltpu.VMEM((8, heads), f32),
            pltpu.VMEM((3, width, heads), bf16),
        ]
    if sent:
        scratch += [pltpu.VMEM(a.shape, bf16) for a in sent]
    return call(
        functools.partial(attend_back_body, pair, n_seq),
        (1,),
        in_specs,
        [whole(a.shape) for a in outs],
        outs,
        scratch=scratch,
    )(scalars, *args)


def feed_body(
    packed, s, x_hbm, dy_hbm, dy_pair_hbm, dy_far_hbm, dy_far_pair_hbm, attn_hbm, attn_pair_hbm, wo_hbm, gain, *refs
):
    refs = list(refs)
    take = lambda count: [refs.pop(0) for _ in range(count)]
    wg_hbm, wu_hbm, wd_hbm = take(3)
    hidden_out, dyb_out, dn_out, layer_out, send_out = take(5)
    grads_out = take(6 if packed else 3)
    x, attn, wo, wg, wu, wd, dyb = take(7)
    hidden, hidden_low, low, low_t, dyb_t, acts, dgs, dus, dn, layer, send = take(11)
    blocks = take(12)
    sems, late_sems = take(2)
    core = s[CORE]
    tokens, width = x.shape
    heads = width // 2
    steps = 4
    cols = wg.shape[1] // steps
    used = [0]

    def copy(source, target):
        made = pltpu.make_async_copy(source, target, sems.at[used[0]])
        used[0] += 1
        made.start()
        return made

    chunks = [slice(t * PIECE, (t + 1) * PIECE) for t in range(GROUP)]
    unit = [2 * ((3 - step) ^ s[OWN_B]) + core for step in range(steps)]

    wo_copies = [
        copy(
            wo_hbm.at[pl.ds(pl.multiple_of(place * heads + head * HEAD_FEATURES, HEAD_FEATURES), HEAD_FEATURES), :],
            wo.at[at * heads + index * HEAD_FEATURES : at * heads + (index + 1) * HEAD_FEATURES, :],
        )
        for at, place in enumerate((core, 1 - core))
        for index, head in enumerate(HEAD_ORDER)
    ]
    token_copies = [
        [
            copy(x_hbm.at[rows, :], x.at[rows, :]),
            copy(attn_hbm.at[rows, :], attn.at[rows, :heads]),
            copy(attn_pair_hbm.at[rows, :], attn.at[rows, heads:]),
        ]
        for rows in chunks
    ]
    def weights_of(step):
        at = pl.ds(pl.multiple_of(unit[step] * cols, cols), cols)
        here = slice(step * cols, (step + 1) * cols)
        return [
            copy(wg_hbm.at[:, at], wg.at[:, here]),
            copy(wu_hbm.at[:, at], wu.at[:, here]),
            copy(wd_hbm.at[at, :], wd.at[here, :]),
        ]

    dy_copies = [
        copy(source, dyb.at[piece_rows(half, place), :])
        for source, half, place in (
            (dy_hbm.at[s[CHIP]], s[CHIP], core),
            (dy_pair_hbm.at[s[CHIP]], s[CHIP], 1 - core),
            (dy_far_hbm.at[0], s[OTHER_CHIP], core),
            (dy_far_pair_hbm.at[0], s[OTHER_CHIP], 1 - core),
        )
    ]
    out_copies, side_copies = [], []

    for made in wo_copies:
        made.wait()
    scale = gain[1:2, :].astype(f32)
    weight_copies = [weights_of(0)]
    for t, rows in enumerate(chunks):
        for made in token_copies[t]:
            made.wait()
        h = x[rows, :].astype(f32) + mm(attn[rows, :], wo[...])
        hidden[rows, :] = h
        hidden_low[rows, :] = h.astype(bf16)
        out_copies.append(copy(hidden_low.at[rows, :], hidden_out.at[rows, :]))
        r = lax.rsqrt(jnp.mean(h * h, axis=-1, keepdims=True) + epsilon)
        low[rows, :] = (h * r * scale).astype(bf16)
    low_t[...] = jnp.transpose(low[...])
    for made in dy_copies:
        made.wait()
    for t, rows in enumerate(chunks):
        dyb[rows, :] = jnp.where(slots(t * PIECE) < s[LENGTH], dyb[rows, :], jnp.zeros((), bf16))
    dyb_t[...] = jnp.transpose(dyb[...])
    out_copies.append(copy(dyb, dyb_out))

    def products(step, t):
        if t == 0:
            for made in weight_copies.pop():
                made.wait()
            if step + 1 < steps:
                weight_copies.append(weights_of(step + 1))
        rows, here = chunks[t], slice(step * cols, (step + 1) * cols)
        return mm(low[rows, :], wg[:, here]), mm(low[rows, :], wu[:, here]), mm_nt(dyb[rows, :], wd[here, :])

    def pointwise(step, t, gate, up, dact):
        rows, here = chunks[t], slice(step * cols, (step + 1) * cols)
        sig = 1.0 / (1.0 + jnp.exp2(gate * -LOG2E))
        silu = gate * sig
        acts[rows, here] = (silu * up).astype(bf16)
        dgs[rows, here] = (dact * up * (sig + silu * (1.0 - sig))).astype(bf16)
        dus[rows, here] = (dact * silu).astype(bf16)

    def weight_grads(step, which):
        here = slice(step * cols, (step + 1) * cols)
        left, right = ((low_t, dgs), (low_t, dus), (dyb_t, acts))[which]
        grad = blocks[3 * step + which]
        grad[...] = mm(left[...], right[:, here]).astype(bf16)
        if not packed:
            at = pl.ds(pl.multiple_of(unit[step] // 2 * cols, cols), cols)
            out_copies.append(copy(grad, grads_out[which].at[:, at]))
            return
        rows = width // 4
        y, x = (3 - step) // 2, (3 - step) % 2
        own = s[OWN_B] if which == 2 else s[OWN_Z]
        z = (unit[step] // 2) ^ s[OWN_Z]
        for high in range(2):
            for low_bit in range(2):
                source = grad.at[pl.ds(pl.multiple_of(((2 * high + low_bit) ^ own) * rows, 16), rows), :]
                if which == 0:
                    out_copies.append(copy(source, grads_out[0 if x else 1].at[y, low_bit, high]))
                elif which == 1:
                    out_copies.append(copy(source, grads_out[2 if y else 3].at[low_bit, x, high]))
                else:
                    sem = sems.at[used[0]]
                    used[0] += 1
                    for side, target in ((1, grads_out[4]), (0, grads_out[5])):
                        made = pltpu.make_async_copy(source, target.at[low_bit, high, z // 2], sem)
                        pl.when(z % 2 == side)(made.start)
                        side_copies.append((z % 2 == side, made))

    units = [(step, t) for step in range(steps) for t in range(GROUP)]
    ahead = products(*units[0])
    for index, (step, t) in enumerate(units):
        now = ahead
        if index + 1 < len(units):
            ahead = products(*units[index + 1])
        pointwise(step, t, *now)
        if step and t < 3:
            weight_grads(step - 1, t)
    for which in range(3):
        weight_grads(steps - 1, which)
    def late_copies(t):
        rows = pl.ds(pl.multiple_of(t * PIECE, PIECE), PIECE)
        return pltpu.make_async_copy(dn.at[rows, :], dn_out.at[rows, :], late_sems.at[t])

    @pl.loop(0, 2)
    def _(half):
        send[half] = mm(acts[piece_rows(half, 1 - core), :], wd[...]).astype(bf16)
        rows = piece_rows(half, core)
        layer[half] = hidden[rows, :] + mm(acts[rows, :], wd[...])

    out_copies.append(copy(send, send_out))
    out_copies.append(copy(layer, layer_out))

    @pl.loop(0, GROUP)
    def _(t):
        rows = pl.ds(pl.multiple_of(t * PIECE, PIECE), PIECE)
        dn[rows, :] = (mm_nt(dgs[rows, :], wg[...]) + mm_nt(dus[rows, :], wu[...])).astype(bf16)
        late_copies(t).start()

    for t in range(GROUP):
        late_copies(t).wait()
    for made in out_copies:
        made.wait()
    for when, made in side_copies:
        pl.when(when)(made.wait)


def feed(scalars, x, dy, dy_pair, dy_far, dy_far_pair, attn, attn_pair, wo, gain, wg, wu, wd, packed):
    tokens, width = x.shape
    units = wg.shape[1] // 2
    cols = units // 4
    token_shape = (2, PIECE, width)
    if packed:
        shapes = [(2, 2, 2, width // 4, cols)] * 6
    else:
        shapes = [(width, units)] * 3
    outs = [
        sds((tokens, width), bf16),
        sds((tokens, width), bf16),
        sds((tokens, width), bf16),
        sds(token_shape, f32),
        sds(token_shape, bf16),
    ] + [sds(a, bf16) for a in shapes]
    args = [x, dy, dy_pair, dy_far, dy_far_pair, attn, attn_pair, wo, gain, wg, wu, wd]
    in_specs = [pl.BlockSpec(memory_space=pl.ANY)] * len(args)
    in_specs[8] = whole((2, width))
    low = pltpu.VMEM((tokens, width), bf16)
    high = pltpu.VMEM((tokens, width), f32)
    turned = pltpu.VMEM((width, tokens), bf16)
    hidden_units = pltpu.VMEM((tokens, units), bf16)
    return call(
        functools.partial(feed_body, packed),
        (1,),
        in_specs,
        [pl.BlockSpec(memory_space=pl.ANY)] * len(outs),
        outs,
        scratch=[
            low,
            low,
            pltpu.VMEM((width, width), bf16),
            pltpu.VMEM((width, units), bf16),
            pltpu.VMEM((width, units), bf16),
            pltpu.VMEM((units, width), bf16),
            low,
            high,
            low,
            low,
            turned,
            turned,
            hidden_units,
            hidden_units,
            hidden_units,
            low,
            pltpu.VMEM(token_shape, f32),
            pltpu.VMEM(token_shape, bf16),
        ]
        + [pltpu.VMEM((width, cols), bf16)] * 12
        + [pltpu.SemaphoreType.DMA((112,)), pltpu.SemaphoreType.DMA((GROUP,))],
    )(scalars, *args)


def piece_of(half, side):
    return pl.ds(pl.multiple_of((2 * half + side) * PIECE, PIECE), PIECE)


def finish_body(s, x, keep, recv, dh, gain, stay, leave):
    scale = gain[0:1, :].astype(f32)
    for out, half in ((leave, s[OTHER_CHIP]), (stay, s[CHIP])):
        h = x[half, 0].astype(f32)
        there = jnp.concatenate([recv[piece_of(half, side), :] for side in range(2)], axis=1)
        dn = keep[half].astype(f32) + there.astype(f32)
        r = lax.rsqrt(jnp.mean(h * h, axis=-1, keepdims=True) + epsilon)
        scaled = dn * scale
        inner = jnp.mean(scaled * h, axis=-1, keepdims=True)
        out[...] = (dh[half, 0].astype(f32) + r * scaled - h * (r * r * r) * inner).astype(bf16)


def finish(scalars, x, keep, recv, dh, gain):
    width = x.shape[1]
    shape = (2, PIECE, width)
    own = pl.BlockSpec((2, 1, PIECE, width), lambda f, s: (0, s[CORE], 0, 0))
    return call(
        finish_body,
        (1,),
        [own, whole(shape), whole((MAXLEN, recv.shape[1])), own, whole((2, width))],
        [whole((PIECE, width))] * 2,
        [sds((PIECE, width), bf16)] * 2,
    )(scalars, x.reshape(2, 2, PIECE, width), keep, recv, dh.reshape(2, 2, PIECE, width), gain)


def decode(coded):
    return coded[:8].astype(f32) + coded[8:].astype(f32)


def encode(value):
    high = value.astype(bf16)
    return jnp.concatenate([high, (value - high.astype(f32)).astype(bf16)], axis=0)


def sum_parts(fetch, groups, scratch):
    loads = []
    for group in groups:
        loads.append([])
        for source in group:
            target = scratch.pop(0)
            loads[-1].append((fetch(source, target), target))

    def total(group):
        value = None
        for made, target in group:
            made.wait()
            part = target[...].astype(f32)
            value = part if value is None else value + part
        return value

    return [functools.partial(total, group) for group in loads]


def fetcher(sems):
    used = [0]

    def fetch(source, target):
        made = pltpu.make_async_copy(source, target, sems.at[used[0]])
        used[0] += 1
        made.start()
        return made

    return fetch


def feed_step_body(paths, s, *refs):
    refs = list(refs)
    groups = [[refs.pop(0).at[path] for path in group] for group in paths]
    outs = [refs.pop(0) for _ in groups]
    sems = refs.pop()
    for out, total in zip(outs, sum_parts(fetcher(sems), groups, refs)):
        out[...] = total().astype(bf16)


def feed_step(scalars, reductions):
    groups = [r.paths(1) for r in reductions]
    args = [array for group in groups for array, _ in group]
    paths = [[path for _, path in group] for group in groups]
    slices = [array.shape[len(path) :] for group in groups for array, path in group]
    outs = [sds(group[0][0].shape[len(group[0][1]) :], bf16) for group in groups]
    return call(
        functools.partial(feed_step_body, paths),
        (1,),
        [pl.BlockSpec(memory_space=pl.ANY)] * len(args),
        [whole(a.shape) for a in outs],
        outs,
        scratch=[pltpu.VMEM(a, bf16) for a in slices] + [pltpu.SemaphoreType.DMA((len(args),))],
    )(scalars, *args)


def third_step_body(paths, s, keep_hbm, arrived_hbm, gains, *refs):
    refs = list(refs)
    groups = [[refs.pop(0).at[path] for path in group] for group in paths]
    parts_hbm = [refs.pop(0) for _ in range(4)]
    plane = [refs.pop(0) for _ in range(4)]
    line_send, line_keep = refs.pop(0), refs.pop(0)
    sends, kept = refs.pop(0), refs.pop(0)
    keep, arrived = refs.pop(0), refs.pop(0)
    parts = [refs.pop(0) for _ in range(4)]
    sems = refs.pop()
    fetch = fetcher(sems)
    rows = keep.shape[0] // 8
    first = [
        fetch(keep_hbm, keep),
        fetch(arrived_hbm.at[pl.ds(MAXLEN, arrived.shape[0]), :], arrived),
    ]
    second = [fetch(source, target) for source, target in zip(parts_hbm, parts)]
    totals = sum_parts(fetch, groups, refs)
    for made in first:
        made.wait()
    plane_blocks(s, keep, arrived, plane, rows, False)
    coded = encode(decode(gains[...]) + decode(arrived[8 * rows :, :]))
    for target in plane:
        target[4 * rows :, :] = coded
    for made in second:
        made.wait()
    size = line_keep.shape[0] // 2
    own = s[OWN_Z] % 2
    for target, z0 in ((line_send, 1 - own), (line_keep, own)):
        for z1 in range(2):
            at = pl.ds(pl.multiple_of((2 * z1 + z0) * size, 16), size)
            total = None
            for part in parts:
                value = part[at, :].astype(f32)
                total = value if total is None else total + value
            target[z1 * size : (z1 + 1) * size, :] = total.astype(bf16)
    for index in range(3):
        sends[index] = totals[index]().astype(bf16)
        kept[index] = totals[3 + index]()


def third_step(scalars, keep, arrived, gains, parts, reductions):
    groups = [r.paths(1) for r in reductions] + [r.paths(0) for r in reductions]
    sums = [array for group in groups for array, _ in group]
    paths = [[path for _, path in group] for group in groups]
    slices = [array.shape[len(path) :] for group in groups for array, path in group]
    rows, columns = keep.shape
    outs = [sds((rows // 2 + 16, columns), bf16)] * 4
    outs += [sds((parts[0].shape[0] // 2, columns), bf16)] * 2
    outs += [sds((3,) + slices[0], bf16), sds((3,) + slices[0], f32)]
    hbm = pl.BlockSpec(memory_space=pl.ANY)
    return call(
        functools.partial(third_step_body, paths),
        (1,),
        [hbm, hbm, whole(gains.shape)] + [hbm] * (len(sums) + 4),
        [whole(a.shape) for a in outs],
        outs,
        scratch=[pltpu.VMEM(keep.shape, bf16), pltpu.VMEM((rows + 16, columns), bf16)]
        + [pltpu.VMEM(a.shape, bf16) for a in parts]
        + [pltpu.VMEM(a, bf16) for a in slices]
        + [pltpu.SemaphoreType.DMA((len(sums) + 6,))],
    )(scalars, keep, arrived, gains, *sums, *parts)


def second_line_body(s, *refs):
    refs = list(refs)
    take = lambda count: [refs.pop(0) for _ in range(count)]
    middle_hbm, last_hbm, line_hbm = take(4), take(4), take(2)
    layer_stay_hbm, layer_back_hbm = take(2)
    lines, (last_keep,) = take(4), take(1)
    (layer_out,) = take(1)
    middle, last, (keep0, arrived0) = take(4), take(4), take(2)
    (sems,) = take(1)
    fetch = fetcher(sems)
    first = [fetch(a, b) for a, b in zip(middle_hbm + last_hbm + line_hbm, middle + last + [keep0, arrived0])]
    third = [
        fetch(layer_stay_hbm, layer_out.at[s[CHIP]]),
        fetch(layer_back_hbm, layer_out.at[s[OTHER_CHIP]]),
    ]
    for made in first:
        made.wait()
    rows = middle[0].shape[0] // 4
    coded = [ref[4 * rows :, :] for ref in last]
    gains = encode((decode(coded[0]) + decode(coded[1])) + (decode(coded[2]) + decode(coded[3])))
    for r, target in enumerate(lines):
        at = pl.ds(pl.multiple_of((s[OWN_Z] ^ r) * rows, 16), rows)
        for index, parts in enumerate((middle, last)):
            total = None
            for part in parts:
                value = part[at, :].astype(f32)
                total = value if total is None else total + value
            target[index * rows : (index + 1) * rows, :] = total.astype(bf16)
        target[2 * rows : 2 * rows + 16, :] = gains
    size = keep0.shape[0] // 2
    own = s[OWN_Z] // 2
    for target, z1 in ((last_keep, own), (lines[2].at[2 * rows + 16 :, :], 1 - own)):
        at = pl.ds(pl.multiple_of(z1 * size, 16), size)
        target[...] = (keep0[at, :].astype(f32) + arrived0[at, :].astype(f32)).astype(bf16)
    for made in third:
        made.wait()


def second_line(scalars, middle, last, keep0, arrived0, layer_stay, layer_back):
    rows, columns = middle[0].shape[0] // 4, middle[0].shape[1]
    size = keep0.shape[0] // 2
    outs = [sds((2 * rows + 16 + (size if r == 2 else 0), columns), bf16) for r in range(4)]
    outs += [sds((size, columns), bf16)]
    outs += [sds((2,) + layer_stay.shape, bf16)]
    args = [*middle, *last, keep0, arrived0, layer_stay, layer_back]
    return call(
        second_line_body,
        (1,),
        [pl.BlockSpec(memory_space=pl.ANY)] * len(args),
        [whole(a.shape) for a in outs],
        outs,
        scratch=[pltpu.VMEM(a.shape, a.dtype) for a in args[:-2]] + [pltpu.SemaphoreType.DMA((len(args),))],
    )(scalars, *args)


def feed_total_body(s, feed_keep, feed_arrived, side_keep, side_send, down_out):
    rows = side_keep.shape[1]
    for index in range(2):
        value = feed_keep[index] + feed_arrived[index].astype(f32)
        for part in range(2):
            block = value[part * rows : (part + 1) * rows]

            @pl.when(s[CORE] == part)
            def _():
                side_keep[index] = block

            @pl.when(s[CORE] != part)
            def _():
                side_send[index] = block.astype(bf16)

    down_out[...] = feed_keep[2] + feed_arrived[2].astype(f32)

def feed_total(scalars, keep, arrived):
    rows, cols = keep.shape[1:]
    outs = [sds((2, rows // 2, cols), f32), sds((2, rows // 2, cols), bf16), sds((rows, cols), f32)]
    args = [keep, arrived]
    return call(
        feed_total_body,
        (1,),
        [whole(a.shape) for a in args],
        [whole(a.shape) for a in outs],
        outs,
    )(scalars, *args)


def shards_body(s, keep0, line0, line1, line2, line3, side_keep, side_arrived, stay, back, *outs):
    half, width = outs[0].shape[0] // 2, outs[0].shape[1]
    count = line0.shape[0]
    first = keep0[...].astype(f32) + line2[count:, :].astype(f32)
    rest = (line0[...].astype(f32) + line1[...].astype(f32)) + (
        line2[:count, :].astype(f32) + line3[...].astype(f32)
    )
    out = first[half:]
    outs[3][:half, :] = out[:, :width]
    outs[3][half:, :] = out[:, width:]
    for pair, part in enumerate((first[:half], rest[:half], rest[half : 2 * half])):
        lanes = slice(pair * HEAD_FEATURES, (pair + 1) * HEAD_FEATURES)
        for m in range(3):
            at = m * PAIR
            outs[m][:half, lanes] = part[:, at : at + HEAD_FEATURES]
            outs[m][half:, lanes] = part[:, at + HEAD_FEATURES : at + PAIR]
    gains = rest[2 * half : 2 * half + 8] + rest[2 * half + 8 :]
    for index in range(2):
        row = jnp.concatenate([gains[2 * index : 2 * index + 1], gains[2 * index + 1 : 2 * index + 2]], axis=1)
        for at in range(outs[6].shape[0]):
            outs[6 + index][at : at + 1, :] = row[:, at * PAIR : (at + 1) * PAIR]
    cols = side_keep.shape[2]
    for index in range(2):
        for core in range(2):

            @pl.when(s[CORE] == core)
            def _():
                outs[4 + index][:, core * cols : (core + 1) * cols] = side_keep[index]
                outs[4 + index][:, (1 - core) * cols : (2 - core) * cols] = side_arrived[index].astype(f32)

    outs[8][s[CHIP]] = stay[...]
    outs[8][s[OTHER_CHIP]] = back[...]


def make_shards(scalars, args, rows, columns, width):
    side = sds((rows, 2 * args[5].shape[-1]), f32)
    outs = [sds((rows, columns), f32)] * 4 + [side] * 2 + [sds((width // PAIR, PAIR), f32)] * 2
    outs.append(sds((2,) + args[-1].shape, bf16))
    return call(
        shards_body,
        (1,),
        [whole(a.shape) for a in args],
        [whole(a.shape) for a in outs],
        outs,
    )(scalars, *args)


def exchange_by(block, axis, difference, name):
    count = lax.axis_size(axis)
    with jax.named_scope(name):
        return lax.ppermute(block, axis, [(a, a ^ difference) for a in range(count)])


def exchange(block, axis, bit, name="swap"):
    return exchange_by(block, axis, 1 << bit, name)


def pick(block, index, dim):
    return lax.dynamic_index_in_dim(block, index, dim, keepdims=False)


def together(*values):
    return lax.optimization_barrier(values)


X, Y, Z0, Z1 = ("batch", 0), ("batch", 1), ("seq", 1), ("seq", 2)


class Reduction:
    def __init__(self, order, keep, send):
        self.order, self.level, self.send, self.parts = order, 0, send, [keep]

    def go(self):
        bit = self.order[self.level]
        self.arrived = exchange(self.send, *bit, "feed_" + "_".join(map(str, bit)))
        return self

    def paths(self, side):
        found = []
        for index, array in enumerate([*self.parts, self.arrived]):
            found.append((array, (0,) * (self.level - max(index - 1, 0)) + (side,)))
        return found

    def next(self, send):
        self.parts.append(self.arrived)
        self.send = send
        self.level += 1
        return self


def start_all(reductions, *others):
    sends = together(*[r.send for r in reductions], *others)
    for r, send in zip(reductions, sends):
        r.send = send
        r.go()
    return sends[len(reductions) :]


def wait_all(reductions, *others):
    values = together(*[r.arrived for r in reductions], *others)
    for r, arrived in zip(reductions, values):
        r.arrived = arrived
    return values[len(reductions) :]


def body(
    states,
    lengths,
    first_gain,
    query_weight,
    key_weight,
    value_weight,
    output_weight,
    second_gain,
    gate_weight,
    up_weight,
    down_weight,
    cotangent,
):
    tokens, width = states.shape
    n_seq, n_batch = lax.axis_size("seq"), lax.axis_size("batch")
    packed = n_seq == 8 and n_batch == 4
    place = lax.axis_index("seq")
    batch = lax.axis_index("batch")
    core = place & 1
    chip = place >> 1 & 1
    sequence = (batch * (n_seq // GROUP) + place // GROUP) * 2 + chip
    length = pick(lengths, sequence, 0)
    own_b, own_z = batch & 3, place >> 1 & 3
    scalars = jnp.stack([core, chip, length, 1 - chip, own_b, own_z]).astype(jnp.int32)
    table = rope_tables()
    both_gains = jnp.stack([first_gain, second_gain])
    weights = (query_weight, key_weight, value_weight)

    held = states.reshape(2, PIECE, width)
    held_back = cotangent.reshape(2, PIECE, width)
    far = exchange(pick(held, 1 - chip, 0), *Z0, "states_far")[None]
    held_pair = exchange(held, "seq", 0, "states_pair")
    filled = project(scalars, held, held_pair, CHIP, both_gains, weights, table, None)
    far, leaving, *filled = together(far, pick(held_back, 1 - chip, 0), *filled)
    far_pair = exchange(far, "seq", 0, "states_far_pair")
    back_far = exchange(leaving, *Z0, "cotangent_far")[None]
    back_pair = exchange(held_back, "seq", 0, "cotangent_pair")
    qkv, normed, x, attn, lse = attend(scalars, far, far_pair, both_gains, weights, table, filled)
    attn_pair = exchange(attn, "seq", 0, "attn_pair")
    back_far, attn = together(back_far, attn)
    back_far_pair = exchange(back_far, "seq", 0, "cotangent_far_pair")
    hidden, dyb, dn, layer_keep, layer_send, *feed_grads = feed(
        scalars,
        x,
        held_back,
        back_pair,
        back_far,
        back_far_pair,
        attn,
        attn_pair,
        output_weight,
        both_gains,
        gate_weight,
        up_weight,
        down_weight,
        packed,
    )
    if packed:
        gate_send, gate_keep, up_send, up_keep, down_send, down_keep = feed_grads
        gate = Reduction([X, Y, Z0, Z1], gate_keep, gate_send).go()
        up = Reduction([Y, Z0, X, Z1], up_keep, up_send).go()
        down = Reduction([Z0, X, Y, Z1], down_keep, down_send).go()
    dn_pair = exchange(dn, "seq", 0, "dn_pair")

    def back(pair, given, later, sent=()):
        return attend_back(
            pair, scalars, qkv, attn, lse, given, output_weight, weights, both_gains, normed, table, later, n_seq, sent
        )

    keep0, send0, dhb, second, da, d0 = back(0, [hidden, dyb, dn, dn_pair, both_gains], [])

    def in_order(kept, arrived):
        return jnp.concatenate(
            [jnp.where(chip == 0, kept, arrived), jnp.where(chip == 0, arrived, kept)], axis=0
        )

    if packed:
        rows = width // n_seq // 2

        def to_plane(parts, name):
            return [parts[0]] + [exchange_by(parts[r], "batch", r, name + str(r)) for r in (1, 2, 3)]

        feeds = [gate, up, down]
        keep0, send0, dhb, second, da, d0, layer_send = wait_all(feeds, keep0, send0, dhb, second, da, d0, layer_send)
        layer_arrived = exchange(layer_send, "seq", 0, "layer_pair")
        arrived0 = exchange(send0, "seq", 0, "grad0_pair")
        for r, send in zip(feeds, feed_step(scalars, feeds)):
            r.next(send)
        (da,) = start_all(feeds, da)
        keep1, send1, layer_stay, layer_leave, d1, *plane0 = back(
            1, [da, layer_keep, layer_arrived], [], (keep0, arrived0)
        )

        keep1, send1, layer_stay, layer_leave, d1, *plane0 = wait_all(
            feeds, keep1, send1, layer_stay, layer_leave, d1, *plane0
        )
        arrived1 = exchange(send1, "seq", 0, "grad1_pair")
        flow0 = to_plane(plane0, "plane0_")
        for r, send in zip(feeds, feed_step(scalars, feeds)):
            r.next(send)
        (arrived1, d1) = start_all(feeds, arrived1, d1)
        keep2, norm_keep, norm_send, gains, *plane1 = back(2, [da], [d0, d1, second], (keep1, arrived1))

        flow0[1], flow0[2], flow0[3], keep2, norm_keep, norm_send, gains, layer_leave, *plane1 = wait_all(
            feeds, *flow0[1:], keep2, norm_keep, norm_send, gains, layer_leave, *plane1
        )
        norm_arrived = exchange(norm_send, "seq", 0, "dn1_pair")
        layer_back = exchange(layer_leave, *Z0, "layer_back")
        flow1 = to_plane(plane1, "plane1_")
        *plane2, line0_send, line0_keep, feed_send, feed_keep = third_step(
            scalars, keep2, norm_arrived, gains, flow0, feeds
        )
        line0_send, line0_keep, feed_send, feed_keep, layer_back, *planes = together(
            line0_send, line0_keep, feed_send, feed_keep, layer_back, *plane2, *flow1
        )
        plane2, flow1 = planes[:4], planes[4:]
        flow2 = to_plane(plane2, "plane2_")
        feed_arrived = exchange(feed_send, *Z1, "feed_last")
        arrived0 = exchange(line0_send, *Z0, "line0")
        norm_keep, line0_keep = together(norm_keep, line0_keep)
        stay, leave = finish(scalars, x, norm_keep, norm_arrived, dhb, both_gains)
        leave, stay, arrived0, *flow2 = together(leave, stay, arrived0, *flow2)
        grad_back = exchange(leave, *Z0, "grad_back")
        stay, layer_back, line0_keep, arrived0, *flow12 = together(stay, layer_back, line0_keep, arrived0, *flow1, *flow2)
        *lines, last_keep, layer_out = second_line(
            scalars, flow12[:4], flow12[4:], line0_keep, arrived0, layer_stay, layer_back
        )
        last_keep, feed_arrived, feed_keep = together(last_keep, feed_arrived, feed_keep)
        side_keep, side_send, down_grad = feed_total(scalars, feed_keep, feed_arrived)
        lines = [lines[0]] + [exchange_by(lines[r], "seq", 2 * r, "line12_" + str(r)) for r in (1, 2, 3)]
        side_arrived = exchange(side_send, "seq", 0, "feed_pair")
        down_grad, layer_out = jnp.transpose(down_grad), layer_out.reshape(tokens, width)
        *shards, gate_grad, up_grad, first, second, input_grad = make_shards(
            scalars,
            [last_keep, *lines, side_keep, side_arrived, stay, grad_back],
            2 * rows,
            width // n_batch,
            width,
        )
        first, second, input_grad = first.reshape(width), second.reshape(width), input_grad.reshape(tokens, width)
    else:
        layer_arrived = exchange(layer_send, "seq", 0)
        keep1, _, layer_stay, layer_leave, d1 = back(1, [da, layer_keep, layer_arrived], [])
        layer_back = exchange(layer_leave, *Z0)
        keep2, _, norm_keep, norm_send, gains = back(2, [da], [d0, d1, second])
        norm_arrived = exchange(norm_send, "seq", 0)
        stay, leave = finish(scalars, x, norm_keep, norm_arrived, dhb, both_gains)
        layer_out = in_order(layer_stay, layer_back)
        input_grad = in_order(stay, exchange(leave, *Z0))
        gains = gains[:8].astype(f32) + gains[8:].astype(f32)
        for axis in ("seq", "batch"):
            for bit in range(int(math.log2(lax.axis_size(axis)))):
                gains = gains + exchange(gains, axis, bit)
        first, second = gains[:2].reshape(width), gains[2:4].reshape(width)
        gate_keep, up_keep, down_keep = feed_grads
        units = gate_keep.shape[1]
        zeros = lambda shape: jnp.zeros(shape, bf16)
        blocks = 4

        def spread(array):
            parts = array.reshape(width, blocks, 1, units // blocks)
            full = zeros((width, blocks, 2, units // blocks))
            return lax.dynamic_update_slice_in_dim(full, parts, core, 2).reshape(width, 2 * units)

        heads = attn.shape[1]
        out_keep = jnp.concatenate([keep0[width : width + heads], keep0[width + heads :]], axis=1)
        columns = lambda a: lax.dynamic_update_slice_in_dim(zeros((width, width)), a, core * heads, 1)

        def by_head(m):
            found = {}
            for index, head in enumerate(HEAD_ORDER):
                at = m * PAIR + index % 2 * HEAD_FEATURES
                found[head] = (keep0, keep1, keep2)[index // 2][:width, at : at + HEAD_FEATURES]
            return jnp.concatenate([found[head] for head in sorted(found)], axis=1)

        full = [columns(by_head(m)) for m in range(3)]
        full.append(lax.dynamic_update_slice_in_dim(zeros((width, width)), out_keep, core * heads, 0))
        full += [spread(gate_keep), spread(up_keep), jnp.transpose(spread(down_keep))]
        full = [lax.psum_scatter(a.astype(f32), "seq", scatter_dimension=0, tiled=True) for a in full]
        full = [lax.psum_scatter(a, "batch", scatter_dimension=1, tiled=True) for a in full]
        shards, (gate_grad, up_grad, down_grad) = full[:4], full[4:]

    return (
        layer_out,
        input_grad,
        first,
        shards[0],
        shards[1],
        shards[2],
        shards[3],
        second,
        gate_grad,
        up_grad,
        down_grad,
    )


def solution(mesh):
    split = P(("batch", "seq"), None)
    in_specs = (split,) + (P(),) * 10 + (split,)
    shard = P("seq", "batch")
    out_specs = (split, split, P(), shard, shard, shard, shard, P(), shard, shard, shard)
    return jax.shard_map(body, mesh=mesh, in_specs=in_specs, out_specs=out_specs, check_vma=False)
```

```python
import functools
import math

import jax
import jax.numpy as jnp
import numpy as np
from jax import lax
from jax.experimental import pallas as pl
from jax.experimental.pallas import tpu as pltpu
from jax.sharding import PartitionSpec as P

HEADS = 12
HEAD_FEATURES = 64
MAXLEN = 1024
GROUP = 4
PIECE = MAXLEN // GROUP
PAIR = 2 * HEAD_FEATURES
LOG2E = math.log2(math.e)

epsilon = 1e-06
masked_score = -1e30
f32 = jnp.float32
bf16 = jnp.bfloat16
MIB = 1024 * 1024

SIDES = ((0, 1), (2, 0), (1, 2))
HEAD_ORDER = tuple(h for left, right in SIDES for h in (2 * left, 2 * right + 1))

CORE, CHIP, LENGTH, OTHER_CHIP, OWN_B, OWN_Z = range(6)


def mm(a, b):
    return lax.dot_general(a, b, (((1,), (0,)), ((), ())), preferred_element_type=f32)


def mm_nt(a, b):
    return lax.dot_general(a, b, (((1,), (1,)), ((), ())), preferred_element_type=f32)


def mm_tn(a, b):
    return lax.dot_general(a, b, (((0,), (0,)), ((), ())), preferred_element_type=f32)


def call(body, grid, in_specs, out_specs, out_shape, scratch=(), aliases=None, vmem=64):
    return pl.pallas_call(
        body,
        grid_spec=pltpu.PrefetchScalarGridSpec(
            num_scalar_prefetch=1,
            grid=grid,
            in_specs=in_specs,
            out_specs=out_specs,
            scratch_shapes=list(scratch),
        ),
        out_shape=out_shape,
        input_output_aliases=aliases or {},
        compiler_params=pltpu.CompilerParams(
            dimension_semantics=("arbitrary",) * len(grid), vmem_limit_bytes=vmem * MIB
        ),
        cost_estimate=pl.CostEstimate(flops=1000, bytes_accessed=1000, transcendentals=0),
    )


def whole(shape):
    return pl.BlockSpec(shape, lambda *a: (0,) * len(shape))


def sds(shape, dtype):
    return jax.ShapeDtypeStruct(shape, dtype)


def rope_tables():
    middle = HEAD_FEATURES // 2
    frequency = 10000.0 ** (-np.arange(middle, dtype=np.float64) * 2.0 / HEAD_FEATURES)
    angles = np.arange(MAXLEN, dtype=np.float64)[:, None] * frequency[None, :]
    cosine, sine = np.cos(angles), np.sin(angles)
    half = lax.optimization_barrier(jnp.asarray(np.stack([cosine, sine]).astype(np.float32)))
    return jnp.stack([jnp.tile(half[0], (1, 4)), jnp.concatenate([-half[1], half[1]] * 2, axis=1)])


def rotate(u, table, sign):
    up = pltpu.roll(u, PAIR - HEAD_FEATURES // 2, 1)
    down = pltpu.roll(u, HEAD_FEATURES // 2, 1)
    lane = lax.broadcasted_iota(jnp.int32, (1, PAIR), 1)
    turned = jnp.where(lane % HEAD_FEATURES < HEAD_FEATURES // 2, up, down) * table[1]
    return u * table[0] + turned if sign > 0 else u * table[0] - turned


def pair_of(value, side):
    left, right = (value[:, a * PAIR : (a + 1) * PAIR] for a in side)
    lane = lax.broadcasted_iota(jnp.int32, (1, PAIR), 1)
    return jnp.where(lane < HEAD_FEATURES, left, right)


def slots(start):
    return start + lax.broadcasted_iota(jnp.int32, (PIECE, 1), 0)


def piece_rows(half, place):
    return pl.ds(pl.multiple_of(half * 2 * PIECE + place * PIECE, PIECE), PIECE)


def project_body(s, own, part, gain, wq, wk, wv, table, *rest):
    qkv, normed, copy = rest[-3:]
    low_x = jnp.where(pl.program_id(0) == s[CORE], own[0], part[0])
    copy[...] = low_x
    x = low_x.astype(f32)
    r = lax.rsqrt(jnp.mean(x * x, axis=-1, keepdims=True) + epsilon)
    low = (x * r * gain[0:1, :].astype(f32)).astype(bf16)
    normed[...] = low
    width = wq.shape[1]
    for m, w in enumerate((wq, wk, wv)):
        u = mm(low, w[...])
        if m == 0:
            u = u * (1.0 / math.sqrt(HEAD_FEATURES))
        for p in range(width // PAIR):
            v = pair_of(u, SIDES[p])
            if m < 2:
                v = rotate(v, table, 1)
            at = m * width + p * PAIR
            qkv[:, at : at + PAIR] = v.astype(bf16)


def project(scalars, own, part, half, gain, weights, table, filled):
    width = weights[0].shape[0]
    cols = width // 2
    place = lambda t, s: (s[half] * 2 + t, 0)
    source = lambda a: pl.BlockSpec((1, PIECE, width), lambda t, s: (s[CHIP] if a.shape[0] > 1 else 0, 0, 0))
    weight_spec = pl.BlockSpec((width, cols), lambda t, s: (0, s[CORE]))
    in_specs = [
        source(own),
        source(part),
        whole((2, width)),
        weight_spec,
        weight_spec,
        weight_spec,
        pl.BlockSpec((2, PIECE, PAIR), lambda t, s: (0, s[half] * 2 + t, 0)),
    ]
    args = [scalars, own, part, gain, *weights, table]
    aliases = None
    if filled is not None:
        in_specs += [pl.BlockSpec(memory_space=pl.ANY)] * 3
        aliases = {len(args) + a: a for a in range(3)}
        args += list(filled)
    return call(
        project_body,
        (2,),
        in_specs,
        [pl.BlockSpec((PIECE, 3 * cols), place), pl.BlockSpec((PIECE, width), place), pl.BlockSpec((PIECE, width), place)],
        [sds((MAXLEN, 3 * cols), bf16), sds((MAXLEN, width), bf16), sds((MAXLEN, width), bf16)],
        aliases=aliases,
    )(*args)


def head_mask(h):
    lane = lax.broadcasted_iota(jnp.int32, (1, PAIR), 1)
    return lane < HEAD_FEATURES if h == 0 else lane >= HEAD_FEATURES


def attend_pair(s, q, k, v, out, lse):
    row = lax.broadcasted_iota(jnp.int32, (PIECE, PIECE), 0)
    col = lax.broadcasted_iota(jnp.int32, (PIECE, PIECE), 1)
    lane = lax.broadcasted_iota(jnp.int32, (PIECE, PAIR), 1)
    ones = jnp.ones((MAXLEN, PAIR), bf16)

    def score(b, h):
        at = b * PIECE
        qh = jnp.where(head_mask(h), q[at : at + PIECE, :], jnp.zeros((), bf16))
        near = mm_nt(qh, k[at : at + PIECE, :])
        return near, mm_nt(qh, k[:at, :]) if b else None

    def mix(b, near, far):
        at = b * PIECE
        near = jnp.where(row >= col, near, masked_score)
        top = jnp.max(near, axis=-1, keepdims=True)
        if b:
            top = jnp.maximum(top, jnp.max(far, axis=-1, keepdims=True))
        shift = top * LOG2E
        near = jnp.exp2(near * LOG2E - shift).astype(bf16)
        mixed = mm(near, jnp.concatenate([v[at : at + PIECE, :], ones[:PIECE]], axis=1))
        if b:
            far = jnp.exp2(far * LOG2E - shift).astype(bf16)
            mixed = mixed + mm(far, jnp.concatenate([v[:at, :], ones[:at]], axis=1))
        total = mixed[:, PAIR:]
        return mixed[:, :PAIR] * (1.0 / total), top + jnp.log(total)

    units = [(b, h) for b in range(GROUP) for h in range(2)]
    ahead = score(*units[0])
    done = []
    for at, (b, h) in enumerate(units):
        now = ahead
        if at + 1 < len(units):
            ahead = score(*units[at + 1])
        done.append(mix(b, *now))
        if h == 1:
            rows = slice(b * PIECE, (b + 1) * PIECE)
            (left, left_log), (right, right_log) = done
            done = []
            joined = jnp.where(head_mask(0), left, right)
            out[rows, :] = jnp.where(slots(b * PIECE) < s[LENGTH], joined, 0.0).astype(bf16)
            lse[:, rows] = jnp.transpose(jnp.where(lane == 0, left_log, right_log))[:8]


def attend_body(s, far_hbm, far_pair_hbm, gain, *refs):
    weights_hbm, table_hbm, qkv_in = refs[:3], refs[3], refs[4]
    qkv_out, normed_out, x_out, out, lse = refs[7:12]
    qkv, pieces, lows, weights, table, sems = refs[12:]
    core, half = s[CORE], s[OTHER_CHIP]
    width = weights.shape[1]
    cols = weights.shape[2]
    fetch = fetcher(sems)
    rows_of = lambda side: pl.ds(pl.multiple_of(side * 2 * PIECE, 2 * PIECE), 2 * PIECE)
    first = [fetch(far_hbm.at[0], pieces.at[core]), fetch(far_pair_hbm.at[0], pieces.at[1 - core])]
    for m, w in enumerate(weights_hbm):
        first.append(fetch(w.at[:, pl.ds(pl.multiple_of(core * cols, PAIR), cols)], weights.at[m]))
    first.append(fetch(table_hbm.at[:, rows_of(half), :], table))
    second = fetch(qkv_in.at[rows_of(s[CHIP]), :], qkv.at[rows_of(s[CHIP]), :])
    for made in first:
        made.wait()
    for t in range(2):
        x = pieces[t].astype(f32)
        r = lax.rsqrt(jnp.mean(x * x, axis=-1, keepdims=True) + epsilon)
        low = (x * r * gain[0:1, :].astype(f32)).astype(bf16)
        lows[t] = low
        rows = piece_rows(half, t)
        turn = [table[a, t * PIECE : (t + 1) * PIECE, :] for a in range(2)]
        for m in range(3):
            u = mm(low, weights[m])
            if m == 0:
                u = u * (1.0 / math.sqrt(HEAD_FEATURES))
            for p, side in enumerate(SIDES):
                v = pair_of(u, side)
                if m < 2:
                    v = rotate(v, turn, 1)
                at = m * cols + p * PAIR
                qkv[rows, at : at + PAIR] = v.astype(bf16)
    made = [fetch(qkv.at[rows_of(half), :], qkv_out.at[rows_of(half), :])]
    for t in range(2):
        made.append(fetch(lows.at[t], normed_out.at[piece_rows(half, t), :]))
        made.append(fetch(pieces.at[t], x_out.at[piece_rows(half, t), :]))
    second.wait()

    @pl.loop(0, len(SIDES))
    def _(p):
        q, k, v = (qkv.at[:, pl.ds(pl.multiple_of(m * cols + p * PAIR, PAIR), PAIR)] for m in range(3))
        attend_pair(s, q, k, v, out.at[:, pl.ds(pl.multiple_of(p * PAIR, PAIR), PAIR)], lse.at[p])

    for copy in made:
        copy.wait()


def attend(scalars, far, far_pair, gain, weights, table, filled):
    width = weights[0].shape[0]
    cols = width // 2
    hbm = pl.BlockSpec(memory_space=pl.ANY)
    args = [far, far_pair, gain, *weights, table, *filled]
    outs = [sds(a.shape, a.dtype) for a in filled]
    outs += [sds((MAXLEN, cols), bf16), sds((len(SIDES), 8, MAXLEN), f32)]
    return call(
        attend_body,
        (1,),
        [hbm, hbm, whole(gain.shape)] + [hbm] * 7,
        [hbm] * 3 + [whole(a.shape) for a in outs[3:]],
        outs,
        scratch=[
            pltpu.VMEM((MAXLEN, 3 * cols), bf16),
            pltpu.VMEM((2, PIECE, width), bf16),
            pltpu.VMEM((2, PIECE, width), bf16),
            pltpu.VMEM((3, width, cols), bf16),
            pltpu.VMEM((2, 2 * PIECE, PAIR), f32),
            pltpu.SemaphoreType.DMA((16,)),
        ],
        aliases={8: 0, 9: 1, 10: 2},
    )(scalars, *args)


def pack_rows(block):
    half = block.shape[0] // 2
    lane = lax.broadcasted_iota(jnp.int32, (1, PAIR), 1)
    top, bottom = block[:half], block[half:]
    left = jnp.where(lane < HEAD_FEATURES, top, pltpu.roll(bottom, HEAD_FEATURES, 1))
    right = jnp.where(lane < HEAD_FEATURES, pltpu.roll(top, HEAD_FEATURES, 1), bottom)
    return left, right


def plane_blocks(s, keep, arrived, targets, rows, with_out):
    size = 2 * rows if with_out else rows
    core = s[CORE]
    for r, target in enumerate(targets):
        place = s[OWN_B] ^ r
        for z in range(4):
            at = pl.ds(pl.multiple_of((2 * z + place % 2) * rows, 16), rows)
            target[z * size : z * size + rows, :] = jnp.where(place // 2 == core, keep[at, :], arrived[at, :])
            if with_out:
                at = pl.ds(pl.multiple_of((8 + z % 2 * 4 + place) * rows, 16), rows)
                target[z * size + rows : (z + 1) * size, :] = jnp.where(z // 2 == core, keep[at, :], arrived[at, :])


def attend_back_body(pair, n_seq, s, *refs):
    first, last = pair == 0, pair == len(SIDES) - 1
    refs = list(refs)
    take = lambda count: [refs.pop(0) for _ in range(count)]
    qkv_hbm, attn_hbm, lse_hbm = take(3)
    if first:
        hidden_hbm, dyb_hbm, mine_hbm, theirs_hbm, gain = take(5)
    else:
        (da_hbm,) = take(1)
    middle = pair == 1
    if middle:
        layer_hbm, layer_far_hbm = take(2)
    if last:
        wq_hbm, wk_hbm, wv_hbm, gain = take(4)
    if first:
        (wo_hbm,) = take(1)
    normed_hbm, table_hbm = take(2)
    earlier = take(len(SIDES) - 1) if last else []
    sent = [] if first else take(2) if n_seq == 8 else []
    if last:
        (second_in,) = take(1)
    (keep_out,) = take(1)
    packed = n_seq == 8
    if not (last and packed):
        (send_out,) = take(1)
    if first:
        dhb_out, second, da_out = take(3)
    if middle:
        layer_stay, layer_leave = take(2)
    if last:
        norm_keep, norm_send, gains = take(3)
        if packed:
            send_out = norm_send.at[pl.ds(MAXLEN, norm_send.shape[0] - MAXLEN), :]
    else:
        (d_out,) = take(1)
    plane = take(4) if sent else []
    q, k, v, o, lse, normed, table, sems = take(8)
    da, da_t, q_t, dk_t, dv_t, dq, grads = take(7)
    (shifts,) = take(1)
    if first:
        hidden, dyb, mine, theirs, attn, out_grad, wo = take(7)
        dhb = dhb_out
    if middle:
        layer, layer_far = take(2)
    if last:
        before, joined, gain_rows, weights = take(4)
    before_sent = take(2) if sent else []
    core = s[CORE]
    width = normed.shape[1]
    zero = jnp.zeros((), bf16)
    pairs = len(SIDES)
    heads = pairs * PAIR
    copies = []

    def fetch(source, target):
        copy = pltpu.make_async_copy(source, target, sems.at[len(copies)])
        copy.start()
        copies.append(copy)
        return copy

    lanes_of = lambda m: slice((m * pairs + pair) * PAIR, (m * pairs + pair + 1) * PAIR)
    chunks = [slice(t * PIECE, (t + 1) * PIECE) for t in range(GROUP)]
    chunk_copies = []
    if first:
        for rows in chunks:
            chunk_copies.append(
                [
                    fetch(source.at[rows, :], target.at[rows, :])
                    for source, target in (
                        (mine_hbm, mine),
                        (theirs_hbm, theirs),
                        (hidden_hbm, hidden),
                        (dyb_hbm, dyb),
                    )
                ]
            )
    if first:
        wo_copies = [
            fetch(
                wo_hbm.at[pl.ds(pl.multiple_of(core * heads + head * HEAD_FEATURES, HEAD_FEATURES), HEAD_FEATURES), :],
                wo.at[index * HEAD_FEATURES : (index + 1) * HEAD_FEATURES, :],
            )
            for index, head in enumerate(HEAD_ORDER)
        ]
    else:
        wo_copies = [fetch(da_hbm.at[:, pair * PAIR : (pair + 1) * PAIR], da)]
    q_copies = [
        fetch(qkv_hbm.at[:, lanes_of(0)], q),
        fetch(qkv_hbm.at[:, lanes_of(1)], k),
        fetch(qkv_hbm.at[:, lanes_of(2)], v),
        fetch(attn_hbm.at[:, pair * PAIR : (pair + 1) * PAIR], o),
        fetch(lse_hbm.at[pair], lse),
    ]

    def fetch_late():
        late = [fetch(normed_hbm, normed), fetch(table_hbm, table)]
        late += [fetch(source, target) for source, target in zip(sent, before_sent)]
        if last:
            for m, w in enumerate((wq_hbm, wk_hbm, wv_hbm)):
                late.append(fetch(w.at[:, pl.ds(pl.multiple_of(core * heads, PAIR), heads)], weights.at[m]))
            for at, source in enumerate(earlier):
                late.append(fetch(source, before.at[:, at * heads : (at + 1) * heads]))
        if first:
            late.append(fetch(attn_hbm, attn))
        if middle:
            late += [fetch(layer_hbm, layer), fetch(layer_far_hbm, layer_far)]
        return late

    late_copies = fetch_late()
    if first:
        scale = gain[1:2, :].astype(f32)
        sums = jnp.zeros((1, width), f32)
        for rows, waiting in zip(chunks, chunk_copies):
            for copy in waiting:
                copy.wait()
            h = hidden[rows, :].astype(f32)
            r = lax.rsqrt(jnp.mean(h * h, axis=-1, keepdims=True) + epsilon)
            g = mine[rows, :].astype(f32) + theirs[rows, :].astype(f32)
            sums = sums + jnp.sum(g * h * r, axis=0, keepdims=True)
            scaled = g * scale
            inner = jnp.mean(scaled * h, axis=-1, keepdims=True)
            d = dyb[rows, :].astype(f32) + r * scaled - h * (r * r * r) * inner
            dhb[rows, :] = d.astype(bf16)
        second[...] = sums * 0.5
    for copy in wo_copies:
        copy.wait()
    if first:
        for t, rows in enumerate(chunks):
            d = mm_nt(dhb[rows, :], wo[...])
            da_out[rows, :] = jnp.where(slots(t * PIECE) < s[LENGTH], d, 0.0).astype(bf16)
        da[...] = da_out[:, :PAIR]
    da_t[...] = jnp.transpose(da[...])
    for copy in q_copies:
        copy.wait()
    q_t[...] = jnp.transpose(q[...])
    shifts[...] = jnp.transpose(lse[...]) * LOG2E

    row = lax.broadcasted_iota(jnp.int32, (PIECE, PIECE), 0)
    col = lax.broadcasted_iota(jnp.int32, (PIECE, PIECE), 1)

    def score(a, h):
        at = a * PIECE
        mask = lax.broadcasted_iota(jnp.int32, (1, PAIR), 1) // HEAD_FEATURES == h
        qh = jnp.where(mask, q[at : at + PIECE, :], zero)
        gh = jnp.where(mask, da[at : at + PIECE, :], zero)
        near = mm_nt(qh, k[at : at + PIECE, :]), mm_nt(gh, v[at : at + PIECE, :])
        far = (mm_nt(qh, k[:at, :]), mm_nt(gh, v[:at, :])) if a else None
        return near, far

    def back(a, h, near, far):
        at = a * PIECE
        rows = slice(at, at + PIECE)
        feats = pl.ds(pl.multiple_of(h * HEAD_FEATURES, HEAD_FEATURES), HEAD_FEATURES)
        mask = lax.broadcasted_iota(jnp.int32, (1, PAIR), 1) // HEAD_FEATURES == h
        shift = jnp.where(h == 0, shifts[rows, 0:1], shifts[rows, 1:2])
        product = da[rows, :].astype(f32) * o[rows, :].astype(f32)
        inner = jnp.sum(jnp.where(mask, product, 0.0), axis=-1, keepdims=True)
        near_prob = jnp.exp2(jnp.where(row >= col, near[0] * LOG2E - shift, masked_score))
        near_ds = (near_prob * (near[1] - inner)).astype(bf16)
        query_grad = mm(near_ds, jnp.where(mask, k[rows, :], zero))
        parts = [(rows, near_prob.astype(bf16), near_ds)]
        if a:
            far_prob = jnp.exp2(far[0] * LOG2E - shift)
            far_ds = (far_prob * (far[1] - inner)).astype(bf16)
            query_grad = query_grad + mm(far_ds, jnp.where(mask, k[:at, :], zero))
            parts.append((slice(0, at), far_prob.astype(bf16), far_ds))
        for cols, prob, ds in parts:
            value_grad = mm(da_t[feats, rows], prob)
            key_grad = mm(q_t[feats, rows], ds)
            if a == GROUP - 1:
                dv_t[feats, cols] = value_grad
                dk_t[feats, cols] = key_grad
            else:
                dv_t[feats, cols] += value_grad
                dk_t[feats, cols] += key_grad
        return query_grad

    dq[...] = jnp.zeros_like(dq)

    @pl.loop(0, 2)
    def _(h):
        ahead = score(GROUP - 1, h)
        for a in reversed(range(GROUP)):
            now = ahead
            if a:
                ahead = score(a - 1, h)
            dq[a * PIECE : (a + 1) * PIECE, :] += back(a, h, *now)

    for copy in late_copies:
        copy.wait()
    if sent:
        plane_blocks(s, *before_sent, plane, width // n_seq // 2, pair == 1)
    d = jnp.concatenate(
        [
            rotate(dq[...] * (1.0 / math.sqrt(HEAD_FEATURES)), table, -1).astype(bf16),
            rotate(jnp.transpose(dk_t[...]), table, -1).astype(bf16),
            jnp.transpose(dv_t[...].astype(bf16)),
        ],
        axis=1,
    )
    if last:
        before[:, (pairs - 1) * heads :] = d
    else:
        d_out[...] = d
    grads[...] = mm_tn(normed[...], d)

    rows = width // n_seq
    half_row = rows // 2
    if rows % 16:
        keep_out[:width, :] = grads[...].astype(bf16)
    else:
        left_x = SIDES[pair][0] * 2 // pairs
        for target, place in ((keep_out, core), (send_out, 1 - core)):
            for z in range(n_seq // 2):
                at = pl.ds(pl.multiple_of((2 * z + place) * rows, 8), rows)
                for m in range(3):
                    lanes = slice(m * PAIR, (m + 1) * PAIR)
                    left, right = pack_rows(grads[at, lanes])
                    for x_of, value in ((left_x, left), (1 - left_x, right)):
                        to = (2 * z + x_of) * half_row
                        target[to : to + half_row, lanes] = value.astype(bf16)

    if middle:
        for target, half in ((layer_leave, s[OTHER_CHIP]), (layer_stay, s[CHIP])):
            value = layer[half] + layer_far[half].astype(f32)
            live = slots(half * 2 * PIECE + core * PIECE) < s[LENGTH]
            target[...] = jnp.where(live, value, 0.0).astype(bf16)
    if first:
        g = mm_tn(attn[...], dhb[...])
        for index, head in enumerate(HEAD_ORDER):
            out_grad[head * HEAD_FEATURES : (head + 1) * HEAD_FEATURES, :] = g[
                index * HEAD_FEATURES : (index + 1) * HEAD_FEATURES, :
            ]
        if rows % 16:
            keep_out[width:, :] = jnp.concatenate([out_grad[:, :heads], out_grad[:, heads:]], axis=0).astype(bf16)
        else:
            column = width // 4
            for target, place in ((keep_out, core), (send_out, 1 - core)):
                for z in range(n_seq // 4):
                    block = out_grad[pl.ds(pl.multiple_of((2 * z + place) * rows, 8), rows), :]
                    for b in range(4):
                        lanes = slice(b * column, (b + 1) * column)
                        to = (n_seq + 4 * z + b) * half_row
                        target[to : to + half_row, :] = jnp.concatenate(
                            [block[:half_row, lanes], block[half_row:, lanes]], axis=1
                        ).astype(bf16)
    if last:
        for p, side in enumerate(SIDES):
            for m in range(3):
                at = p * heads + m * PAIR
                joined[:, at : at + PAIR] = pair_of(weights[m], side)
        sums = jnp.zeros((1, width), f32)
        for half in range(2):
            for target, place in ((norm_send, 1 - core), (norm_keep, core)):
                where = piece_rows(half, place)
                part = mm_nt(before[where, :], joined[...])
                if target is norm_keep:
                    target[half] = part.astype(bf16)
                else:
                    for side in range(2):
                        at = (2 * half + side) * PIECE
                        target[at : at + PIECE, :] = part[:, side * heads : (side + 1) * heads].astype(bf16)
                sums = sums + jnp.sum(part * normed[where, :].astype(f32), axis=0, keepdims=True)
        sums = sums / gain[0:1, :].astype(f32)
        gain_rows[...] = jnp.zeros_like(gain_rows)
        for index, value in enumerate((sums, second_in[...])):
            for part in range(2):
                gain_rows[2 * index + part : 2 * index + part + 1, :] = value[:, part * heads : (part + 1) * heads]
        high = gain_rows[...].astype(bf16)
        low = (gain_rows[...] - high.astype(f32)).astype(bf16)
        gains[...] = jnp.concatenate([high, low], axis=0)
        if rows % 16 == 0:
            send_out[n_seq * half_row :, :] = gains[...]


def attend_back(pair, scalars, qkv, attn, lse, given, wo, weights, gains, normed, table, earlier, n_seq, sent=()):
    first, last = pair == 0, pair == len(SIDES) - 1
    heads = attn.shape[1]
    width = wo.shape[1]
    rows = width // n_seq
    token_shape = (2, PIECE, width)
    if rows % 16 == 0:
        count = n_seq * rows // 2 * (2 if first else 1)
        shapes = [(count, heads)] * 2
    else:
        shapes = [(2 * width if first else width, heads), (8, 128)]
    extra = shapes[1][0] + 16 if n_seq == 8 else 0
    outs = [sds(a, bf16) for a in shapes[: 1 if last and n_seq == 8 else 2]]
    hbm = pl.BlockSpec(memory_space=pl.ANY)
    given, later = list(given), []
    given_specs = [hbm] * len(given)
    if first:
        outs += [sds((MAXLEN, width), bf16), sds((1, width), f32), sds((MAXLEN, heads), bf16)]
        given_specs[4] = whole((2, width))
        given.append(wo)
        given_specs.append(hbm)
    if pair == 1:
        outs += [sds((PIECE, width), bf16)] * 2
    if last:
        outs += [sds(token_shape, bf16), sds((MAXLEN + extra, heads), bf16), sds((16, heads), bf16)]
        given += [*weights, gains]
        given_specs += [hbm] * 3 + [whole((2, width))]
    else:
        outs += [sds((MAXLEN, heads), bf16)]
    outs += [sds((2 * rows * (2 if pair == 1 else 1), heads), bf16)] * (4 if sent else 0)
    later = list(earlier[: len(SIDES) - 1]) + list(sent) + list(earlier[len(SIDES) - 1 :])
    args = [qkv, attn, lse, *given, normed, table, *later]
    in_specs = [hbm] * 3 + given_specs + [hbm] * (2 + len(later))
    if last:
        in_specs[-1] = whole((1, width))
    scratch = [
        pltpu.VMEM((MAXLEN, PAIR), bf16),
        pltpu.VMEM((MAXLEN, PAIR), bf16),
        pltpu.VMEM((MAXLEN, PAIR), bf16),
        pltpu.VMEM((MAXLEN, PAIR), bf16),
        pltpu.VMEM((8, MAXLEN), f32),
        pltpu.VMEM((MAXLEN, width), bf16),
        pltpu.VMEM((2, MAXLEN, PAIR), f32),
        pltpu.SemaphoreType.DMA((48,)),
        pltpu.VMEM((MAXLEN, PAIR), bf16),
        pltpu.VMEM((PAIR, MAXLEN), bf16),
        pltpu.VMEM((PAIR, MAXLEN), bf16),
        pltpu.VMEM((PAIR, MAXLEN), f32),
        pltpu.VMEM((PAIR, MAXLEN), f32),
        pltpu.VMEM((MAXLEN, PAIR), f32),
        pltpu.VMEM((width, heads), f32),
        pltpu.VMEM((MAXLEN, 8), f32),
    ]
    if first:
        scratch += [pltpu.VMEM((MAXLEN, width), bf16)] * 4
        scratch += [
            pltpu.VMEM((MAXLEN, heads), bf16),
            pltpu.VMEM((heads, width), f32),
            pltpu.VMEM((heads, width), bf16),
        ]
    if pair == 1:
        scratch += [pltpu.VMEM(token_shape, f32), pltpu.VMEM(token_shape, bf16)]
    if last:
        scratch += [
            pltpu.VMEM((MAXLEN, len(SIDES) * heads), bf16),
            pltpu.VMEM((width, len(SIDES) * heads), bf16),
            pltpu.VMEM((8, heads), f32),
            pltpu.VMEM((3, width, heads), bf16),
        ]
    if sent:
        scratch += [pltpu.VMEM(a.shape, bf16) for a in sent]
    return call(
        functools.partial(attend_back_body, pair, n_seq),
        (1,),
        in_specs,
        [whole(a.shape) for a in outs],
        outs,
        scratch=scratch,
    )(scalars, *args)


def feed_body(
    packed, s, x_hbm, dy_hbm, dy_pair_hbm, dy_far_hbm, dy_far_pair_hbm, attn_hbm, attn_pair_hbm, wo_hbm, gain, *refs
):
    refs = list(refs)
    take = lambda count: [refs.pop(0) for _ in range(count)]
    wg_hbm, wu_hbm, wd_hbm = take(3)
    hidden_out, dyb_out, dn_out, layer_out, send_out = take(5)
    grads_out = take(6 if packed else 3)
    x, attn, wo, wg, wu, wd, dyb = take(7)
    hidden, hidden_low, low, low_t, dyb_t, acts, dgs, dus, dn, layer, send = take(11)
    blocks = take(12)
    sems, late_sems = take(2)
    core = s[CORE]
    tokens, width = x.shape
    heads = width // 2
    steps = 4
    cols = wg.shape[1] // steps
    used = [0]

    def copy(source, target):
        made = pltpu.make_async_copy(source, target, sems.at[used[0]])
        used[0] += 1
        made.start()
        return made

    chunks = [slice(t * PIECE, (t + 1) * PIECE) for t in range(GROUP)]
    unit = [2 * ((3 - step) ^ s[OWN_B]) + core for step in range(steps)]

    wo_copies = [
        copy(
            wo_hbm.at[pl.ds(pl.multiple_of(place * heads + head * HEAD_FEATURES, HEAD_FEATURES), HEAD_FEATURES), :],
            wo.at[at * heads + index * HEAD_FEATURES : at * heads + (index + 1) * HEAD_FEATURES, :],
        )
        for at, place in enumerate((core, 1 - core))
        for index, head in enumerate(HEAD_ORDER)
    ]
    token_copies = [
        [
            copy(x_hbm.at[rows, :], x.at[rows, :]),
            copy(attn_hbm.at[rows, :], attn.at[rows, :heads]),
            copy(attn_pair_hbm.at[rows, :], attn.at[rows, heads:]),
        ]
        for rows in chunks
    ]
    def weights_of(step):
        at = pl.ds(pl.multiple_of(unit[step] * cols, cols), cols)
        here = slice(step * cols, (step + 1) * cols)
        return [
            copy(wg_hbm.at[:, at], wg.at[:, here]),
            copy(wu_hbm.at[:, at], wu.at[:, here]),
            copy(wd_hbm.at[at, :], wd.at[here, :]),
        ]

    dy_copies = [
        copy(source, dyb.at[piece_rows(half, place), :])
        for source, half, place in (
            (dy_hbm.at[s[CHIP]], s[CHIP], core),
            (dy_pair_hbm.at[s[CHIP]], s[CHIP], 1 - core),
            (dy_far_hbm.at[0], s[OTHER_CHIP], core),
            (dy_far_pair_hbm.at[0], s[OTHER_CHIP], 1 - core),
        )
    ]
    out_copies, side_copies = [], []

    for made in wo_copies:
        made.wait()
    scale = gain[1:2, :].astype(f32)
    weight_copies = [weights_of(0)]
    for t, rows in enumerate(chunks):
        for made in token_copies[t]:
            made.wait()
        h = x[rows, :].astype(f32) + mm(attn[rows, :], wo[...])
        hidden[rows, :] = h
        hidden_low[rows, :] = h.astype(bf16)
        out_copies.append(copy(hidden_low.at[rows, :], hidden_out.at[rows, :]))
        r = lax.rsqrt(jnp.mean(h * h, axis=-1, keepdims=True) + epsilon)
        low[rows, :] = (h * r * scale).astype(bf16)
    low_t[...] = jnp.transpose(low[...])
    for made in dy_copies:
        made.wait()
    for t, rows in enumerate(chunks):
        dyb[rows, :] = jnp.where(slots(t * PIECE) < s[LENGTH], dyb[rows, :], jnp.zeros((), bf16))
    dyb_t[...] = jnp.transpose(dyb[...])
    out_copies.append(copy(dyb, dyb_out))

    def products(step, t):
        if t == 0:
            for made in weight_copies.pop():
                made.wait()
            if step + 1 < steps:
                weight_copies.append(weights_of(step + 1))
        rows, here = chunks[t], slice(step * cols, (step + 1) * cols)
        return mm(low[rows, :], wg[:, here]), mm(low[rows, :], wu[:, here]), mm_nt(dyb[rows, :], wd[here, :])

    def pointwise(step, t, gate, up, dact):
        rows, here = chunks[t], slice(step * cols, (step + 1) * cols)
        sig = 1.0 / (1.0 + jnp.exp2(gate * -LOG2E))
        silu = gate * sig
        acts[rows, here] = (silu * up).astype(bf16)
        dgs[rows, here] = (dact * up * (sig + silu * (1.0 - sig))).astype(bf16)
        dus[rows, here] = (dact * silu).astype(bf16)

    def weight_grads(step, which):
        here = slice(step * cols, (step + 1) * cols)
        left, right = ((low_t, dgs), (low_t, dus), (dyb_t, acts))[which]
        grad = blocks[3 * step + which]
        grad[...] = mm(left[...], right[:, here]).astype(bf16)
        if not packed:
            at = pl.ds(pl.multiple_of(unit[step] // 2 * cols, cols), cols)
            out_copies.append(copy(grad, grads_out[which].at[:, at]))
            return
        rows = width // 4
        y, x = (3 - step) // 2, (3 - step) % 2
        own = s[OWN_B] if which == 2 else s[OWN_Z]
        z = (unit[step] // 2) ^ s[OWN_Z]
        for high in range(2):
            for low_bit in range(2):
                source = grad.at[pl.ds(pl.multiple_of(((2 * high + low_bit) ^ own) * rows, 16), rows), :]
                if which == 0:
                    out_copies.append(copy(source, grads_out[0 if x else 1].at[y, low_bit, high]))
                elif which == 1:
                    out_copies.append(copy(source, grads_out[2 if y else 3].at[low_bit, x, high]))
                else:
                    sem = sems.at[used[0]]
                    used[0] += 1
                    for side, target in ((1, grads_out[4]), (0, grads_out[5])):
                        made = pltpu.make_async_copy(source, target.at[low_bit, high, z // 2], sem)
                        pl.when(z % 2 == side)(made.start)
                        side_copies.append((z % 2 == side, made))

    units = [(step, t) for step in range(steps) for t in range(GROUP)]
    ahead = products(*units[0])
    for index, (step, t) in enumerate(units):
        now = ahead
        if index + 1 < len(units):
            ahead = products(*units[index + 1])
        pointwise(step, t, *now)
        if step and t < 3:
            weight_grads(step - 1, t)
    for which in range(3):
        weight_grads(steps - 1, which)
    def late_copies(t):
        rows = pl.ds(pl.multiple_of(t * PIECE, PIECE), PIECE)
        return pltpu.make_async_copy(dn.at[rows, :], dn_out.at[rows, :], late_sems.at[t])

    @pl.loop(0, 2)
    def _(half):
        send[half] = mm(acts[piece_rows(half, 1 - core), :], wd[...]).astype(bf16)
        rows = piece_rows(half, core)
        layer[half] = hidden[rows, :] + mm(acts[rows, :], wd[...])

    out_copies.append(copy(send, send_out))
    out_copies.append(copy(layer, layer_out))

    @pl.loop(0, GROUP)
    def _(t):
        rows = pl.ds(pl.multiple_of(t * PIECE, PIECE), PIECE)
        dn[rows, :] = (mm_nt(dgs[rows, :], wg[...]) + mm_nt(dus[rows, :], wu[...])).astype(bf16)
        late_copies(t).start()

    for t in range(GROUP):
        late_copies(t).wait()
    for made in out_copies:
        made.wait()
    for when, made in side_copies:
        pl.when(when)(made.wait)


def feed(scalars, x, dy, dy_pair, dy_far, dy_far_pair, attn, attn_pair, wo, gain, wg, wu, wd, packed):
    tokens, width = x.shape
    units = wg.shape[1] // 2
    cols = units // 4
    token_shape = (2, PIECE, width)
    if packed:
        shapes = [(2, 2, 2, width // 4, cols)] * 6
    else:
        shapes = [(width, units)] * 3
    outs = [
        sds((tokens, width), bf16),
        sds((tokens, width), bf16),
        sds((tokens, width), bf16),
        sds(token_shape, f32),
        sds(token_shape, bf16),
    ] + [sds(a, bf16) for a in shapes]
    args = [x, dy, dy_pair, dy_far, dy_far_pair, attn, attn_pair, wo, gain, wg, wu, wd]
    in_specs = [pl.BlockSpec(memory_space=pl.ANY)] * len(args)
    in_specs[8] = whole((2, width))
    low = pltpu.VMEM((tokens, width), bf16)
    high = pltpu.VMEM((tokens, width), f32)
    turned = pltpu.VMEM((width, tokens), bf16)
    hidden_units = pltpu.VMEM((tokens, units), bf16)
    return call(
        functools.partial(feed_body, packed),
        (1,),
        in_specs,
        [pl.BlockSpec(memory_space=pl.ANY)] * len(outs),
        outs,
        scratch=[
            low,
            low,
            pltpu.VMEM((width, width), bf16),
            pltpu.VMEM((width, units), bf16),
            pltpu.VMEM((width, units), bf16),
            pltpu.VMEM((units, width), bf16),
            low,
            high,
            low,
            low,
            turned,
            turned,
            hidden_units,
            hidden_units,
            hidden_units,
            low,
            pltpu.VMEM(token_shape, f32),
            pltpu.VMEM(token_shape, bf16),
        ]
        + [pltpu.VMEM((width, cols), bf16)] * 12
        + [pltpu.SemaphoreType.DMA((112,)), pltpu.SemaphoreType.DMA((GROUP,))],
    )(scalars, *args)


def piece_of(half, side):
    return pl.ds(pl.multiple_of((2 * half + side) * PIECE, PIECE), PIECE)


def finish_body(s, x, keep, recv, dh, gain, stay, leave):
    scale = gain[0:1, :].astype(f32)
    for out, half in ((leave, s[OTHER_CHIP]), (stay, s[CHIP])):
        h = x[half, 0].astype(f32)
        there = jnp.concatenate([recv[piece_of(half, side), :] for side in range(2)], axis=1)
        dn = keep[half].astype(f32) + there.astype(f32)
        r = lax.rsqrt(jnp.mean(h * h, axis=-1, keepdims=True) + epsilon)
        scaled = dn * scale
        inner = jnp.mean(scaled * h, axis=-1, keepdims=True)
        out[...] = (dh[half, 0].astype(f32) + r * scaled - h * (r * r * r) * inner).astype(bf16)


def finish(scalars, x, keep, recv, dh, gain):
    width = x.shape[1]
    shape = (2, PIECE, width)
    own = pl.BlockSpec((2, 1, PIECE, width), lambda f, s: (0, s[CORE], 0, 0))
    return call(
        finish_body,
        (1,),
        [own, whole(shape), whole((MAXLEN, recv.shape[1])), own, whole((2, width))],
        [whole((PIECE, width))] * 2,
        [sds((PIECE, width), bf16)] * 2,
    )(scalars, x.reshape(2, 2, PIECE, width), keep, recv, dh.reshape(2, 2, PIECE, width), gain)


def decode(coded):
    return coded[:8].astype(f32) + coded[8:].astype(f32)


def encode(value):
    high = value.astype(bf16)
    return jnp.concatenate([high, (value - high.astype(f32)).astype(bf16)], axis=0)


def sum_parts(fetch, groups, scratch):
    loads = []
    for group in groups:
        loads.append([])
        for source in group:
            target = scratch.pop(0)
            loads[-1].append((fetch(source, target), target))

    def total(group):
        value = None
        for made, target in group:
            made.wait()
            part = target[...].astype(f32)
            value = part if value is None else value + part
        return value

    return [functools.partial(total, group) for group in loads]


def fetcher(sems):
    used = [0]

    def fetch(source, target):
        made = pltpu.make_async_copy(source, target, sems.at[used[0]])
        used[0] += 1
        made.start()
        return made

    return fetch


def feed_step_body(paths, s, *refs):
    refs = list(refs)
    groups = [[refs.pop(0).at[path] for path in group] for group in paths]
    outs = [refs.pop(0) for _ in groups]
    sems = refs.pop()
    for out, total in zip(outs, sum_parts(fetcher(sems), groups, refs)):
        out[...] = total().astype(bf16)


def feed_step(scalars, reductions):
    groups = [r.paths(1) for r in reductions]
    args = [array for group in groups for array, _ in group]
    paths = [[path for _, path in group] for group in groups]
    slices = [array.shape[len(path) :] for group in groups for array, path in group]
    outs = [sds(group[0][0].shape[len(group[0][1]) :], bf16) for group in groups]
    return call(
        functools.partial(feed_step_body, paths),
        (1,),
        [pl.BlockSpec(memory_space=pl.ANY)] * len(args),
        [whole(a.shape) for a in outs],
        outs,
        scratch=[pltpu.VMEM(a, bf16) for a in slices] + [pltpu.SemaphoreType.DMA((len(args),))],
    )(scalars, *args)


def third_step_body(paths, s, keep_hbm, arrived_hbm, gains, *refs):
    refs = list(refs)
    groups = [[refs.pop(0).at[path] for path in group] for group in paths]
    parts_hbm = [refs.pop(0) for _ in range(4)]
    plane = [refs.pop(0) for _ in range(4)]
    line_send, line_keep = refs.pop(0), refs.pop(0)
    sends, kept = refs.pop(0), refs.pop(0)
    keep, arrived = refs.pop(0), refs.pop(0)
    parts = [refs.pop(0) for _ in range(4)]
    sems = refs.pop()
    fetch = fetcher(sems)
    rows = keep.shape[0] // 8
    first = [
        fetch(keep_hbm, keep),
        fetch(arrived_hbm.at[pl.ds(MAXLEN, arrived.shape[0]), :], arrived),
    ]
    second = [fetch(source, target) for source, target in zip(parts_hbm, parts)]
    totals = sum_parts(fetch, groups, refs)
    for made in first:
        made.wait()
    plane_blocks(s, keep, arrived, plane, rows, False)
    coded = encode(decode(gains[...]) + decode(arrived[8 * rows :, :]))
    for target in plane:
        target[4 * rows :, :] = coded
    for made in second:
        made.wait()
    size = line_keep.shape[0] // 2
    own = s[OWN_Z] % 2
    for target, z0 in ((line_send, 1 - own), (line_keep, own)):
        for z1 in range(2):
            at = pl.ds(pl.multiple_of((2 * z1 + z0) * size, 16), size)
            total = None
            for part in parts:
                value = part[at, :].astype(f32)
                total = value if total is None else total + value
            target[z1 * size : (z1 + 1) * size, :] = total.astype(bf16)
    for index in range(3):
        sends[index] = totals[index]().astype(bf16)
        kept[index] = totals[3 + index]()


def third_step(scalars, keep, arrived, gains, parts, reductions):
    groups = [r.paths(1) for r in reductions] + [r.paths(0) for r in reductions]
    sums = [array for group in groups for array, _ in group]
    paths = [[path for _, path in group] for group in groups]
    slices = [array.shape[len(path) :] for group in groups for array, path in group]
    rows, columns = keep.shape
    outs = [sds((rows // 2 + 16, columns), bf16)] * 4
    outs += [sds((parts[0].shape[0] // 2, columns), bf16)] * 2
    outs += [sds((3,) + slices[0], bf16), sds((3,) + slices[0], f32)]
    hbm = pl.BlockSpec(memory_space=pl.ANY)
    return call(
        functools.partial(third_step_body, paths),
        (1,),
        [hbm, hbm, whole(gains.shape)] + [hbm] * (len(sums) + 4),
        [whole(a.shape) for a in outs],
        outs,
        scratch=[pltpu.VMEM(keep.shape, bf16), pltpu.VMEM((rows + 16, columns), bf16)]
        + [pltpu.VMEM(a.shape, bf16) for a in parts]
        + [pltpu.VMEM(a, bf16) for a in slices]
        + [pltpu.SemaphoreType.DMA((len(sums) + 6,))],
    )(scalars, keep, arrived, gains, *sums, *parts)


def second_line_body(s, *refs):
    refs = list(refs)
    take = lambda count: [refs.pop(0) for _ in range(count)]
    middle_hbm, last_hbm, line_hbm = take(4), take(4), take(2)
    layer_stay_hbm, layer_back_hbm = take(2)
    lines, (last_keep,) = take(4), take(1)
    (layer_out,) = take(1)
    middle, last, (keep0, arrived0) = take(4), take(4), take(2)
    (sems,) = take(1)
    fetch = fetcher(sems)
    first = [fetch(a, b) for a, b in zip(middle_hbm + last_hbm + line_hbm, middle + last + [keep0, arrived0])]
    third = [
        fetch(layer_stay_hbm, layer_out.at[s[CHIP]]),
        fetch(layer_back_hbm, layer_out.at[s[OTHER_CHIP]]),
    ]
    for made in first:
        made.wait()
    rows = middle[0].shape[0] // 4
    coded = [ref[4 * rows :, :] for ref in last]
    gains = encode((decode(coded[0]) + decode(coded[1])) + (decode(coded[2]) + decode(coded[3])))
    for r, target in enumerate(lines):
        at = pl.ds(pl.multiple_of((s[OWN_Z] ^ r) * rows, 16), rows)
        for index, parts in enumerate((middle, last)):
            total = None
            for part in parts:
                value = part[at, :].astype(f32)
                total = value if total is None else total + value
            target[index * rows : (index + 1) * rows, :] = total.astype(bf16)
        target[2 * rows : 2 * rows + 16, :] = gains
    size = keep0.shape[0] // 2
    own = s[OWN_Z] // 2
    for target, z1 in ((last_keep, own), (lines[2].at[2 * rows + 16 :, :], 1 - own)):
        at = pl.ds(pl.multiple_of(z1 * size, 16), size)
        target[...] = (keep0[at, :].astype(f32) + arrived0[at, :].astype(f32)).astype(bf16)
    for made in third:
        made.wait()


def second_line(scalars, middle, last, keep0, arrived0, layer_stay, layer_back):
    rows, columns = middle[0].shape[0] // 4, middle[0].shape[1]
    size = keep0.shape[0] // 2
    outs = [sds((2 * rows + 16 + (size if r == 2 else 0), columns), bf16) for r in range(4)]
    outs += [sds((size, columns), bf16)]
    outs += [sds((2,) + layer_stay.shape, bf16)]
    args = [*middle, *last, keep0, arrived0, layer_stay, layer_back]
    return call(
        second_line_body,
        (1,),
        [pl.BlockSpec(memory_space=pl.ANY)] * len(args),
        [whole(a.shape) for a in outs],
        outs,
        scratch=[pltpu.VMEM(a.shape, a.dtype) for a in args[:-2]] + [pltpu.SemaphoreType.DMA((len(args),))],
    )(scalars, *args)


def feed_total_body(s, feed_keep, feed_arrived, side_keep, side_send, down_out):
    rows = side_keep.shape[1]
    for index in range(2):
        value = feed_keep[index] + feed_arrived[index].astype(f32)
        for part in range(2):
            block = value[part * rows : (part + 1) * rows]

            @pl.when(s[CORE] == part)
            def _():
                side_keep[index] = block

            @pl.when(s[CORE] != part)
            def _():
                side_send[index] = block.astype(bf16)

    down_out[...] = feed_keep[2] + feed_arrived[2].astype(f32)

def feed_total(scalars, keep, arrived):
    rows, cols = keep.shape[1:]
    outs = [sds((2, rows // 2, cols), f32), sds((2, rows // 2, cols), bf16), sds((rows, cols), f32)]
    args = [keep, arrived]
    return call(
        feed_total_body,
        (1,),
        [whole(a.shape) for a in args],
        [whole(a.shape) for a in outs],
        outs,
    )(scalars, *args)


def shards_body(s, keep0, line0, line1, line2, line3, side_keep, side_arrived, stay, back, *outs):
    half, width = outs[0].shape[0] // 2, outs[0].shape[1]
    count = line0.shape[0]
    first = keep0[...].astype(f32) + line2[count:, :].astype(f32)
    rest = (line0[...].astype(f32) + line1[...].astype(f32)) + (
        line2[:count, :].astype(f32) + line3[...].astype(f32)
    )
    out = first[half:]
    outs[3][:half, :] = out[:, :width]
    outs[3][half:, :] = out[:, width:]
    for pair, part in enumerate((first[:half], rest[:half], rest[half : 2 * half])):
        lanes = slice(pair * HEAD_FEATURES, (pair + 1) * HEAD_FEATURES)
        for m in range(3):
            at = m * PAIR
            outs[m][:half, lanes] = part[:, at : at + HEAD_FEATURES]
            outs[m][half:, lanes] = part[:, at + HEAD_FEATURES : at + PAIR]
    gains = rest[2 * half : 2 * half + 8] + rest[2 * half + 8 :]
    for index in range(2):
        row = jnp.concatenate([gains[2 * index : 2 * index + 1], gains[2 * index + 1 : 2 * index + 2]], axis=1)
        for at in range(outs[6].shape[0]):
            outs[6 + index][at : at + 1, :] = row[:, at * PAIR : (at + 1) * PAIR]
    cols = side_keep.shape[2]
    for index in range(2):
        for core in range(2):

            @pl.when(s[CORE] == core)
            def _():
                outs[4 + index][:, core * cols : (core + 1) * cols] = side_keep[index]
                outs[4 + index][:, (1 - core) * cols : (2 - core) * cols] = side_arrived[index].astype(f32)

    outs[8][s[CHIP]] = stay[...]
    outs[8][s[OTHER_CHIP]] = back[...]


def make_shards(scalars, args, rows, columns, width):
    side = sds((rows, 2 * args[5].shape[-1]), f32)
    outs = [sds((rows, columns), f32)] * 4 + [side] * 2 + [sds((width // PAIR, PAIR), f32)] * 2
    outs.append(sds((2,) + args[-1].shape, bf16))
    return call(
        shards_body,
        (1,),
        [whole(a.shape) for a in args],
        [whole(a.shape) for a in outs],
        outs,
    )(scalars, *args)


def exchange_by(block, axis, difference, name):
    count = lax.axis_size(axis)
    with jax.named_scope(name):
        return lax.ppermute(block, axis, [(a, a ^ difference) for a in range(count)])


def exchange(block, axis, bit, name="swap"):
    return exchange_by(block, axis, 1 << bit, name)


def pick(block, index, dim):
    return lax.dynamic_index_in_dim(block, index, dim, keepdims=False)


def together(*values):
    return lax.optimization_barrier(values)


X, Y, Z0, Z1 = ("batch", 0), ("batch", 1), ("seq", 1), ("seq", 2)


class Reduction:
    def __init__(self, order, keep, send):
        self.order, self.level, self.send, self.parts = order, 0, send, [keep]

    def go(self):
        bit = self.order[self.level]
        self.arrived = exchange(self.send, *bit, "feed_" + "_".join(map(str, bit)))
        return self

    def paths(self, side):
        found = []
        for index, array in enumerate([*self.parts, self.arrived]):
            found.append((array, (0,) * (self.level - max(index - 1, 0)) + (side,)))
        return found

    def next(self, send):
        self.parts.append(self.arrived)
        self.send = send
        self.level += 1
        return self


def start_all(reductions, *others):
    sends = together(*[r.send for r in reductions], *others)
    for r, send in zip(reductions, sends):
        r.send = send
        r.go()
    return sends[len(reductions) :]


def wait_all(reductions, *others):
    values = together(*[r.arrived for r in reductions], *others)
    for r, arrived in zip(reductions, values):
        r.arrived = arrived
    return values[len(reductions) :]


def body(
    states,
    lengths,
    first_gain,
    query_weight,
    key_weight,
    value_weight,
    output_weight,
    second_gain,
    gate_weight,
    up_weight,
    down_weight,
    cotangent,
):
    tokens, width = states.shape
    n_seq, n_batch = lax.axis_size("seq"), lax.axis_size("batch")
    packed = n_seq == 8 and n_batch == 4
    place = lax.axis_index("seq")
    batch = lax.axis_index("batch")
    core = place & 1
    chip = place >> 1 & 1
    sequence = (batch * (n_seq // GROUP) + place // GROUP) * 2 + chip
    length = pick(lengths, sequence, 0)
    own_b, own_z = batch & 3, place >> 1 & 3
    scalars = jnp.stack([core, chip, length, 1 - chip, own_b, own_z]).astype(jnp.int32)
    table = rope_tables()
    both_gains = jnp.stack([first_gain, second_gain])
    weights = (query_weight, key_weight, value_weight)

    held = states.reshape(2, PIECE, width)
    held_back = cotangent.reshape(2, PIECE, width)
    far = exchange(pick(held, 1 - chip, 0), *Z0, "states_far")[None]
    held_pair = exchange(held, "seq", 0, "states_pair")
    filled = project(scalars, held, held_pair, CHIP, both_gains, weights, table, None)
    far, leaving, *filled = together(far, pick(held_back, 1 - chip, 0), *filled)
    far_pair = exchange(far, "seq", 0, "states_far_pair")
    back_far = exchange(leaving, *Z0, "cotangent_far")[None]
    back_pair = exchange(held_back, "seq", 0, "cotangent_pair")
    qkv, normed, x, attn, lse = attend(scalars, far, far_pair, both_gains, weights, table, filled)
    attn_pair = exchange(attn, "seq", 0, "attn_pair")
    back_far, attn = together(back_far, attn)
    back_far_pair = exchange(back_far, "seq", 0, "cotangent_far_pair")
    hidden, dyb, dn, layer_keep, layer_send, *feed_grads = feed(
        scalars,
        x,
        held_back,
        back_pair,
        back_far,
        back_far_pair,
        attn,
        attn_pair,
        output_weight,
        both_gains,
        gate_weight,
        up_weight,
        down_weight,
        packed,
    )
    if packed:
        gate_send, gate_keep, up_send, up_keep, down_send, down_keep = feed_grads
        gate = Reduction([X, Y, Z0, Z1], gate_keep, gate_send).go()
        up = Reduction([Y, Z0, X, Z1], up_keep, up_send).go()
        down = Reduction([Z0, X, Y, Z1], down_keep, down_send).go()
    dn_pair = exchange(dn, "seq", 0, "dn_pair")

    def back(pair, given, later, sent=()):
        return attend_back(
            pair, scalars, qkv, attn, lse, given, output_weight, weights, both_gains, normed, table, later, n_seq, sent
        )

    keep0, send0, dhb, second, da, d0 = back(0, [hidden, dyb, dn, dn_pair, both_gains], [])

    def in_order(kept, arrived):
        return jnp.concatenate(
            [jnp.where(chip == 0, kept, arrived), jnp.where(chip == 0, arrived, kept)], axis=0
        )

    if packed:
        rows = width // n_seq // 2

        def to_plane(parts, name):
            return [parts[0]] + [exchange_by(parts[r], "batch", r, name + str(r)) for r in (1, 2, 3)]

        feeds = [gate, up, down]
        keep0, send0, dhb, second, da, d0, layer_send = wait_all(feeds, keep0, send0, dhb, second, da, d0, layer_send)
        layer_arrived = exchange(layer_send, "seq", 0, "layer_pair")
        arrived0 = exchange(send0, "seq", 0, "grad0_pair")
        for r, send in zip(feeds, feed_step(scalars, feeds)):
            r.next(send)
        (da,) = start_all(feeds, da)
        keep1, send1, layer_stay, layer_leave, d1, *plane0 = back(
            1, [da, layer_keep, layer_arrived], [], (keep0, arrived0)
        )

        keep1, send1, layer_stay, layer_leave, d1, *plane0 = wait_all(
            feeds, keep1, send1, layer_stay, layer_leave, d1, *plane0
        )
        arrived1 = exchange(send1, "seq", 0, "grad1_pair")
        flow0 = to_plane(plane0, "plane0_")
        for r, send in zip(feeds, feed_step(scalars, feeds)):
            r.next(send)
        (arrived1, d1) = start_all(feeds, arrived1, d1)
        keep2, norm_keep, norm_send, gains, *plane1 = back(2, [da], [d0, d1, second], (keep1, arrived1))

        flow0[1], flow0[2], flow0[3], keep2, norm_keep, norm_send, gains, layer_leave, *plane1 = wait_all(
            feeds, *flow0[1:], keep2, norm_keep, norm_send, gains, layer_leave, *plane1
        )
        norm_arrived = exchange(norm_send, "seq", 0, "dn1_pair")
        layer_back = exchange(layer_leave, *Z0, "layer_back")
        flow1 = to_plane(plane1, "plane1_")
        *plane2, line0_send, line0_keep, feed_send, feed_keep = third_step(
            scalars, keep2, norm_arrived, gains, flow0, feeds
        )
        line0_send, line0_keep, feed_send, feed_keep, layer_back, *planes = together(
            line0_send, line0_keep, feed_send, feed_keep, layer_back, *plane2, *flow1
        )
        plane2, flow1 = planes[:4], planes[4:]
        flow2 = to_plane(plane2, "plane2_")
        feed_arrived = exchange(feed_send, *Z1, "feed_last")
        arrived0 = exchange(line0_send, *Z0, "line0")
        norm_keep, line0_keep = together(norm_keep, line0_keep)
        stay, leave = finish(scalars, x, norm_keep, norm_arrived, dhb, both_gains)
        leave, stay, arrived0, *flow2 = together(leave, stay, arrived0, *flow2)
        grad_back = exchange(leave, *Z0, "grad_back")
        stay, layer_back, line0_keep, arrived0, *flow12 = together(stay, layer_back, line0_keep, arrived0, *flow1, *flow2)
        *lines, last_keep, layer_out = second_line(
            scalars, flow12[:4], flow12[4:], line0_keep, arrived0, layer_stay, layer_back
        )
        last_keep, feed_arrived, feed_keep = together(last_keep, feed_arrived, feed_keep)
        side_keep, side_send, down_grad = feed_total(scalars, feed_keep, feed_arrived)
        lines = [lines[0]] + [exchange_by(lines[r], "seq", 2 * r, "line12_" + str(r)) for r in (1, 2, 3)]
        side_arrived = exchange(side_send, "seq", 0, "feed_pair")
        down_grad, layer_out = jnp.transpose(down_grad), layer_out.reshape(tokens, width)
        *shards, gate_grad, up_grad, first, second, input_grad = make_shards(
            scalars,
            [last_keep, *lines, side_keep, side_arrived, stay, grad_back],
            2 * rows,
            width // n_batch,
            width,
        )
        first, second, input_grad = first.reshape(width), second.reshape(width), input_grad.reshape(tokens, width)
    else:
        layer_arrived = exchange(layer_send, "seq", 0)
        keep1, _, layer_stay, layer_leave, d1 = back(1, [da, layer_keep, layer_arrived], [])
        layer_back = exchange(layer_leave, *Z0)
        keep2, _, norm_keep, norm_send, gains = back(2, [da], [d0, d1, second])
        norm_arrived = exchange(norm_send, "seq", 0)
        stay, leave = finish(scalars, x, norm_keep, norm_arrived, dhb, both_gains)
        layer_out = in_order(layer_stay, layer_back)
        input_grad = in_order(stay, exchange(leave, *Z0))
        gains = gains[:8].astype(f32) + gains[8:].astype(f32)
        for axis in ("seq", "batch"):
            for bit in range(int(math.log2(lax.axis_size(axis)))):
                gains = gains + exchange(gains, axis, bit)
        first, second = gains[:2].reshape(width), gains[2:4].reshape(width)
        gate_keep, up_keep, down_keep = feed_grads
        units = gate_keep.shape[1]
        zeros = lambda shape: jnp.zeros(shape, bf16)
        blocks = 4

        def spread(array):
            parts = array.reshape(width, blocks, 1, units // blocks)
            full = zeros((width, blocks, 2, units // blocks))
            return lax.dynamic_update_slice_in_dim(full, parts, core, 2).reshape(width, 2 * units)

        heads = attn.shape[1]
        out_keep = jnp.concatenate([keep0[width : width + heads], keep0[width + heads :]], axis=1)
        columns = lambda a: lax.dynamic_update_slice_in_dim(zeros((width, width)), a, core * heads, 1)

        def by_head(m):
            found = {}
            for index, head in enumerate(HEAD_ORDER):
                at = m * PAIR + index % 2 * HEAD_FEATURES
                found[head] = (keep0, keep1, keep2)[index // 2][:width, at : at + HEAD_FEATURES]
            return jnp.concatenate([found[head] for head in sorted(found)], axis=1)

        full = [columns(by_head(m)) for m in range(3)]
        full.append(lax.dynamic_update_slice_in_dim(zeros((width, width)), out_keep, core * heads, 0))
        full += [spread(gate_keep), spread(up_keep), jnp.transpose(spread(down_keep))]
        full = [lax.psum_scatter(a.astype(f32), "seq", scatter_dimension=0, tiled=True) for a in full]
        full = [lax.psum_scatter(a, "batch", scatter_dimension=1, tiled=True) for a in full]
        shards, (gate_grad, up_grad, down_grad) = full[:4], full[4:]

    return (
        layer_out,
        input_grad,
        first,
        shards[0],
        shards[1],
        shards[2],
        shards[3],
        second,
        gate_grad,
        up_grad,
        down_grad,
    )


def solution(mesh):
    split = P(("batch", "seq"), None)
    in_specs = (split,) + (P(),) * 10 + (split,)
    shard = P("seq", "batch")
    out_specs = (split, split, P(), shard, shard, shard, shard, P(), shard, shard, shard)
    return jax.shard_map(body, mesh=mesh, in_specs=in_specs, out_specs=out_specs, check_vma=False)
```

```python
import functools
import math

import jax
import jax.numpy as jnp
import numpy as np
from jax import lax
from jax.experimental import pallas as pl
from jax.experimental.pallas import tpu as pltpu
from jax.sharding import PartitionSpec as P

HEADS = 12
HEAD_FEATURES = 64
MAXLEN = 1024
GROUP = 4
PIECE = MAXLEN // GROUP
PAIR = 2 * HEAD_FEATURES
LOG2E = math.log2(math.e)

epsilon = 1e-06
masked_score = -1e30
f32 = jnp.float32
bf16 = jnp.bfloat16
MIB = 1024 * 1024

SIDES = ((0, 1), (2, 0), (1, 2))
HEAD_ORDER = tuple(h for left, right in SIDES for h in (2 * left, 2 * right + 1))

CORE, CHIP, LENGTH, OTHER_CHIP, OWN_B, OWN_Z = range(6)


def mm(a, b):
    return lax.dot_general(a, b, (((1,), (0,)), ((), ())), preferred_element_type=f32)


def mm_nt(a, b):
    return lax.dot_general(a, b, (((1,), (1,)), ((), ())), preferred_element_type=f32)


def mm_tn(a, b):
    return lax.dot_general(a, b, (((0,), (0,)), ((), ())), preferred_element_type=f32)


def call(body, grid, in_specs, out_specs, out_shape, scratch=(), aliases=None, vmem=64):
    return pl.pallas_call(
        body,
        grid_spec=pltpu.PrefetchScalarGridSpec(
            num_scalar_prefetch=1,
            grid=grid,
            in_specs=in_specs,
            out_specs=out_specs,
            scratch_shapes=list(scratch),
        ),
        out_shape=out_shape,
        input_output_aliases=aliases or {},
        compiler_params=pltpu.CompilerParams(
            dimension_semantics=("arbitrary",) * len(grid), vmem_limit_bytes=vmem * MIB
        ),
        cost_estimate=pl.CostEstimate(flops=1000, bytes_accessed=1000, transcendentals=0),
    )


def whole(shape):
    return pl.BlockSpec(shape, lambda *a: (0,) * len(shape))


def sds(shape, dtype):
    return jax.ShapeDtypeStruct(shape, dtype)


def rope_tables():
    middle = HEAD_FEATURES // 2
    frequency = 10000.0 ** (-np.arange(middle, dtype=np.float64) * 2.0 / HEAD_FEATURES)
    angles = np.arange(MAXLEN, dtype=np.float64)[:, None] * frequency[None, :]
    cosine, sine = np.cos(angles), np.sin(angles)
    half = lax.optimization_barrier(jnp.asarray(np.stack([cosine, sine]).astype(np.float32)))
    return jnp.stack([jnp.tile(half[0], (1, 4)), jnp.concatenate([-half[1], half[1]] * 2, axis=1)])


def rotate(u, table, sign):
    up = pltpu.roll(u, PAIR - HEAD_FEATURES // 2, 1)
    down = pltpu.roll(u, HEAD_FEATURES // 2, 1)
    lane = lax.broadcasted_iota(jnp.int32, (1, PAIR), 1)
    turned = jnp.where(lane % HEAD_FEATURES < HEAD_FEATURES // 2, up, down) * table[1]
    return u * table[0] + turned if sign > 0 else u * table[0] - turned


def pair_of(value, side):
    left, right = (value[:, a * PAIR : (a + 1) * PAIR] for a in side)
    lane = lax.broadcasted_iota(jnp.int32, (1, PAIR), 1)
    return jnp.where(lane < HEAD_FEATURES, left, right)


def slots(start):
    return start + lax.broadcasted_iota(jnp.int32, (PIECE, 1), 0)


def piece_rows(half, place):
    return pl.ds(pl.multiple_of(half * 2 * PIECE + place * PIECE, PIECE), PIECE)


def project_body(s, own, part, gain, wq, wk, wv, table, *rest):
    qkv, normed, copy = rest[-3:]
    low_x = jnp.where(pl.program_id(0) == s[CORE], own[0], part[0])
    copy[...] = low_x
    x = low_x.astype(f32)
    r = lax.rsqrt(jnp.mean(x * x, axis=-1, keepdims=True) + epsilon)
    low = (x * r * gain[0:1, :].astype(f32)).astype(bf16)
    normed[...] = low
    width = wq.shape[1]
    for m, w in enumerate((wq, wk, wv)):
        u = mm(low, w[...])
        if m == 0:
            u = u * (1.0 / math.sqrt(HEAD_FEATURES))
        for p in range(width // PAIR):
            v = pair_of(u, SIDES[p])
            if m < 2:
                v = rotate(v, table, 1)
            at = m * width + p * PAIR
            qkv[:, at : at + PAIR] = v.astype(bf16)


def project(scalars, own, part, half, gain, weights, table, filled):
    width = weights[0].shape[0]
    cols = width // 2
    place = lambda t, s: (s[half] * 2 + t, 0)
    source = lambda a: pl.BlockSpec((1, PIECE, width), lambda t, s: (s[CHIP] if a.shape[0] > 1 else 0, 0, 0))
    weight_spec = pl.BlockSpec((width, cols), lambda t, s: (0, s[CORE]))
    in_specs = [
        source(own),
        source(part),
        whole((2, width)),
        weight_spec,
        weight_spec,
        weight_spec,
        pl.BlockSpec((2, PIECE, PAIR), lambda t, s: (0, s[half] * 2 + t, 0)),
    ]
    args = [scalars, own, part, gain, *weights, table]
    aliases = None
    if filled is not None:
        in_specs += [pl.BlockSpec(memory_space=pl.ANY)] * 3
        aliases = {len(args) + a: a for a in range(3)}
        args += list(filled)
    return call(
        project_body,
        (2,),
        in_specs,
        [pl.BlockSpec((PIECE, 3 * cols), place), pl.BlockSpec((PIECE, width), place), pl.BlockSpec((PIECE, width), place)],
        [sds((MAXLEN, 3 * cols), bf16), sds((MAXLEN, width), bf16), sds((MAXLEN, width), bf16)],
        aliases=aliases,
    )(*args)


def head_mask(h):
    lane = lax.broadcasted_iota(jnp.int32, (1, PAIR), 1)
    return lane < HEAD_FEATURES if h == 0 else lane >= HEAD_FEATURES


def attend_pair(s, q, k, v, out, lse):
    row = lax.broadcasted_iota(jnp.int32, (PIECE, PIECE), 0)
    col = lax.broadcasted_iota(jnp.int32, (PIECE, PIECE), 1)
    lane = lax.broadcasted_iota(jnp.int32, (PIECE, PAIR), 1)
    ones = jnp.ones((MAXLEN, PAIR), bf16)

    def score(b, h):
        at = b * PIECE
        qh = jnp.where(head_mask(h), q[at : at + PIECE, :], jnp.zeros((), bf16))
        near = mm_nt(qh, k[at : at + PIECE, :])
        return near, mm_nt(qh, k[:at, :]) if b else None

    def mix(b, near, far):
        at = b * PIECE
        near = jnp.where(row >= col, near, masked_score)
        top = jnp.max(near, axis=-1, keepdims=True)
        if b:
            top = jnp.maximum(top, jnp.max(far, axis=-1, keepdims=True))
        shift = top * LOG2E
        near = jnp.exp2(near * LOG2E - shift).astype(bf16)
        mixed = mm(near, jnp.concatenate([v[at : at + PIECE, :], ones[:PIECE]], axis=1))
        if b:
            far = jnp.exp2(far * LOG2E - shift).astype(bf16)
            mixed = mixed + mm(far, jnp.concatenate([v[:at, :], ones[:at]], axis=1))
        total = mixed[:, PAIR:]
        return mixed[:, :PAIR] * (1.0 / total), top + jnp.log(total)

    units = [(b, h) for b in range(GROUP) for h in range(2)]
    ahead = score(*units[0])
    done = []
    for at, (b, h) in enumerate(units):
        now = ahead
        if at + 1 < len(units):
            ahead = score(*units[at + 1])
        done.append(mix(b, *now))
        if h == 1:
            rows = slice(b * PIECE, (b + 1) * PIECE)
            (left, left_log), (right, right_log) = done
            done = []
            joined = jnp.where(head_mask(0), left, right)
            out[rows, :] = jnp.where(slots(b * PIECE) < s[LENGTH], joined, 0.0).astype(bf16)
            lse[:, rows] = jnp.transpose(jnp.where(lane == 0, left_log, right_log))[:8]


def attend_body(s, far_hbm, far_pair_hbm, gain, *refs):
    weights_hbm, table_hbm, qkv_in = refs[:3], refs[3], refs[4]
    qkv_out, normed_out, x_out, out, lse = refs[7:12]
    qkv, pieces, lows, weights, table, sems = refs[12:]
    core, half = s[CORE], s[OTHER_CHIP]
    width = weights.shape[1]
    cols = weights.shape[2]
    fetch = fetcher(sems)
    rows_of = lambda side: pl.ds(pl.multiple_of(side * 2 * PIECE, 2 * PIECE), 2 * PIECE)
    first = [fetch(far_hbm.at[0], pieces.at[core]), fetch(far_pair_hbm.at[0], pieces.at[1 - core])]
    for m, w in enumerate(weights_hbm):
        first.append(fetch(w.at[:, pl.ds(pl.multiple_of(core * cols, PAIR), cols)], weights.at[m]))
    first.append(fetch(table_hbm.at[:, rows_of(half), :], table))
    second = fetch(qkv_in.at[rows_of(s[CHIP]), :], qkv.at[rows_of(s[CHIP]), :])
    for made in first:
        made.wait()
    for t in range(2):
        x = pieces[t].astype(f32)
        r = lax.rsqrt(jnp.mean(x * x, axis=-1, keepdims=True) + epsilon)
        low = (x * r * gain[0:1, :].astype(f32)).astype(bf16)
        lows[t] = low
        rows = piece_rows(half, t)
        turn = [table[a, t * PIECE : (t + 1) * PIECE, :] for a in range(2)]
        for m in range(3):
            u = mm(low, weights[m])
            if m == 0:
                u = u * (1.0 / math.sqrt(HEAD_FEATURES))
            for p, side in enumerate(SIDES):
                v = pair_of(u, side)
                if m < 2:
                    v = rotate(v, turn, 1)
                at = m * cols + p * PAIR
                qkv[rows, at : at + PAIR] = v.astype(bf16)
    made = [fetch(qkv.at[rows_of(half), :], qkv_out.at[rows_of(half), :])]
    for t in range(2):
        made.append(fetch(lows.at[t], normed_out.at[piece_rows(half, t), :]))
        made.append(fetch(pieces.at[t], x_out.at[piece_rows(half, t), :]))
    second.wait()
    for p in range(len(SIDES)):
        q, k, v = (qkv.at[:, m * cols + p * PAIR : m * cols + (p + 1) * PAIR] for m in range(3))
        attend_pair(s, q, k, v, out.at[:, p * PAIR : (p + 1) * PAIR], lse.at[p])
    for copy in made:
        copy.wait()


def attend(scalars, far, far_pair, gain, weights, table, filled):
    width = weights[0].shape[0]
    cols = width // 2
    hbm = pl.BlockSpec(memory_space=pl.ANY)
    args = [far, far_pair, gain, *weights, table, *filled]
    outs = [sds(a.shape, a.dtype) for a in filled]
    outs += [sds((MAXLEN, cols), bf16), sds((len(SIDES), 8, MAXLEN), f32)]
    return call(
        attend_body,
        (1,),
        [hbm, hbm, whole(gain.shape)] + [hbm] * 7,
        [hbm] * 3 + [whole(a.shape) for a in outs[3:]],
        outs,
        scratch=[
            pltpu.VMEM((MAXLEN, 3 * cols), bf16),
            pltpu.VMEM((2, PIECE, width), bf16),
            pltpu.VMEM((2, PIECE, width), bf16),
            pltpu.VMEM((3, width, cols), bf16),
            pltpu.VMEM((2, 2 * PIECE, PAIR), f32),
            pltpu.SemaphoreType.DMA((16,)),
        ],
        aliases={8: 0, 9: 1, 10: 2},
    )(scalars, *args)


def pack_rows(block):
    half = block.shape[0] // 2
    lane = lax.broadcasted_iota(jnp.int32, (1, PAIR), 1)
    top, bottom = block[:half], block[half:]
    left = jnp.where(lane < HEAD_FEATURES, top, pltpu.roll(bottom, HEAD_FEATURES, 1))
    right = jnp.where(lane < HEAD_FEATURES, pltpu.roll(top, HEAD_FEATURES, 1), bottom)
    return left, right


def plane_blocks(s, keep, arrived, targets, rows, with_out):
    size = 2 * rows if with_out else rows
    core = s[CORE]
    for r, target in enumerate(targets):
        place = s[OWN_B] ^ r
        for z in range(4):
            at = pl.ds(pl.multiple_of((2 * z + place % 2) * rows, 16), rows)
            target[z * size : z * size + rows, :] = jnp.where(place // 2 == core, keep[at, :], arrived[at, :])
            if with_out:
                at = pl.ds(pl.multiple_of((8 + z % 2 * 4 + place) * rows, 16), rows)
                target[z * size + rows : (z + 1) * size, :] = jnp.where(z // 2 == core, keep[at, :], arrived[at, :])


def attend_back_body(pair, n_seq, s, *refs):
    first, last = pair == 0, pair == len(SIDES) - 1
    refs = list(refs)
    take = lambda count: [refs.pop(0) for _ in range(count)]
    qkv_hbm, attn_hbm, lse_hbm = take(3)
    if first:
        hidden_hbm, dyb_hbm, mine_hbm, theirs_hbm, gain = take(5)
    else:
        (da_hbm,) = take(1)
    middle = pair == 1
    if middle:
        layer_hbm, layer_far_hbm = take(2)
    if last:
        wq_hbm, wk_hbm, wv_hbm, gain = take(4)
    if first:
        (wo_hbm,) = take(1)
    normed_hbm, table_hbm = take(2)
    earlier = take(len(SIDES) - 1) if last else []
    sent = [] if first else take(2) if n_seq == 8 else []
    if last:
        (second_in,) = take(1)
    (keep_out,) = take(1)
    packed = n_seq == 8
    if not (last and packed):
        (send_out,) = take(1)
    if first:
        dhb_out, second, da_out = take(3)
    if middle:
        layer_stay, layer_leave = take(2)
    if last:
        norm_keep, norm_send, gains = take(3)
        if packed:
            send_out = norm_send.at[pl.ds(MAXLEN, norm_send.shape[0] - MAXLEN), :]
    else:
        (d_out,) = take(1)
    plane = take(4) if sent else []
    q, k, v, o, lse, normed, table, sems = take(8)
    da, da_t, q_t, dk_t, dv_t, dq, grads = take(7)
    (shifts,) = take(1)
    if first:
        hidden, dyb, mine, theirs, attn, out_grad, wo = take(7)
        dhb = dhb_out
    if middle:
        layer, layer_far = take(2)
    if last:
        before, joined, gain_rows, weights = take(4)
    before_sent = take(2) if sent else []
    core = s[CORE]
    width = normed.shape[1]
    zero = jnp.zeros((), bf16)
    pairs = len(SIDES)
    heads = pairs * PAIR
    copies = []

    def fetch(source, target):
        copy = pltpu.make_async_copy(source, target, sems.at[len(copies)])
        copy.start()
        copies.append(copy)
        return copy

    lanes_of = lambda m: slice((m * pairs + pair) * PAIR, (m * pairs + pair + 1) * PAIR)
    chunks = [slice(t * PIECE, (t + 1) * PIECE) for t in range(GROUP)]
    chunk_copies = []
    if first:
        for rows in chunks:
            chunk_copies.append(
                [
                    fetch(source.at[rows, :], target.at[rows, :])
                    for source, target in (
                        (mine_hbm, mine),
                        (theirs_hbm, theirs),
                        (hidden_hbm, hidden),
                        (dyb_hbm, dyb),
                    )
                ]
            )
    if first:
        wo_copies = [
            fetch(
                wo_hbm.at[pl.ds(pl.multiple_of(core * heads + head * HEAD_FEATURES, HEAD_FEATURES), HEAD_FEATURES), :],
                wo.at[index * HEAD_FEATURES : (index + 1) * HEAD_FEATURES, :],
            )
            for index, head in enumerate(HEAD_ORDER)
        ]
    else:
        wo_copies = [fetch(da_hbm.at[:, pair * PAIR : (pair + 1) * PAIR], da)]
    q_copies = [
        fetch(qkv_hbm.at[:, lanes_of(0)], q),
        fetch(qkv_hbm.at[:, lanes_of(1)], k),
        fetch(qkv_hbm.at[:, lanes_of(2)], v),
        fetch(attn_hbm.at[:, pair * PAIR : (pair + 1) * PAIR], o),
        fetch(lse_hbm.at[pair], lse),
    ]

    def fetch_late():
        late = [fetch(normed_hbm, normed), fetch(table_hbm, table)]
        late += [fetch(source, target) for source, target in zip(sent, before_sent)]
        if last:
            for m, w in enumerate((wq_hbm, wk_hbm, wv_hbm)):
                late.append(fetch(w.at[:, pl.ds(pl.multiple_of(core * heads, PAIR), heads)], weights.at[m]))
            for at, source in enumerate(earlier):
                late.append(fetch(source, before.at[:, at * heads : (at + 1) * heads]))
        if first:
            late.append(fetch(attn_hbm, attn))
        if middle:
            late += [fetch(layer_hbm, layer), fetch(layer_far_hbm, layer_far)]
        return late

    late_copies = fetch_late()
    if first:
        scale = gain[1:2, :].astype(f32)
        sums = jnp.zeros((1, width), f32)
        for rows, waiting in zip(chunks, chunk_copies):
            for copy in waiting:
                copy.wait()
            h = hidden[rows, :].astype(f32)
            r = lax.rsqrt(jnp.mean(h * h, axis=-1, keepdims=True) + epsilon)
            g = mine[rows, :].astype(f32) + theirs[rows, :].astype(f32)
            sums = sums + jnp.sum(g * h * r, axis=0, keepdims=True)
            scaled = g * scale
            inner = jnp.mean(scaled * h, axis=-1, keepdims=True)
            d = dyb[rows, :].astype(f32) + r * scaled - h * (r * r * r) * inner
            dhb[rows, :] = d.astype(bf16)
        second[...] = sums * 0.5
    for copy in wo_copies:
        copy.wait()
    if first:
        for t, rows in enumerate(chunks):
            d = mm_nt(dhb[rows, :], wo[...])
            da_out[rows, :] = jnp.where(slots(t * PIECE) < s[LENGTH], d, 0.0).astype(bf16)
        da[...] = da_out[:, :PAIR]
    da_t[...] = jnp.transpose(da[...])
    for copy in q_copies:
        copy.wait()
    q_t[...] = jnp.transpose(q[...])
    shifts[...] = jnp.transpose(lse[...]) * LOG2E

    row = lax.broadcasted_iota(jnp.int32, (PIECE, PIECE), 0)
    col = lax.broadcasted_iota(jnp.int32, (PIECE, PIECE), 1)

    def score(a, h):
        at = a * PIECE
        mask = head_mask(h)
        qh = jnp.where(mask, q[at : at + PIECE, :], zero)
        gh = jnp.where(mask, da[at : at + PIECE, :], zero)
        near = mm_nt(qh, k[at : at + PIECE, :]), mm_nt(gh, v[at : at + PIECE, :])
        far = (mm_nt(qh, k[:at, :]), mm_nt(gh, v[:at, :])) if a else None
        return near, far

    def back(a, h, near, far):
        at = a * PIECE
        rows = slice(at, at + PIECE)
        feats = slice(h * HEAD_FEATURES, (h + 1) * HEAD_FEATURES)
        mask = head_mask(h)
        shift = shifts[rows, h : h + 1]
        product = da[rows, :].astype(f32) * o[rows, :].astype(f32)
        inner = jnp.sum(jnp.where(mask, product, 0.0), axis=-1, keepdims=True)
        near_prob = jnp.exp2(jnp.where(row >= col, near[0] * LOG2E - shift, masked_score))
        near_ds = (near_prob * (near[1] - inner)).astype(bf16)
        query_grad = mm(near_ds, jnp.where(mask, k[rows, :], zero))
        parts = [(rows, near_prob.astype(bf16), near_ds)]
        if a:
            far_prob = jnp.exp2(far[0] * LOG2E - shift)
            far_ds = (far_prob * (far[1] - inner)).astype(bf16)
            query_grad = query_grad + mm(far_ds, jnp.where(mask, k[:at, :], zero))
            parts.append((slice(0, at), far_prob.astype(bf16), far_ds))
        for cols, prob, ds in parts:
            value_grad = mm(da_t[feats, rows], prob)
            key_grad = mm(q_t[feats, rows], ds)
            if a == GROUP - 1:
                dv_t[feats, cols] = value_grad
                dk_t[feats, cols] = key_grad
            else:
                dv_t[feats, cols] += value_grad
                dk_t[feats, cols] += key_grad
        return query_grad

    units = [(a, h) for a in reversed(range(GROUP)) for h in range(2)]
    ahead = score(*units[0])
    held = None
    for at, (a, h) in enumerate(units):
        now = ahead
        if at + 1 < len(units):
            ahead = score(*units[at + 1])
        g = back(a, h, *now)
        if h == 0:
            held = g
        else:
            dq[a * PIECE : (a + 1) * PIECE, :] = held + g

    for copy in late_copies:
        copy.wait()
    if sent:
        plane_blocks(s, *before_sent, plane, width // n_seq // 2, pair == 1)
    d = jnp.concatenate(
        [
            rotate(dq[...] * (1.0 / math.sqrt(HEAD_FEATURES)), table, -1).astype(bf16),
            rotate(jnp.transpose(dk_t[...]), table, -1).astype(bf16),
            jnp.transpose(dv_t[...].astype(bf16)),
        ],
        axis=1,
    )
    if last:
        before[:, (pairs - 1) * heads :] = d
    else:
        d_out[...] = d
    grads[...] = mm_tn(normed[...], d)

    rows = width // n_seq
    half_row = rows // 2
    if rows % 16:
        keep_out[:width, :] = grads[...].astype(bf16)
    else:
        left_x = SIDES[pair][0] * 2 // pairs
        for target, place in ((keep_out, core), (send_out, 1 - core)):
            for z in range(n_seq // 2):
                at = pl.ds(pl.multiple_of((2 * z + place) * rows, 8), rows)
                for m in range(3):
                    lanes = slice(m * PAIR, (m + 1) * PAIR)
                    left, right = pack_rows(grads[at, lanes])
                    for x_of, value in ((left_x, left), (1 - left_x, right)):
                        to = (2 * z + x_of) * half_row
                        target[to : to + half_row, lanes] = value.astype(bf16)

    if middle:
        for target, half in ((layer_leave, s[OTHER_CHIP]), (layer_stay, s[CHIP])):
            value = layer[half] + layer_far[half].astype(f32)
            live = slots(half * 2 * PIECE + core * PIECE) < s[LENGTH]
            target[...] = jnp.where(live, value, 0.0).astype(bf16)
    if first:
        g = mm_tn(attn[...], dhb[...])
        for index, head in enumerate(HEAD_ORDER):
            out_grad[head * HEAD_FEATURES : (head + 1) * HEAD_FEATURES, :] = g[
                index * HEAD_FEATURES : (index + 1) * HEAD_FEATURES, :
            ]
        if rows % 16:
            keep_out[width:, :] = jnp.concatenate([out_grad[:, :heads], out_grad[:, heads:]], axis=0).astype(bf16)
        else:
            column = width // 4
            for target, place in ((keep_out, core), (send_out, 1 - core)):
                for z in range(n_seq // 4):
                    block = out_grad[pl.ds(pl.multiple_of((2 * z + place) * rows, 8), rows), :]
                    for b in range(4):
                        lanes = slice(b * column, (b + 1) * column)
                        to = (n_seq + 4 * z + b) * half_row
                        target[to : to + half_row, :] = jnp.concatenate(
                            [block[:half_row, lanes], block[half_row:, lanes]], axis=1
                        ).astype(bf16)
    if last:
        for p, side in enumerate(SIDES):
            for m in range(3):
                at = p * heads + m * PAIR
                joined[:, at : at + PAIR] = pair_of(weights[m], side)
        sums = jnp.zeros((1, width), f32)
        for half in range(2):
            for target, place in ((norm_send, 1 - core), (norm_keep, core)):
                where = piece_rows(half, place)
                part = mm_nt(before[where, :], joined[...])
                if target is norm_keep:
                    target[half] = part.astype(bf16)
                else:
                    for side in range(2):
                        at = (2 * half + side) * PIECE
                        target[at : at + PIECE, :] = part[:, side * heads : (side + 1) * heads].astype(bf16)
                sums = sums + jnp.sum(part * normed[where, :].astype(f32), axis=0, keepdims=True)
        sums = sums / gain[0:1, :].astype(f32)
        gain_rows[...] = jnp.zeros_like(gain_rows)
        for index, value in enumerate((sums, second_in[...])):
            for part in range(2):
                gain_rows[2 * index + part : 2 * index + part + 1, :] = value[:, part * heads : (part + 1) * heads]
        high = gain_rows[...].astype(bf16)
        low = (gain_rows[...] - high.astype(f32)).astype(bf16)
        gains[...] = jnp.concatenate([high, low], axis=0)
        if rows % 16 == 0:
            send_out[n_seq * half_row :, :] = gains[...]


def attend_back(pair, scalars, qkv, attn, lse, given, wo, weights, gains, normed, table, earlier, n_seq, sent=()):
    first, last = pair == 0, pair == len(SIDES) - 1
    heads = attn.shape[1]
    width = wo.shape[1]
    rows = width // n_seq
    token_shape = (2, PIECE, width)
    if rows % 16 == 0:
        count = n_seq * rows // 2 * (2 if first else 1)
        shapes = [(count, heads)] * 2
    else:
        shapes = [(2 * width if first else width, heads), (8, 128)]
    extra = shapes[1][0] + 16 if n_seq == 8 else 0
    outs = [sds(a, bf16) for a in shapes[: 1 if last and n_seq == 8 else 2]]
    hbm = pl.BlockSpec(memory_space=pl.ANY)
    given, later = list(given), []
    given_specs = [hbm] * len(given)
    if first:
        outs += [sds((MAXLEN, width), bf16), sds((1, width), f32), sds((MAXLEN, heads), bf16)]
        given_specs[4] = whole((2, width))
        given.append(wo)
        given_specs.append(hbm)
    if pair == 1:
        outs += [sds((PIECE, width), bf16)] * 2
    if last:
        outs += [sds(token_shape, bf16), sds((MAXLEN + extra, heads), bf16), sds((16, heads), bf16)]
        given += [*weights, gains]
        given_specs += [hbm] * 3 + [whole((2, width))]
    else:
        outs += [sds((MAXLEN, heads), bf16)]
    outs += [sds((2 * rows * (2 if pair == 1 else 1), heads), bf16)] * (4 if sent else 0)
    later = list(earlier[: len(SIDES) - 1]) + list(sent) + list(earlier[len(SIDES) - 1 :])
    args = [qkv, attn, lse, *given, normed, table, *later]
    in_specs = [hbm] * 3 + given_specs + [hbm] * (2 + len(later))
    if last:
        in_specs[-1] = whole((1, width))
    scratch = [
        pltpu.VMEM((MAXLEN, PAIR), bf16),
        pltpu.VMEM((MAXLEN, PAIR), bf16),
        pltpu.VMEM((MAXLEN, PAIR), bf16),
        pltpu.VMEM((MAXLEN, PAIR), bf16),
        pltpu.VMEM((8, MAXLEN), f32),
        pltpu.VMEM((MAXLEN, width), bf16),
        pltpu.VMEM((2, MAXLEN, PAIR), f32),
        pltpu.SemaphoreType.DMA((48,)),
        pltpu.VMEM((MAXLEN, PAIR), bf16),
        pltpu.VMEM((PAIR, MAXLEN), bf16),
        pltpu.VMEM((PAIR, MAXLEN), bf16),
        pltpu.VMEM((PAIR, MAXLEN), f32),
        pltpu.VMEM((PAIR, MAXLEN), f32),
        pltpu.VMEM((MAXLEN, PAIR), f32),
        pltpu.VMEM((width, heads), f32),
        pltpu.VMEM((MAXLEN, 8), f32),
    ]
    if first:
        scratch += [pltpu.VMEM((MAXLEN, width), bf16)] * 4
        scratch += [
            pltpu.VMEM((MAXLEN, heads), bf16),
            pltpu.VMEM((heads, width), f32),
            pltpu.VMEM((heads, width), bf16),
        ]
    if pair == 1:
        scratch += [pltpu.VMEM(token_shape, f32), pltpu.VMEM(token_shape, bf16)]
    if last:
        scratch += [
            pltpu.VMEM((MAXLEN, len(SIDES) * heads), bf16),
            pltpu.VMEM((width, len(SIDES) * heads), bf16),
            pltpu.VMEM((8, heads), f32),
            pltpu.VMEM((3, width, heads), bf16),
        ]
    if sent:
        scratch += [pltpu.VMEM(a.shape, bf16) for a in sent]
    return call(
        functools.partial(attend_back_body, pair, n_seq),
        (1,),
        in_specs,
        [whole(a.shape) for a in outs],
        outs,
        scratch=scratch,
    )(scalars, *args)


def feed_body(
    packed, s, x_hbm, dy_hbm, dy_pair_hbm, dy_far_hbm, dy_far_pair_hbm, attn_hbm, attn_pair_hbm, wo_hbm, gain, *refs
):
    refs = list(refs)
    take = lambda count: [refs.pop(0) for _ in range(count)]
    wg_hbm, wu_hbm, wd_hbm = take(3)
    hidden_out, dyb_out, dn_out, layer_out, send_out = take(5)
    grads_out = take(6 if packed else 3)
    x, attn, wo, wg, wu, wd, dyb = take(7)
    hidden, hidden_low, low, low_t, dyb_t, acts, dgs, dus, dn, layer, send = take(11)
    blocks = take(12)
    (sems,) = take(1)
    core = s[CORE]
    tokens, width = x.shape
    heads = width // 2
    steps = 4
    cols = wg.shape[1] // steps
    used = [0]

    def copy(source, target):
        made = pltpu.make_async_copy(source, target, sems.at[used[0]])
        used[0] += 1
        made.start()
        return made

    chunks = [slice(t * PIECE, (t + 1) * PIECE) for t in range(GROUP)]
    unit = [2 * ((3 - step) ^ s[OWN_B]) + core for step in range(steps)]

    wo_copies = [
        copy(
            wo_hbm.at[pl.ds(pl.multiple_of(place * heads + head * HEAD_FEATURES, HEAD_FEATURES), HEAD_FEATURES), :],
            wo.at[at * heads + index * HEAD_FEATURES : at * heads + (index + 1) * HEAD_FEATURES, :],
        )
        for at, place in enumerate((core, 1 - core))
        for index, head in enumerate(HEAD_ORDER)
    ]
    token_copies = [
        [
            copy(x_hbm.at[rows, :], x.at[rows, :]),
            copy(attn_hbm.at[rows, :], attn.at[rows, :heads]),
            copy(attn_pair_hbm.at[rows, :], attn.at[rows, heads:]),
        ]
        for rows in chunks
    ]
    def weights_of(step):
        at = pl.ds(pl.multiple_of(unit[step] * cols, cols), cols)
        here = slice(step * cols, (step + 1) * cols)
        return [
            copy(wg_hbm.at[:, at], wg.at[:, here]),
            copy(wu_hbm.at[:, at], wu.at[:, here]),
            copy(wd_hbm.at[at, :], wd.at[here, :]),
        ]

    dy_copies = [
        copy(source, dyb.at[piece_rows(half, place), :])
        for source, half, place in (
            (dy_hbm.at[s[CHIP]], s[CHIP], core),
            (dy_pair_hbm.at[s[CHIP]], s[CHIP], 1 - core),
            (dy_far_hbm.at[0], s[OTHER_CHIP], core),
            (dy_far_pair_hbm.at[0], s[OTHER_CHIP], 1 - core),
        )
    ]
    out_copies, side_copies = [], []

    for made in wo_copies:
        made.wait()
    scale = gain[1:2, :].astype(f32)
    weight_copies = [weights_of(0)]
    for t, rows in enumerate(chunks):
        for made in token_copies[t]:
            made.wait()
        h = x[rows, :].astype(f32) + mm(attn[rows, :], wo[...])
        hidden[rows, :] = h
        hidden_low[rows, :] = h.astype(bf16)
        out_copies.append(copy(hidden_low.at[rows, :], hidden_out.at[rows, :]))
        r = lax.rsqrt(jnp.mean(h * h, axis=-1, keepdims=True) + epsilon)
        low[rows, :] = (h * r * scale).astype(bf16)
    low_t[...] = jnp.transpose(low[...])
    for made in dy_copies:
        made.wait()
    for t, rows in enumerate(chunks):
        dyb[rows, :] = jnp.where(slots(t * PIECE) < s[LENGTH], dyb[rows, :], jnp.zeros((), bf16))
    dyb_t[...] = jnp.transpose(dyb[...])
    out_copies.append(copy(dyb, dyb_out))

    def products(step, t):
        if t == 0:
            for made in weight_copies.pop():
                made.wait()
            if step + 1 < steps:
                weight_copies.append(weights_of(step + 1))
        rows, here = chunks[t], slice(step * cols, (step + 1) * cols)
        return mm(low[rows, :], wg[:, here]), mm(low[rows, :], wu[:, here]), mm_nt(dyb[rows, :], wd[here, :])

    def pointwise(step, t, gate, up, dact):
        rows, here = chunks[t], slice(step * cols, (step + 1) * cols)
        sig = 1.0 / (1.0 + jnp.exp2(gate * -LOG2E))
        silu = gate * sig
        acts[rows, here] = (silu * up).astype(bf16)
        dgs[rows, here] = (dact * up * (sig + silu * (1.0 - sig))).astype(bf16)
        dus[rows, here] = (dact * silu).astype(bf16)

    def weight_grads(step, which):
        here = slice(step * cols, (step + 1) * cols)
        left, right = ((low_t, dgs), (low_t, dus), (dyb_t, acts))[which]
        grad = blocks[3 * step + which]
        grad[...] = mm(left[...], right[:, here]).astype(bf16)
        if not packed:
            at = pl.ds(pl.multiple_of(unit[step] // 2 * cols, cols), cols)
            out_copies.append(copy(grad, grads_out[which].at[:, at]))
            return
        rows = width // 4
        y, x = (3 - step) // 2, (3 - step) % 2
        own = s[OWN_B] if which == 2 else s[OWN_Z]
        z = (unit[step] // 2) ^ s[OWN_Z]
        for high in range(2):
            for low_bit in range(2):
                source = grad.at[pl.ds(pl.multiple_of(((2 * high + low_bit) ^ own) * rows, 16), rows), :]
                if which == 0:
                    out_copies.append(copy(source, grads_out[0 if x else 1].at[y, low_bit, high]))
                elif which == 1:
                    out_copies.append(copy(source, grads_out[2 if y else 3].at[low_bit, x, high]))
                else:
                    sem = sems.at[used[0]]
                    used[0] += 1
                    for side, target in ((1, grads_out[4]), (0, grads_out[5])):
                        made = pltpu.make_async_copy(source, target.at[low_bit, high, z // 2], sem)
                        pl.when(z % 2 == side)(made.start)
                        side_copies.append((z % 2 == side, made))

    units = [(step, t) for step in range(steps) for t in range(GROUP)]
    ahead = products(*units[0])
    for index, (step, t) in enumerate(units):
        now = ahead
        if index + 1 < len(units):
            ahead = products(*units[index + 1])
        pointwise(step, t, *now)
        if step and t < 3:
            weight_grads(step - 1, t)
    for which in range(3):
        weight_grads(steps - 1, which)
    for half in range(2):
        send[half] = mm(acts[piece_rows(half, 1 - core), :], wd[...]).astype(bf16)
        out_copies.append(copy(send.at[half], send_out.at[half]))
    for half in range(2):
        rows = piece_rows(half, core)
        layer[half] = hidden[rows, :] + mm(acts[rows, :], wd[...])
        out_copies.append(copy(layer.at[half], layer_out.at[half]))
    for rows in chunks:
        dn[rows, :] = (mm_nt(dgs[rows, :], wg[...]) + mm_nt(dus[rows, :], wu[...])).astype(bf16)
        out_copies.append(copy(dn.at[rows, :], dn_out.at[rows, :]))
    for made in out_copies:
        made.wait()
    for when, made in side_copies:
        pl.when(when)(made.wait)


def feed(scalars, x, dy, dy_pair, dy_far, dy_far_pair, attn, attn_pair, wo, gain, wg, wu, wd, packed):
    tokens, width = x.shape
    units = wg.shape[1] // 2
    cols = units // 4
    token_shape = (2, PIECE, width)
    if packed:
        shapes = [(2, 2, 2, width // 4, cols)] * 6
    else:
        shapes = [(width, units)] * 3
    outs = [
        sds((tokens, width), bf16),
        sds((tokens, width), bf16),
        sds((tokens, width), bf16),
        sds(token_shape, f32),
        sds(token_shape, bf16),
    ] + [sds(a, bf16) for a in shapes]
    args = [x, dy, dy_pair, dy_far, dy_far_pair, attn, attn_pair, wo, gain, wg, wu, wd]
    in_specs = [pl.BlockSpec(memory_space=pl.ANY)] * len(args)
    in_specs[8] = whole((2, width))
    low = pltpu.VMEM((tokens, width), bf16)
    high = pltpu.VMEM((tokens, width), f32)
    turned = pltpu.VMEM((width, tokens), bf16)
    hidden_units = pltpu.VMEM((tokens, units), bf16)
    return call(
        functools.partial(feed_body, packed),
        (1,),
        in_specs,
        [pl.BlockSpec(memory_space=pl.ANY)] * len(outs),
        outs,
        scratch=[
            low,
            low,
            pltpu.VMEM((width, width), bf16),
            pltpu.VMEM((width, units), bf16),
            pltpu.VMEM((width, units), bf16),
            pltpu.VMEM((units, width), bf16),
            low,
            high,
            low,
            low,
            turned,
            turned,
            hidden_units,
            hidden_units,
            hidden_units,
            low,
            pltpu.VMEM(token_shape, f32),
            pltpu.VMEM(token_shape, bf16),
        ]
        + [pltpu.VMEM((width, cols), bf16)] * 12
        + [pltpu.SemaphoreType.DMA((112,))],
    )(scalars, *args)


def piece_of(half, side):
    return pl.ds(pl.multiple_of((2 * half + side) * PIECE, PIECE), PIECE)


def finish_body(s, x, keep, recv, dh, gain, stay, leave):
    scale = gain[0:1, :].astype(f32)
    for out, half in ((leave, s[OTHER_CHIP]), (stay, s[CHIP])):
        h = x[half, 0].astype(f32)
        there = jnp.concatenate([recv[piece_of(half, side), :] for side in range(2)], axis=1)
        dn = keep[half].astype(f32) + there.astype(f32)
        r = lax.rsqrt(jnp.mean(h * h, axis=-1, keepdims=True) + epsilon)
        scaled = dn * scale
        inner = jnp.mean(scaled * h, axis=-1, keepdims=True)
        out[...] = (dh[half, 0].astype(f32) + r * scaled - h * (r * r * r) * inner).astype(bf16)


def finish(scalars, x, keep, recv, dh, gain):
    width = x.shape[1]
    shape = (2, PIECE, width)
    own = pl.BlockSpec((2, 1, PIECE, width), lambda f, s: (0, s[CORE], 0, 0))
    return call(
        finish_body,
        (1,),
        [own, whole(shape), whole((MAXLEN, recv.shape[1])), own, whole((2, width))],
        [whole((PIECE, width))] * 2,
        [sds((PIECE, width), bf16)] * 2,
    )(scalars, x.reshape(2, 2, PIECE, width), keep, recv, dh.reshape(2, 2, PIECE, width), gain)


def decode(coded):
    return coded[:8].astype(f32) + coded[8:].astype(f32)


def encode(value):
    high = value.astype(bf16)
    return jnp.concatenate([high, (value - high.astype(f32)).astype(bf16)], axis=0)


def sum_parts(fetch, groups, scratch):
    loads = []
    for group in groups:
        loads.append([])
        for source in group:
            target = scratch.pop(0)
            loads[-1].append((fetch(source, target), target))

    def total(group):
        value = None
        for made, target in group:
            made.wait()
            part = target[...].astype(f32)
            value = part if value is None else value + part
        return value

    return [functools.partial(total, group) for group in loads]


def fetcher(sems):
    used = [0]

    def fetch(source, target):
        made = pltpu.make_async_copy(source, target, sems.at[used[0]])
        used[0] += 1
        made.start()
        return made

    return fetch


def feed_step_body(paths, s, *refs):
    refs = list(refs)
    groups = [[refs.pop(0).at[path] for path in group] for group in paths]
    outs = [refs.pop(0) for _ in groups]
    sems = refs.pop()
    for out, total in zip(outs, sum_parts(fetcher(sems), groups, refs)):
        out[...] = total().astype(bf16)


def feed_step(scalars, reductions):
    groups = [r.paths(1) for r in reductions]
    args = [array for group in groups for array, _ in group]
    paths = [[path for _, path in group] for group in groups]
    slices = [array.shape[len(path) :] for group in groups for array, path in group]
    outs = [sds(group[0][0].shape[len(group[0][1]) :], bf16) for group in groups]
    return call(
        functools.partial(feed_step_body, paths),
        (1,),
        [pl.BlockSpec(memory_space=pl.ANY)] * len(args),
        [whole(a.shape) for a in outs],
        outs,
        scratch=[pltpu.VMEM(a, bf16) for a in slices] + [pltpu.SemaphoreType.DMA((len(args),))],
    )(scalars, *args)


def third_step_body(paths, s, keep_hbm, arrived_hbm, gains, *refs):
    refs = list(refs)
    groups = [[refs.pop(0).at[path] for path in group] for group in paths]
    parts_hbm = [refs.pop(0) for _ in range(4)]
    plane = [refs.pop(0) for _ in range(4)]
    line_send, line_keep = refs.pop(0), refs.pop(0)
    sends, kept = refs.pop(0), refs.pop(0)
    keep, arrived = refs.pop(0), refs.pop(0)
    parts = [refs.pop(0) for _ in range(4)]
    sems = refs.pop()
    fetch = fetcher(sems)
    rows = keep.shape[0] // 8
    first = [
        fetch(keep_hbm, keep),
        fetch(arrived_hbm.at[pl.ds(MAXLEN, arrived.shape[0]), :], arrived),
    ]
    second = [fetch(source, target) for source, target in zip(parts_hbm, parts)]
    totals = sum_parts(fetch, groups, refs)
    for made in first:
        made.wait()
    plane_blocks(s, keep, arrived, plane, rows, False)
    coded = encode(decode(gains[...]) + decode(arrived[8 * rows :, :]))
    for target in plane:
        target[4 * rows :, :] = coded
    for made in second:
        made.wait()
    size = line_keep.shape[0] // 2
    own = s[OWN_Z] % 2
    for target, z0 in ((line_send, 1 - own), (line_keep, own)):
        for z1 in range(2):
            at = pl.ds(pl.multiple_of((2 * z1 + z0) * size, 16), size)
            total = None
            for part in parts:
                value = part[at, :].astype(f32)
                total = value if total is None else total + value
            target[z1 * size : (z1 + 1) * size, :] = total.astype(bf16)
    for index in range(3):
        sends[index] = totals[index]().astype(bf16)
        kept[index] = totals[3 + index]()


def third_step(scalars, keep, arrived, gains, parts, reductions):
    groups = [r.paths(1) for r in reductions] + [r.paths(0) for r in reductions]
    sums = [array for group in groups for array, _ in group]
    paths = [[path for _, path in group] for group in groups]
    slices = [array.shape[len(path) :] for group in groups for array, path in group]
    rows, columns = keep.shape
    outs = [sds((rows // 2 + 16, columns), bf16)] * 4
    outs += [sds((parts[0].shape[0] // 2, columns), bf16)] * 2
    outs += [sds((3,) + slices[0], bf16), sds((3,) + slices[0], f32)]
    hbm = pl.BlockSpec(memory_space=pl.ANY)
    return call(
        functools.partial(third_step_body, paths),
        (1,),
        [hbm, hbm, whole(gains.shape)] + [hbm] * (len(sums) + 4),
        [whole(a.shape) for a in outs],
        outs,
        scratch=[pltpu.VMEM(keep.shape, bf16), pltpu.VMEM((rows + 16, columns), bf16)]
        + [pltpu.VMEM(a.shape, bf16) for a in parts]
        + [pltpu.VMEM(a, bf16) for a in slices]
        + [pltpu.SemaphoreType.DMA((len(sums) + 6,))],
    )(scalars, keep, arrived, gains, *sums, *parts)


def second_line_body(s, *refs):
    refs = list(refs)
    take = lambda count: [refs.pop(0) for _ in range(count)]
    middle_hbm, last_hbm, line_hbm = take(4), take(4), take(2)
    layer_stay_hbm, layer_back_hbm = take(2)
    lines, (last_keep,) = take(4), take(1)
    (layer_out,) = take(1)
    middle, last, (keep0, arrived0) = take(4), take(4), take(2)
    (sems,) = take(1)
    fetch = fetcher(sems)
    first = [fetch(a, b) for a, b in zip(middle_hbm + last_hbm + line_hbm, middle + last + [keep0, arrived0])]
    third = [
        fetch(layer_stay_hbm, layer_out.at[s[CHIP]]),
        fetch(layer_back_hbm, layer_out.at[s[OTHER_CHIP]]),
    ]
    for made in first:
        made.wait()
    rows = middle[0].shape[0] // 4
    coded = [ref[4 * rows :, :] for ref in last]
    gains = encode((decode(coded[0]) + decode(coded[1])) + (decode(coded[2]) + decode(coded[3])))
    for r, target in enumerate(lines):
        at = pl.ds(pl.multiple_of((s[OWN_Z] ^ r) * rows, 16), rows)
        for index, parts in enumerate((middle, last)):
            total = None
            for part in parts:
                value = part[at, :].astype(f32)
                total = value if total is None else total + value
            target[index * rows : (index + 1) * rows, :] = total.astype(bf16)
        target[2 * rows : 2 * rows + 16, :] = gains
    size = keep0.shape[0] // 2
    own = s[OWN_Z] // 2
    for target, z1 in ((last_keep, own), (lines[2].at[2 * rows + 16 :, :], 1 - own)):
        at = pl.ds(pl.multiple_of(z1 * size, 16), size)
        target[...] = (keep0[at, :].astype(f32) + arrived0[at, :].astype(f32)).astype(bf16)
    for made in third:
        made.wait()


def second_line(scalars, middle, last, keep0, arrived0, layer_stay, layer_back):
    rows, columns = middle[0].shape[0] // 4, middle[0].shape[1]
    size = keep0.shape[0] // 2
    outs = [sds((2 * rows + 16 + (size if r == 2 else 0), columns), bf16) for r in range(4)]
    outs += [sds((size, columns), bf16)]
    outs += [sds((2,) + layer_stay.shape, bf16)]
    args = [*middle, *last, keep0, arrived0, layer_stay, layer_back]
    return call(
        second_line_body,
        (1,),
        [pl.BlockSpec(memory_space=pl.ANY)] * len(args),
        [whole(a.shape) for a in outs],
        outs,
        scratch=[pltpu.VMEM(a.shape, a.dtype) for a in args[:-2]] + [pltpu.SemaphoreType.DMA((len(args),))],
    )(scalars, *args)


def feed_total_body(s, feed_keep, feed_arrived, side_keep, side_send, down_out):
    rows = side_keep.shape[1]
    for index in range(2):
        value = feed_keep[index] + feed_arrived[index].astype(f32)
        for part in range(2):
            block = value[part * rows : (part + 1) * rows]

            @pl.when(s[CORE] == part)
            def _():
                side_keep[index] = block

            @pl.when(s[CORE] != part)
            def _():
                side_send[index] = block.astype(bf16)

    down_out[...] = feed_keep[2] + feed_arrived[2].astype(f32)

def feed_total(scalars, keep, arrived):
    rows, cols = keep.shape[1:]
    outs = [sds((2, rows // 2, cols), f32), sds((2, rows // 2, cols), bf16), sds((rows, cols), f32)]
    args = [keep, arrived]
    return call(
        feed_total_body,
        (1,),
        [whole(a.shape) for a in args],
        [whole(a.shape) for a in outs],
        outs,
    )(scalars, *args)


def shards_body(s, keep0, line0, line1, line2, line3, side_keep, side_arrived, stay, back, *outs):
    half, width = outs[0].shape[0] // 2, outs[0].shape[1]
    count = line0.shape[0]
    first = keep0[...].astype(f32) + line2[count:, :].astype(f32)
    rest = (line0[...].astype(f32) + line1[...].astype(f32)) + (
        line2[:count, :].astype(f32) + line3[...].astype(f32)
    )
    out = first[half:]
    outs[3][:half, :] = out[:, :width]
    outs[3][half:, :] = out[:, width:]
    for pair, part in enumerate((first[:half], rest[:half], rest[half : 2 * half])):
        lanes = slice(pair * HEAD_FEATURES, (pair + 1) * HEAD_FEATURES)
        for m in range(3):
            at = m * PAIR
            outs[m][:half, lanes] = part[:, at : at + HEAD_FEATURES]
            outs[m][half:, lanes] = part[:, at + HEAD_FEATURES : at + PAIR]
    gains = rest[2 * half : 2 * half + 8] + rest[2 * half + 8 :]
    for index in range(2):
        row = jnp.concatenate([gains[2 * index : 2 * index + 1], gains[2 * index + 1 : 2 * index + 2]], axis=1)
        for at in range(outs[6].shape[0]):
            outs[6 + index][at : at + 1, :] = row[:, at * PAIR : (at + 1) * PAIR]
    cols = side_keep.shape[2]
    for index in range(2):
        for core in range(2):

            @pl.when(s[CORE] == core)
            def _():
                outs[4 + index][:, core * cols : (core + 1) * cols] = side_keep[index]
                outs[4 + index][:, (1 - core) * cols : (2 - core) * cols] = side_arrived[index].astype(f32)

    outs[8][s[CHIP]] = stay[...]
    outs[8][s[OTHER_CHIP]] = back[...]


def make_shards(scalars, args, rows, columns, width):
    side = sds((rows, 2 * args[5].shape[-1]), f32)
    outs = [sds((rows, columns), f32)] * 4 + [side] * 2 + [sds((width // PAIR, PAIR), f32)] * 2
    outs.append(sds((2,) + args[-1].shape, bf16))
    return call(
        shards_body,
        (1,),
        [whole(a.shape) for a in args],
        [whole(a.shape) for a in outs],
        outs,
    )(scalars, *args)


def exchange_by(block, axis, difference, name):
    count = lax.axis_size(axis)
    with jax.named_scope(name):
        return lax.ppermute(block, axis, [(a, a ^ difference) for a in range(count)])


def exchange(block, axis, bit, name="swap"):
    return exchange_by(block, axis, 1 << bit, name)


def pick(block, index, dim):
    return lax.dynamic_index_in_dim(block, index, dim, keepdims=False)


def together(*values):
    return lax.optimization_barrier(values)


X, Y, Z0, Z1 = ("batch", 0), ("batch", 1), ("seq", 1), ("seq", 2)


class Reduction:
    def __init__(self, order, keep, send):
        self.order, self.level, self.send, self.parts = order, 0, send, [keep]

    def go(self):
        bit = self.order[self.level]
        self.arrived = exchange(self.send, *bit, "feed_" + "_".join(map(str, bit)))
        return self

    def paths(self, side):
        found = []
        for index, array in enumerate([*self.parts, self.arrived]):
            found.append((array, (0,) * (self.level - max(index - 1, 0)) + (side,)))
        return found

    def next(self, send):
        self.parts.append(self.arrived)
        self.send = send
        self.level += 1
        return self


def start_all(reductions, *others):
    sends = together(*[r.send for r in reductions], *others)
    for r, send in zip(reductions, sends):
        r.send = send
        r.go()
    return sends[len(reductions) :]


def wait_all(reductions, *others):
    values = together(*[r.arrived for r in reductions], *others)
    for r, arrived in zip(reductions, values):
        r.arrived = arrived
    return values[len(reductions) :]


def body(
    states,
    lengths,
    first_gain,
    query_weight,
    key_weight,
    value_weight,
    output_weight,
    second_gain,
    gate_weight,
    up_weight,
    down_weight,
    cotangent,
):
    tokens, width = states.shape
    n_seq, n_batch = lax.axis_size("seq"), lax.axis_size("batch")
    packed = n_seq == 8 and n_batch == 4
    place = lax.axis_index("seq")
    batch = lax.axis_index("batch")
    core = place & 1
    chip = place >> 1 & 1
    sequence = (batch * (n_seq // GROUP) + place // GROUP) * 2 + chip
    length = pick(lengths, sequence, 0)
    own_b, own_z = batch & 3, place >> 1 & 3
    scalars = jnp.stack([core, chip, length, 1 - chip, own_b, own_z]).astype(jnp.int32)
    table = rope_tables()
    both_gains = jnp.stack([first_gain, second_gain])
    weights = (query_weight, key_weight, value_weight)

    held = states.reshape(2, PIECE, width)
    held_back = cotangent.reshape(2, PIECE, width)
    far = exchange(pick(held, 1 - chip, 0), *Z0, "states_far")[None]
    held_pair = exchange(held, "seq", 0, "states_pair")
    filled = project(scalars, held, held_pair, CHIP, both_gains, weights, table, None)
    far, leaving, *filled = together(far, pick(held_back, 1 - chip, 0), *filled)
    far_pair = exchange(far, "seq", 0, "states_far_pair")
    back_far = exchange(leaving, *Z0, "cotangent_far")[None]
    back_pair = exchange(held_back, "seq", 0, "cotangent_pair")
    qkv, normed, x, attn, lse = attend(scalars, far, far_pair, both_gains, weights, table, filled)
    attn_pair = exchange(attn, "seq", 0, "attn_pair")
    back_far, attn = together(back_far, attn)
    back_far_pair = exchange(back_far, "seq", 0, "cotangent_far_pair")
    hidden, dyb, dn, layer_keep, layer_send, *feed_grads = feed(
        scalars,
        x,
        held_back,
        back_pair,
        back_far,
        back_far_pair,
        attn,
        attn_pair,
        output_weight,
        both_gains,
        gate_weight,
        up_weight,
        down_weight,
        packed,
    )
    if packed:
        gate_send, gate_keep, up_send, up_keep, down_send, down_keep = feed_grads
        gate = Reduction([X, Y, Z0, Z1], gate_keep, gate_send).go()
        up = Reduction([Y, Z0, X, Z1], up_keep, up_send).go()
        down = Reduction([Z0, X, Y, Z1], down_keep, down_send).go()
    dn_pair = exchange(dn, "seq", 0, "dn_pair")

    def back(pair, given, later, sent=()):
        return attend_back(
            pair, scalars, qkv, attn, lse, given, output_weight, weights, both_gains, normed, table, later, n_seq, sent
        )

    keep0, send0, dhb, second, da, d0 = back(0, [hidden, dyb, dn, dn_pair, both_gains], [])

    def in_order(kept, arrived):
        return jnp.concatenate(
            [jnp.where(chip == 0, kept, arrived), jnp.where(chip == 0, arrived, kept)], axis=0
        )

    if packed:
        rows = width // n_seq // 2

        def to_plane(parts, name):
            return [parts[0]] + [exchange_by(parts[r], "batch", r, name + str(r)) for r in (1, 2, 3)]

        feeds = [gate, up, down]
        keep0, send0, dhb, second, da, d0, layer_send = wait_all(feeds, keep0, send0, dhb, second, da, d0, layer_send)
        layer_arrived = exchange(layer_send, "seq", 0, "layer_pair")
        arrived0 = exchange(send0, "seq", 0, "grad0_pair")
        for r, send in zip(feeds, feed_step(scalars, feeds)):
            r.next(send)
        (da,) = start_all(feeds, da)
        keep1, send1, layer_stay, layer_leave, d1, *plane0 = back(
            1, [da, layer_keep, layer_arrived], [], (keep0, arrived0)
        )

        keep1, send1, layer_stay, layer_leave, d1, *plane0 = wait_all(
            feeds, keep1, send1, layer_stay, layer_leave, d1, *plane0
        )
        arrived1 = exchange(send1, "seq", 0, "grad1_pair")
        flow0 = to_plane(plane0, "plane0_")
        for r, send in zip(feeds, feed_step(scalars, feeds)):
            r.next(send)
        (arrived1, d1) = start_all(feeds, arrived1, d1)
        keep2, norm_keep, norm_send, gains, *plane1 = back(2, [da], [d0, d1, second], (keep1, arrived1))

        flow0[1], flow0[2], flow0[3], keep2, norm_keep, norm_send, gains, layer_leave, *plane1 = wait_all(
            feeds, *flow0[1:], keep2, norm_keep, norm_send, gains, layer_leave, *plane1
        )
        norm_arrived = exchange(norm_send, "seq", 0, "dn1_pair")
        layer_back = exchange(layer_leave, *Z0, "layer_back")
        flow1 = to_plane(plane1, "plane1_")
        *plane2, line0_send, line0_keep, feed_send, feed_keep = third_step(
            scalars, keep2, norm_arrived, gains, flow0, feeds
        )
        line0_send, line0_keep, feed_send, feed_keep, layer_back, *planes = together(
            line0_send, line0_keep, feed_send, feed_keep, layer_back, *plane2, *flow1
        )
        plane2, flow1 = planes[:4], planes[4:]
        flow2 = to_plane(plane2, "plane2_")
        feed_arrived = exchange(feed_send, *Z1, "feed_last")
        arrived0 = exchange(line0_send, *Z0, "line0")
        norm_keep, line0_keep = together(norm_keep, line0_keep)
        stay, leave = finish(scalars, x, norm_keep, norm_arrived, dhb, both_gains)
        leave, stay, arrived0, *flow2 = together(leave, stay, arrived0, *flow2)
        grad_back = exchange(leave, *Z0, "grad_back")
        stay, layer_back, line0_keep, arrived0, *flow12 = together(stay, layer_back, line0_keep, arrived0, *flow1, *flow2)
        *lines, last_keep, layer_out = second_line(
            scalars, flow12[:4], flow12[4:], line0_keep, arrived0, layer_stay, layer_back
        )
        last_keep, feed_arrived, feed_keep = together(last_keep, feed_arrived, feed_keep)
        side_keep, side_send, down_grad = feed_total(scalars, feed_keep, feed_arrived)
        lines = [lines[0]] + [exchange_by(lines[r], "seq", 2 * r, "line12_" + str(r)) for r in (1, 2, 3)]
        side_arrived = exchange(side_send, "seq", 0, "feed_pair")
        down_grad, layer_out = jnp.transpose(down_grad), layer_out.reshape(tokens, width)
        *shards, gate_grad, up_grad, first, second, input_grad = make_shards(
            scalars,
            [last_keep, *lines, side_keep, side_arrived, stay, grad_back],
            2 * rows,
            width // n_batch,
            width,
        )
        first, second, input_grad = first.reshape(width), second.reshape(width), input_grad.reshape(tokens, width)
    else:
        layer_arrived = exchange(layer_send, "seq", 0)
        keep1, _, layer_stay, layer_leave, d1 = back(1, [da, layer_keep, layer_arrived], [])
        layer_back = exchange(layer_leave, *Z0)
        keep2, _, norm_keep, norm_send, gains = back(2, [da], [d0, d1, second])
        norm_arrived = exchange(norm_send, "seq", 0)
        stay, leave = finish(scalars, x, norm_keep, norm_arrived, dhb, both_gains)
        layer_out = in_order(layer_stay, layer_back)
        input_grad = in_order(stay, exchange(leave, *Z0))
        gains = gains[:8].astype(f32) + gains[8:].astype(f32)
        for axis in ("seq", "batch"):
            for bit in range(int(math.log2(lax.axis_size(axis)))):
                gains = gains + exchange(gains, axis, bit)
        first, second = gains[:2].reshape(width), gains[2:4].reshape(width)
        gate_keep, up_keep, down_keep = feed_grads
        units = gate_keep.shape[1]
        zeros = lambda shape: jnp.zeros(shape, bf16)
        blocks = 4

        def spread(array):
            parts = array.reshape(width, blocks, 1, units // blocks)
            full = zeros((width, blocks, 2, units // blocks))
            return lax.dynamic_update_slice_in_dim(full, parts, core, 2).reshape(width, 2 * units)

        heads = attn.shape[1]
        out_keep = jnp.concatenate([keep0[width : width + heads], keep0[width + heads :]], axis=1)
        columns = lambda a: lax.dynamic_update_slice_in_dim(zeros((width, width)), a, core * heads, 1)

        def by_head(m):
            found = {}
            for index, head in enumerate(HEAD_ORDER):
                at = m * PAIR + index % 2 * HEAD_FEATURES
                found[head] = (keep0, keep1, keep2)[index // 2][:width, at : at + HEAD_FEATURES]
            return jnp.concatenate([found[head] for head in sorted(found)], axis=1)

        full = [columns(by_head(m)) for m in range(3)]
        full.append(lax.dynamic_update_slice_in_dim(zeros((width, width)), out_keep, core * heads, 0))
        full += [spread(gate_keep), spread(up_keep), jnp.transpose(spread(down_keep))]
        full = [lax.psum_scatter(a.astype(f32), "seq", scatter_dimension=0, tiled=True) for a in full]
        full = [lax.psum_scatter(a, "batch", scatter_dimension=1, tiled=True) for a in full]
        shards, (gate_grad, up_grad, down_grad) = full[:4], full[4:]

    return (
        layer_out,
        input_grad,
        first,
        shards[0],
        shards[1],
        shards[2],
        shards[3],
        second,
        gate_grad,
        up_grad,
        down_grad,
    )


def solution(mesh):
    split = P(("batch", "seq"), None)
    in_specs = (split,) + (P(),) * 10 + (split,)
    shard = P("seq", "batch")
    out_specs = (split, split, P(), shard, shard, shard, shard, P(), shard, shard, shard)
    return jax.shard_map(body, mesh=mesh, in_specs=in_specs, out_specs=out_specs, check_vma=False)
```
